32 devices in a mesh: img: 8 (over z, x), ha: 4 (over y, core).
Axes of the slice: x: 2, y: 2, z: 4, core: 2. Of those that a mesh axis runs over, the one named last changes fastest.
Arguments:
- inputs: bfloat16 [128, 28, 28, 1024], P('img', 'ha'), may hold values from -6 to 6
- image_count: int32 [8], P('img'), may hold values from 8 to 16, as said below
- pixel_mask: int32 [128, 28, 28], P('img', 'ha'), may hold values 0 or 1
- w_first: bfloat16 [1024, 256], replicated, may hold values from -0.1875 to 0.1875
- gain_first: float32 [256], replicated, may hold values from 0.25 to 1.75
- bias_first: float32 [256], replicated, may hold values from -1.5 to 1.5
- w_group: bfloat16 [2, 3, 3, 128, 256], replicated, may hold values from -0.1875 to 0.1875
- gain_group: float32 [512], replicated, may hold values from 0.25 to 1.75
- bias_group: float32 [512], replicated, may hold values from -1.5 to 1.5
- w_squeeze: bfloat16 [256, 128], replicated, may hold values from -0.75 to 0.75
- gain_squeeze: float32 [128], replicated, may hold values from 0.25 to 1.75
- bias_squeeze: float32 [128], replicated, may hold values from -1.5 to 1.5
- w_excite: bfloat16 [128, 512], replicated, may hold values from -1 to 1
- bias_excite: float32 [512], replicated, may hold values from -2.5 to 2.5
- w_last: bfloat16 [256, 1024], replicated, may hold values from -0.375 to 0.375
- gain_last: float32 [1024], replicated, may hold values from 0.25 to 1.75
- bias_last: float32 [1024], replicated, may hold values from -1.5 to 1.5
- cotangent: bfloat16 [128, 28, 28, 1024], P('img', 'ha'), may hold values from -6 to 6
Outputs:
- output: bfloat16 [128, 28, 28, 1024], P('img', 'ha')
- grad_inputs: bfloat16 [128, 28, 28, 1024], P('img', 'ha')
- grad_w_first: float32 [1024, 256], replicated
- grad_gain_first: float32 [256], replicated
- grad_bias_first: float32 [256], replicated
- grad_w_group: float32 [2, 3, 3, 128, 256], replicated
- grad_gain_group: float32 [512], replicated
- grad_bias_group: float32 [512], replicated
- grad_w_squeeze: float32 [256, 128], replicated
- grad_gain_squeeze: float32 [128], replicated
- grad_bias_squeeze: float32 [128], replicated
- grad_w_excite: float32 [128, 512], replicated
- grad_bias_excite: float32 [512], replicated
- grad_w_last: float32 [256, 1024], replicated
- grad_gain_last: float32 [1024], replicated
- grad_bias_last: float32 [1024], replicated
The draws below stay inside these ranges and needn't reach their ends.
Inputs may be any that keep to these rules, and one draw needn't show every extreme that they name: `image_count`: some index of img has all 16 slots live and some has 8; live slots come first on every index.
All inputs are finite; a program needn't handle non-finite values. No bound on the sum of `pixel_mask` on one device may be relied on, other than what follows from the above.
Results may differ from the reference program's by a relative error of at most 0.012.
Values may be sent and summed in bfloat16 or wider, within the bound.
A program may use at most 192 MiB of HBM per device.

```python
import jax
import jax.numpy as jnp
from jax import lax

CIN = 1024
WIDTH = 256
RADIX = 2
INTER = 128
GIN = 128
IMG_DEV = 16
COLS = 28
IMAGES = 128
HEIGHT = 28
N_IMG = 8


def draw_image_count(key, part):
    key = jax.random.fold_in(key, 11)
    first, second, third = jax.random.split(key, 3)
    counts = jax.random.randint(first, (N_IMG,), IMG_DEV // 2, IMG_DEV + 1)
    chosen = jax.random.randint(second, (), 0, N_IMG)
    offset = jax.random.randint(third, (), 1, N_IMG)
    counts = counts.at[chosen].set(IMG_DEV)
    counts = counts.at[(chosen + offset) % N_IMG].set(IMG_DEV // 2)
    return counts.astype(jnp.int32)


def plant(values, stream_key, low, largest):
    dims = values.shape
    spot = [jax.random.randint(jax.random.fold_in(stream_key, axis), (), 0, dims[axis]) for axis in range(len(dims))]
    values = values.at[tuple(spot)].set(low)
    longest = dims.index(max(dims))
    spot[longest] = (spot[longest] + 1) % dims[longest]
    return values.at[tuple(spot)].set(largest)


def steps_of(key, shape, cuts, smallest, high):
    factor_of, own = 1.0, jax.random.fold_in(key, 6)
    for dim, shards_of in cuts:
        draws = jnp.exp(jax.random.uniform(jax.random.fold_in(own, dim), (shards_of,), jnp.float32, smallest / len(cuts), high / len(cuts)))
        factor_of = factor_of * jnp.repeat(draws, shape[dim] // shards_of).reshape([-1 if axis == dim else 1 for axis in range(len(shape))])
    return factor_of


def gaussian(stream_key, dims, width, reach, shards=(), kind=jnp.bfloat16):
    array = jax.random.normal(stream_key, dims, jnp.float32) * width
    if len(shards) > 0:
        array = steps_of(stream_key, dims, shards, -0.22, 0.18) * array
    return jnp.clip(array, min=-reach, max=reach).astype(kind)


def setup_inputs(seed: int = 0) -> dict:
    key_list = jax.random.split(jax.random.key(seed), 19)
    inputs = gaussian(key_list[0], (IMAGES, HEIGHT, COLS, CIN), 1.0, 6.0, ((0, 8), (1, 4)))
    image_count = draw_image_count(jax.random.fold_in(key_list[18], 71), 0)
    pixel_mask = plant((jax.random.randint(key_list[2], (IMAGES, HEIGHT, COLS), 0, 8) < 7).astype(jnp.int32), jax.random.fold_in(key_list[2], 1), 0, 1)
    w_first = gaussian(key_list[3], (CIN, WIDTH), CIN ** -0.5, 0.1875)
    gain_first = jnp.clip(1.0 + 0.15 * jax.random.normal(key_list[4], (WIDTH,), jnp.float32), 0.25, 1.75)
    bias_first = gaussian(key_list[5], (WIDTH,), 0.3, 1.5, (), jnp.float32)
    w_group = gaussian(key_list[6], (RADIX, 3, 3, GIN, WIDTH), (9 * GIN) ** -0.5, 0.1875)
    gain_group = jnp.clip(1.0 + 0.15 * jax.random.normal(key_list[7], (RADIX * WIDTH,), jnp.float32), 0.25, 1.75)
    bias_group = gaussian(key_list[8], (RADIX * WIDTH,), 0.3, 1.5, (), jnp.float32)
    w_squeeze = gaussian(key_list[9], (WIDTH, INTER), (WIDTH // 4) ** -0.5, 0.75)
    gain_squeeze = jnp.clip(1.0 + 0.15 * jax.random.normal(key_list[10], (INTER,), jnp.float32), 0.25, 1.75)
    bias_squeeze = gaussian(key_list[11], (INTER,), 0.3, 1.5, (), jnp.float32)
    w_excite = gaussian(key_list[12], (INTER, RADIX * WIDTH), (INTER // 4) ** -0.5, 1.0)
    bias_excite = gaussian(key_list[13], (RADIX * WIDTH,), 0.5, 2.5, (), jnp.float32)
    w_last = gaussian(key_list[14], (WIDTH, CIN), WIDTH ** -0.5, 0.375)
    gain_last = jnp.clip(1.0 + 0.15 * jax.random.normal(key_list[15], (CIN,), jnp.float32), 0.25, 1.75)
    bias_last = gaussian(key_list[16], (CIN,), 0.3, 1.5, (), jnp.float32)
    cotangent = gaussian(key_list[17], (IMAGES, HEIGHT, COLS, CIN), 1.0, 6.0, ((0, 8), (1, 4)))
    return {"inputs": inputs, "image_count": image_count, "pixel_mask": pixel_mask, "w_first": w_first, "gain_first": gain_first, "bias_first": bias_first, "w_group": w_group, "gain_group": gain_group, "bias_group": bias_group, "w_squeeze": w_squeeze, "gain_squeeze": gain_squeeze, "bias_squeeze": bias_squeeze, "w_excite": w_excite, "bias_excite": bias_excite, "w_last": w_last, "gain_last": gain_last, "bias_last": bias_last, "cotangent": cotangent}


epsilon = 1e-05
highest = lax.Precision.HIGHEST

@jax.custom_vjp
def low(v):
    return lax.optimization_barrier(v.astype(jnp.bfloat16)).astype(jnp.float32)

@jax.custom_vjp
def low_back(v):
    return v

def low_keep(v):
    return (low(v), None)

def low_pass(kept, grad):
    return (grad,)

def back_keep(v):
    return (v, None)

def back_low(kept, grad):
    return (low(grad),)
low.defvjp(low_keep, low_pass)
low_back.defvjp(back_keep, back_low)

def normalize(values, weight, gain, bias, total):
    mean = lax.optimization_barrier(jnp.sum(values * weight, axis=0)) / total
    spread = lax.optimization_barrier(jnp.sum(values * values * weight, axis=0)) / total - mean * mean
    return (values - mean) * lax.rsqrt(spread + epsilon) * gain + bias

def forward(inputs, w_first, gain_first, bias_first, w_group, gain_group, bias_group, w_squeeze, gain_squeeze, bias_squeeze, w_excite, bias_excite, w_last, gain_last, bias_last, valid, live):
    images, height, columns, channels = inputs.shape
    radix_count = w_group.shape[0]
    group_in = w_group.shape[3]
    mid_width = w_group.shape[4]
    flat_in = inputs.reshape(-1, channels)
    weight = valid.reshape(-1, 1)
    total = jnp.sum(valid)
    y_first = low_back(jnp.dot(flat_in, w_first, precision=highest))
    act_first = low(jax.nn.silu(normalize(y_first, weight, gain_first, bias_first, total)) * weight)
    act_first = act_first.reshape(images, height, columns, mid_width)
    padded = jnp.pad(act_first, ((0, 0), (1, 1), (1, 1), (0, 0)))
    outputs = []
    for branch in range(radix_count):
        taps = [padded[:, row_tap:row_tap + height, col_tap:col_tap + columns, branch * group_in:(branch + 1) * group_in] for row_tap in range(3) for col_tap in range(3)]
        patch = jnp.concatenate(taps, axis=-1).reshape(-1, 9 * group_in)
        outputs.append(jnp.dot(patch, w_group[branch].reshape(9 * group_in, mid_width), precision=highest))
    y_group = low_back(jnp.concatenate(outputs, axis=1))
    act_group = jax.nn.silu(normalize(y_group, weight, gain_group, bias_group, total)) * weight
    split_view = act_group.reshape(images, height * columns, radix_count, mid_width)
    pixel_count = lax.optimization_barrier(jnp.sum(valid.reshape(images, -1), axis=1))
    pooled = lax.optimization_barrier(jnp.sum(lax.optimization_barrier(jnp.sum(split_view, axis=2)), axis=1)) / jnp.maximum(pixel_count, 1.0)[:, None]
    squeezed = jnp.dot(pooled, w_squeeze, precision=highest)
    hidden_fc = jax.nn.silu(normalize(squeezed, live[:, None], gain_squeeze, bias_squeeze, jnp.sum(live)))
    logits = (jnp.dot(hidden_fc, w_excite, precision=highest) + bias_excite).reshape(images, radix_count, mid_width)
    attention = jax.nn.softmax(logits, axis=1)
    mixed = low(lax.optimization_barrier(jnp.sum(split_view * attention[:, None], axis=2)).reshape(-1, mid_width))
    y_last = low_back(jnp.dot(mixed, w_last, precision=highest))
    before = normalize(y_last, weight, gain_last, bias_last, total) + flat_in
    return (jax.nn.silu(before) * weight).reshape(inputs.shape)

def reference(inputs, image_count, pixel_mask, w_first, gain_first, bias_first, w_group, gain_group, bias_group, w_squeeze, gain_squeeze, bias_squeeze, w_excite, bias_excite, w_last, gain_last, bias_last, cotangent):
    slots = jnp.arange(IMG_DEV * N_IMG, dtype=jnp.int32)
    owner_count = image_count[slots // IMG_DEV]
    live = (slots % IMG_DEV < owner_count).astype(jnp.float32)
    valid = pixel_mask.astype(jnp.float32) * live[:, None, None]
    params = (inputs, w_first, gain_first, bias_first, w_group, gain_group, bias_group, w_squeeze, gain_squeeze, bias_squeeze, w_excite, bias_excite, w_last, gain_last, bias_last)
    params = tuple((item.astype(jnp.float32) for item in params))

    def closed(*values):
        return forward(*values, valid, live)
    result, pullback = jax.vjp(closed, *params)
    grads = pullback(cotangent.astype(jnp.float32))
    return (result.astype(jnp.bfloat16), grads[0].astype(jnp.bfloat16), grads[1], grads[2], grads[3], grads[4], grads[5], grads[6], grads[7], grads[8], grads[9], grads[10], grads[11], grads[12], grads[13], grads[14])
```

```python
import functools

import jax
import jax.numpy as jnp
from jax import lax
from jax.experimental import pallas as pl
from jax.experimental.pallas import tpu as pltpu
from jax.sharding import PartitionSpec as P

EPS = 1e-05
F32 = jnp.float32
BF16 = jnp.bfloat16
HIGH = lax.Precision.HIGHEST
MESH = pl.DeviceIdType.MESH
LANES = 128


def dot(a, b, precision=None):
    return jnp.dot(a, b, preferred_element_type=F32, precision=precision)


def dot_nt(a, b, precision=None):
    return lax.dot_general(
        a, b, (((1,), (1,)), ((), ())), preferred_element_type=F32, precision=precision
    )


def dot_tn(a, b, precision=None):
    return lax.dot_general(
        a, b, (((0,), (0,)), ((), ())), preferred_element_type=F32, precision=precision
    )


def wide(cell, lanes):
    return jnp.concatenate([cell] * (lanes // LANES), axis=1)


def fold(cells):
    rows, lanes = cells.shape
    return jnp.sum(cells.reshape(rows // 8, 8, lanes), axis=0)


def fold_images(cells, images):
    rows, lanes = cells.shape
    return jnp.sum(cells.reshape(rows // images, images, lanes), axis=0)


def total_row(cells):
    return jnp.sum(cells, axis=0, keepdims=True)


def put(ref, at, row, vector):
    for j in range(vector.shape[1] // LANES):
        ref[at, row + j : row + j + 1, :] = vector[:, j * LANES : (j + 1) * LANES]


def get(cells, row, lanes):
    return jnp.concatenate(
        [cells[row + j : row + j + 1, :] for j in range(lanes // LANES)], axis=1
    )


def moments(sums, squares, total):
    mean = sums / total
    spread = squares / total - mean * mean
    return mean, lax.rsqrt(spread + EPS)


def gate(half):
    bend = jnp.tanh(half)
    rise = 1.0 + bend
    return half * rise, 0.5 * (rise + half * (1.0 - bend * bend))


def split_bf16(cells):
    high = cells.astype(BF16)
    return high, (cells - high.astype(F32)).astype(BF16)


class Dims:
    def __init__(self, n_img, n_ha, inputs, w_group, w_squeeze):
        self.n_img, self.n_ha = n_img, n_ha
        self.nb, self.nh, self.nw, self.cin = inputs
        self.radix, _, _, self.gin, self.width = w_group
        self.mid = self.radix * self.gin
        self.wide = self.radix * self.width
        self.inter = w_squeeze[1]
        self.line = self.nw * self.nb
        self.rows = self.nh * self.line
        self.padded = (self.nw + 2) * self.nb
        self.half = (
            self.cin // 2,
            9 * self.gin + self.width,
            self.cin // 2,
        )
        self.inside = n_img == 8 and n_ha == 4


def block_kernel(
    d,
    x_hbm, ct_hbm, m, live, w1, g1, c1, w2, g2, c2, wsq, gs, cs, wex, bex, w3, g3, c3,
    out_hbm, dn_hbm, dy_hbm, wg0_hbm, wg1_hbm, wg2_hbm, small,
    xv, ctv, y1, a1p, y2, act2, slope2, mixed, y3, ostage, dm, acc_c, acc_g, w3p, w2t,
    att, q2, q4, vecs, pools,
    part0, part1, part2, rc0, rc1, rc2, rxy0, rxy1, rxy2, rz0, rz1, rz2, p0, p1, p2, res0, res1, res2,
    sa, si, ba, bi, ga_src, ga_buf, pf_src, pf_buf,
    sem_x, sem_ct, sem_out, sem_dn, sem_misc, ssa, rsa, ssi, rsi, ssh, rsh, ssw, rsw,
):
    n_img, n_ha = d.n_img, d.n_ha
    nb, nh, nw = d.nb, d.nh, d.nw
    cin, mid, wd, wide2, line, rows = d.cin, d.mid, d.width, d.wide, d.line, d.rows
    gin = d.gin
    dyp = ctv
    half = cin // 2
    i = lax.axis_index("img")
    h = lax.axis_index("ha")

    def ha_peer(k):
        return (i, lax.rem(h + k, n_ha))

    def img_peer(k):
        return (lax.rem(i + k, n_img), h)

    z_of, x_of, y_of, core = i // 2, lax.rem(i, 2), h // 2, lax.rem(h, 2)
    spot = x_of * 2 + y_of

    def core_peer():
        return (i, y_of * 2 + (1 - core))

    def plane_peer(k):
        other = lax.rem(spot + k, 4)
        return (z_of * 2 + other // 2, lax.rem(other, 2) * 2 + core)

    def z_peer(k):
        return (lax.rem(z_of + k, 4) * 2 + x_of, h)

    def line_rows(t):
        return pl.ds(pl.multiple_of(t * line, line), line)

    def x_copy(t):
        return pltpu.make_async_copy(x_hbm.at[line_rows(t)], xv.at[line_rows(t)], sem_x.at[t])

    def half_rows(t, c):
        return pl.ds(pl.multiple_of(c * rows + t * line, nb), line)

    def ct_copy(t, c):
        return pltpu.make_async_copy(
            ct_hbm.at[line_rows(t), pl.ds(c * half, half)], ctv.at[half_rows(t, c)], sem_ct.at[c, t]
        )

    def start_inputs(t, carry):
        x_copy(t).start()
        return carry

    lax.fori_loop(0, nh, start_inputs, 0)

    barrier = pltpu.get_barrier_semaphore()
    peers = [ha_peer(k) for k in range(1, n_ha)] + [img_peer(k) for k in range(1, n_img)]
    if d.inside:
        peers.append(((z_of * 2 + (1 - x_of)), (1 - y_of) * 2 + core))
    for peer in peers:
        pl.semaphore_signal(barrier, inc=1, device_id=peer, device_id_type=MESH)

    padded = d.padded

    def inner_rows(t, at=nb, count=line):
        return pl.ds(pl.multiple_of(t * padded + at, nb), count)

    def clear(ref):
        zero = jnp.zeros((nb, ref.shape[1]), BF16)

        def body(t, carry):
            ref[inner_rows(t, 0, nb), :] = zero
            ref[inner_rows(t, nb + line, nb), :] = zero
            return carry

        lax.fori_loop(0, nh + 2, body, 0)

        def edge(t, carry):
            ref[inner_rows(0, t * nb, nb), :] = zero
            ref[inner_rows(nh + 1, t * nb, nb), :] = zero
            return carry

        lax.fori_loop(0, nw + 2, edge, 0)

    clear(a1p)
    pl.semaphore_wait(barrier, len(peers))

    def swap(src, buf, send, recv, peer, n):
        def copy(k):
            return pltpu.make_async_remote_copy(
                src_ref=src,
                dst_ref=buf.at[k],
                send_sem=send.at[k],
                recv_sem=recv.at[k],
                device_id=peer(k),
                device_id_type=MESH,
            )

        def start(k, carry):
            copy(k).start()
            return carry

        def sent(k, carry):
            copy(k).wait_send()
            return carry

        def take(k, carry):
            copy(k).wait_recv()
            return carry + buf[k].astype(F32)

        if n <= 8:
            for k in range(1, n):
                start(k, 0)
            total = src[...].astype(F32)
            for k in range(1, n):
                total = take(k, total)
            for k in range(1, n):
                sent(k, 0)
            return total
        lax.fori_loop(1, n, start, 0)
        total = lax.fori_loop(1, n, take, src[...].astype(F32))
        lax.fori_loop(1, n, sent, 0)
        return total

    def sum_ha(at, count):
        span = pl.ds(0, count)
        return swap(
            sa.at[at, span], ba.at[at, :, span], ssa.at[at], rsa.at[at], ha_peer, n_ha
        )

    def sum_img(at, count):
        span = pl.ds(0, count)
        return swap(
            si.at[at, span], bi.at[at, :, span], ssi.at[at], rsi.at[at], img_peer, n_img
        )

    def sum_all(at, count):
        si[at, 0:count, :] = sum_ha(at, count)
        return sum_img(at, count)

    def halo(ref, at):
        def down():
            return pltpu.make_async_remote_copy(
                src_ref=ref.at[inner_rows(nh)], dst_ref=ref.at[inner_rows(0)],
                send_sem=ssh.at[at, 0], recv_sem=rsh.at[at, 0],
                device_id=(i, jnp.minimum(h + 1, n_ha - 1)), device_id_type=MESH,
            )

        def up():
            return pltpu.make_async_remote_copy(
                src_ref=ref.at[inner_rows(1)], dst_ref=ref.at[inner_rows(nh + 1)],
                send_sem=ssh.at[at, 1], recv_sem=rsh.at[at, 1],
                device_id=(i, jnp.maximum(h - 1, 0)), device_id_type=MESH,
            )

        def start():
            @pl.when(h < n_ha - 1)
            def _():
                down().start()

            @pl.when(h > 0)
            def _():
                up().start()

        def wait_recv():
            @pl.when(h > 0)
            def _():
                down().wait_recv()

            @pl.when(h < n_ha - 1)
            def _():
                up().wait_recv()

        def wait_send():
            @pl.when(h < n_ha - 1)
            def _():
                down().wait_send()

            @pl.when(h > 0)
            def _():
                up().wait_send()

        return start, wait_recv, wait_send

    parts, rcs, rxys, rzs, mids = (
        (part0, part1, part2), (rc0, rc1, rc2), (rxy0, rxy1, rxy2), (rz0, rz1, rz2), (p0, p1, p2),
    )
    ress = (res0, res1, res2)
    plane_rows, z_rows = wd // 4, wd // 16

    def w_copy(s, stage, k):
        sem = (s, stage * 4 + k)
        part, res, inner = parts[s], ress[s], mids[s]
        own_plane = pl.ds(pl.multiple_of(spot * plane_rows, plane_rows), plane_rows)
        own_rows = pl.ds(pl.multiple_of(spot * plane_rows + z_of * z_rows, z_rows), z_rows)
        if stage == 0:
            src, dst, peer = part.at[1 - core], rcs[s], core_peer()
        elif stage == 1:
            other = lax.rem(spot + k, 4)
            src = part.at[core, pl.ds(pl.multiple_of(other * plane_rows, plane_rows), plane_rows)]
            dst, peer = rxys[s].at[k - 1], plane_peer(k)
        elif stage == 2:
            other = lax.rem(z_of + k, 4)
            src = inner.at[pl.ds(pl.multiple_of(other * z_rows, z_rows), z_rows)]
            dst, peer = rzs[s].at[k - 1], z_peer(k)
        elif stage == 3:
            src = dst = res.at[core, own_rows]
            peer = z_peer(k)
        elif stage == 4:
            src = dst = res.at[core, own_plane]
            peer = plane_peer(k)
        else:
            src = dst = res.at[core]
            peer = core_peer()
        return pltpu.make_async_remote_copy(
            src_ref=src, dst_ref=dst, send_sem=ssw.at[sem], recv_sem=rsw.at[sem], device_id=peer, device_id_type=MESH
        )

    def w_ks(stage):
        return (1,) if stage in (0, 5) else (1, 2, 3)

    def w_arrival(s, stage, k):
        res = ress[s]
        sem = (s, stage * 4 + k)
        if stage == 3:
            other = lax.rem(z_of - k + 4, 4)
            dst = res.at[core, pl.ds(pl.multiple_of(spot * plane_rows + other * z_rows, z_rows), z_rows)]
        elif stage == 4:
            other = lax.rem(spot - k + 4, 4)
            dst = res.at[core, pl.ds(pl.multiple_of(other * plane_rows, plane_rows), plane_rows)]
        else:
            dst = res.at[1 - core]
        return pltpu.make_async_remote_copy(
            src_ref=dst, dst_ref=dst, send_sem=ssw.at[sem], recv_sem=rsw.at[sem], device_id=core_peer(), device_id_type=MESH
        )

    def w_start(s, stage):
        if d.inside:
            for k in w_ks(stage):
                w_copy(s, stage, k).start()

    def w_finish(s, stage):
        if not d.inside:
            return
        for k in w_ks(stage):
            if stage <= 2:
                w_copy(s, stage, k).wait_recv()
            else:
                w_arrival(s, stage, k).wait_recv()
        part, res, inner = parts[s], ress[s], mids[s]
        if stage == 0:
            rc = rcs[s]

            def add(t, carry):
                at = pl.ds(pl.multiple_of(t * 16, 16), 16)
                part[core, at, :] = (part[core, at, :].astype(F32) + rc[at, :].astype(F32)).astype(BF16)
                return carry

            lax.fori_loop(0, wd // 16, add, 0)
        elif stage == 1:
            buf = rxys[s]

            def add(t, carry):
                at = pl.ds(pl.multiple_of(t * 16, 16), 16)
                own = pl.ds(pl.multiple_of(spot * plane_rows + t * 16, 16), 16)
                total = part[core, own, :].astype(F32)
                for k in range(3):
                    total = total + buf[k, at, :].astype(F32)
                inner[at, :] = total.astype(BF16)
                return carry

            lax.fori_loop(0, plane_rows // 16, add, 0)
        elif stage == 2:
            buf = rzs[s]
            total = inner[pl.ds(pl.multiple_of(z_of * z_rows, z_rows), z_rows), :].astype(F32)
            for k in range(3):
                total = total + buf[k].astype(F32)
            res[core, pl.ds(pl.multiple_of(spot * plane_rows + z_of * z_rows, z_rows), z_rows), :] = total.astype(BF16)

    def w_step(s, stage):
        w_finish(s, stage)
        if stage < 5:
            w_start(s, stage + 1)

    def w_sent(s):
        if d.inside:
            for stage in range(6):
                for k in w_ks(stage):
                    w_copy(s, stage, k).wait_send()

    def first(t, carry):
        sums, squares = carry
        x_copy(t).wait()
        ct_copy(t, 0).start()
        ct_copy(t, 1).start()
        at = line_rows(t)
        y = dot(xv[at, :], w1[...])
        y1[at, :] = y
        masked = y * wide(m[at, :], mid)
        return sums + fold(masked), squares + fold(masked * y)

    zeros = jnp.zeros((8, mid), F32)
    sums, squares = lax.fori_loop(0, nh, first, (zeros, zeros))

    def count_pixels(t, carry):
        return carry + fold_images(m[line_rows(t), :], nb)

    pixels = lax.fori_loop(0, nh, count_pixels, jnp.zeros((nb, LANES), F32))
    sa[0, 0:8, :] = jnp.zeros((8, LANES), F32)
    put(sa, 0, 0, total_row(sums))
    put(sa, 0, 2, total_row(squares))
    put(sa, 0, 4, total_row(pixels))
    put(sa, 0, 5, total_row(live[...]) * (1.0 / n_ha))
    got = sum_all(0, 8)
    total = got[4:5, :]
    images = got[5:6, :]
    mean1, scale1 = moments(get(got, 0, mid), get(got, 2, mid), wide(total, mid))
    half_a1 = 0.5 * g1[...] * scale1
    half_b1 = 0.5 * c1[...] - half_a1 * mean1

    step1 = 4 * nb

    def act_first(t, carry):
        def cells(u, carry):
            at = pl.ds(pl.multiple_of(t * line + u * step1, step1), step1)
            value, _ = gate(y1[at, :] * half_a1 + half_b1)
            value = value * wide(m[at, :], mid)
            a1p[inner_rows(t + 1, nb + u * step1, step1), :] = value.astype(BF16)
            return carry + fold(value)

        return lax.fori_loop(0, line // step1, cells, carry)

    sum_act1 = total_row(lax.fori_loop(0, nh, act_first, jnp.zeros((8, mid), F32)))
    halo1_start, halo1_recv, halo1_sent = halo(a1p, 0)
    halo1_start()

    def taps(t, r):
        return jnp.concatenate(
            [
                a1p[inner_rows(t + ky, kx * nb), r * gin : (r + 1) * gin]
                for ky in range(3)
                for kx in range(3)
            ],
            axis=1,
        )

    def group(t, carry):
        at = line_rows(t)
        done = []
        for r in range(d.radix):
            sums, squares = carry[r]
            y = dot(taps(t, r), w2[r])
            y2[at, r * wd : (r + 1) * wd] = y
            masked = y * wide(m[at, :], wd)
            done.append((sums + fold(masked), squares + fold(masked * y)))
        return tuple(done)

    zeros = jnp.zeros((8, wd), F32)
    sums2 = lax.fori_loop(1, nh - 1, group, ((zeros, zeros),) * d.radix)
    halo1_recv()
    sums2 = lax.fori_loop(0, 2, lambda t, carry: group(t * (nh - 1), carry), sums2)
    put(sa, 1, 0, jnp.concatenate([total_row(s) for s, _ in sums2], axis=1))
    put(sa, 1, 4, jnp.concatenate([total_row(q) for _, q in sums2], axis=1))
    got = sum_all(1, 8)
    mean2, scale2 = moments(get(got, 0, wide2), get(got, 4, wide2), wide(total, wide2))
    half_a2 = 0.5 * g2[...] * scale2
    half_b2 = 0.5 * c2[...] - half_a2 * mean2

    lane_blocks = wd // LANES
    step2 = 4 * nb
    for r in range(d.radix):
        for j in range(lane_blocks):
            col = r * wd + j * LANES
            lanes = slice(col, col + LANES)
            ha2, hb2 = half_a2[:, lanes], half_b2[:, lanes]

            def act_group(t, carry):
                pool, slopes, bends = carry
                at = pl.ds(pl.multiple_of(t * step2, step2), step2)
                y = y2[at, lanes]
                mask = m[at, :]
                value, slope = gate(y * ha2 + hb2)
                value = value * mask
                slope = slope * mask
                act2[at, lanes] = value.astype(BF16)
                slope2[at, lanes] = slope.astype(BF16)
                return (
                    pool + fold_images(value, nb),
                    slopes + fold_images(slope, nb),
                    bends + fold_images(slope * y, nb),
                )

            zero = jnp.zeros((nb, LANES), F32)
            pool, slopes, bends = lax.fori_loop(0, rows // step2, act_group, (zero, zero, zero))
            q2[:, lanes] = slopes
            q4[:, lanes] = bends
            at = slice(j * LANES, (j + 1) * LANES)
            if r == 0:
                pools[:, at] = pool
            else:
                pools[:, at] = pools[:, at] + pool

    pool = pools[...]
    squeeze = wsq[...].astype(F32)
    excite = wex[...].astype(F32)
    pf_src[:, 0 : d.inter] = dot(pool, squeeze, HIGH)
    pf_src[:, d.inter :] = pixels
    both = swap(pf_src, pf_buf, ssa.at[8], rsa.at[8], ha_peer, n_ha)
    floor = jnp.maximum(both[:, d.inter :], 1.0)
    squeezed = both[:, 0 : d.inter] / floor
    live_now = live[...]
    si[2, 0:8, :] = jnp.zeros((8, LANES), F32)
    put(si, 2, 0, total_row(squeezed * live_now))
    put(si, 2, 1, total_row(squeezed * squeezed * live_now))
    got = sum_img(2, 8)
    mean_s, scale_s = moments(got[0:1, :], got[1:2, :], images)
    centered = (squeezed - mean_s) * scale_s
    hidden, hidden_slope = gate(0.5 * (centered * gs[...] + cs[...]))
    logits = dot(hidden, excite, HIGH) + bex[...]
    gap = logits[:, 0:wd] - logits[:, wd:]
    att[:, 0:wd] = jax.nn.sigmoid(gap)
    att[:, wd:] = jax.nn.sigmoid(-gap)

    step3 = 2 * nb

    def mix(t, carry):
        def cells(u, carry):
            at = pl.ds(pl.multiple_of(t * line + u * step3, step3), step3)
            weight = att[...]
            weight = jnp.concatenate([weight] * (step3 // nb), axis=0)
            both = act2[at, :].astype(F32) * weight
            mixed[at, :] = (both[:, 0:wd] + both[:, wd:]).astype(BF16)
            return carry

        lax.fori_loop(0, line // step3, cells, 0)
        gram, sums = carry
        cells = mixed[line_rows(t), :]
        return gram + dot_tn(cells, cells), sums + fold(cells.astype(F32))

    gram, sums = lax.fori_loop(
        0, nh, mix, (jnp.zeros((wd, wd), F32), jnp.zeros((8, wd), F32))
    )
    mix_sum = total_row(sums)
    gram_high, gram_low = split_bf16(gram)
    acc_g[0, :, 0:cin] = dot(gram_high, w3[...]) + dot(gram_low, w3[...])
    mix_high, mix_low = split_bf16(mix_sum)
    sum_last = dot(jnp.broadcast_to(mix_high, (16, wd)), w3[...]) + dot(
        jnp.broadcast_to(mix_low, (16, wd)), w3[...]
    )
    put(sa, 3, 0, sum_last[0:1, :])
    put(sa, 3, 8, total_row(acc_g[0, :, 0:cin] * w3[...].astype(F32)))
    got = sum_all(3, 16)
    mean3, scale3 = moments(get(got, 0, cin), get(got, 8, cin), wide(total, cin))
    grow3 = g3[...] * scale3
    half_a3 = 0.5 * grow3
    half_b3 = 0.5 * c3[...] - half_a3 * mean3
    w3p[...] = (w3[...].astype(F32) * grow3).astype(BF16)

    step4 = 4 * nb
    blocks4 = 2 * LANES

    def out_copy(t):
        return pltpu.make_async_copy(ostage.at[lax.rem(t, 2)], out_hbm.at[line_rows(t)], sem_out.at[t])

    def dn_copy(t, c):
        return pltpu.make_async_copy(
            ctv.at[half_rows(t, c)], dn_hbm.at[line_rows(t), pl.ds(c * half, half)], sem_dn.at[c, t]
        )

    acc_c[...] = jnp.zeros((wd, cin), F32)
    vecs[...] = jnp.zeros((8, cin), F32)

    def last(t, carry):
        at_line = line_rows(t)
        y3[...] = dot(mixed[at_line, :], w3[...])
        ct_copy(t, 0).wait()
        ct_copy(t, 1).wait()

        @pl.when(t >= 2)
        def _():
            out_copy(t - 2).wait()

        slot = lax.rem(t, 2)
        for j in range(cin // blocks4):
            lanes = slice(j * blocks4, (j + 1) * blocks4)
            a3, b3 = half_a3[:, lanes], half_b3[:, lanes]

            def cells(u, carry):
                own = pl.ds(pl.multiple_of(u * step4, step4), step4)
                at = pl.ds(pl.multiple_of(t * line + u * step4, step4), step4)
                value, slope = gate(y3[own, lanes] * a3 + (b3 + 0.5 * xv[at, lanes].astype(F32)))
                mask = wide(m[at, :], blocks4)
                ostage[slot, own, lanes] = (value * mask).astype(BF16)
                side = j * blocks4 // half
                there = pl.ds(pl.multiple_of(side * rows + t * line + u * step4, nb), step4)
                inner = slice(j * blocks4 - side * half, (j + 1) * blocks4 - side * half)
                grad = ctv[there, inner].astype(F32) * mask * slope
                ctv[there, inner] = grad.astype(BF16)
                return carry + fold(grad)

            vecs[:, lanes] = lax.fori_loop(0, line // step4, cells, vecs[:, lanes])
        out_copy(t).start()
        dn_copy(t, 0).start()
        dn_copy(t, 1).start()
        grad = jnp.concatenate([ctv[half_rows(t, 0), :], ctv[half_rows(t, 1), :]], axis=1)
        dm[at_line, :] = dot_nt(grad, w3p[...])
        acc_c[...] += dot_tn(mixed[at_line, :], grad)
        return carry

    lax.fori_loop(0, nh, last, 0)
    sum_grad = total_row(vecs[...])
    put(sa, 4, 0, sum_grad)
    put(sa, 4, 8, scale3 * (total_row(acc_c[...] * w3[...].astype(F32)) - mean3 * sum_grad))
    got = sum_all(4, 16)
    bias3, gain3 = get(got, 0, cin), get(got, 8, cin)
    put(small, 0, 0, bias3)
    put(small, 0, 8, gain3)
    all_wide = wide(total, cin)
    slant3 = scale3 * gain3 / all_wide
    level3 = bias3 / all_wide - mean3 * slant3
    fix = (w3[...].astype(F32) * slant3).astype(BF16)
    fix = dot_nt(fix, w3p[...]).astype(BF16)
    level_high, level_low = split_bf16(level3)
    shift = dot_nt(jnp.broadcast_to(level_high, (16, cin)), w3p[...]) + dot_nt(
        jnp.broadcast_to(level_low, (16, cin)), w3p[...]
    )
    shift = shift[0:1, :]
    mix_column = jnp.transpose(jnp.broadcast_to(mix_sum, (LANES, wd)))
    for j in range(cin // LANES):
        lanes = slice(j * LANES, (j + 1) * LANES)
        to = j * LANES - (0 if j * LANES < cin // 2 else cin // 2)
        grad = grow3[:, lanes] * (
            acc_c[:, lanes]
            - mix_column * level3[:, lanes]
            - acc_g[0, :, lanes] * slant3[:, lanes]
        )
        part2[0 if j * LANES < cin // 2 else 1, :, to : to + LANES] = grad.astype(BF16)
    w_start(2, 0)

    def back_mix(t, carry):
        at = line_rows(t)
        mask = wide(m[at, :], wd)
        dm[at, :] = dm[at, :] - dot(mixed[at, :], fix) - mask * shift
        return carry

    lax.fori_loop(0, nh, back_mix, 0)
    w_step(2, 0)
    step5 = 4 * nb
    sums5 = []
    for j in range(lane_blocks):
        lanes = slice(j * LANES, (j + 1) * LANES)

        def image_sums(t, carry):
            at = pl.ds(pl.multiple_of(t * step5, step5), step5)
            grad = dm[at, lanes]
            done = []
            for r in range(d.radix):
                own = slice(r * wd + j * LANES, r * wd + (j + 1) * LANES)
                a, b, c = carry[r]
                a = a + fold_images(grad * act2[at, own].astype(F32), nb)
                part = grad * slope2[at, own].astype(F32)
                b = b + fold_images(part, nb)
                c = c + fold_images(part * y2[at, own], nb)
                done.append((a, b, c))
            return tuple(done)

        zero = jnp.zeros((nb, LANES), F32)
        sums5.append(
            lax.fori_loop(0, rows // step5, image_sums, ((zero, zero, zero),) * d.radix)
        )
    pick = lambda which: jnp.concatenate(
        [sums5[j][r][which] for r in range(d.radix) for j in range(lane_blocks)], axis=1
    )
    def dn_out(t, carry):
        dn_copy(t, 0).wait()
        dn_copy(t, 1).wait()
        return carry

    lax.fori_loop(0, nh, dn_out, 0)
    clear(dyp)
    ga_src[...] = pick(0).astype(BF16)
    q1, q3 = pick(1), pick(2)
    w_step(2, 1)
    grad_att = swap(ga_src, ga_buf, ssa.at[9], rsa.at[9], ha_peer, n_ha)
    w_step(2, 2)

    weight = att[...]
    weighed = weight * grad_att
    both = weighed[:, 0:wd] + weighed[:, wd:]
    grad_logits = weight * (grad_att - jnp.concatenate([both, both], axis=1))
    grad_excite = dot_tn(hidden, grad_logits, HIGH)
    grad_bex = total_row(grad_logits) * (1.0 / n_ha)
    grad_fc = dot_nt(grad_logits, excite, HIGH) * hidden_slope
    si[5, 0:8, :] = jnp.zeros((8, LANES), F32)
    put(si, 5, 0, total_row(grad_fc))
    put(si, 5, 1, total_row(grad_fc * centered))
    pooled = pool / wide(floor, wd)
    put(si, 5, 2, total_row(pooled))
    got = sum_img(5, 8)
    bias_s, gain_s = got[0:1, :], got[1:2, :]
    w_step(2, 3)
    put(small, 0, 16, bias_s)
    put(small, 0, 17, gain_s)
    grad_squeezed = (gs[...] * scale_s) * (
        grad_fc - live_now * (bias_s + centered * gain_s) / images
    )
    level = get(got, 2, wd) / wide(images, wd)
    grad_squeeze = dot_tn(pooled - level, grad_squeezed, HIGH)
    grad_pool = dot_nt(grad_squeezed, squeeze, HIGH) / wide(floor, wd)
    pool2 = jnp.concatenate([grad_pool] * d.radix, axis=1)
    sum_grad = total_row(weight * q1 + pool2 * q2[...])
    sum_bend = total_row(weight * q3 + pool2 * q4[...])
    sa[6, 14:16, :] = jnp.zeros((2, LANES), F32)
    put(sa, 6, 12, sum_act1)
    put(sa, 6, 0, sum_grad)
    put(sa, 6, 4, scale2 * (sum_bend - mean2 * sum_grad))
    put(sa, 6, 8, grad_bex)
    got = sum_all(6, 16)
    w_step(2, 4)
    bias2, gain2 = get(got, 0, wide2), get(got, 4, wide2)
    mean_act1 = get(got, 12, mid) / (wide(images, mid) * float(nh * n_ha * nw))
    put(small, 0, 20, bias2)
    put(small, 0, 24, gain2)
    put(small, 0, 28, get(got, 8, wide2))
    grow2 = g2[...] * scale2
    slant2 = grow2 * scale2 * gain2 / wide(total, wide2)
    level2 = grow2 * bias2 / wide(total, wide2) - mean2 * slant2
    att[...] = weight * grow2
    q2[...] = pool2 * grow2

    step6 = 2 * nb

    def back_group(t, carry):
        def cells(u, carry):
            at = pl.ds(pl.multiple_of(t * line + u * step6, step6), step6)
            to = inner_rows(t + 1, nb + u * step6, step6)
            again = step6 // nb
            grad = dm[at, :]
            sums = []
            for r in range(d.radix):
                own = slice(r * wd, (r + 1) * wd)
                grow = jnp.concatenate([att[:, own]] * again, axis=0)
                lift = jnp.concatenate([q2[:, own]] * again, axis=0)
                push = (grow * grad + lift) * slope2[at, own].astype(F32)
                pull = wide(m[at, :], wd) * (level2[:, own] + slant2[:, own] * y2[at, own])
                dyp[to, own] = (push - pull).astype(BF16)
                sums.append(carry[r] + fold(push - pull))
            return tuple(sums)

        return lax.fori_loop(0, line // step6, cells, carry)

    zeros = jnp.zeros((8, wd), F32)
    sum_dy2 = [total_row(s) for s in lax.fori_loop(0, nh, back_group, (zeros,) * d.radix)]
    halo2_start, halo2_recv, halo2_sent = halo(dyp, 1)
    halo2_start()

    acc_g[...] = jnp.zeros((d.radix, wd, 9 * gin), F32)

    def weights_group(t, carry):
        for r in range(d.radix):
            grad = dyp[inner_rows(t + 1), r * wd : (r + 1) * wd]
            acc_g[r] += dot_tn(grad, taps(t, r))
        return carry

    lax.fori_loop(0, nh, weights_group, 0)
    for r in range(d.radix):
        base = wide(mean_act1[:, r * gin : (r + 1) * gin], 9 * gin)
        column = jnp.transpose(jnp.broadcast_to(sum_dy2[r], (LANES, wd)))
        part1[r, :, 0 : 9 * gin] = (acc_g[r] - wide(column, 9 * gin) * base).astype(BF16)
    part1[0, :, 9 * gin :] = jnp.concatenate(
        [grad_excite[:, 0:wd], grad_excite[:, wd:]], axis=0
    ).astype(BF16) * (1.0 / n_ha)
    part1[1, :, 9 * gin : 9 * gin + LANES] = grad_squeeze.astype(BF16)
    part1[1, :, 9 * gin + LANES :] = jnp.zeros((wd, wd - LANES), BF16)
    w_start(1, 0)
    w_step(2, 5)

    for r in range(d.radix):
        for tap in range(9):
            w2t[r, :, tap * wd : (tap + 1) * wd] = w2[r, tap * gin : (tap + 1) * gin, :]
    halo2_recv()

    def transposed(t, carry):
        sums, bends = carry
        at = line_rows(t)
        done = []
        for r in range(d.radix):
            cells = jnp.concatenate(
                [
                    dyp[inner_rows(t + 2 - ky, (2 - kx) * nb), r * wd : (r + 1) * wd]
                    for ky in range(3)
                    for kx in range(3)
                ],
                axis=1,
            )
            done.append(dot_nt(cells, w2t[r]))
        dm[at, :] = jnp.concatenate(done, axis=1)

        def cells(u, carry):
            sums, bends = carry
            at = pl.ds(pl.multiple_of(t * line + u * step1, step1), step1)
            y = y1[at, :]
            _, slope = gate(y * half_a1 + half_b1)
            grad = dm[at, :] * (slope * wide(m[at, :], mid))
            dm[at, :] = grad
            return sums + fold(grad), bends + fold(grad * y)

        return lax.fori_loop(0, line // step1, cells, (sums, bends))

    zeros = jnp.zeros((8, mid), F32)
    sums, bends = lax.fori_loop(0, nh, transposed, (zeros, zeros))
    w_step(1, 0)
    sum_grad = total_row(sums)
    put(sa, 7, 0, sum_grad)
    put(sa, 7, 4, jnp.concatenate(sum_dy2, axis=1))
    put(sa, 7, 2, scale1 * (total_row(bends) - mean1 * sum_grad))
    got = sum_all(7, 8)
    w_step(1, 1)
    bias1, gain1 = get(got, 0, mid), get(got, 2, mid)
    put(small, 0, 32, bias1)
    put(small, 0, 34, gain1)
    put(small, 0, 36, mean_act1)
    small[0, 38:40, :] = jnp.zeros((2, LANES), F32)
    put(small, 0, 40, get(got, 4, wide2))
    small[0, 44:48, :] = jnp.zeros((4, LANES), F32)
    small[0, 18:20, :] = jnp.zeros((2, LANES), F32)
    grow1 = g1[...] * scale1
    slant1 = grow1 * scale1 * gain1 / wide(total, mid)
    level1 = grow1 * bias1 / wide(total, mid) - mean1 * slant1

    acc_c[...] = jnp.zeros((wd, cin), F32)

    def dy_copy(t):
        return pltpu.make_async_copy(mixed.at[line_rows(t)], dy_hbm.at[line_rows(t)], sem_misc.at[t])

    def back_first(t, carry):
        def cells(u, carry):
            at = pl.ds(pl.multiple_of(t * line + u * step1, step1), step1)
            pull = wide(m[at, :], mid) * (level1 + slant1 * y1[at, :])
            mixed[at, :] = (grow1 * dm[at, :] - pull).astype(BF16)
            return carry

        lax.fori_loop(0, line // step1, cells, 0)
        dy_copy(t).start()
        at = line_rows(t)
        acc_c[...] += dot_tn(mixed[at, :], xv[at, :])
        return carry

    lax.fori_loop(0, nh, back_first, 0)
    w_step(1, 2)
    part0[0] = acc_c[:, 0 : cin // 2].astype(BF16)
    part0[1] = acc_c[:, cin // 2 :].astype(BF16)
    w_start(0, 0)
    w_step(1, 3)
    w_step(0, 0)
    w_step(1, 4)
    w_step(0, 1)
    w_step(1, 5)
    for stage in range(2, 6):
        w_step(0, stage)

    results = ((wg0_hbm, 0), (wg1_hbm, 1), (wg2_hbm, 2))
    for hbm, s in results:
        pltpu.make_async_copy((ress if d.inside else parts)[s], hbm, sem_misc.at[nh + s]).start()

    def finish(t, carry):
        dy_copy(t).wait()
        return carry

    lax.fori_loop(0, nh, finish, 0)
    for t in range(max(nh - 2, 0), nh):
        out_copy(t).wait()
    for s in range(3):
        w_sent(s)
    halo1_sent()
    halo2_sent()
    for hbm, s in results:
        pltpu.make_async_copy((ress if d.inside else parts)[s], hbm, sem_misc.at[nh + s]).wait()


def call_block(d, args):
    f32, bf16 = F32, BF16
    cin, wd, mid, rows, nb, nh = d.cin, d.width, d.mid, d.rows, d.nb, d.nh
    vmem, dma = pltpu.VMEM, pltpu.SemaphoreType.DMA
    halves = [(2, wd, lanes) for lanes in d.half]
    shape = jax.ShapeDtypeStruct
    outs = [
        shape((rows, cin), bf16),
        shape((rows, cin), bf16),
        shape((rows, mid), bf16),
        *[shape(s, bf16) for s in halves],
        shape((1, 48, LANES), f32),
    ]
    anywhere = pl.BlockSpec(memory_space=pl.ANY)
    inside = pl.BlockSpec(memory_space=pltpu.VMEM)
    plane, zed = wd // 4, wd // 16
    scratch = [
        vmem((rows, cin), bf16),
        vmem((max(2 * rows, (nh + 2) * d.padded), cin // 2), bf16),
        vmem((rows, mid), f32),
        vmem(((nh + 2) * d.padded, mid), bf16),
        vmem((rows, d.wide), f32),
        vmem((rows, d.wide), bf16),
        vmem((rows, d.wide), bf16),
        vmem((rows, wd), bf16),
        vmem((d.line, cin), f32),
        vmem((2, d.line, cin), bf16),
        vmem((rows, wd), f32),
        vmem((wd, cin), f32),
        vmem((d.radix, wd, 9 * d.gin), f32),
        vmem((wd, cin), bf16),
        vmem((d.radix, d.gin, 9 * wd), bf16),
        vmem((nb, d.wide), f32),
        vmem((nb, d.wide), f32),
        vmem((nb, d.wide), f32),
        vmem((8, cin), f32),
        vmem((nb, wd), f32),
        *[vmem(s, bf16) for s in halves],
        *[vmem((wd, lanes), bf16) for lanes in d.half],
        *[vmem((3, plane, lanes), bf16) for lanes in d.half],
        *[vmem((3, zed, lanes), bf16) for lanes in d.half],
        *[vmem((plane, lanes), bf16) for lanes in d.half],
        *[vmem(s, bf16) for s in halves],
        vmem((8, 16, LANES), f32),
        vmem((8, 16, LANES), f32),
        vmem((8, d.n_ha, 16, LANES), f32),
        vmem((8, d.n_img, 16, LANES), f32),
        vmem((nb, d.wide), bf16),
        vmem((d.n_ha, nb, d.wide), bf16),
        vmem((nb, 2 * LANES), f32),
        vmem((d.n_ha, nb, 2 * LANES), f32),
        dma((nh,)),
        dma((2, nh)),
        dma((nh,)),
        dma((2, nh)),
        dma((nh + 3,)),
        dma((10, d.n_ha)),
        dma((10, d.n_ha)),
        dma((8, d.n_img)),
        dma((8, d.n_img)),
        dma((2, 2)),
        dma((2, 2)),
        dma((3, 24)),
        dma((3, 24)),
    ]
    return pl.pallas_call(
        functools.partial(block_kernel, d),
        out_shape=outs,
        in_specs=[anywhere, anywhere] + [inside] * 16,
        out_specs=[anywhere] * 6 + [inside],
        scratch_shapes=scratch,
        name="block",
        compiler_params=pltpu.CompilerParams(
            collective_id=0, has_side_effects=True, vmem_limit_bytes=60 << 20
        ),
    )(*args)


def finish_kernel(d, out_in, dn, dy, w1, wg0, wg1, wg2, small, *outs):
    (out, gin, gw1, gg1, gb1, gw2, gg2, gb2, gwsq, ggs, gbs, gwex, gbex, gw3, gg3, gb3) = outs
    wd, gin_group = d.width, d.gin
    out[...] = out_in[...]
    gin[...] = (dn[...].astype(F32) + dot_nt(dy[...], w1[...])).astype(BF16)

    @pl.when(pl.program_id(0) == 0)
    def _():
        half = d.cin // 2
        for c in range(2):
            gw1[c * half : (c + 1) * half, :] = jnp.transpose(wg0[c].astype(F32))
            gw3[:, c * half : (c + 1) * half] = wg2[c].astype(F32)
        rows = small[0]
        means, taken = get(rows, 36, d.mid), get(rows, 40, d.wide)
        for r in range(d.radix):
            mean = means[:, r * gin_group : (r + 1) * gin_group]
            mean = jnp.transpose(jnp.broadcast_to(mean, (LANES, gin_group)))
            back = wide(mean, wd) * taken[:, r * wd : (r + 1) * wd]
            for tap in range(9):
                cells = wg1[r, :, tap * gin_group : (tap + 1) * gin_group]
                gw2[r, tap] = jnp.transpose(cells.astype(F32)) + back
        cells = wg1[0, :, 9 * gin_group :].astype(F32)
        gwex[:, 0:wd] = cells[0 : d.inter, :]
        gwex[:, wd:] = cells[d.inter :, :]
        gwsq[...] = wg1[1, :, 9 * gin_group : 9 * gin_group + d.inter].astype(F32)
        gb3[...] = get(rows, 0, d.cin)
        gg3[...] = get(rows, 8, d.cin)
        gbs[...] = rows[16:17, :]
        ggs[...] = rows[17:18, :]
        gb2[...] = get(rows, 20, d.wide)
        gg2[...] = get(rows, 24, d.wide)
        gbex[...] = get(rows, 28, d.wide)
        gb1[...] = get(rows, 32, d.mid)
        gg1[...] = get(rows, 34, d.mid)


def call_finish(d, out_in, dn, dy, w1, wg0, wg1, wg2, small):
    shape = jax.ShapeDtypeStruct
    cin, wd, mid, line = d.cin, d.width, d.mid, d.line

    def whole(*dims):
        return pl.BlockSpec(dims, lambda t: (0,) * len(dims))

    def block(lanes):
        return pl.BlockSpec((line, lanes), lambda t: (t, 0))

    small_dims = [
        (cin, mid), (1, mid), (1, mid), (d.radix, 9, d.gin, wd), (1, d.wide), (1, d.wide), (wd, d.inter),
        (1, d.inter), (1, d.inter), (d.inter, d.wide), (1, d.wide), (wd, cin), (1, cin), (1, cin),
    ]
    return pl.pallas_call(
        functools.partial(finish_kernel, d),
        grid=(d.nh,),
        out_shape=[shape((d.rows, cin), BF16), shape((d.rows, cin), BF16)]
        + [shape(s, F32) for s in small_dims],
        in_specs=[
            block(cin), block(cin), block(mid), whole(cin, mid),
            whole(*wg0.shape), whole(*wg1.shape), whole(*wg2.shape), whole(*small.shape),
        ],
        out_specs=[block(cin), block(cin)] + [whole(*s) for s in small_dims],
        name="finish",
        compiler_params=pltpu.CompilerParams(vmem_limit_bytes=60 << 20),
    )(out_in, dn, dy, w1, wg0, wg1, wg2, small)


def on_device(
    inputs, image_count, pixel_mask, w_first, gain_first, bias_first, w_group, gain_group, bias_group,
    w_squeeze, gain_squeeze, bias_squeeze, w_excite, bias_excite, w_last, gain_last, bias_last, cotangent,
):
    n_img, n_ha = lax.axis_size("img"), lax.axis_size("ha")
    d = Dims(n_img, n_ha, inputs.shape, w_group.shape, w_squeeze.shape)
    nb, nh, nw, cin = inputs.shape

    def by_rows(cells):
        return jnp.transpose(cells, (1, 2, 0, 3)).reshape(d.rows, cin)

    def by_image(cells):
        return jnp.transpose(cells.reshape(nh, nw, nb, cin), (2, 0, 1, 3))

    live = (lax.broadcasted_iota(jnp.int32, (nb,), 0) < image_count[0]).astype(F32)
    valid = pixel_mask.astype(F32) * live[:, None, None]
    valid = jnp.transpose(valid, (1, 2, 0)).reshape(d.rows, 1)
    valid = jnp.broadcast_to(valid, (d.rows, LANES))
    live = jnp.broadcast_to(live[:, None], (nb, LANES))
    row = lambda v: v.reshape(1, -1)
    args = (
        by_rows(inputs), by_rows(cotangent), valid, live,
        w_first, row(gain_first), row(bias_first),
        w_group.reshape(d.radix, 9 * d.gin, d.width), row(gain_group), row(bias_group),
        w_squeeze, row(gain_squeeze), row(bias_squeeze), w_excite, row(bias_excite),
        w_last, row(gain_last), row(bias_last),
    )
    out, dn, dy, wg0, wg1, wg2, small = call_block(d, args)
    if not d.inside:
        wg0, wg1, wg2 = lax.psum((wg0, wg1, wg2), ("img", "ha"))
    done = call_finish(d, out, dn, dy, w_first, wg0, wg1, wg2, small)
    (out, gin, gw1, gg1, gb1, gw2, gg2, gb2, gwsq, ggs, gbs, gwex, gbex, gw3, gg3, gb3) = done
    flat = lambda v: v.reshape(-1)
    return (
        by_image(out), by_image(gin), gw1, flat(gg1), flat(gb1), gw2.reshape(w_group.shape), flat(gg2), flat(gb2),
        gwsq, flat(ggs), flat(gbs), gwex, flat(gbex), gw3, flat(gg3), flat(gb3),
    )


def solution(mesh):
    cells = P("img", "ha", None, None)
    placed = (cells, P("img"), P("img", "ha", None)) + (P(),) * 14 + (cells,)
    return jax.shard_map(
        on_device,
        mesh=mesh,
        in_specs=placed,
        out_specs=(cells, cells) + (P(),) * 14,
        check_vma=False,
    )
```

```python
import functools

import jax
import jax.numpy as jnp
from jax import lax
from jax.experimental import pallas as pl
from jax.experimental.pallas import tpu as pltpu
from jax.sharding import PartitionSpec as P

EPS = 1e-05
F32 = jnp.float32
BF16 = jnp.bfloat16
HIGH = lax.Precision.HIGHEST
MESH = pl.DeviceIdType.MESH
LANES = 128


def dot(a, b, precision=None):
    return jnp.dot(a, b, preferred_element_type=F32, precision=precision)


def dot_nt(a, b, precision=None):
    return lax.dot_general(
        a, b, (((1,), (1,)), ((), ())), preferred_element_type=F32, precision=precision
    )


def dot_tn(a, b, precision=None):
    return lax.dot_general(
        a, b, (((0,), (0,)), ((), ())), preferred_element_type=F32, precision=precision
    )


def wide(cell, lanes):
    return jnp.concatenate([cell] * (lanes // LANES), axis=1)


def fold(cells):
    rows, lanes = cells.shape
    return jnp.sum(cells.reshape(rows // 8, 8, lanes), axis=0)


def fold_images(cells, images):
    rows, lanes = cells.shape
    return jnp.sum(cells.reshape(rows // images, images, lanes), axis=0)


def total_row(cells):
    return jnp.sum(cells, axis=0, keepdims=True)


def put(ref, row, vector):
    for j in range(vector.shape[1] // LANES):
        ref[row + j : row + j + 1, :] = vector[:, j * LANES : (j + 1) * LANES]


def get(cells, row, lanes):
    return jnp.concatenate(
        [cells[row + j : row + j + 1, :] for j in range(lanes // LANES)], axis=1
    )


def moments(sums, squares, total):
    mean = sums / total
    spread = squares / total - mean * mean
    return mean, lax.rsqrt(spread + EPS)


def gate(half):
    bend = jnp.tanh(half)
    rise = 1.0 + bend
    value = half * rise
    return value, 0.5 * (rise + value * (1.0 - bend))


def split_bf16(cells):
    high = cells.astype(BF16)
    return high, (cells - high.astype(F32)).astype(BF16)


class Dims:
    def __init__(self, n_img, n_ha, inputs, w_group, w_squeeze):
        self.n_img, self.n_ha = n_img, n_ha
        self.nb, self.nh, self.nw, self.cin = inputs
        self.radix, _, _, self.gin, self.width = w_group
        self.mid = self.radix * self.gin
        self.wide = self.radix * self.width
        self.inter = w_squeeze[1]
        self.line = self.nw * self.nb
        self.rows = self.nh * self.line
        self.padded = (self.nw + 2) * self.nb
        self.half = (self.cin // 2, 6 * self.gin, self.cin // 2, 3 * self.gin + self.width, self.cin // 2)
        self.sets = 4
        self.inside = n_img == 8 and n_ha == 4
        self.sums = dict(cnt=4, s1=4, s2=8, act=4, v0=8, s3=16, b3=16, b2=8, misc=8, b1=4)
        self.paired = ("s3", "b3")


def block_kernel(
    d,
    x_hbm, ct_hbm, mask_in, count_in, w1, g1, c1, w2, g2, c2, wsq, gs, cs, wex, bex, w3, g3, c3,
    out_hbm, dn_hbm, dy_hbm, wg0_hbm, wg1_hbm, wg2_hbm, wg3_hbm, small,
    mb, live, xv, ctv, y1, a1p, y2, act2, slope2, mixed, ost, dm, acc_c, acc_g, w3p, w2x, w2l, w2r,
    att, q2, q4, vecs, pools, v0, cols,
    parts, rcs, rxys, rzs, mids, ress, vres, sums, ga_src, ga_buf, pf_src, pf_buf, fc_src, fc_buf,
    sem_x, sem_ct, sem_out, sem_dn, sem_misc, ssa, rsa, ssi, rsi, ssh, rsh, ssw, rsw,
):
    n_img, n_ha = d.n_img, d.n_ha
    nb, nh, nw = d.nb, d.nh, d.nw
    cin, mid, wd, wide2, line, rows = d.cin, d.mid, d.width, d.wide, d.line, d.rows
    gin, padded = d.gin, d.padded
    dyp = ctv
    half = cin // 2
    i = lax.axis_index("img")
    h = lax.axis_index("ha")

    def ha_peer(k):
        return (i, lax.rem(h + k, n_ha))

    def img_peer(k):
        return (lax.rem(i + k, n_img), h)

    z_of, x_of, y_of, core = i // 2, lax.rem(i, 2), h // 2, lax.rem(h, 2)
    spot = x_of * 2 + y_of

    def core_peer():
        return (i, y_of * 2 + (1 - core))

    def plane_peer(k):
        other = lax.rem(spot + k, 4)
        return (z_of * 2 + other // 2, lax.rem(other, 2) * 2 + core)

    def z_peer(k):
        return (lax.rem(z_of + k, 4) * 2 + x_of, h)

    def any_peer(k):
        return (lax.rem(i + k // 4, 8), lax.rem(h + k % 4, 4))

    def chip_peer(k):
        return (lax.rem(i + k // 2, 8), lax.rem(y_of + k % 2, 2) * 2 + core)

    def remote(src, dst, send, recv, peer):
        return pltpu.make_async_remote_copy(
            src_ref=src, dst_ref=dst, send_sem=send, recv_sem=recv, device_id=peer, device_id_type=MESH
        )

    def line_rows(t):
        return pl.ds(pl.multiple_of(t * line, line), line)

    def block_rows(t, u, step):
        return pl.ds(pl.multiple_of(t * line + u * step, nb), step)

    def x_copy(t):
        return pltpu.make_async_copy(x_hbm.at[line_rows(t)], xv.at[line_rows(t)], sem_x.at[t])

    def half_rows(t, c):
        return pl.ds(pl.multiple_of(c * rows + t * line, nb), line)

    def ct_copy(t, c):
        return pltpu.make_async_copy(
            ct_hbm.at[line_rows(t), pl.ds(c * half, half)], ctv.at[half_rows(t, c)], sem_ct.at[c, t]
        )

    def start_inputs(t, carry):
        x_copy(t).start()
        return carry

    lax.fori_loop(0, nh, start_inputs, 0)

    barrier = pltpu.get_barrier_semaphore()
    if d.inside:
        peers = [any_peer(k) for k in range(1, 32)]
    else:
        peers = [ha_peer(k) for k in range(1, n_ha)] + [img_peer(k) for k in range(1, n_img)]
    for peer in peers:
        pl.semaphore_signal(barrier, inc=1, device_id=peer, device_id_type=MESH)

    slots = lax.broadcasted_iota(jnp.int32, (nb, LANES), 0)
    live[...] = (slots < count_in[0]).astype(F32)

    def spread(t, carry):
        cells = mask_in[t].astype(F32)
        alive = live[...]
        for w in range(nw):
            cell = jnp.broadcast_to(cells[:, w : w + 1], (nb, LANES)) * alive
            mb[block_rows(t, w, nb), :] = cell.astype(BF16)
            carry = carry + cell
        return carry

    pixels = lax.fori_loop(0, nh, spread, jnp.zeros((nb, LANES), F32))

    def mask_of(at, lanes):
        return wide(mb[at, :].astype(F32), lanes)

    def inner_rows(t, at=nb, count=line):
        return pl.ds(pl.multiple_of(t * padded + at, nb), count)

    def clear(ref):
        zero = jnp.zeros((nb, ref.shape[1]), BF16)

        def body(t, carry):
            ref[inner_rows(t, 0, nb), :] = zero
            ref[inner_rows(t, nb + line, nb), :] = zero
            return carry

        lax.fori_loop(0, nh + 2, body, 0)

        def edge(t, carry):
            ref[inner_rows(0, t * nb, nb), :] = zero
            ref[inner_rows(nh + 1, t * nb, nb), :] = zero
            return carry

        lax.fori_loop(0, nw + 2, edge, 0)

    clear(a1p)
    pl.semaphore_wait(barrier, len(peers))

    def swap(src, buf, send, recv, peer, n):
        def copy(k):
            return remote(src, buf.at[k], send.at[k], recv.at[k], peer(k))

        def each(act, carry):
            if n > 32:
                return lax.fori_loop(1, n, act, carry)
            for k in range(1, n):
                carry = act(k, carry)
            return carry

        def begin(k, carry):
            copy(k).start()
            return carry

        def sent(k, carry):
            copy(k).wait_send()
            return carry

        def take(k, carry):
            copy(k).wait_recv()
            return carry + buf[k].astype(F32)

        def finish():
            total = each(take, src[...].astype(F32))
            each(sent, 0)
            return total

        return (lambda: each(begin, 0)), finish

    class Everywhere:
        def __init__(self, name):
            self.at, refs = sums[name]["src"], sums[name]
            self.refs = refs
            if not d.inside:
                return
            send, recv = refs["send"], refs["recv"]
            if name in d.paired:
                self.pair = remote(self.at, refs["other"], send.at[0], recv.at[0], core_peer())
                self.start_far, self.finish_far = swap(refs["mid"], refs["buf"], send, recv, chip_peer, 16)
            else:
                self.pair = None
                self.start_far, self.finish_far = swap(self.at, refs["buf"], send, recv, any_peer, 32)

        def start(self):
            if d.inside:
                if self.pair is not None:
                    self.pair.start()
                    self.pair.wait_recv()
                    self.refs["mid"][...] = self.at[...] + self.refs["other"][...]
                self.start_far()

        def finish(self):
            if d.inside:
                total = self.finish_far()
                if self.pair is not None:
                    self.pair.wait_send()
                return total
            refs = self.refs
            start, finish = swap(self.at, refs["buf_ha"], refs["send_ha"], refs["recv_ha"], ha_peer, n_ha)
            start()
            refs["mid"][...] = finish()
            start, finish = swap(refs["mid"], refs["buf_img"], refs["send"], refs["recv"], img_peer, n_img)
            start()
            return finish()

    def halo(ref, at):
        def down():
            return remote(
                ref.at[inner_rows(nh)], ref.at[inner_rows(0)], ssh.at[at, 0], rsh.at[at, 0],
                (i, jnp.minimum(h + 1, n_ha - 1)),
            )

        def up():
            return remote(
                ref.at[inner_rows(1)], ref.at[inner_rows(nh + 1)], ssh.at[at, 1], rsh.at[at, 1],
                (i, jnp.maximum(h - 1, 0)),
            )

        def start():
            @pl.when(h < n_ha - 1)
            def _():
                down().start()

            @pl.when(h > 0)
            def _():
                up().start()

        def wait_recv():
            @pl.when(h > 0)
            def _():
                down().wait_recv()

            @pl.when(h < n_ha - 1)
            def _():
                up().wait_recv()

        def wait_send():
            @pl.when(h < n_ha - 1)
            def _():
                down().wait_send()

            @pl.when(h > 0)
            def _():
                up().wait_send()

        return start, wait_recv, wait_send

    plane_rows, z_rows = wd // 4, wd // 16

    def plane_at(other):
        return pl.ds(pl.multiple_of(other * plane_rows, plane_rows), plane_rows)

    def z_at(other, base=0):
        return pl.ds(pl.multiple_of(base + other * z_rows, z_rows), z_rows)

    def w_copy(s, stage, k):
        sem = (s, stage * 4 + k)
        if stage == 0:
            src, dst, peer = parts[s].at[1 - core], rcs[s], core_peer()
        elif stage == 1:
            src = parts[s].at[core, plane_at(lax.rem(spot + k, 4))]
            dst, peer = rxys[s].at[k - 1], plane_peer(k)
        elif stage == 2:
            src = mids[s].at[z_at(lax.rem(z_of + k, 4))]
            dst, peer = rzs[s].at[k - 1], z_peer(k)
        elif stage == 3:
            src = dst = ress[s].at[core, z_at(z_of, spot * plane_rows)]
            peer = z_peer(k)
        elif stage == 4:
            src = dst = ress[s].at[core, plane_at(spot)]
            peer = plane_peer(k)
        else:
            src = dst = ress[s].at[core]
            peer = core_peer()
        return remote(src, dst, ssw.at[sem], rsw.at[sem], peer)

    def w_ks(stage):
        return (1,) if stage in (0, 5) else (1, 2, 3)

    def w_arrival(s, stage, k):
        sem = (s, stage * 4 + k)
        if stage == 3:
            dst = ress[s].at[core, z_at(lax.rem(z_of - k + 4, 4), spot * plane_rows)]
        elif stage == 4:
            dst = ress[s].at[core, plane_at(lax.rem(spot - k + 4, 4))]
        else:
            dst = ress[s].at[1 - core]
        return remote(dst, dst, ssw.at[sem], rsw.at[sem], core_peer())

    def w_start(s, stage):
        if d.inside:
            for k in w_ks(stage):
                w_copy(s, stage, k).start()

    def w_finish(s, stage, fix=None):
        if not d.inside:
            return
        for k in w_ks(stage):
            if stage <= 2:
                w_copy(s, stage, k).wait_recv()
            else:
                w_arrival(s, stage, k).wait_recv()
        part, inner = parts[s], mids[s]
        if stage == 0:
            rc = rcs[s]

            def add(t, carry):
                at = pl.ds(pl.multiple_of(t * 16, 16), 16)
                part[core, at, :] = (part[core, at, :].astype(F32) + rc[at, :].astype(F32)).astype(BF16)
                return carry

            lax.fori_loop(0, wd // 16, add, 0)
        elif stage == 1:
            buf = rxys[s]

            def add(t, carry):
                at = pl.ds(pl.multiple_of(t * 16, 16), 16)
                own = pl.ds(pl.multiple_of(spot * plane_rows + t * 16, 16), 16)
                total = part[core, own, :].astype(F32)
                for k in range(3):
                    total = total + buf[k, at, :].astype(F32)
                inner[at, :] = total.astype(BF16)
                return carry

            lax.fori_loop(0, plane_rows // 16, add, 0)
        elif stage == 2:
            buf = rzs[s]
            total = inner[z_at(z_of), :].astype(F32)
            for k in range(3):
                total = total + buf[k].astype(F32)
            if s >= d.sets:
                vres[...] = total
                return
            if fix is not None:
                total = fix(total)
            ress[s][core, z_at(z_of, spot * plane_rows), :] = total.astype(BF16)

    def w_step(s, stage, fix=None):
        w_finish(s, stage, fix)
        if stage < 5:
            w_start(s, stage + 1)

    def w_sent(s):
        if d.inside:
            for stage in range(6 if s < d.sets else 3):
                for k in w_ks(stage):
                    w_copy(s, stage, k).wait_send()

    count = Everywhere("cnt")
    count.at[...] = jnp.zeros((4, LANES), F32)
    count.at[0:1, :] = total_row(pixels)
    count.at[1:2, :] = total_row(live[...]) * (1.0 / n_ha)
    count.start()

    def first(t, carry):
        sums, squares = carry
        x_copy(t).wait()
        ct_copy(t, 0).start()
        ct_copy(t, 1).start()
        at = line_rows(t)
        y = dot(xv[at, :], w1[...])
        y1[at, :] = y
        masked = y * mask_of(at, mid)
        return sums + fold(masked), squares + fold(masked * y)

    zeros = jnp.zeros((8, mid), F32)
    totals, squares = lax.fori_loop(0, nh, first, (zeros, zeros))
    norm1 = Everywhere("s1")
    put(norm1.at, 0, total_row(totals))
    put(norm1.at, 2, total_row(squares))
    norm1.start()
    for r in range(d.radix):
        for ky in range(3):
            for e in range(4):
                if e <= 2:
                    left = w2[r, (ky * 3 + 2 - e) * gin : (ky * 3 + 3 - e) * gin, :]
                if e >= 1:
                    right = w2[r, (ky * 3 + 3 - e) * gin : (ky * 3 + 4 - e) * gin, :]
                if e == 0:
                    w2l[r, :, ky * wd : (ky + 1) * wd] = left
                elif e == 3:
                    w2r[r, :, ky * wd : (ky + 1) * wd] = right
                else:
                    lanes = slice((ky * 2 + e - 1) * wd, (ky * 2 + e) * wd)
                    w2x[r, 0:gin, lanes] = left
                    w2x[r, gin:, lanes] = right
    got = count.finish()
    total, images = got[0:1, :], got[1:2, :]
    got = norm1.finish()
    mean1, scale1 = moments(get(got, 0, mid), get(got, 2, mid), wide(total, mid))
    half_a1 = 0.5 * g1[...] * scale1
    half_b1 = 0.5 * c1[...] - half_a1 * mean1

    step1 = 4 * nb

    def act_first(t, carry):
        def cells(u, carry):
            at = block_rows(t, u, step1)
            value, _ = gate(y1[at, :] * half_a1 + half_b1)
            value = value * mask_of(at, mid)
            a1p[inner_rows(t + 1, nb + u * step1, step1), :] = value.astype(BF16)
            return carry + fold(value)

        return lax.fori_loop(0, line // step1, cells, carry)

    def edges(body, carry):
        return lax.fori_loop(0, 2, lambda t, c: body(t * (nh - 1), c), carry)

    totals = edges(act_first, jnp.zeros((8, mid), F32))
    halo1_start, halo1_recv, halo1_sent = halo(a1p, 0)
    halo1_start()
    totals = lax.fori_loop(1, nh - 1, act_first, totals)
    act_sum = Everywhere("act")
    act_sum.at[...] = jnp.zeros((4, LANES), F32)
    put(act_sum.at, 0, total_row(totals))
    act_sum.start()

    def taps(t, r, first=0, last=9):
        return jnp.concatenate(
            [
                a1p[inner_rows(t + tap // 3, (tap % 3) * nb), r * gin : (r + 1) * gin]
                for tap in range(first, last)
            ],
            axis=1,
        )

    def group(t, carry):
        at = line_rows(t)
        mask = mask_of(at, wd)
        done = []
        for r in range(d.radix):
            sums, squares = carry[r]
            y = dot(taps(t, r), w2[r])
            y2[at, r * wd : (r + 1) * wd] = y.astype(BF16)
            masked = y * mask
            done.append((sums + fold(masked), squares + fold(masked * y)))
        return tuple(done)

    zeros = jnp.zeros((8, wd), F32)
    sums2 = lax.fori_loop(1, nh - 1, group, ((zeros, zeros),) * d.radix)
    halo1_recv()
    sums2 = edges(group, sums2)
    norm2 = Everywhere("s2")
    put(norm2.at, 0, jnp.concatenate([total_row(s) for s, _ in sums2], axis=1))
    put(norm2.at, 4, jnp.concatenate([total_row(q) for _, q in sums2], axis=1))
    norm2.start()

    acc_c[...] = jnp.zeros((wd, cin), F32)
    vecs[...] = jnp.zeros((8, cin), F32)

    def norm_products(t, carry):
        at = line_rows(t)
        mask = mask_of(at, mid)
        hat = ((y1[at, :] - mean1) * scale1 * mask).astype(BF16)
        x = xv[at, :]
        acc_c[...] += dot_tn(hat, x)
        vecs[...] += dot_tn(mb[at, :], x)[0:8, :]
        return carry

    lax.fori_loop(0, nh, norm_products, 0)
    norm2_done = norm2.finish()
    for c in range(2):
        parts[4][c] = acc_c[:, c * half : (c + 1) * half].astype(BF16)
    w_start(4, 0)
    v0_sum = Everywhere("v0")
    put(v0_sum.at, 0, vecs[0:1, :])
    v0_sum.start()
    mean2, scale2 = moments(get(norm2_done, 0, wide2), get(norm2_done, 4, wide2), wide(total, wide2))
    half_a2 = 0.5 * g2[...] * scale2
    half_b2 = 0.5 * c2[...] - half_a2 * mean2

    lane_blocks = wd // LANES
    step2 = 4 * nb
    zero = jnp.zeros((nb, LANES), F32)
    for j in range(lane_blocks):
        own = slice(j * LANES, (j + 1) * LANES)

        def act_group(t, pool):
            at = pl.ds(pl.multiple_of(t * step2, step2), step2)
            mask = mb[at, :]
            full = mask.astype(F32)
            for r in range(d.radix):
                lanes = slice(r * wd + j * LANES, r * wd + (j + 1) * LANES)
                value, _ = gate(y2[at, lanes].astype(F32) * half_a2[:, lanes] + half_b2[:, lanes])
                value = value * full
                act2[at, lanes] = value.astype(BF16)
                pool = pool + fold_images(value, nb)
            return pool

        pools[:, own] = lax.fori_loop(0, rows // step2, act_group, zero)

    pool = pools[...]
    squeeze = wsq[...].astype(F32)
    excite = wex[...].astype(F32)
    pf_src[:, 0 : d.inter] = dot(pool, squeeze, HIGH)
    pf_src[:, d.inter :] = pixels
    pf_start, pf_finish = swap(pf_src, pf_buf, ssa.at[0], rsa.at[0], ha_peer, n_ha)
    pf_start()

    def slopes(block):
        lanes = slice(block * LANES, (block + 1) * LANES)
        ha2, hb2 = half_a2[:, lanes], half_b2[:, lanes]

        def body(t, carry):
            slopes, bends = carry
            at = pl.ds(pl.multiple_of(t * step2, step2), step2)
            y = y2[at, lanes].astype(F32)
            _, slope = gate(y * ha2 + hb2)
            slope = slope * mb[at, :].astype(F32)
            slope2[at, lanes] = slope.astype(BF16)
            return slopes + fold_images(slope, nb), bends + fold_images(slope * y, nb)

        q2[:, lanes], q4[:, lanes] = lax.fori_loop(0, rows // step2, body, (zero, zero))

    total_blocks = d.radix * lane_blocks
    for block in range(total_blocks // 4):
        slopes(block)
    w_step(4, 0)
    both = pf_finish()
    floor = jnp.maximum(both[:, d.inter :], 1.0)
    squeezed = both[:, 0 : d.inter] / floor
    live_now = live[...]
    fc_src[...] = jnp.zeros(fc_src.shape, F32)
    put(fc_src.at[0], 0, total_row(squeezed * live_now))
    put(fc_src.at[0], 1, total_row(squeezed * squeezed * live_now))
    fc_start, fc_finish = swap(fc_src.at[0], fc_buf.at[0], ssi.at[0], rsi.at[0], img_peer, n_img)
    fc_start()
    for block in range(total_blocks // 4, total_blocks):
        slopes(block)
    got = fc_finish()
    mean_s, scale_s = moments(got[0:1, :], got[1:2, :], images)
    centered = (squeezed - mean_s) * scale_s
    hidden, hidden_slope = gate(0.5 * (centered * gs[...] + cs[...]))
    logits = dot(hidden, excite, HIGH) + bex[...]
    gap = logits[:, 0:wd] - logits[:, wd:]
    att[:, 0:wd] = jax.nn.sigmoid(gap)
    att[:, wd:] = jax.nn.sigmoid(-gap)

    step3 = 2 * nb

    def mix(t, carry):
        def cells(u, carry):
            at = block_rows(t, u, step3)
            weight = jnp.concatenate([att[...]] * (step3 // nb), axis=0)
            both = act2[at, :].astype(F32) * weight
            mixed[at, :] = (both[:, 0:wd] + both[:, wd:]).astype(BF16)
            return carry

        lax.fori_loop(0, line // step3, cells, 0)
        gram, sums = carry
        cells = mixed[line_rows(t), :]
        return gram + dot_tn(cells, cells), sums + fold(cells.astype(F32))

    gram, totals = lax.fori_loop(0, nh, mix, (jnp.zeros((wd, wd), F32), jnp.zeros((8, wd), F32)))
    mix_sum = total_row(totals)
    gram_high, gram_low = split_bf16(gram)
    acc_g[0, :, 0:cin] = dot(gram_high, w3[...]) + dot(gram_low, w3[...])
    mix_high, mix_low = split_bf16(mix_sum)
    sum_last = dot(jnp.broadcast_to(mix_high, (16, wd)), w3[...]) + dot(
        jnp.broadcast_to(mix_low, (16, wd)), w3[...]
    )
    norm3 = Everywhere("s3")
    put(norm3.at, 0, sum_last[0:1, :])
    put(norm3.at, 8, total_row(acc_g[0, :, 0:cin] * w3[...].astype(F32)))
    norm3.start()

    def last_product(t, carry):
        at = line_rows(t)
        ost[at, :] = dot(mixed[at, :], w3[...]).astype(BF16)
        ct_copy(t, 0).wait()
        ct_copy(t, 1).wait()
        return carry

    lax.fori_loop(0, nh, last_product, 0)
    w_step(4, 1)
    got = norm3.finish()
    mean3, scale3 = moments(get(got, 0, cin), get(got, 8, cin), wide(total, cin))
    grow3 = g3[...] * scale3
    half_a3 = 0.5 * grow3
    half_b3 = 0.5 * c3[...] - half_a3 * mean3

    step4 = 4 * nb
    blocks4 = 2 * LANES

    def out_copy(t):
        return pltpu.make_async_copy(ost.at[line_rows(t)], out_hbm.at[line_rows(t)], sem_out.at[t])

    def dn_copy(t, c):
        return pltpu.make_async_copy(
            ctv.at[half_rows(t, c)], dn_hbm.at[line_rows(t), pl.ds(c * half, half)], sem_dn.at[c, t]
        )

    def grad_of(t):
        return jnp.concatenate([ctv[half_rows(t, 0), :], ctv[half_rows(t, 1), :]], axis=1)

    acc_c[...] = jnp.zeros((wd, cin), F32)
    vecs[...] = jnp.zeros((8, cin), F32)

    def last(t, carry):
        for j in range(cin // blocks4):
            lanes = slice(j * blocks4, (j + 1) * blocks4)
            a3, b3 = half_a3[:, lanes], half_b3[:, lanes]

            def cells(u, carry):
                at = block_rows(t, u, step4)
                mask = wide(mb[at, :], blocks4)
                x = xv[at, lanes] * jnp.asarray(0.5, BF16)
                arg = ost[at, lanes].astype(F32) * a3 + (b3 + x.astype(F32))
                bend = jnp.tanh(arg)
                rise = 1.0 + bend
                value = arg * rise
                ost[at, lanes] = value.astype(BF16) * mask
                side = j * blocks4 // half
                there = pl.ds(pl.multiple_of(side * rows + t * line + u * step4, nb), step4)
                inner = slice(j * blocks4 - side * half, (j + 1) * blocks4 - side * half)
                push = ctv[there, inner] * (mask * jnp.asarray(0.5, BF16))
                grad = push.astype(F32) * (rise + value * (1.0 - bend))
                ctv[there, inner] = grad.astype(BF16)
                return carry + fold(grad)

            vecs[:, lanes] = lax.fori_loop(0, line // step4, cells, vecs[:, lanes])
        out_copy(t).start()
        dn_copy(t, 0).start()
        dn_copy(t, 1).start()
        acc_c[...] += dot_tn(mixed[line_rows(t), :], grad_of(t))
        return carry

    lax.fori_loop(0, nh, last, 0)
    sum_grad = total_row(vecs[...])
    back3 = Everywhere("b3")
    put(back3.at, 0, sum_grad)
    put(back3.at, 8, scale3 * (total_row(acc_c[...] * w3[...].astype(F32)) - mean3 * sum_grad))
    back3.start()

    w3p[...] = (w3[...].astype(F32) * grow3).astype(BF16)

    def plain_back(t, carry):
        dm[line_rows(t), :] = dot_nt(grad_of(t), w3p[...])
        return carry

    lax.fori_loop(0, nh, plain_back, 0)
    w_finish(4, 2)
    got = back3.finish()
    bias3, gain3 = get(got, 0, cin), get(got, 8, cin)
    put(small.at[0], 0, bias3)
    put(small.at[0], 8, gain3)
    all_wide = wide(total, cin)
    slant3 = scale3 * gain3 / all_wide
    level3 = bias3 / all_wide - mean3 * slant3
    fix = (w3[...].astype(F32) * slant3).astype(BF16)
    fix = dot_nt(fix, w3p[...]).astype(BF16)
    level_high, level_low = split_bf16(level3)
    shift = dot_nt(jnp.broadcast_to(level_high, (16, cin)), w3p[...]) + dot_nt(
        jnp.broadcast_to(level_low, (16, cin)), w3p[...]
    )
    shift = shift[0:1, :]

    def back_mix(t, carry):
        at = line_rows(t)
        dm[at, :] = dm[at, :] - dot(mixed[at, :], fix) - mask_of(at, wd) * shift
        return carry

    lax.fori_loop(0, nh, back_mix, 0)

    step5 = 4 * nb
    sums5 = []
    for j in range(lane_blocks):
        lanes = slice(j * LANES, (j + 1) * LANES)

        def image_sums(t, carry):
            at = pl.ds(pl.multiple_of(t * step5, step5), step5)
            grad = dm[at, lanes]
            done = []
            for r in range(d.radix):
                own = slice(r * wd + j * LANES, r * wd + (j + 1) * LANES)
                a, b, c = carry[r]
                a = a + fold_images(grad * act2[at, own].astype(F32), nb)
                part = grad * slope2[at, own].astype(F32)
                b = b + fold_images(part, nb)
                c = c + fold_images(part * y2[at, own].astype(F32), nb)
                done.append((a, b, c))
            return tuple(done)

        sums5.append(lax.fori_loop(0, rows // step5, image_sums, ((zero, zero, zero),) * d.radix))
    pick = lambda which: jnp.concatenate(
        [sums5[j][r][which] for r in range(d.radix) for j in range(lane_blocks)], axis=1
    )
    q1, q3 = pick(1), pick(2)

    def dn_out(t, carry):
        dn_copy(t, 0).wait()
        dn_copy(t, 1).wait()
        return carry

    lax.fori_loop(0, nh, dn_out, 0)
    clear(dyp)
    ga_src[...] = pick(0).astype(BF16)
    ga_start, ga_finish = swap(ga_src, ga_buf, ssa.at[1], rsa.at[1], ha_peer, n_ha)
    ga_start()

    mix_column = jnp.transpose(jnp.broadcast_to(mix_sum, (LANES, wd)))
    for j in range(cin // LANES):
        lanes = slice(j * LANES, (j + 1) * LANES)
        c = 0 if j * LANES < half else 1
        grad = grow3[:, lanes] * (
            acc_c[:, lanes] - mix_column * level3[:, lanes] - acc_g[0, :, lanes] * slant3[:, lanes]
        )
        parts[2][c, :, j * LANES - c * half : (j + 1) * LANES - c * half] = grad.astype(BF16)
    w_start(2, 0)

    grad_att = ga_finish()
    weight = att[...]
    weighed = weight * grad_att
    both = weighed[:, 0:wd] + weighed[:, wd:]
    grad_logits = weight * (grad_att - jnp.concatenate([both, both], axis=1))
    grad_fc = dot_nt(grad_logits, excite, HIGH) * hidden_slope
    put(fc_src.at[1], 0, total_row(grad_fc))
    put(fc_src.at[1], 1, total_row(grad_fc * centered))
    pooled = pool / wide(floor, wd)
    put(fc_src.at[1], 2, total_row(pooled))
    fc_start, fc_finish = swap(fc_src.at[1], fc_buf.at[1], ssi.at[1], rsi.at[1], img_peer, n_img)
    fc_start()
    w_step(2, 0)
    grad_excite = dot_tn(hidden, grad_logits, HIGH)
    grad_bex = total_row(grad_logits) * (1.0 / n_ha)
    acc_g[...] = jnp.zeros((d.radix, wd, 9 * gin), F32)
    got = fc_finish()
    bias_s, gain_s = got[0:1, :], got[1:2, :]
    put(small.at[0], 16, bias_s)
    put(small.at[0], 17, gain_s)
    grad_squeezed = (gs[...] * scale_s) * (
        grad_fc - live_now * (bias_s + centered * gain_s) / images
    )
    grad_pool = dot_nt(grad_squeezed, squeeze, HIGH) / wide(floor, wd)
    pool2 = jnp.concatenate([grad_pool] * d.radix, axis=1)
    sum_grad = total_row(weight * q1 + pool2 * q2[...])
    sum_bend = total_row(weight * q3 + pool2 * q4[...])
    back2 = Everywhere("b2")
    put(back2.at, 0, sum_grad)
    put(back2.at, 4, scale2 * (sum_bend - mean2 * sum_grad))
    back2.start()
    level = get(got, 2, wd) / wide(images, wd)
    grad_squeeze = dot_tn(pooled - level, grad_squeezed, HIGH)
    grow2 = g2[...] * scale2
    att[...] = weight * grow2
    q2[...] = pool2 * grow2
    w_step(2, 1)
    mean_act1 = get(act_sum.finish(), 0, mid) / (wide(images, mid) * float(nh * n_ha * nw))
    got = back2.finish()
    bias2, gain2 = get(got, 0, wide2), get(got, 4, wide2)
    put(small.at[0], 20, bias2)
    put(small.at[0], 24, gain2)
    slant2 = grow2 * scale2 * gain2 / wide(total, wide2)
    level2 = grow2 * bias2 / wide(total, wide2) - mean2 * slant2

    step6 = 2 * nb

    def back_group(t, carry):
        def cells(u, carry):
            at = block_rows(t, u, step6)
            to = inner_rows(t + 1, nb + u * step6, step6)
            again = step6 // nb
            grad = dm[at, :]
            mask = mask_of(at, wd)
            sums = []
            for r in range(d.radix):
                own = slice(r * wd, (r + 1) * wd)
                grow = jnp.concatenate([att[:, own]] * again, axis=0)
                lift = jnp.concatenate([q2[:, own]] * again, axis=0)
                push = (grow * grad + lift) * slope2[at, own].astype(F32)
                pull = mask * (level2[:, own] + slant2[:, own] * y2[at, own].astype(F32))
                dyp[to, own] = (push - pull).astype(BF16)
                sums.append(carry[r] + fold(push - pull))
            return tuple(sums)

        return lax.fori_loop(0, line // step6, cells, carry)

    zeros = jnp.zeros((8, wd), F32)
    sums2 = edges(back_group, (zeros,) * d.radix)
    halo2_start, halo2_recv, halo2_sent = halo(dyp, 1)
    halo2_start()
    sums2 = lax.fori_loop(1, nh - 1, back_group, sums2)
    sum_dy2 = [total_row(s) for s in sums2]
    misc = Everywhere("misc")
    put(misc.at, 0, jnp.concatenate(sum_dy2, axis=1))
    put(misc.at, 4, grad_bex)
    misc.start()
    w_step(2, 2)

    def weights_group(first, last):
        def body(t, carry):
            for r in range(d.radix):
                grad = dyp[inner_rows(t + 1), r * wd : (r + 1) * wd]
                acc_g[r, :, first * gin : last * gin] += dot_tn(grad, taps(t, r, first, last))
            return carry

        lax.fori_loop(0, nh, body, 0)

    def send_group(s, first, last):
        lanes = (last - first) * gin
        for r in range(d.radix):
            base = wide(mean_act1[:, r * gin : (r + 1) * gin], lanes)
            column = jnp.transpose(jnp.broadcast_to(sum_dy2[r], (LANES, wd)))
            grad = acc_g[r, :, first * gin : last * gin] - wide(column, lanes) * base
            parts[s][r, :, 0:lanes] = grad.astype(BF16)
        w_start(s, 0)

    weights_group(0, 6)
    send_group(1, 0, 6)
    parts[3][0, :, 3 * gin :] = jnp.concatenate(
        [grad_excite[:, 0:wd], grad_excite[:, wd:]], axis=0
    ).astype(BF16) * jnp.asarray(1.0 / n_ha, BF16)
    parts[3][1, :, 3 * gin : 3 * gin + d.inter] = grad_squeeze.astype(BF16)
    parts[3][1, :, 3 * gin + d.inter :] = jnp.zeros((wd, wd - d.inter), BF16)
    weights_group(6, 9)
    send_group(3, 6, 9)
    w_step(1, 0)
    w_step(2, 3)

    pairs = nw // 2

    def back_taps(t, r, which):
        cells = []
        for ky in range(3):
            for e in which:
                block = dyp[inner_rows(t + 2 - ky, e * nb), r * wd : (r + 1) * wd]
                block = block.reshape(pairs, 2 * nb, wd)[:, 0:nb, :].reshape(pairs * nb, wd)
                cells.append(block)
        return jnp.concatenate(cells, axis=1)

    def transposed(t, carry):
        sums, bends = carry
        at = line_rows(t)
        done = []
        for r in range(d.radix):
            both = dot_nt(back_taps(t, r, (1, 2)), w2x[r])
            left = both[:, 0:gin] + dot_nt(back_taps(t, r, (0,)), w2l[r])
            right = both[:, gin:] + dot_nt(back_taps(t, r, (3,)), w2r[r])
            both = jnp.concatenate(
                [left.reshape(pairs, nb, gin), right.reshape(pairs, nb, gin)], axis=1
            )
            done.append(both.reshape(line, gin))
        dm[at, :] = jnp.concatenate(done, axis=1)

        def cells(u, carry):
            sums, bends = carry
            at = block_rows(t, u, step1)
            y = y1[at, :]
            _, slope = gate(y * half_a1 + half_b1)
            grad = dm[at, :] * (slope * mask_of(at, mid))
            dm[at, :] = grad
            mixed[at, :] = grad.astype(BF16)
            return sums + fold(grad), bends + fold(grad * y)

        return lax.fori_loop(0, line // step1, cells, (sums, bends))

    zeros = jnp.zeros((8, mid), F32)
    sums1 = lax.fori_loop(1, nh - 1, transposed, (zeros, zeros))
    halo2_recv()
    sums1 = edges(transposed, sums1)
    sum_grad = total_row(sums1[0])
    back1 = Everywhere("b1")
    put(back1.at, 0, sum_grad)
    put(back1.at, 2, scale1 * (total_row(sums1[1]) - mean1 * sum_grad))
    back1.start()

    acc_c[...] = jnp.zeros((wd, cin), F32)

    def first_weights(t, carry):
        at = line_rows(t)
        acc_c[...] += dot_tn(mixed[at, :], xv[at, :])
        return carry

    lax.fori_loop(0, nh, first_weights, 0)
    w_step(1, 1)
    w_step(3, 0)
    if d.inside:
        for c in range(2):
            parts[0][c] = acc_c[:, c * half : (c + 1) * half].astype(BF16)
    w_start(0, 0)
    got = back1.finish()
    bias1, gain1 = get(got, 0, mid), get(got, 2, mid)
    grow1 = g1[...] * scale1
    bias_all, gain_all = bias1 / wide(total, mid), gain1 / wide(total, mid)
    slant1 = grow1 * scale1 * gain_all
    level1 = grow1 * bias_all - mean1 * slant1
    w_step(0, 0)

    def dy_copy(t):
        return pltpu.make_async_copy(mixed.at[line_rows(t)], dy_hbm.at[line_rows(t)], sem_misc.at[t])

    def back_first(t, carry):
        def cells(u, carry):
            at = block_rows(t, u, step1)
            pull = mask_of(at, mid) * (level1 + slant1 * y1[at, :])
            mixed[at, :] = (grow1 * dm[at, :] - pull).astype(BF16)
            return carry

        lax.fori_loop(0, line // step1, cells, 0)
        dy_copy(t).start()
        return carry

    lax.fori_loop(0, nh, back_first, 0)
    put(small.at[0], 32, bias1)
    put(small.at[0], 34, gain1)
    put(small.at[0], 36, mean_act1)
    small[0, 18:20, :] = jnp.zeros((2, LANES), F32)
    small[0, 38:40, :] = jnp.zeros((2, LANES), F32)
    small[0, 44:48, :] = jnp.zeros((4, LANES), F32)
    got = misc.finish()
    put(small.at[0], 28, get(got, 4, wide2))
    put(small.at[0], 40, get(got, 0, wide2))
    got = v0_sum.finish()
    for c in range(2):
        v0[c] = jnp.broadcast_to(get(got, 0, cin)[:, c * half : (c + 1) * half], (8, half))
    for j, vector in enumerate((grow1, bias_all, gain_all)):
        cols[j] = jnp.transpose(jnp.broadcast_to(vector, (LANES, mid)))

    def norm_terms(total, at, taken, flat):
        lanes = total.shape[1]
        grow, level, slant = (wide(cols[j, at, :], lanes) for j in range(3))
        return grow * (total - level * flat - slant * taken)

    def fix_first(total):
        return norm_terms(total, z_at(z_of, spot * plane_rows), vres[...], v0[core, 0:1, :])

    w_step(1, 2)
    w_step(0, 1)
    w_step(3, 1)
    w_step(1, 3)
    w_step(0, 2, fix_first)
    w_step(3, 2)
    w_step(1, 4)
    w_step(0, 3)
    w_step(3, 3)
    w_step(0, 4)
    w_step(3, 4)
    w_step(2, 4)
    for s in (1, 0, 3, 2):
        w_step(s, 5)
    if not d.inside:
        whole = slice(0, wd)
        for c in range(2):
            lanes = slice(c * half, (c + 1) * half)
            local = wide(cols[0, whole, :], half) * (
                acc_c[:, lanes]
                - wide(cols[1, whole, :], half) * get(v0_sum.at[...], 0, cin)[:, lanes]
                - wide(cols[2, whole, :], half) * parts[4][c].astype(F32)
            )
            parts[0][c] = local.astype(BF16)

    results = tuple(enumerate((wg0_hbm, wg1_hbm, wg2_hbm, wg3_hbm)))
    for s, hbm in results:
        pltpu.make_async_copy((ress if d.inside else parts)[s], hbm, sem_misc.at[nh + s]).start()

    def finish(t, carry):
        dy_copy(t).wait()
        out_copy(t).wait()
        return carry

    lax.fori_loop(0, nh, finish, 0)
    for s in range(d.sets + 1):
        w_sent(s)
    halo1_sent()
    halo2_sent()
    for s, hbm in results:
        pltpu.make_async_copy((ress if d.inside else parts)[s], hbm, sem_misc.at[nh + s]).wait()


def call_block(d, args):
    f32, bf16 = F32, BF16
    cin, wd, mid, rows, nb, nh = d.cin, d.width, d.mid, d.rows, d.nb, d.nh
    vmem, dma = pltpu.VMEM, pltpu.SemaphoreType.DMA
    halves = [(2, wd, lanes) for lanes in d.half]
    shape = jax.ShapeDtypeStruct
    outs = [
        shape((rows, cin), bf16),
        shape((rows, cin), bf16),
        shape((rows, mid), bf16),
        *[shape(s, bf16) for s in halves[: d.sets]],
        shape((1, 48, LANES), f32),
    ]
    anywhere = pl.BlockSpec(memory_space=pl.ANY)
    inside = pl.BlockSpec(memory_space=pltpu.VMEM)
    plane, zed = wd // 4, wd // 16

    def sums_of(name, count):
        if not d.inside:
            return dict(
                src=vmem((count, LANES), f32),
                mid=vmem((count, LANES), f32),
                buf_ha=vmem((d.n_ha, count, LANES), f32),
                buf_img=vmem((d.n_img, count, LANES), f32),
                send_ha=dma((d.n_ha,)), recv_ha=dma((d.n_ha,)),
                send=dma((d.n_img,)), recv=dma((d.n_img,)),
            )
        if name in d.paired:
            return dict(
                src=vmem((count, LANES), f32),
                mid=vmem((count, LANES), f32),
                other=vmem((count, LANES), f32),
                buf=vmem((16, count, LANES), f32),
                send=dma((16,)), recv=dma((16,)),
            )
        return dict(
            src=vmem((count, LANES), f32),
            buf=vmem((32, count, LANES), f32),
            send=dma((32,)), recv=dma((32,)),
        )

    scratch = [
        vmem((rows, LANES), bf16),
        vmem((nb, LANES), f32),
        vmem((rows, cin), bf16),
        vmem((max(2 * rows, (nh + 2) * d.padded), cin // 2), bf16),
        vmem((rows, mid), f32),
        vmem(((nh + 2) * d.padded, mid), bf16),
        vmem((rows, d.wide), bf16),
        vmem((rows, d.wide), bf16),
        vmem((rows, d.wide), bf16),
        vmem((rows, wd), bf16),
        vmem((rows, cin), bf16),
        vmem((rows, wd), f32),
        vmem((wd, cin), f32),
        vmem((d.radix, wd, 9 * d.gin), f32),
        vmem((wd, cin), bf16),
        vmem((d.radix, 2 * d.gin, 6 * wd), bf16),
        vmem((d.radix, d.gin, 3 * wd), bf16),
        vmem((d.radix, d.gin, 3 * wd), bf16),
        vmem((nb, d.wide), f32),
        vmem((nb, d.wide), f32),
        vmem((nb, d.wide), f32),
        vmem((8, cin), f32),
        vmem((nb, wd), f32),
        vmem((2, 8, cin // 2), f32),
        vmem((3, mid, LANES), f32),
        [vmem(s, bf16) for s in halves],
        [vmem((wd, lanes), bf16) for lanes in d.half],
        [vmem((3, plane, lanes), bf16) for lanes in d.half],
        [vmem((3, zed, lanes), bf16) for lanes in d.half],
        [vmem((plane, lanes), bf16) for lanes in d.half],
        [vmem(s, bf16) for s in halves[: d.sets]],
        vmem((zed, d.half[0]), f32),
        {name: sums_of(name, count) for name, count in d.sums.items()},
        vmem((nb, d.wide), bf16),
        vmem((d.n_ha, nb, d.wide), bf16),
        vmem((nb, 2 * LANES), f32),
        vmem((d.n_ha, nb, 2 * LANES), f32),
        vmem((2, 4, LANES), f32),
        vmem((2, d.n_img, 4, LANES), f32),
        dma((nh,)),
        dma((2, nh)),
        dma((nh,)),
        dma((2, nh)),
        dma((nh + 4,)),
        dma((2, d.n_ha)),
        dma((2, d.n_ha)),
        dma((2, d.n_img)),
        dma((2, d.n_img)),
        dma((2, 2)),
        dma((2, 2)),
        dma((5, 24)),
        dma((5, 24)),
    ]
    return pl.pallas_call(
        functools.partial(block_kernel, d),
        out_shape=outs,
        in_specs=[anywhere, anywhere, inside, pl.BlockSpec(memory_space=pltpu.SMEM)] + [inside] * 14,
        out_specs=[anywhere] * 7 + [inside],
        scratch_shapes=scratch,
        name="block",
        compiler_params=pltpu.CompilerParams(
            collective_id=0, has_side_effects=True, vmem_limit_bytes=61 << 20
        ),
    )(*args)


def finish_kernel(
    d, out_in, dn_hbm, dy_hbm, w1_hbm, wg0_hbm, wg1_hbm, wg2_hbm, wg3_hbm, small_hbm,
    out, gin_hbm, gw1_hbm, gg1, gb1, gw2_hbm, gg2, gb2, gwsq, ggs, gbs, gwex, gbex, gw3_hbm, gg3, gb3,
    passing, dn, dy, w1, wg0, wg1, wg2, wg3, small, gw1, gw2, gw3, sem_in, sem_out, sem_w, sem_gw,
):
    nh, line, wd, taps = d.nh, d.line, d.width, 3 * d.gin

    def at(t):
        return pl.ds(t * line, line)

    def copy(t, which):
        src, dst = ((out_in, passing), (dn_hbm, dn), (dy_hbm, dy))[which]
        return pltpu.make_async_copy(src.at[at(t)], dst.at[at(t)], sem_in.at[which, t])

    def back(t, which):
        src, dst = ((passing, out), (dn, gin_hbm))[which]
        return pltpu.make_async_copy(src.at[at(t)], dst.at[at(t)], sem_out.at[which, t])

    loads = [
        pltpu.make_async_copy(src, dst, sem_w.at[j])
        for j, (src, dst) in enumerate(
            ((w1_hbm, w1), (small_hbm, small), (wg0_hbm, wg0), (wg2_hbm, wg2), (wg1_hbm, wg1), (wg3_hbm, wg3))
        )
    ]
    stores = [
        pltpu.make_async_copy(src, dst, sem_gw.at[j])
        for j, (src, dst) in enumerate(((gw1, gw1_hbm), (gw3, gw3_hbm), (gw2, gw2_hbm)))
    ]
    loads[0].start()
    for t in range(nh):
        for which in (1, 2, 0):
            copy(t, which).start()
        if t < 5:
            loads[t + 1].start()

    def weights(step):
        half = d.cin // 2
        if step == 0:
            loads[2].wait()
            loads[3].wait()
        elif step == 2:
            loads[1].wait()
            loads[4].wait()
            loads[5].wait()
        if step < 2:
            gw1[step * half : (step + 1) * half, :] = jnp.transpose(wg0[step].astype(F32))
            gw3[:, step * half : (step + 1) * half] = wg2[step].astype(F32)
        elif step < 4:
            r = step - 2
            rows = small[0]
            mean = get(rows, 36, d.mid)[:, r * d.gin : (r + 1) * d.gin]
            taken = get(rows, 40, d.wide)[:, r * wd : (r + 1) * wd]
            mean = jnp.transpose(jnp.broadcast_to(mean, (LANES, d.gin)))
            back = wide(mean, wd) * taken
            for tap in range(9):
                held, first = (wg1, 0) if tap < 6 else (wg3, 6)
                cells = held[r, :, (tap - first) * d.gin : (tap - first + 1) * d.gin]
                gw2[r, tap] = jnp.transpose(cells.astype(F32)) + back
        elif step == 4:
            cells = wg3[0, :, taps:].astype(F32)
            gwex[:, 0:wd] = cells[0 : d.inter, :]
            gwex[:, wd:] = cells[d.inter :, :]
            gwsq[...] = wg3[1, :, taps : taps + d.inter].astype(F32)
            rows = small[0]
            gb3[...] = get(rows, 0, d.cin)
            gg3[...] = get(rows, 8, d.cin)
            gbs[...] = rows[16:17, :]
            ggs[...] = rows[17:18, :]
            gb2[...] = get(rows, 20, d.wide)
            gg2[...] = get(rows, 24, d.wide)
            gbex[...] = get(rows, 28, d.wide)
            gb1[...] = get(rows, 32, d.mid)
            gg1[...] = get(rows, 34, d.mid)

    for t in range(max(nh, 5)):
        if t == 0:
            loads[0].wait()
        if t < nh:
            copy(t, 1).wait()
            copy(t, 2).wait()
            dn[at(t), :] = (dn[at(t), :].astype(F32) + dot_nt(dy[at(t), :], w1[...])).astype(BF16)
            back(t, 1).start()
            copy(t, 0).wait()
            back(t, 0).start()
        weights(t)
        if t == 1:
            stores[0].start()
            stores[1].start()
        elif t == 3:
            stores[2].start()
    for store in stores:
        store.wait()
    for t in range(nh):
        back(t, 0).wait()
        back(t, 1).wait()


def call_finish(d, out_in, dn, dy, w1, wg0, wg1, wg2, wg3, small):
    shape = jax.ShapeDtypeStruct
    cin, wd, mid = d.cin, d.width, d.mid
    vmem, dma = pltpu.VMEM, pltpu.SemaphoreType.DMA
    small_dims = [
        (cin, mid), (1, mid), (1, mid), (d.radix, 9, d.gin, wd), (1, d.wide), (1, d.wide), (wd, d.inter),
        (1, d.inter), (1, d.inter), (d.inter, d.wide), (1, d.wide), (wd, cin), (1, cin), (1, cin),
    ]
    anywhere = pl.BlockSpec(memory_space=pl.ANY)
    inside = pl.BlockSpec(memory_space=pltpu.VMEM)
    return pl.pallas_call(
        functools.partial(finish_kernel, d),
        out_shape=[shape((d.rows, cin), BF16), shape((d.rows, cin), BF16)]
        + [shape(s, F32) for s in small_dims],
        in_specs=[anywhere] * 9,
        out_specs=[anywhere] * 3 + [inside] * 2 + [anywhere] + [inside] * 7 + [anywhere] + [inside] * 2,
        scratch_shapes=[
            vmem((d.rows, cin), BF16), vmem((d.rows, cin), BF16), vmem((d.rows, mid), BF16),
            vmem((cin, mid), BF16), vmem(wg0.shape, BF16), vmem(wg1.shape, BF16), vmem(wg2.shape, BF16), vmem(wg3.shape, BF16),
            vmem(small.shape, F32), vmem((cin, mid), F32), vmem((d.radix, 9, d.gin, wd), F32), vmem((wd, cin), F32),
            dma((3, d.nh)), dma((2, d.nh)), dma((6,)), dma((3,)),
        ],
        name="finish",
        compiler_params=pltpu.CompilerParams(vmem_limit_bytes=60 << 20),
    )(out_in, dn, dy, w1, wg0, wg1, wg2, wg3, small)


def on_device(
    inputs, image_count, pixel_mask, w_first, gain_first, bias_first, w_group, gain_group, bias_group,
    w_squeeze, gain_squeeze, bias_squeeze, w_excite, bias_excite, w_last, gain_last, bias_last, cotangent,
):
    n_img, n_ha = lax.axis_size("img"), lax.axis_size("ha")
    d = Dims(n_img, n_ha, inputs.shape, w_group.shape, w_squeeze.shape)
    nb, nh, nw, cin = inputs.shape

    def by_rows(cells):
        return jnp.transpose(cells, (1, 2, 0, 3)).reshape(d.rows, cin)

    def by_image(cells):
        return jnp.transpose(cells.reshape(nh, nw, nb, cin), (2, 0, 1, 3))

    row = lambda v: v.reshape(1, -1)
    args = (
        by_rows(inputs), by_rows(cotangent), jnp.transpose(pixel_mask, (1, 0, 2)), image_count,
        w_first, row(gain_first), row(bias_first),
        w_group.reshape(d.radix, 9 * d.gin, d.width), row(gain_group), row(bias_group),
        w_squeeze, row(gain_squeeze), row(bias_squeeze), w_excite, row(bias_excite),
        w_last, row(gain_last), row(bias_last),
    )
    out, dn, dy, *sets, small = call_block(d, args)
    if not d.inside:
        sets = lax.psum(sets, ("img", "ha"))
    done = call_finish(d, out, dn, dy, w_first, *sets, small)
    (out, gin, gw1, gg1, gb1, gw2, gg2, gb2, gwsq, ggs, gbs, gwex, gbex, gw3, gg3, gb3) = done
    flat = lambda v: v.reshape(-1)
    return (
        by_image(out), by_image(gin), gw1, flat(gg1), flat(gb1), gw2.reshape(w_group.shape), flat(gg2), flat(gb2),
        gwsq, flat(ggs), flat(gbs), gwex, flat(gbex), gw3, flat(gg3), flat(gb3),
    )


def solution(mesh):
    cells = P("img", "ha", None, None)
    placed = (cells, P("img"), P("img", "ha", None)) + (P(),) * 14 + (cells,)
    return jax.shard_map(
        on_device,
        mesh=mesh,
        in_specs=placed,
        out_specs=(cells, cells) + (P(),) * 14,
        check_vma=False,
    )
```

```python
import functools

import jax
import jax.numpy as jnp
from jax import lax
from jax.experimental import pallas as pl
from jax.experimental.pallas import tpu as pltpu
from jax.sharding import PartitionSpec as P

EPS = 1e-05
F32 = jnp.float32
BF16 = jnp.bfloat16
HIGH = lax.Precision.HIGHEST
MESH = pl.DeviceIdType.MESH
LANES = 128


def dot(a, b, precision=None):
    return jnp.dot(a, b, preferred_element_type=F32, precision=precision)


def dot_nt(a, b, precision=None):
    return lax.dot_general(
        a, b, (((1,), (1,)), ((), ())), preferred_element_type=F32, precision=precision
    )


def dot_tn(a, b, precision=None):
    return lax.dot_general(
        a, b, (((0,), (0,)), ((), ())), preferred_element_type=F32, precision=precision
    )


def wide(cell, lanes):
    return jnp.concatenate([cell] * (lanes // LANES), axis=1)


def fold(cells):
    rows, lanes = cells.shape
    return jnp.sum(cells.reshape(rows // 8, 8, lanes), axis=0)


def fold_images(cells, images):
    rows, lanes = cells.shape
    return jnp.sum(cells.reshape(rows // images, images, lanes), axis=0)


def total_row(cells):
    return jnp.sum(cells, axis=0, keepdims=True)


def put(ref, row, vector):
    for j in range(vector.shape[1] // LANES):
        ref[row + j : row + j + 1, :] = vector[:, j * LANES : (j + 1) * LANES]


def get(cells, row, lanes):
    return jnp.concatenate(
        [cells[row + j : row + j + 1, :] for j in range(lanes // LANES)], axis=1
    )


def moments(sums, squares, total):
    mean = sums / total
    spread = squares / total - mean * mean
    return mean, lax.rsqrt(spread + EPS)


def gate(half):
    bend = jnp.tanh(half)
    rise = 1.0 + bend
    value = half * rise
    return value, 0.5 * (rise + value * (1.0 - bend))


def split_bf16(cells):
    high = cells.astype(BF16)
    return high, (cells - high.astype(F32)).astype(BF16)


class Dims:
    def __init__(self, n_img, n_ha, inputs, w_group, w_squeeze):
        self.n_img, self.n_ha = n_img, n_ha
        self.nb, self.nh, self.nw, self.cin = inputs
        self.radix, _, _, self.gin, self.width = w_group
        self.mid = self.radix * self.gin
        self.wide = self.radix * self.width
        self.inter = w_squeeze[1]
        self.line = self.nw * self.nb
        self.rows = self.nh * self.line
        self.padded = (self.nw + 2) * self.nb
        self.half = (self.cin // 2, 6 * self.gin, self.cin // 2, 3 * self.gin + self.width, self.cin // 2)
        self.sets = 4
        self.inside = n_img == 8 and n_ha == 4
        self.sums = dict(cnt=4, s1=4, s2=8, act=4, v0=8, s3=16, b3=16, b2=8, misc=8, b1=4)
        self.paired = ("s3", "b3")
        self.shared = dict(b1="s1", b2="s2")


def block_kernel(
    d,
    x_hbm, ct_hbm, mask_in, count_in, w1_hbm, g1, c1, w2_hbm, g2, c2, wsq, gs, cs, wex, bex, w3_hbm, g3, c3,
    dn_hbm, ost, xv, wg0, wg1, wg2, wg3, small,
    w1, w2, w3, mb, live, ctv, y1, a1p, y2, act2, slope2, mixed, dm, acc_c, acc_g, w3p, w2x, w2l, w2r,
    mix_t, att, q2, q4, vecs, pools, v0, cols,
    parts, rcs, rxys, rzs, mids, vres, sums, ga_src, ga_buf, pf_src, pf_buf, fc_src, fc_buf,
    sem_w, sem_x, sem_ct, sem_dn, sem_back, ssa, rsa, ssi, rsi, ssh, rsh, ssw, rsw,
):
    n_img, n_ha = d.n_img, d.n_ha
    nb, nh, nw = d.nb, d.nh, d.nw
    cin, mid, wd, wide2, line, rows = d.cin, d.mid, d.width, d.wide, d.line, d.rows
    gin, padded = d.gin, d.padded
    dyp = ctv
    ress = (wg0, wg1, wg2, wg3)
    half = cin // 2
    i = lax.axis_index("img")
    h = lax.axis_index("ha")

    def ha_peer(k):
        return (i, lax.rem(h + k, n_ha))

    def img_peer(k):
        return (lax.rem(i + k, n_img), h)

    z_of, x_of, y_of, core = i // 2, lax.rem(i, 2), h // 2, lax.rem(h, 2)
    spot = x_of * 2 + y_of

    def core_peer():
        return (i, y_of * 2 + (1 - core))

    def plane_peer(k):
        other = lax.rem(spot + k, 4)
        return (z_of * 2 + other // 2, lax.rem(other, 2) * 2 + core)

    def z_peer(k):
        return (lax.rem(z_of + k, 4) * 2 + x_of, h)

    def any_peer(k):
        return (lax.rem(i + k // 4, 8), lax.rem(h + k % 4, 4))

    def chip_peer(k):
        return (lax.rem(i + k // 2, 8), lax.rem(y_of + k % 2, 2) * 2 + core)

    def remote(src, dst, send, recv, peer):
        return pltpu.make_async_remote_copy(
            src_ref=src, dst_ref=dst, send_sem=send, recv_sem=recv, device_id=peer, device_id_type=MESH
        )

    def line_rows(t):
        return pl.ds(pl.multiple_of(t * line, line), line)

    def block_rows(t, u, step):
        return pl.ds(pl.multiple_of(t * line + u * step, nb), step)

    def x_copy(t):
        return pltpu.make_async_copy(x_hbm.at[line_rows(t)], xv.at[line_rows(t)], sem_x.at[t])

    def half_rows(t, c):
        return pl.ds(pl.multiple_of(c * rows + t * line, nb), line)

    def ct_copy(t, c):
        return pltpu.make_async_copy(
            ct_hbm.at[line_rows(t), pl.ds(c * half, half)], ctv.at[half_rows(t, c)], sem_ct.at[c, t]
        )

    def start_inputs(t, carry):
        x_copy(t).start()
        return carry

    loads = [
        pltpu.make_async_copy(src, dst, sem_w.at[j])
        for j, (src, dst) in enumerate(((w1_hbm, w1), (w2_hbm, w2), (w3_hbm, w3)))
    ]
    loads[0].start()
    lax.fori_loop(0, nh, start_inputs, 0)
    loads[1].start()
    loads[2].start()

    barrier = pltpu.get_barrier_semaphore()
    if d.inside:
        peers = [any_peer(k) for k in range(1, 32)]
    else:
        peers = [ha_peer(k) for k in range(1, n_ha)] + [img_peer(k) for k in range(1, n_img)]
    for peer in peers:
        pl.semaphore_signal(barrier, inc=1, device_id=peer, device_id_type=MESH)

    slots = lax.broadcasted_iota(jnp.int32, (nb, LANES), 0)
    live[...] = (slots < count_in[0]).astype(F32)

    def spread(t, carry):
        cells = mask_in[t].astype(F32)
        alive = live[...]
        for w in range(nw):
            cell = jnp.broadcast_to(cells[:, w : w + 1], (nb, LANES)) * alive
            mb[block_rows(t, w, nb), :] = cell.astype(BF16)
            carry = carry + cell
        return carry

    pixels = lax.fori_loop(0, nh, spread, jnp.zeros((nb, LANES), F32))

    def mask_of(at, lanes):
        return wide(mb[at, :].astype(F32), lanes)

    def inner_rows(t, at=nb, count=line):
        return pl.ds(pl.multiple_of(t * padded + at, nb), count)

    def clear(ref):
        zero = jnp.zeros((nb, ref.shape[1]), BF16)

        def body(t, carry):
            ref[inner_rows(t, 0, nb), :] = zero
            ref[inner_rows(t, nb + line, nb), :] = zero
            return carry

        lax.fori_loop(0, nh + 2, body, 0)

        def edge(t, carry):
            ref[inner_rows(0, t * nb, nb), :] = zero
            ref[inner_rows(nh + 1, t * nb, nb), :] = zero
            return carry

        lax.fori_loop(0, nw + 2, edge, 0)

    clear(a1p)
    pl.semaphore_wait(barrier, len(peers))

    def swap(src, buf, send, recv, peer, n):
        def copy(k):
            return remote(src, buf.at[k], send.at[k], recv.at[k], peer(k))

        def each(act, carry):
            if n > 32:
                return lax.fori_loop(1, n, act, carry)
            for k in range(1, n):
                carry = act(k, carry)
            return carry

        def begin(k, carry):
            copy(k).start()
            return carry

        def sent(k, carry):
            copy(k).wait_send()
            return carry

        def take(k, carry):
            copy(k).wait_recv()
            return carry + buf[k].astype(F32)

        def finish():
            total = each(take, src[...].astype(F32))
            each(sent, 0)
            return total

        return (lambda: each(begin, 0)), finish

    class Everywhere:
        def __init__(self, name):
            refs = sums[d.shared.get(name, name)]
            self.at = refs["src"]
            self.refs = refs
            if not d.inside:
                return
            send, recv = refs["send"], refs["recv"]
            if name in d.paired:
                self.pair = remote(self.at, refs["other"], send.at[0], recv.at[0], core_peer())
                self.start_far, self.finish_far = swap(refs["mid"], refs["buf"], send, recv, chip_peer, 16)
            else:
                self.pair = None
                self.start_far, self.finish_far = swap(self.at, refs["buf"], send, recv, any_peer, 32)

        def start(self):
            if d.inside:
                if self.pair is not None:
                    self.pair.start()
                    self.pair.wait_recv()
                    self.refs["mid"][...] = self.at[...] + self.refs["other"][...]
                self.start_far()

        def finish(self):
            if d.inside:
                total = self.finish_far()
                if self.pair is not None:
                    self.pair.wait_send()
                return total
            refs = self.refs
            start, finish = swap(self.at, refs["buf_ha"], refs["send_ha"], refs["recv_ha"], ha_peer, n_ha)
            start()
            refs["mid"][...] = finish()
            start, finish = swap(refs["mid"], refs["buf_img"], refs["send"], refs["recv"], img_peer, n_img)
            start()
            return finish()

    def halo(ref, at):
        def down():
            return remote(
                ref.at[inner_rows(nh)], ref.at[inner_rows(0)], ssh.at[at, 0], rsh.at[at, 0],
                (i, jnp.minimum(h + 1, n_ha - 1)),
            )

        def up():
            return remote(
                ref.at[inner_rows(1)], ref.at[inner_rows(nh + 1)], ssh.at[at, 1], rsh.at[at, 1],
                (i, jnp.maximum(h - 1, 0)),
            )

        def start():
            @pl.when(h < n_ha - 1)
            def _():
                down().start()

            @pl.when(h > 0)
            def _():
                up().start()

        def wait_recv():
            @pl.when(h > 0)
            def _():
                down().wait_recv()

            @pl.when(h < n_ha - 1)
            def _():
                up().wait_recv()

        def wait_send():
            @pl.when(h < n_ha - 1)
            def _():
                down().wait_send()

            @pl.when(h > 0)
            def _():
                up().wait_send()

        return start, wait_recv, wait_send

    plane_rows, z_rows = wd // 4, wd // 16

    def plane_at(other):
        return pl.ds(pl.multiple_of(other * plane_rows, plane_rows), plane_rows)

    def z_at(other, base=0):
        return pl.ds(pl.multiple_of(base + other * z_rows, z_rows), z_rows)

    def w_copy(s, stage, k):
        sem = (s, stage * 4 + k)
        if stage == 0:
            src, dst, peer = parts[s].at[1 - core], rcs[s], core_peer()
        elif stage == 1:
            src = parts[s].at[core, plane_at(lax.rem(spot + k, 4))]
            dst, peer = rxys[s].at[k - 1], plane_peer(k)
        elif stage == 2:
            src = mids[s].at[z_at(lax.rem(z_of + k, 4))]
            dst, peer = rzs[s].at[k - 1], z_peer(k)
        elif stage == 3:
            src = dst = ress[s].at[core, z_at(z_of, spot * plane_rows)]
            peer = z_peer(k)
        elif stage == 4:
            src = dst = ress[s].at[core, plane_at(spot)]
            peer = plane_peer(k)
        else:
            src = dst = ress[s].at[core]
            peer = core_peer()
        return remote(src, dst, ssw.at[sem], rsw.at[sem], peer)

    def w_ks(stage):
        return (1,) if stage in (0, 5) else (1, 2, 3)

    def w_arrival(s, stage, k):
        sem = (s, stage * 4 + k)
        if stage == 3:
            dst = ress[s].at[core, z_at(lax.rem(z_of - k + 4, 4), spot * plane_rows)]
        elif stage == 4:
            dst = ress[s].at[core, plane_at(lax.rem(spot - k + 4, 4))]
        else:
            dst = ress[s].at[1 - core]
        return remote(dst, dst, ssw.at[sem], rsw.at[sem], core_peer())

    def w_start(s, stage):
        if d.inside:
            for k in w_ks(stage):
                w_copy(s, stage, k).start()

    def w_finish(s, stage, fix=None):
        if not d.inside:
            return
        for k in w_ks(stage):
            if stage <= 2:
                w_copy(s, stage, k).wait_recv()
            else:
                w_arrival(s, stage, k).wait_recv()
        part, inner = parts[s], mids[s]
        if stage == 0:
            rc = rcs[s]

            def add(t, carry):
                at = pl.ds(pl.multiple_of(t * 16, 16), 16)
                part[core, at, :] = (part[core, at, :].astype(F32) + rc[at, :].astype(F32)).astype(BF16)
                return carry

            lax.fori_loop(0, wd // 16, add, 0)
        elif stage == 1:
            buf = rxys[s]

            def add(t, carry):
                at = pl.ds(pl.multiple_of(t * 16, 16), 16)
                own = pl.ds(pl.multiple_of(spot * plane_rows + t * 16, 16), 16)
                total = part[core, own, :].astype(F32)
                for k in range(3):
                    total = total + buf[k, at, :].astype(F32)
                inner[at, :] = total.astype(BF16)
                return carry

            lax.fori_loop(0, plane_rows // 16, add, 0)
        elif stage == 2:
            buf = rzs[s]
            total = inner[z_at(z_of), :].astype(F32)
            for k in range(3):
                total = total + buf[k].astype(F32)
            if s >= d.sets:
                vres[...] = total
                return
            if fix is not None:
                total = fix(total)
            ress[s][core, z_at(z_of, spot * plane_rows), :] = total.astype(BF16)

    def w_step(s, stage, fix=None):
        w_finish(s, stage, fix)
        if stage < 5:
            w_start(s, stage + 1)

    def w_sent(s):
        if d.inside:
            for stage in range(6 if s < d.sets else 3):
                for k in w_ks(stage):
                    w_copy(s, stage, k).wait_send()

    count = Everywhere("cnt")
    count.at[...] = jnp.zeros((4, LANES), F32)
    count.at[0:1, :] = total_row(pixels)
    count.at[1:2, :] = total_row(live[...]) * (1.0 / n_ha)
    count.start()

    def first(t, carry):
        sums, squares = carry
        x_copy(t).wait()
        ct_copy(t, 0).start()
        ct_copy(t, 1).start()
        at = line_rows(t)
        y = dot(xv[at, :], w1[...])
        y1[at, :] = y
        masked = y * mask_of(at, mid)
        return sums + fold(masked), squares + fold(masked * y)

    loads[0].wait()
    zeros = jnp.zeros((8, mid), F32)
    totals, squares = lax.fori_loop(0, nh, first, (zeros, zeros))
    norm1 = Everywhere("s1")
    put(norm1.at, 0, total_row(totals))
    put(norm1.at, 2, total_row(squares))
    norm1.start()
    loads[1].wait()
    loads[2].wait()
    for r in range(d.radix):
        for ky in range(3):
            for e in range(4):
                if e <= 2:
                    left = w2[r, (ky * 3 + 2 - e) * gin : (ky * 3 + 3 - e) * gin, :]
                if e >= 1:
                    right = w2[r, (ky * 3 + 3 - e) * gin : (ky * 3 + 4 - e) * gin, :]
                if e == 0:
                    w2l[r, :, ky * wd : (ky + 1) * wd] = left
                elif e == 3:
                    w2r[r, :, ky * wd : (ky + 1) * wd] = right
                else:
                    lanes = slice((ky * 2 + e - 1) * wd, (ky * 2 + e) * wd)
                    w2x[r, 0:gin, lanes] = left
                    w2x[r, gin:, lanes] = right
    got = count.finish()
    total, images = got[0:1, :], got[1:2, :]
    got = norm1.finish()
    mean1, scale1 = moments(get(got, 0, mid), get(got, 2, mid), wide(total, mid))
    half_a1 = 0.5 * g1[...] * scale1
    half_b1 = 0.5 * c1[...] - half_a1 * mean1

    step1 = 4 * nb

    def act_first(t, carry):
        def cells(u, carry):
            at = block_rows(t, u, step1)
            value, _ = gate(y1[at, :] * half_a1 + half_b1)
            value = value * mask_of(at, mid)
            a1p[inner_rows(t + 1, nb + u * step1, step1), :] = value.astype(BF16)
            return carry + fold(value)

        return lax.fori_loop(0, line // step1, cells, carry)

    def edges(body, carry):
        return lax.fori_loop(0, 2, lambda t, c: body(t * (nh - 1), c), carry)

    totals = edges(act_first, jnp.zeros((8, mid), F32))
    halo1_start, halo1_recv, halo1_sent = halo(a1p, 0)
    halo1_start()
    totals = lax.fori_loop(1, nh - 1, act_first, totals)
    act_sum = Everywhere("act")
    act_sum.at[...] = jnp.zeros((4, LANES), F32)
    put(act_sum.at, 0, total_row(totals))
    act_sum.start()

    def taps(t, r, first=0, last=9):
        return jnp.concatenate(
            [
                a1p[inner_rows(t + tap // 3, (tap % 3) * nb), r * gin : (r + 1) * gin]
                for tap in range(first, last)
            ],
            axis=1,
        )

    def group(t, carry):
        at = line_rows(t)
        mask = mask_of(at, wd)
        done = []
        for r in range(d.radix):
            sums, squares = carry[r]
            y = dot(taps(t, r), w2[r])
            y2[at, r * wd : (r + 1) * wd] = y.astype(BF16)
            masked = y * mask
            done.append((sums + fold(masked), squares + fold(masked * y)))
        return tuple(done)

    zeros = jnp.zeros((8, wd), F32)
    sums2 = lax.fori_loop(1, nh - 1, group, ((zeros, zeros),) * d.radix)
    halo1_recv()
    sums2 = edges(group, sums2)
    norm2 = Everywhere("s2")
    put(norm2.at, 0, jnp.concatenate([total_row(s) for s, _ in sums2], axis=1))
    put(norm2.at, 4, jnp.concatenate([total_row(q) for _, q in sums2], axis=1))
    norm2.start()

    acc_c[...] = jnp.zeros((wd, cin), F32)
    vecs[...] = jnp.zeros((8, cin), F32)

    def norm_products(t, carry):
        at = line_rows(t)
        mask = mask_of(at, mid)
        hat = ((y1[at, :] - mean1) * scale1 * mask).astype(BF16)
        x = xv[at, :]
        acc_c[...] += dot_tn(hat, x)
        vecs[...] += dot_tn(mb[at, :], x)[0:8, :]
        return carry

    lax.fori_loop(0, nh, norm_products, 0)
    norm2_done = norm2.finish()
    for c in range(2):
        parts[4][c] = acc_c[:, c * half : (c + 1) * half].astype(BF16)
    w_start(4, 0)
    v0_sum = Everywhere("v0")
    put(v0_sum.at, 0, vecs[0:1, :])
    v0_sum.start()
    mean2, scale2 = moments(get(norm2_done, 0, wide2), get(norm2_done, 4, wide2), wide(total, wide2))
    half_a2 = 0.5 * g2[...] * scale2
    half_b2 = 0.5 * c2[...] - half_a2 * mean2

    lane_blocks = wd // LANES
    step2 = (nw // 2) * nb
    zero = jnp.zeros((nb, LANES), F32)
    for j in range(lane_blocks):
        own = slice(j * LANES, (j + 1) * LANES)

        def act_group(t, pool):
            at = pl.ds(pl.multiple_of(t * step2, step2), step2)
            mask = mb[at, :]
            full = mask.astype(F32)
            for r in range(d.radix):
                lanes = slice(r * wd + j * LANES, r * wd + (j + 1) * LANES)
                value, _ = gate(y2[at, lanes].astype(F32) * half_a2[:, lanes] + half_b2[:, lanes])
                value = value * full
                act2[at, lanes] = value.astype(BF16)
                pool = pool + fold_images(value, nb)
            return pool

        pools[:, own] = lax.fori_loop(0, rows // step2, act_group, zero)

    pool = pools[...]
    squeeze = wsq[...].astype(F32)
    excite = wex[...].astype(F32)
    pf_src[:, 0 : d.inter] = dot(pool, squeeze, HIGH)
    pf_src[:, d.inter :] = pixels
    pf_start, pf_finish = swap(pf_src, pf_buf, ssa.at[0], rsa.at[0], ha_peer, n_ha)
    pf_start()

    def slopes(block):
        lanes = slice(block * LANES, (block + 1) * LANES)
        ha2, hb2 = half_a2[:, lanes], half_b2[:, lanes]

        def body(t, carry):
            slopes, bends = carry
            at = pl.ds(pl.multiple_of(t * step2, step2), step2)
            y = y2[at, lanes].astype(F32)
            _, slope = gate(y * ha2 + hb2)
            slope = slope * mb[at, :].astype(F32)
            slope2[at, lanes] = slope.astype(BF16)
            return slopes + fold_images(slope, nb), bends + fold_images(slope * y, nb)

        q2[:, lanes], q4[:, lanes] = lax.fori_loop(0, rows // step2, body, (zero, zero))

    total_blocks = d.radix * lane_blocks
    for block in range(total_blocks // 4):
        slopes(block)
    w_step(4, 0)
    both = pf_finish()
    floor = jnp.maximum(both[:, d.inter :], 1.0)
    squeezed = both[:, 0 : d.inter] / floor
    live_now = live[...]
    fc_src[...] = jnp.zeros(fc_src.shape, F32)
    put(fc_src.at[0], 0, total_row(squeezed * live_now))
    put(fc_src.at[0], 1, total_row(squeezed * squeezed * live_now))
    fc_start, fc_finish = swap(fc_src.at[0], fc_buf.at[0], ssi.at[0], rsi.at[0], img_peer, n_img)
    fc_start()
    for block in range(total_blocks // 4, total_blocks):
        slopes(block)
    got = fc_finish()
    mean_s, scale_s = moments(got[0:1, :], got[1:2, :], images)
    centered = (squeezed - mean_s) * scale_s
    hidden, hidden_slope = gate(0.5 * (centered * gs[...] + cs[...]))
    logits = dot(hidden, excite, HIGH) + bex[...]
    gap = logits[:, 0:wd] - logits[:, wd:]
    att[:, 0:wd] = jax.nn.sigmoid(gap)
    att[:, wd:] = jax.nn.sigmoid(-gap)

    step3 = 2 * nb

    def mix(t, carry):
        def cells(u, carry):
            at = block_rows(t, u, step3)
            weight = jnp.concatenate([att[...]] * (step3 // nb), axis=0)
            both = act2[at, :].astype(F32) * weight
            mixed[at, :] = (both[:, 0:wd] + both[:, wd:]).astype(BF16)
            return carry

        lax.fori_loop(0, line // step3, cells, 0, unroll=7)
        gram, sums = carry
        cells = mixed[line_rows(t), :]
        mix_t[t] = jnp.transpose(cells)
        return gram + dot(mix_t[t], cells), sums + fold(cells.astype(F32))

    gram, totals = lax.fori_loop(0, nh, mix, (jnp.zeros((wd, wd), F32), jnp.zeros((8, wd), F32)))
    mix_sum = total_row(totals)
    gram_high, gram_low = split_bf16(gram)
    acc_g[0, :, 0:cin] = dot(gram_high, w3[...]) + dot(gram_low, w3[...])
    mix_high, mix_low = split_bf16(mix_sum)
    sum_last = dot(jnp.broadcast_to(mix_high, (16, wd)), w3[...]) + dot(
        jnp.broadcast_to(mix_low, (16, wd)), w3[...]
    )
    norm3 = Everywhere("s3")
    put(norm3.at, 0, sum_last[0:1, :])
    put(norm3.at, 8, total_row(acc_g[0, :, 0:cin] * w3[...].astype(F32)))
    norm3.start()

    def last_product(t, carry):
        at = line_rows(t)
        ost[at, :] = dot(mixed[at, :], w3[...]).astype(BF16)
        ct_copy(t, 0).wait()
        ct_copy(t, 1).wait()
        return carry

    lax.fori_loop(0, nh, last_product, 0)
    w_step(4, 1)
    got = norm3.finish()
    mean3, scale3 = moments(get(got, 0, cin), get(got, 8, cin), wide(total, cin))
    grow3 = g3[...] * scale3
    half_a3 = 0.5 * grow3
    half_b3 = 0.5 * c3[...] - half_a3 * mean3

    step4 = (nw // 4) * nb
    blocks4 = 2 * LANES

    def dn_copy(t, c):
        return pltpu.make_async_copy(
            ctv.at[half_rows(t, c)], dn_hbm.at[line_rows(t), pl.ds(c * half, half)], sem_dn.at[c, t]
        )

    def dn_back(t, c):
        return pltpu.make_async_copy(
            dn_hbm.at[line_rows(t), pl.ds(c * half, half)], ctv.at[half_rows(t, c)], sem_back.at[c, t]
        )

    def grad_of(t):
        return jnp.concatenate([ctv[half_rows(t, 0), :], ctv[half_rows(t, 1), :]], axis=1)

    acc_c[...] = jnp.zeros((wd, cin), F32)
    vecs[...] = jnp.zeros((8, cin), F32)

    def last(t, carry):
        for j in range(cin // blocks4):
            lanes = slice(j * blocks4, (j + 1) * blocks4)
            a3, b3 = half_a3[:, lanes], half_b3[:, lanes]

            def cells(u, carry):
                at = block_rows(t, u, step4)
                mask = wide(mb[at, :], blocks4)
                x = xv[at, lanes] * jnp.asarray(0.5, BF16)
                arg = ost[at, lanes].astype(F32) * a3 + (b3 + x.astype(F32))
                bend = jnp.tanh(arg)
                rise = 1.0 + bend
                value = arg * rise
                ost[at, lanes] = value.astype(BF16) * mask
                side = j * blocks4 // half
                there = pl.ds(pl.multiple_of(side * rows + t * line + u * step4, nb), step4)
                inner = slice(j * blocks4 - side * half, (j + 1) * blocks4 - side * half)
                push = ctv[there, inner] * (mask * jnp.asarray(0.5, BF16))
                grad = push.astype(F32) * (rise + value * (1.0 - bend))
                ctv[there, inner] = grad.astype(BF16)
                return carry + fold(grad)

            vecs[:, lanes] = lax.fori_loop(0, line // step4, cells, vecs[:, lanes])
        dn_copy(t, 0).start()
        dn_copy(t, 1).start()
        acc_c[...] += dot(mix_t[t], grad_of(t))
        return carry

    lax.fori_loop(0, nh, last, 0)
    sum_grad = total_row(vecs[...])
    back3 = Everywhere("b3")
    put(back3.at, 0, sum_grad)
    put(back3.at, 8, scale3 * (total_row(acc_c[...] * w3[...].astype(F32)) - mean3 * sum_grad))
    back3.start()

    w3p[...] = (w3[...].astype(F32) * grow3).astype(BF16)

    def plain_back(t, carry):
        dm[line_rows(t), :] = dot_nt(grad_of(t), w3p[...])
        return carry

    lax.fori_loop(0, nh, plain_back, 0)
    w_finish(4, 2)
    got = back3.finish()
    bias3, gain3 = get(got, 0, cin), get(got, 8, cin)
    put(small.at[0], 0, bias3)
    put(small.at[0], 8, gain3)
    all_wide = wide(total, cin)
    slant3 = scale3 * gain3 / all_wide
    level3 = bias3 / all_wide - mean3 * slant3
    fix = (w3[...].astype(F32) * slant3).astype(BF16)
    fix = dot_nt(fix, w3p[...]).astype(BF16)
    level_high, level_low = split_bf16(level3)
    shift = dot_nt(jnp.broadcast_to(level_high, (16, cin)), w3p[...]) + dot_nt(
        jnp.broadcast_to(level_low, (16, cin)), w3p[...]
    )
    shift = shift[0:1, :]

    def back_mix(t, carry):
        at = line_rows(t)
        dm[at, :] = dm[at, :] - dot(mixed[at, :], fix) - mask_of(at, wd) * shift
        return carry

    lax.fori_loop(0, nh, back_mix, 0)

    step5 = 4 * nb
    sums5 = []
    for j in range(lane_blocks):
        lanes = slice(j * LANES, (j + 1) * LANES)

        def image_sums(t, carry):
            at = pl.ds(pl.multiple_of(t * step5, step5), step5)
            grad = dm[at, lanes]
            done = []
            for r in range(d.radix):
                own = slice(r * wd + j * LANES, r * wd + (j + 1) * LANES)
                a, b, c = carry[r]
                a = a + fold_images(grad * act2[at, own].astype(F32), nb)
                part = grad * slope2[at, own].astype(F32)
                b = b + fold_images(part, nb)
                c = c + fold_images(part * y2[at, own].astype(F32), nb)
                done.append((a, b, c))
            return tuple(done)

        sums5.append(lax.fori_loop(0, rows // step5, image_sums, ((zero, zero, zero),) * d.radix))
    pick = lambda which: jnp.concatenate(
        [sums5[j][r][which] for r in range(d.radix) for j in range(lane_blocks)], axis=1
    )
    q1, q3 = pick(1), pick(2)

    def dn_out(t, carry):
        dn_copy(t, 0).wait()
        dn_copy(t, 1).wait()
        return carry

    lax.fori_loop(0, nh, dn_out, 0)
    clear(dyp)
    ga_src[...] = pick(0).astype(BF16)
    ga_start, ga_finish = swap(ga_src, ga_buf, ssa.at[1], rsa.at[1], ha_peer, n_ha)
    ga_start()

    mix_column = jnp.transpose(jnp.broadcast_to(mix_sum, (LANES, wd)))
    for j in range(cin // LANES):
        lanes = slice(j * LANES, (j + 1) * LANES)
        c = 0 if j * LANES < half else 1
        grad = grow3[:, lanes] * (
            acc_c[:, lanes] - mix_column * level3[:, lanes] - acc_g[0, :, lanes] * slant3[:, lanes]
        )
        parts[2][c, :, j * LANES - c * half : (j + 1) * LANES - c * half] = grad.astype(BF16)
    w_start(2, 0)

    grad_att = ga_finish()
    weight = att[...]
    weighed = weight * grad_att
    both = weighed[:, 0:wd] + weighed[:, wd:]
    grad_logits = weight * (grad_att - jnp.concatenate([both, both], axis=1))
    grad_fc = dot_nt(grad_logits, excite, HIGH) * hidden_slope
    put(fc_src.at[1], 0, total_row(grad_fc))
    put(fc_src.at[1], 1, total_row(grad_fc * centered))
    pooled = pool / wide(floor, wd)
    put(fc_src.at[1], 2, total_row(pooled))
    fc_start, fc_finish = swap(fc_src.at[1], fc_buf.at[1], ssi.at[1], rsi.at[1], img_peer, n_img)
    fc_start()
    w_step(2, 0)
    grad_excite = dot_tn(hidden, grad_logits, HIGH)
    grad_bex = total_row(grad_logits) * (1.0 / n_ha)
    acc_g[...] = jnp.zeros((d.radix, wd, 9 * gin), F32)
    got = fc_finish()
    bias_s, gain_s = got[0:1, :], got[1:2, :]
    put(small.at[0], 16, bias_s)
    put(small.at[0], 17, gain_s)
    grad_squeezed = (gs[...] * scale_s) * (
        grad_fc - live_now * (bias_s + centered * gain_s) / images
    )
    grad_pool = dot_nt(grad_squeezed, squeeze, HIGH) / wide(floor, wd)
    pool2 = jnp.concatenate([grad_pool] * d.radix, axis=1)
    sum_grad = total_row(weight * q1 + pool2 * q2[...])
    sum_bend = total_row(weight * q3 + pool2 * q4[...])
    back2 = Everywhere("b2")
    put(back2.at, 0, sum_grad)
    put(back2.at, 4, scale2 * (sum_bend - mean2 * sum_grad))
    back2.start()
    level = get(got, 2, wd) / wide(images, wd)
    grad_squeeze = dot_tn(pooled - level, grad_squeezed, HIGH)
    grow2 = g2[...] * scale2
    att[...] = weight * grow2
    q2[...] = pool2 * grow2
    w_step(2, 1)
    mean_act1 = get(act_sum.finish(), 0, mid) / (wide(images, mid) * float(nh * n_ha * nw))
    got = back2.finish()
    bias2, gain2 = get(got, 0, wide2), get(got, 4, wide2)
    put(small.at[0], 20, bias2)
    put(small.at[0], 24, gain2)
    slant2 = grow2 * scale2 * gain2 / wide(total, wide2)
    level2 = grow2 * bias2 / wide(total, wide2) - mean2 * slant2

    step6 = 2 * nb

    def back_group(t, carry):
        def cells(u, carry):
            at = block_rows(t, u, step6)
            to = inner_rows(t + 1, nb + u * step6, step6)
            again = step6 // nb
            grad = dm[at, :]
            mask = mask_of(at, wd)
            sums = []
            for r in range(d.radix):
                own = slice(r * wd, (r + 1) * wd)
                grow = jnp.concatenate([att[:, own]] * again, axis=0)
                lift = jnp.concatenate([q2[:, own]] * again, axis=0)
                push = (grow * grad + lift) * slope2[at, own].astype(F32)
                pull = mask * (level2[:, own] + slant2[:, own] * y2[at, own].astype(F32))
                dyp[to, own] = (push - pull).astype(BF16)
                sums.append(carry[r] + fold(push - pull))
            return tuple(sums)

        return lax.fori_loop(0, line // step6, cells, carry, unroll=7)

    zeros = jnp.zeros((8, wd), F32)
    sums2 = edges(back_group, (zeros,) * d.radix)
    halo2_start, halo2_recv, halo2_sent = halo(dyp, 1)
    halo2_start()
    sums2 = lax.fori_loop(1, nh - 1, back_group, sums2)
    sum_dy2 = [total_row(s) for s in sums2]
    misc = Everywhere("misc")
    put(misc.at, 0, jnp.concatenate(sum_dy2, axis=1))
    put(misc.at, 4, grad_bex)
    misc.start()
    w_step(2, 2)

    def weights_group(t, carry):
        for r in range(d.radix):
            grad = jnp.transpose(dyp[inner_rows(t + 1), r * wd : (r + 1) * wd])
            acc_g[r] += dot(grad, taps(t, r))
        return carry

    lax.fori_loop(0, nh, weights_group, 0)

    def send_group(s, first, last):
        lanes = (last - first) * gin
        for r in range(d.radix):
            base = wide(mean_act1[:, r * gin : (r + 1) * gin], lanes)
            column = jnp.transpose(jnp.broadcast_to(sum_dy2[r], (LANES, wd)))
            grad = acc_g[r, :, first * gin : last * gin] - wide(column, lanes) * base
            parts[s][r, :, 0:lanes] = grad.astype(BF16)
        w_start(s, 0)

    send_group(1, 0, 6)
    parts[3][0, :, 3 * gin :] = jnp.concatenate(
        [grad_excite[:, 0:wd], grad_excite[:, wd:]], axis=0
    ).astype(BF16) * jnp.asarray(1.0 / n_ha, BF16)
    parts[3][1, :, 3 * gin : 3 * gin + d.inter] = grad_squeeze.astype(BF16)
    parts[3][1, :, 3 * gin + d.inter :] = jnp.zeros((wd, wd - d.inter), BF16)
    send_group(3, 6, 9)
    w_step(1, 0)
    w_step(2, 3)

    pairs = nw // 2

    def back_taps(t, r, which):
        cells = []
        for ky in range(3):
            for e in which:
                block = dyp[inner_rows(t + 2 - ky, e * nb), r * wd : (r + 1) * wd]
                block = block.reshape(pairs, 2 * nb, wd)[:, 0:nb, :].reshape(pairs * nb, wd)
                cells.append(block)
        return jnp.concatenate(cells, axis=1)

    def transposed(t, carry):
        sums, bends = carry
        at = line_rows(t)
        done = []
        for r in range(d.radix):
            both = dot_nt(back_taps(t, r, (1, 2)), w2x[r])
            left = both[:, 0:gin] + dot_nt(back_taps(t, r, (0,)), w2l[r])
            right = both[:, gin:] + dot_nt(back_taps(t, r, (3,)), w2r[r])
            both = jnp.concatenate(
                [left.reshape(pairs, nb, gin), right.reshape(pairs, nb, gin)], axis=1
            )
            done.append(both.reshape(line, gin))
        dm[at, :] = jnp.concatenate(done, axis=1)

        def cells(u, carry):
            sums, bends = carry
            at = block_rows(t, u, step1)
            y = y1[at, :]
            _, slope = gate(y * half_a1 + half_b1)
            grad = dm[at, :] * (slope * mask_of(at, mid))
            dm[at, :] = grad
            mixed[at, :] = grad.astype(BF16)
            return sums + fold(grad), bends + fold(grad * y)

        return lax.fori_loop(0, line // step1, cells, (sums, bends))

    zeros = jnp.zeros((8, mid), F32)
    sums1 = lax.fori_loop(1, nh - 1, transposed, (zeros, zeros))
    halo2_recv()
    sums1 = edges(transposed, sums1)
    sum_grad = total_row(sums1[0])
    back1 = Everywhere("b1")
    put(back1.at, 0, sum_grad)
    put(back1.at, 2, scale1 * (total_row(sums1[1]) - mean1 * sum_grad))
    back1.start()
    halo2_sent()

    def fetch_back(t, carry):
        dn_back(t, 0).start()
        dn_back(t, 1).start()
        return carry

    lax.fori_loop(0, nh, fetch_back, 0)

    acc_c[...] = jnp.zeros((wd, cin), F32)

    def first_weights(t, carry):
        at = line_rows(t)
        acc_c[...] += dot_tn(mixed[at, :], xv[at, :])
        return carry

    lax.fori_loop(0, nh, first_weights, 0)
    w_step(1, 1)
    w_step(3, 0)
    if d.inside:
        for c in range(2):
            parts[0][c] = acc_c[:, c * half : (c + 1) * half].astype(BF16)
    w_start(0, 0)
    got = back1.finish()
    bias1, gain1 = get(got, 0, mid), get(got, 2, mid)
    grow1 = g1[...] * scale1
    bias_all, gain_all = bias1 / wide(total, mid), gain1 / wide(total, mid)
    slant1 = grow1 * scale1 * gain_all
    level1 = grow1 * bias_all - mean1 * slant1
    w_step(0, 0)

    def back_first(t, carry):
        def cells(u, carry):
            at = block_rows(t, u, step1)
            pull = mask_of(at, mid) * (level1 + slant1 * y1[at, :])
            mixed[at, :] = (grow1 * dm[at, :] - pull).astype(BF16)
            return carry

        lax.fori_loop(0, line // step1, cells, 0)
        return carry

    lax.fori_loop(0, nh, back_first, 0)
    put(small.at[0], 32, bias1)
    put(small.at[0], 34, gain1)
    put(small.at[0], 36, mean_act1)
    small[0, 18:20, :] = jnp.zeros((2, LANES), F32)
    small[0, 38:40, :] = jnp.zeros((2, LANES), F32)
    small[0, 44:48, :] = jnp.zeros((4, LANES), F32)
    got = misc.finish()
    put(small.at[0], 28, get(got, 4, wide2))
    put(small.at[0], 40, get(got, 0, wide2))
    got = v0_sum.finish()
    for c in range(2):
        v0[c] = jnp.broadcast_to(get(got, 0, cin)[:, c * half : (c + 1) * half], (8, half))
    for j, vector in enumerate((grow1, bias_all, gain_all)):
        cols[j] = jnp.transpose(jnp.broadcast_to(vector, (LANES, mid)))

    def norm_terms(total, at, taken, flat):
        lanes = total.shape[1]
        grow, level, slant = (wide(cols[j, at, :], lanes) for j in range(3))
        return grow * (total - level * flat - slant * taken)

    def fix_first(total):
        return norm_terms(total, z_at(z_of, spot * plane_rows), vres[...], v0[core, 0:1, :])

    def grad_inputs(t, carry):
        at = line_rows(t)
        for c in range(2):
            lanes = slice(c * half, (c + 1) * half)
            dn_back(t, c).wait()
            grad = ctv[half_rows(t, c), :].astype(F32) + dot_nt(mixed[at, :], w1[lanes, :])
            xv[at, lanes] = grad.astype(BF16)
        return carry

    lax.fori_loop(0, nh // 2, grad_inputs, 0)
    w_step(1, 2)
    w_step(0, 1)
    lax.fori_loop(nh // 2, nh, grad_inputs, 0)
    w_step(3, 1)
    w_step(1, 3)
    w_step(0, 2, fix_first)
    w_step(3, 2)
    w_step(1, 4)
    w_step(0, 3)
    w_step(3, 3)
    w_step(0, 4)
    w_step(3, 4)
    w_step(2, 4)
    for s in (1, 0, 3, 2):
        w_step(s, 5)
    if not d.inside:
        whole = slice(0, wd)
        for c in range(2):
            lanes = slice(c * half, (c + 1) * half)
            local = wide(cols[0, whole, :], half) * (
                acc_c[:, lanes]
                - wide(cols[1, whole, :], half) * get(v0_sum.at[...], 0, cin)[:, lanes]
                - wide(cols[2, whole, :], half) * parts[4][c].astype(F32)
            )
            parts[0][c] = local.astype(BF16)

    for s in range(d.sets + 1):
        w_sent(s)
    halo1_sent()
    if not d.inside:
        for s in range(d.sets):
            ress[s][...] = parts[s][...]


def call_block(d, args):
    f32, bf16 = F32, BF16
    cin, wd, mid, rows, nb, nh = d.cin, d.width, d.mid, d.rows, d.nb, d.nh
    vmem, dma = pltpu.VMEM, pltpu.SemaphoreType.DMA
    halves = [(2, wd, lanes) for lanes in d.half]
    shape = jax.ShapeDtypeStruct
    outs = [
        shape((rows, cin), bf16),
        vmem((rows, cin), bf16),
        vmem((rows, cin), bf16),
        *[vmem(s, bf16) for s in halves[: d.sets]],
        vmem((1, 48, LANES), f32),
    ]
    anywhere = pl.BlockSpec(memory_space=pl.ANY)
    inside = pl.BlockSpec(memory_space=pltpu.VMEM)
    plane, zed = wd // 4, wd // 16

    def sums_of(name, count):
        if not d.inside:
            return dict(
                src=vmem((count, LANES), f32),
                mid=vmem((count, LANES), f32),
                buf_ha=vmem((d.n_ha, count, LANES), f32),
                buf_img=vmem((d.n_img, count, LANES), f32),
                send_ha=dma((d.n_ha,)), recv_ha=dma((d.n_ha,)),
                send=dma((d.n_img,)), recv=dma((d.n_img,)),
            )
        if name in d.paired:
            return dict(
                src=vmem((count, LANES), f32),
                mid=vmem((count, LANES), f32),
                other=vmem((count, LANES), f32),
                buf=vmem((16, count, LANES), f32),
                send=dma((16,)), recv=dma((16,)),
            )
        return dict(
            src=vmem((count, LANES), f32),
            buf=vmem((32, count, LANES), f32),
            send=dma((32,)), recv=dma((32,)),
        )

    scratch = [
        vmem((cin, mid), bf16),
        vmem((d.radix, 9 * d.gin, wd), bf16),
        vmem((wd, cin), bf16),
        vmem((rows, LANES), bf16),
        vmem((nb, LANES), f32),
        vmem((max(2 * rows, (nh + 2) * d.padded), cin // 2), bf16),
        vmem((rows, mid), f32),
        vmem(((nh + 2) * d.padded, mid), bf16),
        vmem((rows, d.wide), bf16),
        vmem((rows, d.wide), bf16),
        vmem((rows, d.wide), bf16),
        vmem((rows, wd), bf16),
        vmem((rows, wd), f32),
        vmem((wd, cin), f32),
        vmem((d.radix, wd, 9 * d.gin), f32),
        vmem((wd, cin), bf16),
        vmem((d.radix, 2 * d.gin, 6 * wd), bf16),
        vmem((d.radix, d.gin, 3 * wd), bf16),
        vmem((d.radix, d.gin, 3 * wd), bf16),
        vmem((nh, wd, d.line), bf16),
        vmem((nb, d.wide), f32),
        vmem((nb, d.wide), f32),
        vmem((nb, d.wide), f32),
        vmem((8, cin), f32),
        vmem((nb, wd), f32),
        vmem((2, 8, cin // 2), f32),
        vmem((3, mid, LANES), f32),
        [vmem(s, bf16) for s in halves],
        [vmem((wd, lanes), bf16) for lanes in d.half],
        [vmem((3, plane, lanes), bf16) for lanes in d.half],
        [vmem((3, zed, lanes), bf16) for lanes in d.half],
        [vmem((plane, lanes), bf16) for lanes in d.half],
        vmem((zed, d.half[0]), f32),
        {name: sums_of(name, count) for name, count in d.sums.items() if name not in d.shared},
        vmem((nb, d.wide), bf16),
        vmem((d.n_ha, nb, d.wide), bf16),
        vmem((nb, 2 * LANES), f32),
        vmem((d.n_ha, nb, 2 * LANES), f32),
        vmem((2, 4, LANES), f32),
        vmem((2, d.n_img, 4, LANES), f32),
        dma((3,)),
        dma((nh,)),
        dma((2, nh)),
        dma((2, nh)),
        dma((2, nh)),
        dma((2, d.n_ha)),
        dma((2, d.n_ha)),
        dma((2, d.n_img)),
        dma((2, d.n_img)),
        dma((2, 2)),
        dma((2, 2)),
        dma((5, 24)),
        dma((5, 24)),
    ]
    return pl.pallas_call(
        functools.partial(block_kernel, d),
        out_shape=outs,
        in_specs=[anywhere, anywhere, inside, pl.BlockSpec(memory_space=pltpu.SMEM)]
        + [anywhere, inside, inside, anywhere] + [inside] * 7 + [anywhere, inside, inside],
        out_specs=[anywhere] + [inside] * 7,
        scratch_shapes=scratch,
        name="block",
        compiler_params=pltpu.CompilerParams(
            collective_id=0, has_side_effects=True, vmem_limit_bytes=47 << 20
        ),
    )(*args)


def finish_kernel(
    d, out_in, gin_in, wg0, wg1, wg2, wg3, small,
    out, gin_hbm, gw1_hbm, gg1, gb1, gw2_hbm, gg2, gb2, gwsq, ggs, gbs, gwex, gbex, gw3_hbm, gg3, gb3,
    gw1, gw2, gw3, sem_out, sem_gw,
):
    wd, taps = d.width, 3 * d.gin
    parts = 4
    copies = [
        pltpu.make_async_copy(src.at[at], dst.at[at], sem_out.at[which, t])
        for which, (src, dst) in enumerate(((out_in, out), (gin_in, gin_hbm)))
        for t in range(parts)
        for at in (pl.ds(t * (d.rows // parts), d.rows // parts),)
    ]
    for copy in copies:
        copy.start()
    stores = [
        pltpu.make_async_copy(src, dst, sem_gw.at[j])
        for j, (src, dst) in enumerate(((gw1, gw1_hbm), (gw3, gw3_hbm), (gw2, gw2_hbm)))
    ]

    def weights(step):
        half = d.cin // 2
        if step < 2:
            gw1[step * half : (step + 1) * half, :] = jnp.transpose(wg0[step].astype(F32))
            gw3[:, step * half : (step + 1) * half] = wg2[step].astype(F32)
        elif step < 4:
            r = step - 2
            rows = small[0]
            mean = get(rows, 36, d.mid)[:, r * d.gin : (r + 1) * d.gin]
            taken = get(rows, 40, d.wide)[:, r * wd : (r + 1) * wd]
            mean = jnp.transpose(jnp.broadcast_to(mean, (LANES, d.gin)))
            back = wide(mean, wd) * taken
            for tap in range(9):
                held, first = (wg1, 0) if tap < 6 else (wg3, 6)
                cells = held[r, :, (tap - first) * d.gin : (tap - first + 1) * d.gin]
                gw2[r, tap] = jnp.transpose(cells.astype(F32)) + back
        elif step == 4:
            cells = wg3[0, :, taps:].astype(F32)
            gwex[:, 0:wd] = cells[0 : d.inter, :]
            gwex[:, wd:] = cells[d.inter :, :]
            gwsq[...] = wg3[1, :, taps : taps + d.inter].astype(F32)
            rows = small[0]
            gb3[...] = get(rows, 0, d.cin)
            gg3[...] = get(rows, 8, d.cin)
            gbs[...] = rows[16:17, :]
            ggs[...] = rows[17:18, :]
            gb2[...] = get(rows, 20, d.wide)
            gg2[...] = get(rows, 24, d.wide)
            gbex[...] = get(rows, 28, d.wide)
            gb1[...] = get(rows, 32, d.mid)
            gg1[...] = get(rows, 34, d.mid)

    for t in range(5):
        weights(t)
        if t == 1:
            stores[0].start()
            stores[1].start()
        elif t == 3:
            stores[2].start()
    for copy in stores + copies:
        copy.wait()


def call_finish(d, *args):
    shape = jax.ShapeDtypeStruct
    cin, wd, mid = d.cin, d.width, d.mid
    vmem, dma = pltpu.VMEM, pltpu.SemaphoreType.DMA
    small_dims = [
        (cin, mid), (1, mid), (1, mid), (d.radix, 9, d.gin, wd), (1, d.wide), (1, d.wide), (wd, d.inter),
        (1, d.inter), (1, d.inter), (d.inter, d.wide), (1, d.wide), (wd, cin), (1, cin), (1, cin),
    ]
    anywhere = pl.BlockSpec(memory_space=pl.ANY)
    inside = pl.BlockSpec(memory_space=pltpu.VMEM)
    return pl.pallas_call(
        functools.partial(finish_kernel, d),
        out_shape=[shape((d.rows, cin), BF16), shape((d.rows, cin), BF16)]
        + [shape(s, F32) for s in small_dims],
        in_specs=[inside] * 7,
        out_specs=[anywhere] * 3 + [inside] * 2 + [anywhere] + [inside] * 7 + [anywhere] + [inside] * 2,
        scratch_shapes=[
            vmem((cin, mid), F32), vmem((d.radix, 9, d.gin, wd), F32), vmem((wd, cin), F32),
            dma((2, 4)), dma((3,)),
        ],
        name="finish",
        compiler_params=pltpu.CompilerParams(vmem_limit_bytes=16 << 20),
    )(*[pltpu.with_memory_space_constraint(arg, pltpu.VMEM) for arg in args])


def on_device(
    inputs, image_count, pixel_mask, w_first, gain_first, bias_first, w_group, gain_group, bias_group,
    w_squeeze, gain_squeeze, bias_squeeze, w_excite, bias_excite, w_last, gain_last, bias_last, cotangent,
):
    n_img, n_ha = lax.axis_size("img"), lax.axis_size("ha")
    d = Dims(n_img, n_ha, inputs.shape, w_group.shape, w_squeeze.shape)
    nb, nh, nw, cin = inputs.shape

    def by_rows(cells):
        return jnp.transpose(cells, (1, 2, 0, 3)).reshape(d.rows, cin)

    def by_image(cells):
        return jnp.transpose(cells.reshape(nh, nw, nb, cin), (2, 0, 1, 3))

    row = lambda v: v.reshape(1, -1)
    args = (
        by_rows(inputs), by_rows(cotangent), jnp.transpose(pixel_mask, (1, 0, 2)), image_count,
        w_first, row(gain_first), row(bias_first),
        w_group.reshape(d.radix, 9 * d.gin, d.width), row(gain_group), row(bias_group),
        w_squeeze, row(gain_squeeze), row(bias_squeeze), w_excite, row(bias_excite),
        w_last, row(gain_last), row(bias_last),
    )
    _, out, gin, *sets, small = call_block(d, args)
    if not d.inside:
        sets = lax.psum(sets, ("img", "ha"))
    done = call_finish(d, out, gin, *sets, small)
    (out, gin, gw1, gg1, gb1, gw2, gg2, gb2, gwsq, ggs, gbs, gwex, gbex, gw3, gg3, gb3) = done
    flat = lambda v: v.reshape(-1)
    return (
        by_image(out), by_image(gin), gw1, flat(gg1), flat(gb1), gw2.reshape(w_group.shape), flat(gg2), flat(gb2),
        gwsq, flat(ggs), flat(gbs), gwex, flat(gbex), gw3, flat(gg3), flat(gb3),
    )


def solution(mesh):
    cells = P("img", "ha", None, None)
    placed = (cells, P("img"), P("img", "ha", None)) + (P(),) * 14 + (cells,)
    return jax.shard_map(
        on_device,
        mesh=mesh,
        in_specs=placed,
        out_specs=(cells, cells) + (P(),) * 14,
        check_vma=False,
    )
```

```python
import functools

import jax
import jax.numpy as jnp
from jax import lax
from jax.experimental import pallas as pl
from jax.experimental.pallas import tpu as pltpu
from jax.sharding import PartitionSpec as P

EPS = 1e-05
F32 = jnp.float32
BF16 = jnp.bfloat16
HIGH = lax.Precision.HIGHEST
MESH = pl.DeviceIdType.MESH
LANES = 128


def dot(a, b, precision=None):
    return jnp.dot(a, b, preferred_element_type=F32, precision=precision)


def dot_nt(a, b, precision=None):
    return lax.dot_general(
        a, b, (((1,), (1,)), ((), ())), preferred_element_type=F32, precision=precision
    )


def dot_tn(a, b, precision=None):
    return lax.dot_general(
        a, b, (((0,), (0,)), ((), ())), preferred_element_type=F32, precision=precision
    )


def wide(cell, lanes):
    return jnp.concatenate([cell] * (lanes // LANES), axis=1)


def fold(cells):
    rows, lanes = cells.shape
    return jnp.sum(cells.reshape(rows // 8, 8, lanes), axis=0)


def fold_images(cells, images):
    rows, lanes = cells.shape
    return jnp.sum(cells.reshape(rows // images, images, lanes), axis=0)


def total_row(cells):
    return jnp.sum(cells, axis=0, keepdims=True)


def put(ref, row, vector):
    for j in range(vector.shape[1] // LANES):
        ref[row + j : row + j + 1, :] = vector[:, j * LANES : (j + 1) * LANES]


def get(cells, row, lanes):
    return jnp.concatenate(
        [cells[row + j : row + j + 1, :] for j in range(lanes // LANES)], axis=1
    )


def moments(sums, squares, total):
    mean = sums / total
    spread = squares / total - mean * mean
    return mean, lax.rsqrt(spread + EPS)


def gate(half):
    bend = jnp.tanh(half)
    rise = 1.0 + bend
    value = half * rise
    return value, 0.5 * (rise + value * (1.0 - bend))


def split_bf16(cells):
    high = cells.astype(BF16)
    return high, (cells - high.astype(F32)).astype(BF16)


class Dims:
    def __init__(self, n_img, n_ha, inputs, w_group, w_squeeze):
        self.n_img, self.n_ha = n_img, n_ha
        self.nb, self.nh, self.nw, self.cin = inputs
        self.radix, _, _, self.gin, self.width = w_group
        self.mid = self.radix * self.gin
        self.wide = self.radix * self.width
        self.inter = w_squeeze[1]
        self.line = self.nw * self.nb
        self.rows = self.nh * self.line
        self.padded = (self.nw + 2) * self.nb
        self.split = 5
        self.half = (self.cin // 2, 5 * self.gin, self.cin // 2, 4 * self.gin, self.width, self.cin // 2)
        self.sets = 5
        self.inside = n_img == 8 and n_ha == 4
        self.sums = dict(cnt=4, s1=4, s2=8, act=4, v0=8, s3=16, b3=16, b2=8, misc=8, b1=4)
        self.paired = ("s3", "b3")
        self.shared = dict(b1="s1", b2="s2")


def block_kernel(
    d,
    x_hbm, ct_hbm, mask_in, count_in, w1_hbm, g1, c1, w2_hbm, g2, c2, wsq, gs, cs, wex, bex, w3_hbm, g3, c3,
    dn_hbm, ost, xv, wg0, wg1, wg2, wg3, wg4, small,
    w1, w2, w3, mb, live, ctv, y1, a1p, y2, act2, slope2, mixed, dm, acc_c, acc_g, w3p, w2x, w2l, w2r,
    mix_t, att, q2, q4, vecs, pools, v0, cols,
    parts, rcs, rxys, rzs, mids, vres, sums, ga_src, ga_buf, pf_src, pf_buf, fc_src, fc_buf,
    sem_w, sem_x, sem_ct, sem_dn, sem_back, ssa, rsa, ssi, rsi, ssh, rsh, ssw, rsw,
):
    n_img, n_ha = d.n_img, d.n_ha
    nb, nh, nw = d.nb, d.nh, d.nw
    cin, mid, wd, wide2, line, rows = d.cin, d.mid, d.width, d.wide, d.line, d.rows
    gin, padded = d.gin, d.padded
    dyp = ctv
    ress = (wg0, wg1, wg2, wg3, wg4)
    half = cin // 2
    i = lax.axis_index("img")
    h = lax.axis_index("ha")

    def ha_peer(k):
        return (i, lax.rem(h + k, n_ha))

    def img_peer(k):
        return (lax.rem(i + k, n_img), h)

    z_of, x_of, y_of, core = i // 2, lax.rem(i, 2), h // 2, lax.rem(h, 2)
    spot = x_of * 2 + y_of

    def core_peer():
        return (i, y_of * 2 + (1 - core))

    def plane_peer(k):
        other = lax.rem(spot + k, 4)
        return (z_of * 2 + other // 2, lax.rem(other, 2) * 2 + core)

    def z_peer(k):
        return (lax.rem(z_of + k, 4) * 2 + x_of, h)

    def any_peer(k):
        return (lax.rem(i + k // 4, 8), lax.rem(h + k % 4, 4))

    def chip_peer(k):
        return (lax.rem(i + k // 2, 8), lax.rem(y_of + k % 2, 2) * 2 + core)

    def remote(src, dst, send, recv, peer):
        return pltpu.make_async_remote_copy(
            src_ref=src, dst_ref=dst, send_sem=send, recv_sem=recv, device_id=peer, device_id_type=MESH
        )

    def line_rows(t):
        return pl.ds(pl.multiple_of(t * line, line), line)

    def block_rows(t, u, step):
        return pl.ds(pl.multiple_of(t * line + u * step, nb), step)

    def x_copy(t):
        return pltpu.make_async_copy(x_hbm.at[line_rows(t)], xv.at[line_rows(t)], sem_x.at[t])

    def half_rows(t, c):
        return pl.ds(pl.multiple_of(c * rows + t * line, nb), line)

    def ct_copy(t, c):
        return pltpu.make_async_copy(
            ct_hbm.at[line_rows(t), pl.ds(c * half, half)], ctv.at[half_rows(t, c)], sem_ct.at[c, t]
        )

    def start_inputs(t, carry):
        x_copy(t).start()
        return carry

    loads = [
        pltpu.make_async_copy(src, dst, sem_w.at[j])
        for j, (src, dst) in enumerate(((w1_hbm, w1), (w2_hbm, w2), (w3_hbm, w3)))
    ]
    loads[0].start()
    lax.fori_loop(0, nh, start_inputs, 0)
    loads[1].start()
    loads[2].start()

    barrier = pltpu.get_barrier_semaphore()
    if d.inside:
        peers = [any_peer(k) for k in range(1, 32)]
    else:
        peers = [ha_peer(k) for k in range(1, n_ha)] + [img_peer(k) for k in range(1, n_img)]
    for peer in peers:
        pl.semaphore_signal(barrier, inc=1, device_id=peer, device_id_type=MESH)

    slots = lax.broadcasted_iota(jnp.int32, (nb, LANES), 0)
    live[...] = (slots < count_in[0]).astype(F32)

    def spread(t, carry):
        cells = mask_in[t].astype(F32)
        alive = live[...]
        for w in range(nw):
            cell = jnp.broadcast_to(cells[:, w : w + 1], (nb, LANES)) * alive
            mb[block_rows(t, w, nb), :] = cell.astype(BF16)
            carry = carry + cell
        return carry

    pixels = lax.fori_loop(0, nh, spread, jnp.zeros((nb, LANES), F32))

    def mask_of(at, lanes):
        return wide(mb[at, :].astype(F32), lanes)

    def inner_rows(t, at=nb, count=line):
        return pl.ds(pl.multiple_of(t * padded + at, nb), count)

    def clear(ref):
        zero = jnp.zeros((nb, ref.shape[1]), BF16)

        def body(t, carry):
            ref[inner_rows(t, 0, nb), :] = zero
            ref[inner_rows(t, nb + line, nb), :] = zero
            return carry

        lax.fori_loop(0, nh + 2, body, 0)

        def edge(t, carry):
            ref[inner_rows(0, t * nb, nb), :] = zero
            ref[inner_rows(nh + 1, t * nb, nb), :] = zero
            return carry

        lax.fori_loop(0, nw + 2, edge, 0)

    clear(a1p)

    def swap(src, buf, send, recv, peer, n):
        def copy(k):
            return remote(src, buf.at[k], send.at[k], recv.at[k], peer(k))

        def each(act, carry):
            if n > 32:
                return lax.fori_loop(1, n, act, carry)
            for k in range(1, n):
                carry = act(k, carry)
            return carry

        def begin(k, carry):
            copy(k).start()
            return carry

        def sent(k, carry):
            copy(k).wait_send()
            return carry

        def take(k, carry):
            copy(k).wait_recv()
            return carry + buf[k].astype(F32)

        def finish():
            total = each(take, src[...].astype(F32))
            each(sent, 0)
            return total

        return (lambda: each(begin, 0)), finish

    class Everywhere:
        def __init__(self, name):
            refs = sums[d.shared.get(name, name)]
            self.at = refs["src"]
            self.refs = refs
            if not d.inside:
                return
            send, recv = refs["send"], refs["recv"]
            if name in d.paired:
                self.pair = remote(self.at, refs["other"], send.at[0], recv.at[0], core_peer())
                self.start_far, self.finish_far = swap(refs["mid"], refs["buf"], send, recv, chip_peer, 16)
            else:
                self.pair = None
                self.start_far, self.finish_far = swap(self.at, refs["buf"], send, recv, any_peer, 32)

        def start(self):
            if d.inside:
                if self.pair is not None:
                    self.pair.start()
                    self.pair.wait_recv()
                    self.refs["mid"][...] = self.at[...] + self.refs["other"][...]
                self.start_far()

        def finish(self):
            if d.inside:
                total = self.finish_far()
                if self.pair is not None:
                    self.pair.wait_send()
                return total
            refs = self.refs
            start, finish = swap(self.at, refs["buf_ha"], refs["send_ha"], refs["recv_ha"], ha_peer, n_ha)
            start()
            refs["mid"][...] = finish()
            start, finish = swap(refs["mid"], refs["buf_img"], refs["send"], refs["recv"], img_peer, n_img)
            start()
            return finish()

    def halo(ref, at):
        def down():
            return remote(
                ref.at[inner_rows(nh)], ref.at[inner_rows(0)], ssh.at[at, 0], rsh.at[at, 0],
                (i, jnp.minimum(h + 1, n_ha - 1)),
            )

        def up():
            return remote(
                ref.at[inner_rows(1)], ref.at[inner_rows(nh + 1)], ssh.at[at, 1], rsh.at[at, 1],
                (i, jnp.maximum(h - 1, 0)),
            )

        def start():
            @pl.when(h < n_ha - 1)
            def _():
                down().start()

            @pl.when(h > 0)
            def _():
                up().start()

        def wait_recv():
            @pl.when(h > 0)
            def _():
                down().wait_recv()

            @pl.when(h < n_ha - 1)
            def _():
                up().wait_recv()

        def wait_send():
            @pl.when(h < n_ha - 1)
            def _():
                down().wait_send()

            @pl.when(h > 0)
            def _():
                up().wait_send()

        return start, wait_recv, wait_send

    plane_rows, z_rows = wd // 4, wd // 16

    def plane_at(other):
        return pl.ds(pl.multiple_of(other * plane_rows, plane_rows), plane_rows)

    def z_at(other, base=0):
        return pl.ds(pl.multiple_of(base + other * z_rows, z_rows), z_rows)

    def w_copy(s, stage, k):
        sem = (s, stage * 4 + k)
        if stage == 0:
            src, dst, peer = parts[s].at[1 - core], rcs[s], core_peer()
        elif stage == 1:
            src = parts[s].at[core, plane_at(lax.rem(spot + k, 4))]
            dst, peer = rxys[s].at[k - 1], plane_peer(k)
        elif stage == 2:
            src = mids[s].at[z_at(lax.rem(z_of + k, 4))]
            dst, peer = rzs[s].at[k - 1], z_peer(k)
        elif stage == 3:
            src = dst = ress[s].at[core, z_at(z_of, spot * plane_rows)]
            peer = z_peer(k)
        elif stage == 4:
            src = dst = ress[s].at[core, plane_at(spot)]
            peer = plane_peer(k)
        else:
            src = dst = ress[s].at[core]
            peer = core_peer()
        return remote(src, dst, ssw.at[sem], rsw.at[sem], peer)

    def w_ks(stage):
        return (1,) if stage in (0, 5) else (1, 2, 3)

    def w_arrival(s, stage, k):
        sem = (s, stage * 4 + k)
        if stage == 3:
            dst = ress[s].at[core, z_at(lax.rem(z_of - k + 4, 4), spot * plane_rows)]
        elif stage == 4:
            dst = ress[s].at[core, plane_at(lax.rem(spot - k + 4, 4))]
        else:
            dst = ress[s].at[1 - core]
        return remote(dst, dst, ssw.at[sem], rsw.at[sem], core_peer())

    def w_start(s, stage):
        if d.inside:
            for k in w_ks(stage):
                w_copy(s, stage, k).start()

    def w_finish(s, stage, fix=None):
        if not d.inside:
            return
        for k in w_ks(stage):
            if stage <= 2:
                w_copy(s, stage, k).wait_recv()
            else:
                w_arrival(s, stage, k).wait_recv()
        part, inner = parts[s], mids[s]
        if stage == 0:
            rc = rcs[s]

            def add(t, carry):
                at = pl.ds(pl.multiple_of(t * 16, 16), 16)
                part[core, at, :] = (part[core, at, :].astype(F32) + rc[at, :].astype(F32)).astype(BF16)
                return carry

            lax.fori_loop(0, wd // 16, add, 0)
        elif stage == 1:
            buf = rxys[s]

            def add(t, carry):
                at = pl.ds(pl.multiple_of(t * 16, 16), 16)
                own = pl.ds(pl.multiple_of(spot * plane_rows + t * 16, 16), 16)
                total = part[core, own, :].astype(F32)
                for k in range(3):
                    total = total + buf[k, at, :].astype(F32)
                inner[at, :] = total.astype(BF16)
                return carry

            lax.fori_loop(0, plane_rows // 16, add, 0)
        elif stage == 2:
            buf = rzs[s]
            total = inner[z_at(z_of), :].astype(F32)
            for k in range(3):
                total = total + buf[k].astype(F32)
            if s >= d.sets:
                vres[...] = total
                return
            if fix is not None:
                total = fix(total)
            ress[s][core, z_at(z_of, spot * plane_rows), :] = total.astype(BF16)

    def w_step(s, stage, fix=None):
        w_finish(s, stage, fix)
        if stage < 5:
            w_start(s, stage + 1)

    def w_sent(s):
        if d.inside:
            for stage in range(6 if s < d.sets else 3):
                for k in w_ks(stage):
                    w_copy(s, stage, k).wait_send()

    def first(t, carry):
        sums, squares = carry
        x_copy(t).wait()
        ct_copy(t, 0).start()
        ct_copy(t, 1).start()
        at = line_rows(t)
        y = dot(xv[at, :], w1[...])
        y1[at, :] = y
        masked = y * mask_of(at, mid)
        return sums + fold(masked), squares + fold(masked * y)

    loads[0].wait()
    zeros = jnp.zeros((8, mid), F32)
    totals, squares = lax.fori_loop(0, nh, first, (zeros, zeros))
    pl.semaphore_wait(barrier, len(peers))
    count = Everywhere("cnt")
    count.at[...] = jnp.zeros((4, LANES), F32)
    count.at[0:1, :] = total_row(pixels)
    count.at[1:2, :] = total_row(live[...]) * (1.0 / n_ha)
    norm1 = Everywhere("s1")
    put(norm1.at, 0, total_row(totals))
    put(norm1.at, 2, total_row(squares))
    norm1.start()
    count.start()
    loads[1].wait()
    loads[2].wait()
    for r in range(d.radix):
        for ky in range(3):
            for e in range(4):
                if e <= 2:
                    left = w2[r, (ky * 3 + 2 - e) * gin : (ky * 3 + 3 - e) * gin, :]
                if e >= 1:
                    right = w2[r, (ky * 3 + 3 - e) * gin : (ky * 3 + 4 - e) * gin, :]
                if e == 0:
                    w2l[r, :, ky * wd : (ky + 1) * wd] = left
                elif e == 3:
                    w2r[r, :, ky * wd : (ky + 1) * wd] = right
                else:
                    lanes = slice((ky * 2 + e - 1) * wd, (ky * 2 + e) * wd)
                    w2x[r, 0:gin, lanes] = left
                    w2x[r, gin:, lanes] = right
    got = count.finish()
    total, images = got[0:1, :], got[1:2, :]
    got = norm1.finish()
    mean1, scale1 = moments(get(got, 0, mid), get(got, 2, mid), wide(total, mid))
    half_a1 = 0.5 * g1[...] * scale1
    half_b1 = 0.5 * c1[...] - half_a1 * mean1

    step1 = 4 * nb

    def act_first(t, carry):
        def cells(u, carry):
            at = block_rows(t, u, step1)
            value, _ = gate(y1[at, :] * half_a1 + half_b1)
            value = value * mask_of(at, mid)
            a1p[inner_rows(t + 1, nb + u * step1, step1), :] = value.astype(BF16)
            return carry + fold(value)

        return lax.fori_loop(0, line // step1, cells, carry)

    def edges(body, carry):
        return lax.fori_loop(0, 2, lambda t, c: body(t * (nh - 1), c), carry)

    totals = edges(act_first, jnp.zeros((8, mid), F32))
    halo1_start, halo1_recv, halo1_sent = halo(a1p, 0)
    halo1_start()
    totals = lax.fori_loop(1, nh - 1, act_first, totals)
    act_sum = Everywhere("act")
    act_sum.at[...] = jnp.zeros((4, LANES), F32)
    put(act_sum.at, 0, total_row(totals))
    act_sum.start()

    def taps(t, r, first=0, last=9):
        return jnp.concatenate(
            [
                a1p[inner_rows(t + tap // 3, (tap % 3) * nb), r * gin : (r + 1) * gin]
                for tap in range(first, last)
            ],
            axis=1,
        )

    def group(t, carry):
        at = line_rows(t)
        mask = mask_of(at, wd)
        done = []
        for r in range(d.radix):
            sums, squares = carry[r]
            y = dot(taps(t, r), w2[r])
            y2[at, r * wd : (r + 1) * wd] = y.astype(BF16)
            masked = y * mask
            done.append((sums + fold(masked), squares + fold(masked * y)))
        return tuple(done)

    zeros = jnp.zeros((8, wd), F32)
    sums2 = lax.fori_loop(1, nh - 1, group, ((zeros, zeros),) * d.radix)
    halo1_recv()
    sums2 = edges(group, sums2)
    norm2 = Everywhere("s2")
    put(norm2.at, 0, jnp.concatenate([total_row(s) for s, _ in sums2], axis=1))
    put(norm2.at, 4, jnp.concatenate([total_row(q) for _, q in sums2], axis=1))
    norm2.start()

    acc_c[...] = jnp.zeros((wd, cin), F32)
    vecs[...] = jnp.zeros((8, cin), F32)

    def norm_products(t, carry):
        at = line_rows(t)
        mask = mask_of(at, mid)
        hat = ((y1[at, :] - mean1) * scale1 * mask).astype(BF16)
        x = xv[at, :]
        acc_c[...] += dot_tn(hat, x)
        vecs[...] += dot_tn(mb[at, :], x)[0:8, :]
        return carry

    lax.fori_loop(0, nh, norm_products, 0)
    norm2_done = norm2.finish()
    for c in range(2):
        parts[5][c] = acc_c[:, c * half : (c + 1) * half].astype(BF16)
    w_start(5, 0)
    v0_sum = Everywhere("v0")
    put(v0_sum.at, 0, vecs[0:1, :])
    v0_sum.start()
    mean2, scale2 = moments(get(norm2_done, 0, wide2), get(norm2_done, 4, wide2), wide(total, wide2))
    half_a2 = 0.5 * g2[...] * scale2
    half_b2 = 0.5 * c2[...] - half_a2 * mean2

    lane_blocks = wd // LANES
    step2 = (nw // 2) * nb
    zero = jnp.zeros((nb, LANES), F32)
    for j in range(lane_blocks):
        own = slice(j * LANES, (j + 1) * LANES)

        def act_group(t, pool):
            at = pl.ds(pl.multiple_of(t * step2, step2), step2)
            mask = mb[at, :]
            full = mask.astype(F32)
            for r in range(d.radix):
                lanes = slice(r * wd + j * LANES, r * wd + (j + 1) * LANES)
                value, _ = gate(y2[at, lanes].astype(F32) * half_a2[:, lanes] + half_b2[:, lanes])
                value = value * full
                act2[at, lanes] = value.astype(BF16)
                pool = pool + fold_images(value, nb)
            return pool

        pools[:, own] = lax.fori_loop(0, rows // step2, act_group, zero)

    pool = pools[...]
    squeeze = wsq[...].astype(F32)
    excite = wex[...].astype(F32)
    pf_src[:, 0 : d.inter] = dot(pool, squeeze, HIGH)
    pf_src[:, d.inter :] = pixels
    pf_start, pf_finish = swap(pf_src, pf_buf, ssa.at[0], rsa.at[0], ha_peer, n_ha)
    pf_start()

    def slopes(block):
        lanes = slice(block * LANES, (block + 1) * LANES)
        ha2, hb2 = half_a2[:, lanes], half_b2[:, lanes]

        def body(t, carry):
            slopes, bends = carry
            at = pl.ds(pl.multiple_of(t * step2, step2), step2)
            y = y2[at, lanes].astype(F32)
            _, slope = gate(y * ha2 + hb2)
            slope = slope * mb[at, :].astype(F32)
            slope2[at, lanes] = slope.astype(BF16)
            return slopes + fold_images(slope, nb), bends + fold_images(slope * y, nb)

        q2[:, lanes], q4[:, lanes] = lax.fori_loop(0, rows // step2, body, (zero, zero))

    total_blocks = d.radix * lane_blocks
    for block in range(total_blocks // 4):
        slopes(block)
    w_step(5, 0)
    both = pf_finish()
    floor = jnp.maximum(both[:, d.inter :], 1.0)
    squeezed = both[:, 0 : d.inter] / floor
    live_now = live[...]
    fc_src[...] = jnp.zeros(fc_src.shape, F32)
    put(fc_src.at[0], 0, total_row(squeezed * live_now))
    put(fc_src.at[0], 1, total_row(squeezed * squeezed * live_now))
    fc_start, fc_finish = swap(fc_src.at[0], fc_buf.at[0], ssi.at[0], rsi.at[0], img_peer, n_img)
    fc_start()
    for block in range(total_blocks // 4, total_blocks):
        slopes(block)
    got = fc_finish()
    mean_s, scale_s = moments(got[0:1, :], got[1:2, :], images)
    centered = (squeezed - mean_s) * scale_s
    hidden, hidden_slope = gate(0.5 * (centered * gs[...] + cs[...]))
    logits = dot(hidden, excite, HIGH) + bex[...]
    gap = logits[:, 0:wd] - logits[:, wd:]
    att[:, 0:wd] = jax.nn.sigmoid(gap)
    att[:, wd:] = jax.nn.sigmoid(-gap)

    step3 = 2 * nb

    def mix(t, carry):
        def cells(u, carry):
            at = block_rows(t, u, step3)
            weight = jnp.concatenate([att[...]] * (step3 // nb), axis=0)
            both = act2[at, :].astype(F32) * weight
            mixed[at, :] = (both[:, 0:wd] + both[:, wd:]).astype(BF16)
            return carry

        lax.fori_loop(0, line // step3, cells, 0, unroll=7)
        gram, sums = carry
        cells = mixed[line_rows(t), :]
        mix_t[t] = jnp.transpose(cells)
        return gram + dot(mix_t[t], cells), sums + fold(cells.astype(F32))

    gram, totals = lax.fori_loop(0, nh, mix, (jnp.zeros((wd, wd), F32), jnp.zeros((8, wd), F32)))
    mix_sum = total_row(totals)
    gram_high, gram_low = split_bf16(gram)
    acc_g[0, :, 0:cin] = dot(gram_high, w3[...]) + dot(gram_low, w3[...])
    mix_high, mix_low = split_bf16(mix_sum)
    sum_last = dot(jnp.broadcast_to(mix_high, (16, wd)), w3[...]) + dot(
        jnp.broadcast_to(mix_low, (16, wd)), w3[...]
    )
    norm3 = Everywhere("s3")
    put(norm3.at, 0, sum_last[0:1, :])
    put(norm3.at, 8, total_row(acc_g[0, :, 0:cin] * w3[...].astype(F32)))
    norm3.start()

    def last_product(t, carry):
        at = line_rows(t)
        ost[at, :] = dot(mixed[at, :], w3[...]).astype(BF16)
        ct_copy(t, 0).wait()
        ct_copy(t, 1).wait()
        return carry

    lax.fori_loop(0, nh, last_product, 0)
    w_step(5, 1)
    got = norm3.finish()
    mean3, scale3 = moments(get(got, 0, cin), get(got, 8, cin), wide(total, cin))
    grow3 = g3[...] * scale3
    half_a3 = 0.5 * grow3
    half_b3 = 0.5 * c3[...] - half_a3 * mean3

    step4 = (nw // 4) * nb
    blocks4 = 2 * LANES

    def dn_copy(t, c):
        return pltpu.make_async_copy(
            ctv.at[half_rows(t, c)], dn_hbm.at[line_rows(t), pl.ds(c * half, half)], sem_dn.at[c, t]
        )

    def dn_back(t, c):
        return pltpu.make_async_copy(
            dn_hbm.at[line_rows(t), pl.ds(c * half, half)], ctv.at[half_rows(t, c)], sem_back.at[c, t]
        )

    def grad_of(t):
        return jnp.concatenate([ctv[half_rows(t, 0), :], ctv[half_rows(t, 1), :]], axis=1)

    acc_c[...] = jnp.zeros((wd, cin), F32)
    vecs[...] = jnp.zeros((8, cin), F32)

    def last(t, carry):
        for j in range(cin // blocks4):
            lanes = slice(j * blocks4, (j + 1) * blocks4)
            a3, b3 = half_a3[:, lanes], half_b3[:, lanes]

            def cells(u, carry):
                at = block_rows(t, u, step4)
                mask = wide(mb[at, :], blocks4)
                x = xv[at, lanes] * jnp.asarray(0.5, BF16)
                arg = ost[at, lanes].astype(F32) * a3 + (b3 + x.astype(F32))
                bend = jnp.tanh(arg)
                rise = 1.0 + bend
                value = arg * rise
                ost[at, lanes] = value.astype(BF16) * mask
                side = j * blocks4 // half
                there = pl.ds(pl.multiple_of(side * rows + t * line + u * step4, nb), step4)
                inner = slice(j * blocks4 - side * half, (j + 1) * blocks4 - side * half)
                push = ctv[there, inner] * (mask * jnp.asarray(0.5, BF16))
                grad = push.astype(F32) * (rise + value * (1.0 - bend))
                ctv[there, inner] = grad.astype(BF16)
                return carry + fold(grad)

            vecs[:, lanes] = lax.fori_loop(0, line // step4, cells, vecs[:, lanes])
        dn_copy(t, 0).start()
        dn_copy(t, 1).start()
        acc_c[...] += dot(mix_t[t], grad_of(t))
        return carry

    lax.fori_loop(0, nh, last, 0)
    sum_grad = total_row(vecs[...])
    back3 = Everywhere("b3")
    put(back3.at, 0, sum_grad)
    put(back3.at, 8, scale3 * (total_row(acc_c[...] * w3[...].astype(F32)) - mean3 * sum_grad))
    back3.start()

    w3p[...] = (w3[...].astype(F32) * grow3).astype(BF16)

    def plain_back(t, carry):
        dm[line_rows(t), :] = dot_nt(grad_of(t), w3p[...])
        return carry

    lax.fori_loop(0, nh, plain_back, 0)
    w_finish(5, 2)
    got = back3.finish()
    bias3, gain3 = get(got, 0, cin), get(got, 8, cin)
    put(small.at[0], 0, bias3)
    put(small.at[0], 8, gain3)
    all_wide = wide(total, cin)
    slant3 = scale3 * gain3 / all_wide
    level3 = bias3 / all_wide - mean3 * slant3
    fix = (w3[...].astype(F32) * slant3).astype(BF16)
    fix = dot_nt(fix, w3p[...]).astype(BF16)
    level_high, level_low = split_bf16(level3)
    shift = dot_nt(jnp.broadcast_to(level_high, (16, cin)), w3p[...]) + dot_nt(
        jnp.broadcast_to(level_low, (16, cin)), w3p[...]
    )
    shift = shift[0:1, :]

    def back_mix(t, carry):
        at = line_rows(t)
        dm[at, :] = dm[at, :] - dot(mixed[at, :], fix) - mask_of(at, wd) * shift
        return carry

    lax.fori_loop(0, nh, back_mix, 0)

    step5 = 4 * nb
    sums5 = []
    for j in range(lane_blocks):
        lanes = slice(j * LANES, (j + 1) * LANES)

        def image_sums(t, carry):
            at = pl.ds(pl.multiple_of(t * step5, step5), step5)
            grad = dm[at, lanes]
            done = []
            for r in range(d.radix):
                own = slice(r * wd + j * LANES, r * wd + (j + 1) * LANES)
                a, b, c = carry[r]
                a = a + fold_images(grad * act2[at, own].astype(F32), nb)
                part = grad * slope2[at, own].astype(F32)
                b = b + fold_images(part, nb)
                c = c + fold_images(part * y2[at, own].astype(F32), nb)
                done.append((a, b, c))
            return tuple(done)

        sums5.append(lax.fori_loop(0, rows // step5, image_sums, ((zero, zero, zero),) * d.radix))
    pick = lambda which: jnp.concatenate(
        [sums5[j][r][which] for r in range(d.radix) for j in range(lane_blocks)], axis=1
    )
    q1, q3 = pick(1), pick(2)

    def dn_out(t, carry):
        dn_copy(t, 0).wait()
        dn_copy(t, 1).wait()
        return carry

    lax.fori_loop(0, nh, dn_out, 0)
    clear(dyp)
    ga_src[...] = pick(0).astype(BF16)
    ga_start, ga_finish = swap(ga_src, ga_buf, ssa.at[1], rsa.at[1], ha_peer, n_ha)
    ga_start()

    mix_column = jnp.transpose(jnp.broadcast_to(mix_sum, (LANES, wd)))
    for j in range(cin // LANES):
        lanes = slice(j * LANES, (j + 1) * LANES)
        c = 0 if j * LANES < half else 1
        grad = grow3[:, lanes] * (
            acc_c[:, lanes] - mix_column * level3[:, lanes] - acc_g[0, :, lanes] * slant3[:, lanes]
        )
        parts[2][c, :, j * LANES - c * half : (j + 1) * LANES - c * half] = grad.astype(BF16)
    w_start(2, 0)

    grad_att = ga_finish()
    weight = att[...]
    weighed = weight * grad_att
    both = weighed[:, 0:wd] + weighed[:, wd:]
    grad_logits = weight * (grad_att - jnp.concatenate([both, both], axis=1))
    grad_fc = dot_nt(grad_logits, excite, HIGH) * hidden_slope
    put(fc_src.at[1], 0, total_row(grad_fc))
    put(fc_src.at[1], 1, total_row(grad_fc * centered))
    pooled = pool / wide(floor, wd)
    put(fc_src.at[1], 2, total_row(pooled))
    fc_start, fc_finish = swap(fc_src.at[1], fc_buf.at[1], ssi.at[1], rsi.at[1], img_peer, n_img)
    fc_start()
    w_step(2, 0)
    grad_excite = dot_tn(hidden, grad_logits, HIGH)
    grad_bex = total_row(grad_logits) * (1.0 / n_ha)
    got = fc_finish()
    bias_s, gain_s = got[0:1, :], got[1:2, :]
    put(small.at[0], 16, bias_s)
    put(small.at[0], 17, gain_s)
    grad_squeezed = (gs[...] * scale_s) * (
        grad_fc - live_now * (bias_s + centered * gain_s) / images
    )
    grad_pool = dot_nt(grad_squeezed, squeeze, HIGH) / wide(floor, wd)
    pool2 = jnp.concatenate([grad_pool] * d.radix, axis=1)
    sum_grad = total_row(weight * q1 + pool2 * q2[...])
    sum_bend = total_row(weight * q3 + pool2 * q4[...])
    back2 = Everywhere("b2")
    put(back2.at, 0, sum_grad)
    put(back2.at, 4, scale2 * (sum_bend - mean2 * sum_grad))
    back2.start()
    level = get(got, 2, wd) / wide(images, wd)
    grad_squeeze = dot_tn(pooled - level, grad_squeezed, HIGH)
    grow2 = g2[...] * scale2
    att[...] = weight * grow2
    q2[...] = pool2 * grow2
    parts[4][0] = jnp.concatenate([grad_excite[:, 0:wd], grad_excite[:, wd:]], axis=0).astype(
        BF16
    ) * jnp.asarray(1.0 / n_ha, BF16)
    parts[4][1, :, 0 : d.inter] = grad_squeeze.astype(BF16)
    parts[4][1, :, d.inter :] = jnp.zeros((wd, wd - d.inter), BF16)
    w_start(4, 0)
    w_step(2, 1)
    acc_g[...] = jnp.zeros((d.radix, wd, 9 * gin), F32)
    mean_act1 = get(act_sum.finish(), 0, mid) / (wide(images, mid) * float(nh * n_ha * nw))
    w_step(4, 0)
    got = back2.finish()
    bias2, gain2 = get(got, 0, wide2), get(got, 4, wide2)
    put(small.at[0], 20, bias2)
    put(small.at[0], 24, gain2)
    slant2 = grow2 * scale2 * gain2 / wide(total, wide2)
    level2 = grow2 * bias2 / wide(total, wide2) - mean2 * slant2

    step6 = 2 * nb

    def back_group(t, carry):
        def cells(u, carry):
            at = block_rows(t, u, step6)
            to = inner_rows(t + 1, nb + u * step6, step6)
            again = step6 // nb
            grad = dm[at, :]
            mask = mask_of(at, wd)
            sums = []
            for r in range(d.radix):
                own = slice(r * wd, (r + 1) * wd)
                grow = jnp.concatenate([att[:, own]] * again, axis=0)
                lift = jnp.concatenate([q2[:, own]] * again, axis=0)
                push = (grow * grad + lift) * slope2[at, own].astype(F32)
                pull = mask * (level2[:, own] + slant2[:, own] * y2[at, own].astype(F32))
                dyp[to, own] = (push - pull).astype(BF16)
                sums.append(carry[r] + fold(push - pull))
            return tuple(sums)

        return lax.fori_loop(0, line // step6, cells, carry, unroll=7)

    zeros = jnp.zeros((8, wd), F32)
    sums2 = edges(back_group, (zeros,) * d.radix)
    halo2_start, halo2_recv, halo2_sent = halo(dyp, 1)
    halo2_start()
    sums2 = lax.fori_loop(1, nh - 1, back_group, sums2)
    sum_dy2 = [total_row(s) for s in sums2]
    misc = Everywhere("misc")
    put(misc.at, 0, jnp.concatenate(sum_dy2, axis=1))
    put(misc.at, 4, grad_bex)
    misc.start()
    w_step(2, 2)
    w_step(4, 1)

    def weights_group(t, carry):
        for r in range(d.radix):
            grad = jnp.transpose(dyp[inner_rows(t + 1), r * wd : (r + 1) * wd])
            acc_g[r] += dot(grad, taps(t, r))
        return carry

    lax.fori_loop(0, nh, weights_group, 0)

    def send_group(s, first, last):
        lanes = (last - first) * gin
        for r in range(d.radix):
            base = wide(mean_act1[:, r * gin : (r + 1) * gin], lanes)
            column = jnp.transpose(jnp.broadcast_to(sum_dy2[r], (LANES, wd)))
            grad = acc_g[r, :, first * gin : last * gin] - wide(column, lanes) * base
            parts[s][r, :, 0:lanes] = grad.astype(BF16)
        w_start(s, 0)

    send_group(1, 0, d.split)
    send_group(3, d.split, 9)
    w_step(2, 3)
    w_step(4, 2)

    pairs = nw // 2

    def back_taps(t, r, which):
        cells = []
        for ky in range(3):
            for e in which:
                block = dyp[inner_rows(t + 2 - ky, e * nb), r * wd : (r + 1) * wd]
                block = block.reshape(pairs, 2 * nb, wd)[:, 0:nb, :].reshape(pairs * nb, wd)
                cells.append(block)
        return jnp.concatenate(cells, axis=1)

    def transposed(t, carry):
        sums, bends = carry
        at = line_rows(t)
        done = []
        for r in range(d.radix):
            both = dot_nt(back_taps(t, r, (1, 2)), w2x[r])
            left = both[:, 0:gin] + dot_nt(back_taps(t, r, (0,)), w2l[r])
            right = both[:, gin:] + dot_nt(back_taps(t, r, (3,)), w2r[r])
            both = jnp.concatenate(
                [left.reshape(pairs, nb, gin), right.reshape(pairs, nb, gin)], axis=1
            )
            done.append(both.reshape(line, gin))
        dm[at, :] = jnp.concatenate(done, axis=1)

        def cells(u, carry):
            sums, bends = carry
            at = block_rows(t, u, step1)
            y = y1[at, :]
            _, slope = gate(y * half_a1 + half_b1)
            grad = dm[at, :] * (slope * mask_of(at, mid))
            dm[at, :] = grad
            mixed[at, :] = grad.astype(BF16)
            return sums + fold(grad), bends + fold(grad * y)

        return lax.fori_loop(0, line // step1, cells, (sums, bends))

    zeros = jnp.zeros((8, mid), F32)
    middle = 1 + (nh - 2) // 3
    sums1 = lax.fori_loop(1, middle, transposed, (zeros, zeros))
    w_step(1, 0)
    w_step(3, 0)
    sums1 = lax.fori_loop(middle, nh - 1, transposed, sums1)
    w_step(4, 3)
    halo2_recv()
    sums1 = edges(transposed, sums1)
    sum_grad = total_row(sums1[0])
    back1 = Everywhere("b1")
    put(back1.at, 0, sum_grad)
    put(back1.at, 2, scale1 * (total_row(sums1[1]) - mean1 * sum_grad))
    back1.start()
    halo2_sent()

    def fetch_back(t, carry):
        dn_back(t, 0).start()
        dn_back(t, 1).start()
        return carry

    lax.fori_loop(0, nh, fetch_back, 0)

    acc_c[...] = jnp.zeros((wd, cin), F32)

    def first_weights(t, carry):
        at = line_rows(t)
        acc_c[...] += dot_tn(mixed[at, :], xv[at, :])
        return carry

    lax.fori_loop(0, nh, first_weights, 0)
    if d.inside:
        for c in range(2):
            parts[0][c] = acc_c[:, c * half : (c + 1) * half].astype(BF16)
    w_start(0, 0)
    w_step(1, 1)
    w_step(0, 0)
    w_step(3, 1)
    got = back1.finish()
    bias1, gain1 = get(got, 0, mid), get(got, 2, mid)
    grow1 = g1[...] * scale1
    bias_all, gain_all = bias1 / wide(total, mid), gain1 / wide(total, mid)
    slant1 = grow1 * scale1 * gain_all
    level1 = grow1 * bias_all - mean1 * slant1
    w_step(2, 4)
    w_step(4, 4)

    def back_first(t, carry):
        def cells(u, carry):
            at = block_rows(t, u, step1)
            pull = mask_of(at, mid) * (level1 + slant1 * y1[at, :])
            mixed[at, :] = (grow1 * dm[at, :] - pull).astype(BF16)
            return carry

        lax.fori_loop(0, line // step1, cells, 0)
        return carry

    lax.fori_loop(0, nh, back_first, 0)
    put(small.at[0], 32, bias1)
    put(small.at[0], 34, gain1)
    put(small.at[0], 36, mean_act1)
    small[0, 18:20, :] = jnp.zeros((2, LANES), F32)
    small[0, 38:40, :] = jnp.zeros((2, LANES), F32)
    small[0, 44:48, :] = jnp.zeros((4, LANES), F32)
    got = misc.finish()
    put(small.at[0], 28, get(got, 4, wide2))
    put(small.at[0], 40, get(got, 0, wide2))
    got = v0_sum.finish()
    for c in range(2):
        v0[c] = jnp.broadcast_to(get(got, 0, cin)[:, c * half : (c + 1) * half], (8, half))
    for j, vector in enumerate((grow1, bias_all, gain_all)):
        cols[j] = jnp.transpose(jnp.broadcast_to(vector, (LANES, mid)))

    def norm_terms(total, at, taken, flat):
        lanes = total.shape[1]
        grow, level, slant = (wide(cols[j, at, :], lanes) for j in range(3))
        return grow * (total - level * flat - slant * taken)

    def fix_first(total):
        return norm_terms(total, z_at(z_of, spot * plane_rows), vres[...], v0[core, 0:1, :])

    def grad_inputs(t, carry):
        at = line_rows(t)
        for c in range(2):
            lanes = slice(c * half, (c + 1) * half)
            dn_back(t, c).wait()
            grad = ctv[half_rows(t, c), :].astype(F32) + dot_nt(mixed[at, :], w1[lanes, :])
            xv[at, lanes] = grad.astype(BF16)
        return carry

    w_step(1, 2)
    lax.fori_loop(0, nh // 2, grad_inputs, 0)
    w_step(3, 2)
    w_step(0, 1)
    w_step(1, 3)
    w_step(3, 3)
    w_step(0, 2, fix_first)
    lax.fori_loop(nh // 2, nh, grad_inputs, 0)
    w_step(1, 4)
    w_step(0, 3)
    w_step(3, 4)
    w_step(0, 4)
    for s in (2, 4, 1, 3, 0):
        w_step(s, 5)
    if not d.inside:
        whole = slice(0, wd)
        for c in range(2):
            lanes = slice(c * half, (c + 1) * half)
            local = wide(cols[0, whole, :], half) * (
                acc_c[:, lanes]
                - wide(cols[1, whole, :], half) * get(v0_sum.at[...], 0, cin)[:, lanes]
                - wide(cols[2, whole, :], half) * parts[5][c].astype(F32)
            )
            parts[0][c] = local.astype(BF16)

    for s in range(d.sets + 1):
        w_sent(s)
    halo1_sent()
    if not d.inside:
        for s in range(d.sets):
            ress[s][...] = parts[s][...]


def call_block(d, args):
    f32, bf16 = F32, BF16
    cin, wd, mid, rows, nb, nh = d.cin, d.width, d.mid, d.rows, d.nb, d.nh
    vmem, dma = pltpu.VMEM, pltpu.SemaphoreType.DMA
    halves = [(2, wd, lanes) for lanes in d.half]
    shape = jax.ShapeDtypeStruct
    outs = [
        shape((rows, cin), bf16),
        vmem((rows, cin), bf16),
        vmem((rows, cin), bf16),
        *[vmem(s, bf16) for s in halves[: d.sets]],
        vmem((1, 48, LANES), f32),
    ]
    anywhere = pl.BlockSpec(memory_space=pl.ANY)
    inside = pl.BlockSpec(memory_space=pltpu.VMEM)
    plane, zed = wd // 4, wd // 16

    def sums_of(name, count):
        if not d.inside:
            return dict(
                src=vmem((count, LANES), f32),
                mid=vmem((count, LANES), f32),
                buf_ha=vmem((d.n_ha, count, LANES), f32),
                buf_img=vmem((d.n_img, count, LANES), f32),
                send_ha=dma((d.n_ha,)), recv_ha=dma((d.n_ha,)),
                send=dma((d.n_img,)), recv=dma((d.n_img,)),
            )
        if name in d.paired:
            return dict(
                src=vmem((count, LANES), f32),
                mid=vmem((count, LANES), f32),
                other=vmem((count, LANES), f32),
                buf=vmem((16, count, LANES), f32),
                send=dma((16,)), recv=dma((16,)),
            )
        return dict(
            src=vmem((count, LANES), f32),
            buf=vmem((32, count, LANES), f32),
            send=dma((32,)), recv=dma((32,)),
        )

    scratch = [
        vmem((cin, mid), bf16),
        vmem((d.radix, 9 * d.gin, wd), bf16),
        vmem((wd, cin), bf16),
        vmem((rows, LANES), bf16),
        vmem((nb, LANES), f32),
        vmem((max(2 * rows, (nh + 2) * d.padded), cin // 2), bf16),
        vmem((rows, mid), f32),
        vmem(((nh + 2) * d.padded, mid), bf16),
        vmem((rows, d.wide), bf16),
        vmem((rows, d.wide), bf16),
        vmem((rows, d.wide), bf16),
        vmem((rows, wd), bf16),
        vmem((rows, wd), f32),
        vmem((wd, cin), f32),
        vmem((d.radix, wd, 9 * d.gin), f32),
        vmem((wd, cin), bf16),
        vmem((d.radix, 2 * d.gin, 6 * wd), bf16),
        vmem((d.radix, d.gin, 3 * wd), bf16),
        vmem((d.radix, d.gin, 3 * wd), bf16),
        vmem((nh, wd, d.line), bf16),
        vmem((nb, d.wide), f32),
        vmem((nb, d.wide), f32),
        vmem((nb, d.wide), f32),
        vmem((8, cin), f32),
        vmem((nb, wd), f32),
        vmem((2, 8, cin // 2), f32),
        vmem((3, mid, LANES), f32),
        [vmem(s, bf16) for s in halves],
        [vmem((wd, lanes), bf16) for lanes in d.half],
        [vmem((3, plane, lanes), bf16) for lanes in d.half],
        [vmem((3, zed, lanes), bf16) for lanes in d.half],
        [vmem((plane, lanes), bf16) for lanes in d.half],
        vmem((zed, d.half[0]), f32),
        {name: sums_of(name, count) for name, count in d.sums.items() if name not in d.shared},
        vmem((nb, d.wide), bf16),
        vmem((d.n_ha, nb, d.wide), bf16),
        vmem((nb, 2 * LANES), f32),
        vmem((d.n_ha, nb, 2 * LANES), f32),
        vmem((2, 4, LANES), f32),
        vmem((2, d.n_img, 4, LANES), f32),
        dma((3,)),
        dma((nh,)),
        dma((2, nh)),
        dma((2, nh)),
        dma((2, nh)),
        dma((2, d.n_ha)),
        dma((2, d.n_ha)),
        dma((2, d.n_img)),
        dma((2, d.n_img)),
        dma((2, 2)),
        dma((2, 2)),
        dma((6, 24)),
        dma((6, 24)),
    ]
    return pl.pallas_call(
        functools.partial(block_kernel, d),
        out_shape=outs,
        in_specs=[anywhere, anywhere, inside, pl.BlockSpec(memory_space=pltpu.SMEM)]
        + [anywhere, inside, inside, anywhere] + [inside] * 7 + [anywhere, inside, inside],
        out_specs=[anywhere] + [inside] * 8,
        scratch_shapes=scratch,
        name="block",
        compiler_params=pltpu.CompilerParams(
            collective_id=0, has_side_effects=True, vmem_limit_bytes=47 << 20
        ),
    )(*args)


def finish_kernel(
    d, out_in, gin_in, wg0, wg1, wg2, wg3, wg4, small,
    out, gin_hbm, gw1_hbm, gg1, gb1, gw2_hbm, gg2, gb2, gwsq, ggs, gbs, gwex, gbex, gw3_hbm, gg3, gb3,
    gw1, gw2, gw3, sem_out, sem_gw,
):
    wd = d.width
    parts = 4
    copies = [
        pltpu.make_async_copy(src.at[at], dst.at[at], sem_out.at[which, t])
        for which, (src, dst) in enumerate(((out_in, out), (gin_in, gin_hbm)))
        for t in range(parts)
        for at in (pl.ds(t * (d.rows // parts), d.rows // parts),)
    ]
    for copy in copies:
        copy.start()
    stores = [
        pltpu.make_async_copy(src, dst, sem_gw.at[j])
        for j, (src, dst) in enumerate(((gw1, gw1_hbm), (gw3, gw3_hbm), (gw2, gw2_hbm)))
    ]

    def weights(step):
        half = d.cin // 2
        if step < 2:
            gw1[step * half : (step + 1) * half, :] = jnp.transpose(wg0[step].astype(F32))
            gw3[:, step * half : (step + 1) * half] = wg2[step].astype(F32)
        elif step < 4:
            r = step - 2
            rows = small[0]
            mean = get(rows, 36, d.mid)[:, r * d.gin : (r + 1) * d.gin]
            taken = get(rows, 40, d.wide)[:, r * wd : (r + 1) * wd]
            mean = jnp.transpose(jnp.broadcast_to(mean, (LANES, d.gin)))
            back = wide(mean, wd) * taken
            for tap in range(9):
                held, first = (wg1, 0) if tap < d.split else (wg3, d.split)
                cells = held[r, :, (tap - first) * d.gin : (tap - first + 1) * d.gin]
                gw2[r, tap] = jnp.transpose(cells.astype(F32)) + back
        elif step == 4:
            cells = wg4[0].astype(F32)
            gwex[:, 0:wd] = cells[0 : d.inter, :]
            gwex[:, wd:] = cells[d.inter :, :]
            gwsq[...] = wg4[1, :, 0 : d.inter].astype(F32)
            rows = small[0]
            gb3[...] = get(rows, 0, d.cin)
            gg3[...] = get(rows, 8, d.cin)
            gbs[...] = rows[16:17, :]
            ggs[...] = rows[17:18, :]
            gb2[...] = get(rows, 20, d.wide)
            gg2[...] = get(rows, 24, d.wide)
            gbex[...] = get(rows, 28, d.wide)
            gb1[...] = get(rows, 32, d.mid)
            gg1[...] = get(rows, 34, d.mid)

    for t in range(5):
        weights(t)
        if t == 1:
            stores[0].start()
            stores[1].start()
        elif t == 3:
            stores[2].start()
    for copy in stores + copies:
        copy.wait()


def call_finish(d, *args):
    shape = jax.ShapeDtypeStruct
    cin, wd, mid = d.cin, d.width, d.mid
    vmem, dma = pltpu.VMEM, pltpu.SemaphoreType.DMA
    small_dims = [
        (cin, mid), (1, mid), (1, mid), (d.radix, 9, d.gin, wd), (1, d.wide), (1, d.wide), (wd, d.inter),
        (1, d.inter), (1, d.inter), (d.inter, d.wide), (1, d.wide), (wd, cin), (1, cin), (1, cin),
    ]
    anywhere = pl.BlockSpec(memory_space=pl.ANY)
    inside = pl.BlockSpec(memory_space=pltpu.VMEM)
    return pl.pallas_call(
        functools.partial(finish_kernel, d),
        out_shape=[shape((d.rows, cin), BF16), shape((d.rows, cin), BF16)]
        + [shape(s, F32) for s in small_dims],
        in_specs=[inside] * 8,
        out_specs=[anywhere] * 3 + [inside] * 2 + [anywhere] + [inside] * 7 + [anywhere] + [inside] * 2,
        scratch_shapes=[
            vmem((cin, mid), F32), vmem((d.radix, 9, d.gin, wd), F32), vmem((wd, cin), F32),
            dma((2, 4)), dma((3,)),
        ],
        name="finish",
        compiler_params=pltpu.CompilerParams(vmem_limit_bytes=16 << 20),
    )(*[pltpu.with_memory_space_constraint(arg, pltpu.VMEM) for arg in args])


def on_device(
    inputs, image_count, pixel_mask, w_first, gain_first, bias_first, w_group, gain_group, bias_group,
    w_squeeze, gain_squeeze, bias_squeeze, w_excite, bias_excite, w_last, gain_last, bias_last, cotangent,
):
    n_img, n_ha = lax.axis_size("img"), lax.axis_size("ha")
    d = Dims(n_img, n_ha, inputs.shape, w_group.shape, w_squeeze.shape)
    nb, nh, nw, cin = inputs.shape

    def by_rows(cells):
        return jnp.transpose(cells, (1, 2, 0, 3)).reshape(d.rows, cin)

    def by_image(cells):
        return jnp.transpose(cells.reshape(nh, nw, nb, cin), (2, 0, 1, 3))

    row = lambda v: v.reshape(1, -1)
    args = (
        by_rows(inputs), by_rows(cotangent), jnp.transpose(pixel_mask, (1, 0, 2)), image_count,
        w_first, row(gain_first), row(bias_first),
        w_group.reshape(d.radix, 9 * d.gin, d.width), row(gain_group), row(bias_group),
        w_squeeze, row(gain_squeeze), row(bias_squeeze), w_excite, row(bias_excite),
        w_last, row(gain_last), row(bias_last),
    )
    _, out, gin, *sets, small = call_block(d, args)
    if not d.inside:
        sets = lax.psum(sets, ("img", "ha"))
    done = call_finish(d, out, gin, *sets, small)
    (out, gin, gw1, gg1, gb1, gw2, gg2, gb2, gwsq, ggs, gbs, gwex, gbex, gw3, gg3, gb3) = done
    flat = lambda v: v.reshape(-1)
    return (
        by_image(out), by_image(gin), gw1, flat(gg1), flat(gb1), gw2.reshape(w_group.shape), flat(gg2), flat(gb2),
        gwsq, flat(ggs), flat(gbs), gwex, flat(gbex), gw3, flat(gg3), flat(gb3),
    )


def solution(mesh):
    cells = P("img", "ha", None, None)
    placed = (cells, P("img"), P("img", "ha", None)) + (P(),) * 14 + (cells,)
    return jax.shard_map(
        on_device,
        mesh=mesh,
        in_specs=placed,
        out_specs=(cells, cells) + (P(),) * 14,
        check_vma=False,
    )
```

```python
import functools

import jax
import jax.numpy as jnp
from jax import lax
from jax.experimental import pallas as pl
from jax.experimental.pallas import tpu as pltpu
from jax.sharding import PartitionSpec as P

EPS = 1e-05
F32 = jnp.float32
BF16 = jnp.bfloat16
HIGH = lax.Precision.HIGHEST
MESH = pl.DeviceIdType.MESH
LANES = 128


def dot(a, b, precision=None):
    return jnp.dot(a, b, preferred_element_type=F32, precision=precision)


def dot_nt(a, b, precision=None):
    return lax.dot_general(
        a, b, (((1,), (1,)), ((), ())), preferred_element_type=F32, precision=precision
    )


def dot_tn(a, b, precision=None):
    return lax.dot_general(
        a, b, (((0,), (0,)), ((), ())), preferred_element_type=F32, precision=precision
    )


def wide(cell, lanes):
    return jnp.concatenate([cell] * (lanes // LANES), axis=1)


def fold(cells):
    rows, lanes = cells.shape
    return jnp.sum(cells.reshape(rows // 8, 8, lanes), axis=0)


def fold_images(cells, images):
    rows, lanes = cells.shape
    return jnp.sum(cells.reshape(rows // images, images, lanes), axis=0)


def total_row(cells):
    return jnp.sum(cells, axis=0, keepdims=True)


def put(ref, row, vector):
    for j in range(vector.shape[1] // LANES):
        ref[row + j : row + j + 1, :] = vector[:, j * LANES : (j + 1) * LANES]


def get(cells, row, lanes):
    return jnp.concatenate(
        [cells[row + j : row + j + 1, :] for j in range(lanes // LANES)], axis=1
    )


def moments(sums, squares, total):
    mean = sums / total
    spread = squares / total - mean * mean
    return mean, lax.rsqrt(spread + EPS)


def gate(half):
    bend = jnp.tanh(half)
    rise = 1.0 + bend
    value = half * rise
    return value, 0.5 * (rise + value * (1.0 - bend))


def split_bf16(cells):
    high = cells.astype(BF16)
    return high, (cells - high.astype(F32)).astype(BF16)


def thirds(cells):
    high = cells.astype(BF16)
    rest = cells - high.astype(F32)
    middle = rest.astype(BF16)
    return jnp.concatenate([high, middle, (rest - middle.astype(F32)).astype(BF16)], axis=0)


def add_thirds(cells):
    rows = cells.shape[0] // 3
    return cells[0:rows] + cells[rows : 2 * rows] + cells[2 * rows :]


class Dims:
    def __init__(self, n_img, n_ha, inputs, w_group, w_squeeze):
        self.n_img, self.n_ha = n_img, n_ha
        self.nb, self.nh, self.nw, self.cin = inputs
        self.radix, _, _, self.gin, self.width = w_group
        self.mid = self.radix * self.gin
        self.wide = self.radix * self.width
        self.inter = w_squeeze[1]
        self.line = self.nw * self.nb
        self.rows = self.nh * self.line
        self.padded = (self.nw + 2) * self.nb
        self.split = 5
        self.half = (self.cin // 2, 5 * self.gin, self.cin // 2, 4 * self.gin, self.width, self.cin // 2)
        self.sets = 5
        self.inside = n_img == 8 and n_ha == 4
        self.sums = dict(cnt=4, s1=4, s2=8, act=4, v0=8, s3=16, b3=16, b2=8, misc=8, b1=4)
        self.paired = ("s3",)
        self.narrow = ("b3",)
        self.shared = dict(b1="s1", b2="s2")


def block_kernel(
    d,
    x_hbm, ct_hbm, mask_in, count_in, w1_hbm, g1, c1, w2_hbm, g2, c2, wsq, gs, cs, wex, bex, w3_hbm, g3, c3,
    dn_hbm, ost, xv, wg0, wg1, wg2, wg3, wg4, small,
    w1, w2, w3, mb, live, ctv, y1, a1p, y2, act2, slope2, mixed, dm, acc_c, acc_g, w3p, w2x, w2l, w2r,
    mix_t, rows16, att, q2, q4, vecs, pools, v0, cols,
    parts, rcs, rxys, rzs, mids, vres, sums, ga_src, ga_buf, pf_src, pf_buf, fc_src, fc_buf,
    sem_w, sem_x, sem_ct, sem_dn, sem_back, ssa, rsa, ssi, rsi, ssh, rsh, ssw, rsw,
):
    n_img, n_ha = d.n_img, d.n_ha
    nb, nh, nw = d.nb, d.nh, d.nw
    cin, mid, wd, wide2, line, rows = d.cin, d.mid, d.width, d.wide, d.line, d.rows
    gin, padded = d.gin, d.padded
    dyp = ctv
    ress = (wg0, wg1, wg2, wg3, wg4)
    half = cin // 2
    i = lax.axis_index("img")
    h = lax.axis_index("ha")

    def ha_peer(k):
        return (i, lax.rem(h + k, n_ha))

    def img_peer(k):
        return (lax.rem(i + k, n_img), h)

    z_of, x_of, y_of, core = i // 2, lax.rem(i, 2), h // 2, lax.rem(h, 2)
    spot = x_of * 2 + y_of

    def core_peer():
        return (i, y_of * 2 + (1 - core))

    def plane_peer(k):
        other = lax.rem(spot + k, 4)
        return (z_of * 2 + other // 2, lax.rem(other, 2) * 2 + core)

    def z_peer(k):
        return (lax.rem(z_of + k, 4) * 2 + x_of, h)

    def any_peer(k):
        return (lax.rem(i + k // 4, 8), lax.rem(h + k % 4, 4))

    def chip_peer(k):
        return (lax.rem(i + k // 2, 8), lax.rem(y_of + k % 2, 2) * 2 + core)

    def remote(src, dst, send, recv, peer):
        return pltpu.make_async_remote_copy(
            src_ref=src, dst_ref=dst, send_sem=send, recv_sem=recv, device_id=peer, device_id_type=MESH
        )

    def line_rows(t):
        return pl.ds(pl.multiple_of(t * line, line), line)

    def block_rows(t, u, step):
        return pl.ds(pl.multiple_of(t * line + u * step, nb), step)

    def x_copy(t):
        return pltpu.make_async_copy(x_hbm.at[line_rows(t)], xv.at[line_rows(t)], sem_x.at[t])

    def half_rows(t, c):
        return pl.ds(pl.multiple_of(c * rows + t * line, nb), line)

    def ct_copy(t, c):
        return pltpu.make_async_copy(
            ct_hbm.at[line_rows(t), pl.ds(c * half, half)], ctv.at[half_rows(t, c)], sem_ct.at[c, t]
        )

    def start_inputs(t, carry):
        x_copy(t).start()
        return carry

    loads = [
        pltpu.make_async_copy(src, dst, sem_w.at[j])
        for j, (src, dst) in enumerate(((w1_hbm, w1), (w2_hbm, w2), (w3_hbm, w3)))
    ]
    loads[0].start()
    lax.fori_loop(0, nh, start_inputs, 0)
    loads[1].start()
    loads[2].start()

    barrier = pltpu.get_barrier_semaphore()
    if d.inside:
        peers = [any_peer(k) for k in range(1, 32)]
    else:
        peers = [ha_peer(k) for k in range(1, n_ha)] + [img_peer(k) for k in range(1, n_img)]
    for peer in peers:
        pl.semaphore_signal(barrier, inc=1, device_id=peer, device_id_type=MESH)

    slots = lax.broadcasted_iota(jnp.int32, (nb, LANES), 0)
    live[...] = (slots < count_in[0]).astype(F32)

    def spread(t, carry):
        cells = mask_in[t].astype(F32)
        alive = live[...]
        for w in range(nw):
            cell = jnp.broadcast_to(cells[:, w : w + 1], (nb, LANES)) * alive
            mb[block_rows(t, w, nb), :] = cell.astype(BF16)
            carry = carry + cell
        return carry

    pixels = lax.fori_loop(0, nh, spread, jnp.zeros((nb, LANES), F32))

    def mask_of(at, lanes):
        return wide(mb[at, :].astype(F32), lanes)

    def inner_rows(t, at=nb, count=line):
        return pl.ds(pl.multiple_of(t * padded + at, nb), count)

    def clear(ref):
        zero = jnp.zeros((nb, ref.shape[1]), BF16)

        def body(t, carry):
            ref[inner_rows(t, 0, nb), :] = zero
            ref[inner_rows(t, nb + line, nb), :] = zero
            return carry

        lax.fori_loop(0, nh + 2, body, 0)

        def edge(t, carry):
            ref[inner_rows(0, t * nb, nb), :] = zero
            ref[inner_rows(nh + 1, t * nb, nb), :] = zero
            return carry

        lax.fori_loop(0, nw + 2, edge, 0)

    clear(a1p)

    def swap(src, buf, send, recv, peer, n):
        def copy(k):
            return remote(src, buf.at[k], send.at[k], recv.at[k], peer(k))

        def each(act, carry):
            if n > 32:
                return lax.fori_loop(1, n, act, carry)
            for k in range(1, n):
                carry = act(k, carry)
            return carry

        def begin(k, carry):
            copy(k).start()
            return carry

        def sent(k, carry):
            copy(k).wait_send()
            return carry

        def take(k, carry):
            copy(k).wait_recv()
            return carry + buf[k].astype(F32)

        def finish():
            total = each(take, src[...].astype(F32))
            each(sent, 0)
            return total

        return (lambda: each(begin, 0)), finish

    class Everywhere:
        def __init__(self, name):
            refs = sums[d.shared.get(name, name)]
            self.at = refs["src"]
            self.refs = refs
            if not d.inside:
                return
            send, recv = refs["send"], refs["recv"]
            if name in d.paired:
                self.pair = remote(self.at, refs["other"], send.at[0], recv.at[0], core_peer())
                self.start_far, self.finish_far = swap(refs["mid"], refs["buf"], send, recv, chip_peer, 16)
            else:
                self.pair = None
                self.start_far, self.finish_far = swap(self.at, refs["buf"], send, recv, any_peer, 32)

        def start(self):
            if d.inside:
                if self.pair is not None:
                    self.pair.start()
                    self.pair.wait_recv()
                    self.refs["mid"][...] = self.at[...] + self.refs["other"][...]
                self.start_far()

        def finish(self):
            if d.inside:
                total = self.finish_far()
                if self.pair is not None:
                    self.pair.wait_send()
                return total
            refs = self.refs
            start, finish = swap(self.at, refs["buf_ha"], refs["send_ha"], refs["recv_ha"], ha_peer, n_ha)
            start()
            refs["mid"][...] = finish()
            start, finish = swap(refs["mid"], refs["buf_img"], refs["send"], refs["recv"], img_peer, n_img)
            start()
            return finish()

    def halo(ref, at):
        def down():
            return remote(
                ref.at[inner_rows(nh)], ref.at[inner_rows(0)], ssh.at[at, 0], rsh.at[at, 0],
                (i, jnp.minimum(h + 1, n_ha - 1)),
            )

        def up():
            return remote(
                ref.at[inner_rows(1)], ref.at[inner_rows(nh + 1)], ssh.at[at, 1], rsh.at[at, 1],
                (i, jnp.maximum(h - 1, 0)),
            )

        def start():
            @pl.when(h < n_ha - 1)
            def _():
                down().start()

            @pl.when(h > 0)
            def _():
                up().start()

        def wait_recv():
            @pl.when(h > 0)
            def _():
                down().wait_recv()

            @pl.when(h < n_ha - 1)
            def _():
                up().wait_recv()

        def wait_send():
            @pl.when(h < n_ha - 1)
            def _():
                down().wait_send()

            @pl.when(h > 0)
            def _():
                up().wait_send()

        return start, wait_recv, wait_send

    plane_rows, z_rows = wd // 4, wd // 16

    def plane_at(other):
        return pl.ds(pl.multiple_of(other * plane_rows, plane_rows), plane_rows)

    def z_at(other, base=0):
        return pl.ds(pl.multiple_of(base + other * z_rows, z_rows), z_rows)

    def w_copy(s, stage, k):
        sem = (s, stage * 4 + k)
        if stage == 0:
            src, dst, peer = parts[s].at[1 - core], rcs[s], core_peer()
        elif stage == 1:
            src = parts[s].at[core, plane_at(lax.rem(spot + k, 4))]
            dst, peer = rxys[s].at[k - 1], plane_peer(k)
        elif stage == 2:
            src = mids[s].at[z_at(lax.rem(z_of + k, 4))]
            dst, peer = rzs[s].at[k - 1], z_peer(k)
        elif stage == 3:
            src = dst = ress[s].at[core, z_at(z_of, spot * plane_rows)]
            peer = z_peer(k)
        elif stage == 4:
            src = dst = ress[s].at[core, plane_at(spot)]
            peer = plane_peer(k)
        else:
            src = dst = ress[s].at[core]
            peer = core_peer()
        return remote(src, dst, ssw.at[sem], rsw.at[sem], peer)

    def w_ks(stage):
        return (1,) if stage in (0, 5) else (1, 2, 3)

    def w_arrival(s, stage, k):
        sem = (s, stage * 4 + k)
        if stage == 3:
            dst = ress[s].at[core, z_at(lax.rem(z_of - k + 4, 4), spot * plane_rows)]
        elif stage == 4:
            dst = ress[s].at[core, plane_at(lax.rem(spot - k + 4, 4))]
        else:
            dst = ress[s].at[1 - core]
        return remote(dst, dst, ssw.at[sem], rsw.at[sem], core_peer())

    def w_start(s, stage):
        if d.inside:
            for k in w_ks(stage):
                w_copy(s, stage, k).start()

    def w_finish(s, stage, fix=None):
        if not d.inside:
            return
        for k in w_ks(stage):
            if stage <= 2:
                w_copy(s, stage, k).wait_recv()
            else:
                w_arrival(s, stage, k).wait_recv()
        part, inner = parts[s], mids[s]
        if stage == 0:
            rc = rcs[s]

            def add(t, carry):
                at = pl.ds(pl.multiple_of(t * 16, 16), 16)
                part[core, at, :] = (part[core, at, :].astype(F32) + rc[at, :].astype(F32)).astype(BF16)
                return carry

            lax.fori_loop(0, wd // 16, add, 0)
        elif stage == 1:
            buf = rxys[s]

            def add(t, carry):
                at = pl.ds(pl.multiple_of(t * 16, 16), 16)
                own = pl.ds(pl.multiple_of(spot * plane_rows + t * 16, 16), 16)
                total = part[core, own, :].astype(F32)
                for k in range(3):
                    total = total + buf[k, at, :].astype(F32)
                inner[at, :] = total.astype(BF16)
                return carry

            lax.fori_loop(0, plane_rows // 16, add, 0)
        elif stage == 2:
            buf = rzs[s]
            total = inner[z_at(z_of), :].astype(F32)
            for k in range(3):
                total = total + buf[k].astype(F32)
            if s >= d.sets:
                vres[...] = total
                return
            if fix is not None:
                total = fix(total)
            ress[s][core, z_at(z_of, spot * plane_rows), :] = total.astype(BF16)

    def w_step(s, stage, fix=None):
        w_finish(s, stage, fix)
        if stage < 5:
            w_start(s, stage + 1)

    def w_sent(s):
        if d.inside:
            for stage in range(6 if s < d.sets else 3):
                for k in w_ks(stage):
                    w_copy(s, stage, k).wait_send()

    def first(t, carry):
        sums, squares = carry
        x_copy(t).wait()
        ct_copy(t, 0).start()
        ct_copy(t, 1).start()
        at = line_rows(t)
        y = dot(xv[at, :], w1[...])
        y1[at, :] = y
        masked = y * mask_of(at, mid)
        return sums + fold(masked), squares + fold(masked * y)

    loads[0].wait()
    zeros = jnp.zeros((8, mid), F32)
    sums0 = lax.fori_loop(0, nh // 2, first, (zeros, zeros))
    pl.semaphore_wait(barrier, len(peers))
    count = Everywhere("cnt")
    count.at[...] = jnp.zeros((4, LANES), F32)
    count.at[0:1, :] = total_row(pixels)
    count.at[1:2, :] = total_row(live[...]) * (1.0 / n_ha)
    count.start()
    totals, squares = lax.fori_loop(nh // 2, nh, first, sums0)
    norm1 = Everywhere("s1")
    put(norm1.at, 0, total_row(totals))
    put(norm1.at, 2, total_row(squares))
    norm1.start()
    loads[1].wait()
    loads[2].wait()
    for r in range(d.radix):
        for ky in range(3):
            for e in range(4):
                if e <= 2:
                    left = w2[r, (ky * 3 + 2 - e) * gin : (ky * 3 + 3 - e) * gin, :]
                if e >= 1:
                    right = w2[r, (ky * 3 + 3 - e) * gin : (ky * 3 + 4 - e) * gin, :]
                if e == 0:
                    w2l[r, :, ky * wd : (ky + 1) * wd] = left
                elif e == 3:
                    w2r[r, :, ky * wd : (ky + 1) * wd] = right
                else:
                    lanes = slice((ky * 2 + e - 1) * wd, (ky * 2 + e) * wd)
                    w2x[r, 0:gin, lanes] = left
                    w2x[r, gin:, lanes] = right
    got = count.finish()
    total, images = got[0:1, :], got[1:2, :]
    got = norm1.finish()
    mean1, scale1 = moments(get(got, 0, mid), get(got, 2, mid), wide(total, mid))
    half_a1 = 0.5 * g1[...] * scale1
    half_b1 = 0.5 * c1[...] - half_a1 * mean1

    step1 = 4 * nb

    def act_first(t, carry):
        def cells(u, carry):
            at = block_rows(t, u, step1)
            value, _ = gate(y1[at, :] * half_a1 + half_b1)
            value = value * mask_of(at, mid)
            a1p[inner_rows(t + 1, nb + u * step1, step1), :] = value.astype(BF16)
            return carry + fold(value)

        return lax.fori_loop(0, line // step1, cells, carry)

    def edges(body, carry):
        return lax.fori_loop(0, 2, lambda t, c: body(t * (nh - 1), c), carry)

    totals = edges(act_first, jnp.zeros((8, mid), F32))
    halo1_start, halo1_recv, halo1_sent = halo(a1p, 0)
    halo1_start()
    totals = lax.fori_loop(1, nh - 1, act_first, totals)
    act_sum = Everywhere("act")
    act_sum.at[...] = jnp.zeros((4, LANES), F32)
    put(act_sum.at, 0, total_row(totals))
    act_sum.start()

    def taps(t, r, first=0, last=9):
        return jnp.concatenate(
            [
                a1p[inner_rows(t + tap // 3, (tap % 3) * nb), r * gin : (r + 1) * gin]
                for tap in range(first, last)
            ],
            axis=1,
        )

    def group(t, carry):
        at = line_rows(t)
        mask = mask_of(at, wd)
        done = []
        for r in range(d.radix):
            sums, squares = carry[r]
            y = dot(taps(t, r), w2[r])
            y2[at, r * wd : (r + 1) * wd] = y.astype(BF16)
            masked = y * mask
            done.append((sums + fold(masked), squares + fold(masked * y)))
        return tuple(done)

    zeros = jnp.zeros((8, wd), F32)
    sums2 = lax.fori_loop(1, nh - 1, group, ((zeros, zeros),) * d.radix)
    halo1_recv()
    sums2 = edges(group, sums2)
    norm2 = Everywhere("s2")
    put(norm2.at, 0, jnp.concatenate([total_row(s) for s, _ in sums2], axis=1))
    put(norm2.at, 4, jnp.concatenate([total_row(q) for _, q in sums2], axis=1))
    norm2.start()

    acc_c[...] = jnp.zeros((wd, cin), F32)
    vecs[...] = jnp.zeros((8, cin), F32)

    def norm_products(t, carry):
        at = line_rows(t)
        mask = mask_of(at, mid)
        hat = ((y1[at, :] - mean1) * scale1 * mask).astype(BF16)
        x = xv[at, :]
        acc_c[...] += dot_tn(hat, x)
        vecs[...] += dot_tn(mb[at, :], x)[0:8, :]
        return carry

    lax.fori_loop(0, nh, norm_products, 0)
    norm2_done = norm2.finish()
    for c in range(2):
        parts[5][c] = acc_c[:, c * half : (c + 1) * half].astype(BF16)
    w_start(5, 0)
    v0_sum = Everywhere("v0")
    put(v0_sum.at, 0, vecs[0:1, :])
    v0_sum.start()
    mean2, scale2 = moments(get(norm2_done, 0, wide2), get(norm2_done, 4, wide2), wide(total, wide2))
    half_a2 = 0.5 * g2[...] * scale2
    half_b2 = 0.5 * c2[...] - half_a2 * mean2

    lane_blocks = wd // LANES
    step2 = (nw // 2) * nb
    zero = jnp.zeros((nb, LANES), F32)
    for j in range(lane_blocks):
        own = slice(j * LANES, (j + 1) * LANES)

        def act_group(t, pool):
            at = pl.ds(pl.multiple_of(t * step2, step2), step2)
            mask = mb[at, :]
            full = mask.astype(F32)
            for r in range(d.radix):
                lanes = slice(r * wd + j * LANES, r * wd + (j + 1) * LANES)
                value, _ = gate(y2[at, lanes].astype(F32) * half_a2[:, lanes] + half_b2[:, lanes])
                value = value * full
                act2[at, lanes] = value.astype(BF16)
                pool = pool + fold_images(value, nb)
            return pool

        pools[:, own] = lax.fori_loop(0, rows // step2, act_group, zero)

    pool = pools[...]
    pf_src[:, 0 : d.inter] = add_thirds(dot(thirds(pool), wsq[...]))
    pf_src[:, d.inter :] = pixels
    pf_start, pf_finish = swap(pf_src, pf_buf, ssa.at[0], rsa.at[0], ha_peer, n_ha)
    pf_start()

    def slopes(block):
        lanes = slice(block * LANES, (block + 1) * LANES)
        ha2, hb2 = half_a2[:, lanes], half_b2[:, lanes]

        def body(t, carry):
            slopes, bends = carry
            at = pl.ds(pl.multiple_of(t * step2, step2), step2)
            y = y2[at, lanes].astype(F32)
            _, slope = gate(y * ha2 + hb2)
            slope = slope * mb[at, :].astype(F32)
            slope2[at, lanes] = slope.astype(BF16)
            return slopes + fold_images(slope, nb), bends + fold_images(slope * y, nb)

        q2[:, lanes], q4[:, lanes] = lax.fori_loop(0, rows // step2, body, (zero, zero))

    total_blocks = d.radix * lane_blocks
    for block in range(total_blocks // 4):
        slopes(block)
    w_step(5, 0)
    both = pf_finish()
    floor = jnp.maximum(both[:, d.inter :], 1.0)
    squeezed = both[:, 0 : d.inter] / floor
    live_now = live[...]
    fc_src[...] = jnp.zeros(fc_src.shape, F32)
    put(fc_src.at[0], 0, total_row(squeezed * live_now))
    put(fc_src.at[0], 1, total_row(squeezed * squeezed * live_now))
    fc_start, fc_finish = swap(fc_src.at[0], fc_buf.at[0], ssi.at[0], rsi.at[0], img_peer, n_img)
    fc_start()
    for block in range(total_blocks // 4, total_blocks):
        slopes(block)
    got = fc_finish()
    mean_s, scale_s = moments(got[0:1, :], got[1:2, :], images)
    centered = (squeezed - mean_s) * scale_s
    hidden, hidden_slope = gate(0.5 * (centered * gs[...] + cs[...]))
    logits = add_thirds(dot(thirds(hidden), wex[...])) + bex[...]
    gap = logits[:, 0:wd] - logits[:, wd:]
    att[:, 0:wd] = jax.nn.sigmoid(gap)
    att[:, wd:] = jax.nn.sigmoid(-gap)

    step3 = 2 * nb

    def mix(t, carry):
        def cells(u, carry):
            at = block_rows(t, u, step3)
            weight = jnp.concatenate([att[...]] * (step3 // nb), axis=0)
            both = act2[at, :].astype(F32) * weight
            mixed[at, :] = (both[:, 0:wd] + both[:, wd:]).astype(BF16)
            return carry

        lax.fori_loop(0, line // step3, cells, 0, unroll=7)
        gram, sums = carry
        cells = mixed[line_rows(t), :]
        mix_t[t] = jnp.transpose(cells)
        return gram + dot(mix_t[t], cells), sums + fold(cells.astype(F32))

    gram, totals = lax.fori_loop(0, nh, mix, (jnp.zeros((wd, wd), F32), jnp.zeros((8, wd), F32)))
    mix_sum = total_row(totals)
    gram_high, gram_low = split_bf16(gram)
    acc_g[0, :, 0:cin] = dot(gram_high, w3[...]) + dot(gram_low, w3[...])
    mix_parts = [jnp.broadcast_to(part, (16, wd)) for part in split_bf16(mix_sum)]
    sum_last = dot(jnp.concatenate(mix_parts, axis=0), w3[...])
    sum_last = sum_last[0:1, :] + sum_last[16:17, :]
    norm3 = Everywhere("s3")
    put(norm3.at, 0, sum_last)
    put(norm3.at, 8, total_row(acc_g[0, :, 0:cin] * w3[...].astype(F32)))
    norm3.start()

    def last_product(t, carry):
        at = line_rows(t)
        ost[at, :] = dot(mixed[at, :], w3[...]).astype(BF16)
        ct_copy(t, 0).wait()
        ct_copy(t, 1).wait()
        return carry

    lax.fori_loop(0, nh, last_product, 0)
    w_step(5, 1)
    got = norm3.finish()
    mean3, scale3 = moments(get(got, 0, cin), get(got, 8, cin), wide(total, cin))
    grow3 = g3[...] * scale3
    half_a3 = 0.5 * grow3
    half_b3 = 0.5 * c3[...] - half_a3 * mean3

    step4 = (nw // 4) * nb
    blocks4 = 2 * LANES

    def dn_copy(t, c):
        return pltpu.make_async_copy(
            ctv.at[half_rows(t, c)], dn_hbm.at[line_rows(t), pl.ds(c * half, half)], sem_dn.at[c, t]
        )

    def dn_back(t, c):
        return pltpu.make_async_copy(
            dn_hbm.at[line_rows(t), pl.ds(c * half, half)], ctv.at[half_rows(t, c)], sem_back.at[c, t]
        )

    def grad_of(t):
        return jnp.concatenate([ctv[half_rows(t, 0), :], ctv[half_rows(t, 1), :]], axis=1)

    acc_c[...] = jnp.zeros((wd, cin), F32)
    vecs[...] = jnp.zeros((8, cin), F32)

    def last(t, carry):
        for j in range(cin // blocks4):
            lanes = slice(j * blocks4, (j + 1) * blocks4)
            a3, b3 = half_a3[:, lanes], half_b3[:, lanes]

            def cells(u, carry):
                at = block_rows(t, u, step4)
                mask = wide(mb[at, :], blocks4)
                x = xv[at, lanes] * jnp.asarray(0.5, BF16)
                arg = ost[at, lanes].astype(F32) * a3 + (b3 + x.astype(F32))
                bend = jnp.tanh(arg)
                rise = 1.0 + bend
                value = arg * rise
                ost[at, lanes] = value.astype(BF16) * mask
                side = j * blocks4 // half
                there = pl.ds(pl.multiple_of(side * rows + t * line + u * step4, nb), step4)
                inner = slice(j * blocks4 - side * half, (j + 1) * blocks4 - side * half)
                push = ctv[there, inner] * (mask * jnp.asarray(0.5, BF16))
                grad = push.astype(F32) * (rise + value * (1.0 - bend))
                ctv[there, inner] = grad.astype(BF16)
                return carry + fold(grad)

            vecs[:, lanes] = lax.fori_loop(0, line // step4, cells, vecs[:, lanes])
        dn_copy(t, 0).start()
        dn_copy(t, 1).start()
        acc_c[...] += dot(mix_t[t], grad_of(t))
        return carry

    lax.fori_loop(0, nh, last, 0)
    sum_grad = total_row(vecs[...])
    back3 = Everywhere("b3")
    put(rows16, 0, sum_grad)
    put(rows16, 8, scale3 * (total_row(acc_c[...] * w3[...].astype(F32)) - mean3 * sum_grad))
    back3.at[...] = rows16[...].astype(BF16)
    back3.start()

    w3p[...] = (w3[...].astype(F32) * grow3).astype(BF16)

    def plain_back(t, carry):
        dm[line_rows(t), :] = dot_nt(grad_of(t), w3p[...])
        return carry

    lax.fori_loop(0, nh, plain_back, 0)
    w_finish(5, 2)
    got = back3.finish()
    bias3, gain3 = get(got, 0, cin), get(got, 8, cin)
    put(small.at[0], 0, bias3)
    put(small.at[0], 8, gain3)
    all_wide = wide(total, cin)
    slant3 = scale3 * gain3 / all_wide
    level3 = bias3 / all_wide - mean3 * slant3
    fix = (w3[...].astype(F32) * slant3).astype(BF16)
    level_high, level_low = split_bf16(level3)
    levels = [jnp.broadcast_to(part, (16, cin)) for part in (level_high, level_low)]
    stack = dot_nt(jnp.concatenate([fix, *levels], axis=0), w3p[...])
    fix = stack[0:wd, :].astype(BF16)
    shift = stack[wd : wd + 1, :] + stack[wd + 16 : wd + 17, :]

    def back_mix(t, carry):
        at = line_rows(t)
        dm[at, :] = dm[at, :] - dot(mixed[at, :], fix) - mask_of(at, wd) * shift
        return carry

    lax.fori_loop(0, nh, back_mix, 0)

    step5 = 4 * nb
    sums5 = []
    for j in range(lane_blocks):
        lanes = slice(j * LANES, (j + 1) * LANES)

        def image_sums(t, carry):
            at = pl.ds(pl.multiple_of(t * step5, step5), step5)
            grad = dm[at, lanes]
            done = []
            for r in range(d.radix):
                own = slice(r * wd + j * LANES, r * wd + (j + 1) * LANES)
                a, b, c = carry[r]
                a = a + fold_images(grad * act2[at, own].astype(F32), nb)
                part = grad * slope2[at, own].astype(F32)
                b = b + fold_images(part, nb)
                c = c + fold_images(part * y2[at, own].astype(F32), nb)
                done.append((a, b, c))
            return tuple(done)

        sums5.append(lax.fori_loop(0, rows // step5, image_sums, ((zero, zero, zero),) * d.radix))
    pick = lambda which: jnp.concatenate(
        [sums5[j][r][which] for r in range(d.radix) for j in range(lane_blocks)], axis=1
    )
    q1, q3 = pick(1), pick(2)

    def dn_out(t, carry):
        dn_copy(t, 0).wait()
        dn_copy(t, 1).wait()
        return carry

    lax.fori_loop(0, nh, dn_out, 0)
    clear(dyp)
    ga_src[...] = pick(0).astype(BF16)
    ga_start, ga_finish = swap(ga_src, ga_buf, ssa.at[1], rsa.at[1], ha_peer, n_ha)
    ga_start()

    mix_column = jnp.transpose(jnp.broadcast_to(mix_sum, (LANES, wd)))
    for j in range(cin // LANES):
        lanes = slice(j * LANES, (j + 1) * LANES)
        c = 0 if j * LANES < half else 1
        grad = grow3[:, lanes] * (
            acc_c[:, lanes] - mix_column * level3[:, lanes] - acc_g[0, :, lanes] * slant3[:, lanes]
        )
        parts[2][c, :, j * LANES - c * half : (j + 1) * LANES - c * half] = grad.astype(BF16)
    w_start(2, 0)

    grad_att = ga_finish()
    weight = att[...]
    weighed = weight * grad_att
    both = weighed[:, 0:wd] + weighed[:, wd:]
    grad_logits = weight * (grad_att - jnp.concatenate([both, both], axis=1))
    grad_fc = add_thirds(dot_nt(thirds(grad_logits), wex[...])) * hidden_slope
    put(fc_src.at[1], 0, total_row(grad_fc))
    put(fc_src.at[1], 1, total_row(grad_fc * centered))
    pooled = pool / wide(floor, wd)
    put(fc_src.at[1], 2, total_row(pooled))
    fc_start, fc_finish = swap(fc_src.at[1], fc_buf.at[1], ssi.at[1], rsi.at[1], img_peer, n_img)
    fc_start()
    w_step(2, 0)
    grad_excite = dot_tn(hidden, grad_logits, HIGH)
    grad_bex = total_row(grad_logits) * (1.0 / n_ha)
    got = fc_finish()
    bias_s, gain_s = got[0:1, :], got[1:2, :]
    put(small.at[0], 16, bias_s)
    put(small.at[0], 17, gain_s)
    grad_squeezed = (gs[...] * scale_s) * (
        grad_fc - live_now * (bias_s + centered * gain_s) / images
    )
    grad_pool = add_thirds(dot_nt(thirds(grad_squeezed), wsq[...])) / wide(floor, wd)
    pool2 = jnp.concatenate([grad_pool] * d.radix, axis=1)
    sum_grad = total_row(weight * q1 + pool2 * q2[...])
    sum_bend = total_row(weight * q3 + pool2 * q4[...])
    back2 = Everywhere("b2")
    put(back2.at, 0, sum_grad)
    put(back2.at, 4, scale2 * (sum_bend - mean2 * sum_grad))
    back2.start()
    level = get(got, 2, wd) / wide(images, wd)
    grad_squeeze = dot_tn(pooled - level, grad_squeezed, HIGH)
    grow2 = g2[...] * scale2
    att[...] = weight * grow2
    q2[...] = pool2 * grow2
    def first_slopes(t, carry):
        at = pl.ds(pl.multiple_of(t * step1, step1), step1)
        _, slope = gate(y1[at, :] * half_a1 + half_b1)
        mixed[at, :] = (slope * mask_of(at, mid)).astype(BF16)
        return carry

    lax.fori_loop(0, rows // step1, first_slopes, 0)

    parts[4][0] = jnp.concatenate([grad_excite[:, 0:wd], grad_excite[:, wd:]], axis=0).astype(
        BF16
    ) * jnp.asarray(1.0 / n_ha, BF16)
    parts[4][1, :, 0 : d.inter] = grad_squeeze.astype(BF16)
    parts[4][1, :, d.inter :] = jnp.zeros((wd, wd - d.inter), BF16)
    w_start(4, 0)
    w_step(2, 1)
    acc_g[...] = jnp.zeros((d.radix, wd, 9 * gin), F32)
    mean_act1 = get(act_sum.finish(), 0, mid) / (wide(images, mid) * float(nh * n_ha * nw))
    w_step(4, 0)
    got = back2.finish()
    bias2, gain2 = get(got, 0, wide2), get(got, 4, wide2)
    put(small.at[0], 20, bias2)
    put(small.at[0], 24, gain2)
    slant2 = grow2 * scale2 * gain2 / wide(total, wide2)
    level2 = grow2 * bias2 / wide(total, wide2) - mean2 * slant2

    step6 = 2 * nb

    def back_group(t, carry):
        def cells(u, carry):
            at = block_rows(t, u, step6)
            to = inner_rows(t + 1, nb + u * step6, step6)
            again = step6 // nb
            grad = dm[at, :]
            mask = mask_of(at, wd)
            sums = []
            for r in range(d.radix):
                own = slice(r * wd, (r + 1) * wd)
                grow = jnp.concatenate([att[:, own]] * again, axis=0)
                lift = jnp.concatenate([q2[:, own]] * again, axis=0)
                push = (grow * grad + lift) * slope2[at, own].astype(F32)
                pull = mask * (level2[:, own] + slant2[:, own] * y2[at, own].astype(F32))
                dyp[to, own] = (push - pull).astype(BF16)
                sums.append(carry[r] + fold(push - pull))
            return tuple(sums)

        return lax.fori_loop(0, line // step6, cells, carry, unroll=7)

    zeros = jnp.zeros((8, wd), F32)
    sums2 = edges(back_group, (zeros,) * d.radix)
    halo2_start, halo2_recv, halo2_sent = halo(dyp, 1)
    halo2_start()
    sums2 = lax.fori_loop(1, nh - 1, back_group, sums2)
    sum_dy2 = [total_row(s) for s in sums2]
    misc = Everywhere("misc")
    put(misc.at, 0, jnp.concatenate(sum_dy2, axis=1))
    put(misc.at, 4, grad_bex)
    misc.start()
    w_step(2, 2)
    w_step(4, 1)

    def weights_group(t, carry):
        for r in range(d.radix):
            grad = jnp.transpose(dyp[inner_rows(t + 1), r * wd : (r + 1) * wd])
            acc_g[r] += dot(grad, taps(t, r))
        return carry

    lax.fori_loop(0, nh, weights_group, 0)

    def send_group(s, first, last):
        lanes = (last - first) * gin
        for r in range(d.radix):
            base = wide(mean_act1[:, r * gin : (r + 1) * gin], lanes)
            column = jnp.transpose(jnp.broadcast_to(sum_dy2[r], (LANES, wd)))
            grad = acc_g[r, :, first * gin : last * gin] - wide(column, lanes) * base
            parts[s][r, :, 0:lanes] = grad.astype(BF16)
        w_start(s, 0)

    send_group(1, 0, d.split)
    send_group(3, d.split, 9)
    w_step(2, 3)
    w_step(4, 2)

    pairs = nw // 2

    def back_taps(t, r, which):
        cells = []
        for ky in range(3):
            for e in which:
                block = dyp[inner_rows(t + 2 - ky, e * nb), r * wd : (r + 1) * wd]
                block = block.reshape(pairs, 2 * nb, wd)[:, 0:nb, :].reshape(pairs * nb, wd)
                cells.append(block)
        return jnp.concatenate(cells, axis=1)

    def transposed(t, carry):
        sums, bends = carry
        at = line_rows(t)
        done = []
        for r in range(d.radix):
            both = dot_nt(back_taps(t, r, (1, 2)), w2x[r])
            left = both[:, 0:gin] + dot_nt(back_taps(t, r, (0,)), w2l[r])
            right = both[:, gin:] + dot_nt(back_taps(t, r, (3,)), w2r[r])
            both = jnp.concatenate(
                [left.reshape(pairs, nb, gin), right.reshape(pairs, nb, gin)], axis=1
            )
            done.append(both.reshape(line, gin))
        dm[at, :] = jnp.concatenate(done, axis=1)

        def cells(u, carry):
            sums, bends = carry
            at = block_rows(t, u, step1)
            grad = dm[at, :] * mixed[at, :].astype(F32)
            dm[at, :] = grad
            mixed[at, :] = grad.astype(BF16)
            return sums + fold(grad), bends + fold(grad * y1[at, :])

        return lax.fori_loop(0, line // step1, cells, (sums, bends))

    zeros = jnp.zeros((8, mid), F32)
    middle = 1 + (nh - 2) // 3
    sums1 = lax.fori_loop(1, middle, transposed, (zeros, zeros))
    w_step(1, 0)
    w_step(3, 0)
    sums1 = lax.fori_loop(middle, nh - 1, transposed, sums1)
    w_step(4, 3)
    halo2_recv()
    sums1 = edges(transposed, sums1)
    sum_grad = total_row(sums1[0])
    back1 = Everywhere("b1")
    put(back1.at, 0, sum_grad)
    put(back1.at, 2, scale1 * (total_row(sums1[1]) - mean1 * sum_grad))
    back1.start()
    halo2_sent()

    def fetch_back(t, carry):
        dn_back(t, 0).start()
        dn_back(t, 1).start()
        return carry

    lax.fori_loop(0, nh, fetch_back, 0)

    acc_c[...] = jnp.zeros((wd, cin), F32)

    def first_weights(t, carry):
        at = line_rows(t)
        acc_c[...] += dot_tn(mixed[at, :], xv[at, :])
        return carry

    lax.fori_loop(0, nh, first_weights, 0)
    if d.inside:
        for c in range(2):
            parts[0][c] = acc_c[:, c * half : (c + 1) * half].astype(BF16)
    w_start(0, 0)
    w_step(1, 1)
    w_step(0, 0)
    w_step(3, 1)
    got = back1.finish()
    bias1, gain1 = get(got, 0, mid), get(got, 2, mid)
    grow1 = g1[...] * scale1
    bias_all, gain_all = bias1 / wide(total, mid), gain1 / wide(total, mid)
    slant1 = grow1 * scale1 * gain_all
    level1 = grow1 * bias_all - mean1 * slant1
    w_step(2, 4)
    w_step(4, 4)

    def back_first(t, carry):
        def cells(u, carry):
            at = block_rows(t, u, step1)
            pull = mask_of(at, mid) * (level1 + slant1 * y1[at, :])
            mixed[at, :] = (grow1 * dm[at, :] - pull).astype(BF16)
            return carry

        lax.fori_loop(0, line // step1, cells, 0)
        return carry

    lax.fori_loop(0, nh, back_first, 0)
    put(small.at[0], 32, bias1)
    put(small.at[0], 34, gain1)
    put(small.at[0], 36, mean_act1)
    small[0, 18:20, :] = jnp.zeros((2, LANES), F32)
    small[0, 38:40, :] = jnp.zeros((2, LANES), F32)
    small[0, 44:48, :] = jnp.zeros((4, LANES), F32)
    got = misc.finish()
    put(small.at[0], 28, get(got, 4, wide2))
    put(small.at[0], 40, get(got, 0, wide2))
    got = v0_sum.finish()
    for c in range(2):
        v0[c] = jnp.broadcast_to(get(got, 0, cin)[:, c * half : (c + 1) * half], (8, half))
    for j, vector in enumerate((grow1, bias_all, gain_all)):
        cols[j] = jnp.transpose(jnp.broadcast_to(vector, (LANES, mid)))

    def norm_terms(total, at, taken, flat):
        lanes = total.shape[1]
        grow, level, slant = (wide(cols[j, at, :], lanes) for j in range(3))
        return grow * (total - level * flat - slant * taken)

    def fix_first(total):
        return norm_terms(total, z_at(z_of, spot * plane_rows), vres[...], v0[core, 0:1, :])

    def grad_inputs(t, carry):
        at = line_rows(t)
        for c in range(2):
            lanes = slice(c * half, (c + 1) * half)
            dn_back(t, c).wait()
            grad = ctv[half_rows(t, c), :].astype(F32) + dot_nt(mixed[at, :], w1[lanes, :])
            xv[at, lanes] = grad.astype(BF16)
        return carry

    w_step(1, 2)
    lax.fori_loop(0, nh // 2, grad_inputs, 0)
    w_step(3, 2)
    w_step(0, 1)
    w_step(1, 3)
    w_step(3, 3)
    w_step(0, 2, fix_first)
    lax.fori_loop(nh // 2, nh, grad_inputs, 0)
    w_step(1, 4)
    w_step(0, 3)
    w_step(3, 4)
    w_step(0, 4)
    for s in (2, 4, 1, 3, 0):
        w_step(s, 5)
    if not d.inside:
        whole = slice(0, wd)
        for c in range(2):
            lanes = slice(c * half, (c + 1) * half)
            local = wide(cols[0, whole, :], half) * (
                acc_c[:, lanes]
                - wide(cols[1, whole, :], half) * get(v0_sum.at[...], 0, cin)[:, lanes]
                - wide(cols[2, whole, :], half) * parts[5][c].astype(F32)
            )
            parts[0][c] = local.astype(BF16)

    for s in range(d.sets + 1):
        w_sent(s)
    halo1_sent()
    if not d.inside:
        for s in range(d.sets):
            ress[s][...] = parts[s][...]


def call_block(d, args):
    f32, bf16 = F32, BF16
    cin, wd, mid, rows, nb, nh = d.cin, d.width, d.mid, d.rows, d.nb, d.nh
    vmem, dma = pltpu.VMEM, pltpu.SemaphoreType.DMA
    halves = [(2, wd, lanes) for lanes in d.half]
    shape = jax.ShapeDtypeStruct
    outs = [
        shape((rows, cin), bf16),
        vmem((rows, cin), bf16),
        vmem((rows, cin), bf16),
        *[vmem(s, bf16) for s in halves[: d.sets]],
        vmem((1, 48, LANES), f32),
    ]
    anywhere = pl.BlockSpec(memory_space=pl.ANY)
    inside = pl.BlockSpec(memory_space=pltpu.VMEM)
    plane, zed = wd // 4, wd // 16

    def sums_of(name, count):
        kind = bf16 if name in d.narrow else f32
        if not d.inside:
            return dict(
                src=vmem((count, LANES), kind),
                mid=vmem((count, LANES), f32),
                buf_ha=vmem((d.n_ha, count, LANES), kind),
                buf_img=vmem((d.n_img, count, LANES), f32),
                send_ha=dma((d.n_ha,)), recv_ha=dma((d.n_ha,)),
                send=dma((d.n_img,)), recv=dma((d.n_img,)),
            )
        if name in d.paired:
            return dict(
                src=vmem((count, LANES), kind),
                mid=vmem((count, LANES), f32),
                other=vmem((count, LANES), f32),
                buf=vmem((16, count, LANES), f32),
                send=dma((16,)), recv=dma((16,)),
            )
        return dict(
            src=vmem((count, LANES), kind),
            buf=vmem((32, count, LANES), kind),
            send=dma((32,)), recv=dma((32,)),
        )

    scratch = [
        vmem((cin, mid), bf16),
        vmem((d.radix, 9 * d.gin, wd), bf16),
        vmem((wd, cin), bf16),
        vmem((rows, LANES), bf16),
        vmem((nb, LANES), f32),
        vmem((max(2 * rows, (nh + 2) * d.padded), cin // 2), bf16),
        vmem((rows, mid), f32),
        vmem(((nh + 2) * d.padded, mid), bf16),
        vmem((rows, d.wide), bf16),
        vmem((rows, d.wide), bf16),
        vmem((rows, d.wide), bf16),
        vmem((rows, wd), bf16),
        vmem((rows, wd), f32),
        vmem((wd, cin), f32),
        vmem((d.radix, wd, 9 * d.gin), f32),
        vmem((wd, cin), bf16),
        vmem((d.radix, 2 * d.gin, 6 * wd), bf16),
        vmem((d.radix, d.gin, 3 * wd), bf16),
        vmem((d.radix, d.gin, 3 * wd), bf16),
        vmem((nh, wd, d.line), bf16),
        vmem((16, LANES), f32),
        vmem((nb, d.wide), f32),
        vmem((nb, d.wide), f32),
        vmem((nb, d.wide), f32),
        vmem((8, cin), f32),
        vmem((nb, wd), f32),
        vmem((2, 8, cin // 2), f32),
        vmem((3, mid, LANES), f32),
        [vmem(s, bf16) for s in halves],
        [vmem((wd, lanes), bf16) for lanes in d.half],
        [vmem((3, plane, lanes), bf16) for lanes in d.half],
        [vmem((3, zed, lanes), bf16) for lanes in d.half],
        [vmem((plane, lanes), bf16) for lanes in d.half],
        vmem((zed, d.half[0]), f32),
        {name: sums_of(name, count) for name, count in d.sums.items() if name not in d.shared},
        vmem((nb, d.wide), bf16),
        vmem((d.n_ha, nb, d.wide), bf16),
        vmem((nb, 2 * LANES), f32),
        vmem((d.n_ha, nb, 2 * LANES), f32),
        vmem((2, 4, LANES), f32),
        vmem((2, d.n_img, 4, LANES), f32),
        dma((3,)),
        dma((nh,)),
        dma((2, nh)),
        dma((2, nh)),
        dma((2, nh)),
        dma((2, d.n_ha)),
        dma((2, d.n_ha)),
        dma((2, d.n_img)),
        dma((2, d.n_img)),
        dma((2, 2)),
        dma((2, 2)),
        dma((6, 24)),
        dma((6, 24)),
    ]
    return pl.pallas_call(
        functools.partial(block_kernel, d),
        out_shape=outs,
        in_specs=[anywhere, anywhere, inside, pl.BlockSpec(memory_space=pltpu.SMEM)]
        + [anywhere, inside, inside, anywhere] + [inside] * 7 + [anywhere, inside, inside],
        out_specs=[anywhere] + [inside] * 8,
        scratch_shapes=scratch,
        name="block",
        compiler_params=pltpu.CompilerParams(
            collective_id=0, has_side_effects=True, vmem_limit_bytes=47 << 20
        ),
    )(*args)


def finish_kernel(
    d, out_in, gin_in, wg0, wg1, wg2, wg3, wg4, small,
    out, gin_hbm, gw1_hbm, gg1, gb1, gw2_hbm, gg2, gb2, gwsq, ggs, gbs, gwex, gbex, gw3_hbm, gg3, gb3,
    gw1, gw2, gw3, sem_out, sem_gw,
):
    wd = d.width
    parts = 4
    copies = [
        pltpu.make_async_copy(src.at[at], dst.at[at], sem_out.at[which, t])
        for which, (src, dst) in enumerate(((out_in, out), (gin_in, gin_hbm)))
        for t in range(parts)
        for at in (pl.ds(t * (d.rows // parts), d.rows // parts),)
    ]
    for copy in copies:
        copy.start()
    stores = [
        pltpu.make_async_copy(src, dst, sem_gw.at[j])
        for j, (src, dst) in enumerate(((gw1, gw1_hbm), (gw3, gw3_hbm), (gw2, gw2_hbm)))
    ]

    def weights(step):
        half = d.cin // 2
        if step < 2:
            gw1[step * half : (step + 1) * half, :] = jnp.transpose(wg0[step]).astype(F32)
            gw3[:, step * half : (step + 1) * half] = wg2[step].astype(F32)
        elif step < 4:
            r = step - 2
            rows = small[0]
            mean = get(rows, 36, d.mid)[:, r * d.gin : (r + 1) * d.gin]
            taken = get(rows, 40, d.wide)[:, r * wd : (r + 1) * wd]
            mean = jnp.transpose(jnp.broadcast_to(mean, (LANES, d.gin)))
            back = wide(mean, wd) * taken
            for tap in range(9):
                held, first = (wg1, 0) if tap < d.split else (wg3, d.split)
                cells = held[r, :, (tap - first) * d.gin : (tap - first + 1) * d.gin]
                gw2[r, tap] = jnp.transpose(cells).astype(F32) + back
        elif step == 4:
            cells = wg4[0].astype(F32)
            gwex[:, 0:wd] = cells[0 : d.inter, :]
            gwex[:, wd:] = cells[d.inter :, :]
            gwsq[...] = wg4[1, :, 0 : d.inter].astype(F32)
            rows = small[0]
            gb3[...] = get(rows, 0, d.cin)
            gg3[...] = get(rows, 8, d.cin)
            gbs[...] = rows[16:17, :]
            ggs[...] = rows[17:18, :]
            gb2[...] = get(rows, 20, d.wide)
            gg2[...] = get(rows, 24, d.wide)
            gbex[...] = get(rows, 28, d.wide)
            gb1[...] = get(rows, 32, d.mid)
            gg1[...] = get(rows, 34, d.mid)

    for t in range(5):
        weights(t)
        if t == 1:
            stores[0].start()
            stores[1].start()
        elif t == 3:
            stores[2].start()
    for copy in stores + copies:
        copy.wait()


def call_finish(d, *args):
    shape = jax.ShapeDtypeStruct
    cin, wd, mid = d.cin, d.width, d.mid
    vmem, dma = pltpu.VMEM, pltpu.SemaphoreType.DMA
    small_dims = [
        (cin, mid), (1, mid), (1, mid), (d.radix, 9, d.gin, wd), (1, d.wide), (1, d.wide), (wd, d.inter),
        (1, d.inter), (1, d.inter), (d.inter, d.wide), (1, d.wide), (wd, cin), (1, cin), (1, cin),
    ]
    anywhere = pl.BlockSpec(memory_space=pl.ANY)
    inside = pl.BlockSpec(memory_space=pltpu.VMEM)
    return pl.pallas_call(
        functools.partial(finish_kernel, d),
        out_shape=[shape((d.rows, cin), BF16), shape((d.rows, cin), BF16)]
        + [shape(s, F32) for s in small_dims],
        in_specs=[inside] * 8,
        out_specs=[anywhere] * 3 + [inside] * 2 + [anywhere] + [inside] * 7 + [anywhere] + [inside] * 2,
        scratch_shapes=[
            vmem((cin, mid), F32), vmem((d.radix, 9, d.gin, wd), F32), vmem((wd, cin), F32),
            dma((2, 4)), dma((3,)),
        ],
        name="finish",
        compiler_params=pltpu.CompilerParams(vmem_limit_bytes=16 << 20),
    )(*[pltpu.with_memory_space_constraint(arg, pltpu.VMEM) for arg in args])


def on_device(
    inputs, image_count, pixel_mask, w_first, gain_first, bias_first, w_group, gain_group, bias_group,
    w_squeeze, gain_squeeze, bias_squeeze, w_excite, bias_excite, w_last, gain_last, bias_last, cotangent,
):
    n_img, n_ha = lax.axis_size("img"), lax.axis_size("ha")
    d = Dims(n_img, n_ha, inputs.shape, w_group.shape, w_squeeze.shape)
    nb, nh, nw, cin = inputs.shape

    def by_rows(cells):
        return jnp.transpose(cells, (1, 2, 0, 3)).reshape(d.rows, cin)

    def by_image(cells):
        return jnp.transpose(cells.reshape(nh, nw, nb, cin), (2, 0, 1, 3))

    row = lambda v: v.reshape(1, -1)
    args = (
        by_rows(inputs), by_rows(cotangent), jnp.transpose(pixel_mask, (1, 0, 2)), image_count,
        w_first, row(gain_first), row(bias_first),
        w_group.reshape(d.radix, 9 * d.gin, d.width), row(gain_group), row(bias_group),
        w_squeeze, row(gain_squeeze), row(bias_squeeze), w_excite, row(bias_excite),
        w_last, row(gain_last), row(bias_last),
    )
    _, out, gin, *sets, small = call_block(d, args)
    if not d.inside:
        sets = lax.psum(sets, ("img", "ha"))
    done = call_finish(d, out, gin, *sets, small)
    (out, gin, gw1, gg1, gb1, gw2, gg2, gb2, gwsq, ggs, gbs, gwex, gbex, gw3, gg3, gb3) = done
    flat = lambda v: v.reshape(-1)
    return (
        by_image(out), by_image(gin), gw1, flat(gg1), flat(gb1), gw2.reshape(w_group.shape), flat(gg2), flat(gb2),
        gwsq, flat(ggs), flat(gbs), gwex, flat(gbex), gw3, flat(gg3), flat(gb3),
    )


def solution(mesh):
    cells = P("img", "ha", None, None)
    placed = (cells, P("img"), P("img", "ha", None)) + (P(),) * 14 + (cells,)
    return jax.shard_map(
        on_device,
        mesh=mesh,
        in_specs=placed,
        out_specs=(cells, cells) + (P(),) * 14,
        check_vma=False,
    )
```

```python
import functools

import jax
import jax.numpy as jnp
from jax import lax
from jax.experimental import pallas as pl
from jax.experimental.pallas import tpu as pltpu
from jax.sharding import PartitionSpec as P

EPS = 1e-05
F32 = jnp.float32
BF16 = jnp.bfloat16
HIGH = lax.Precision.HIGHEST
MESH = pl.DeviceIdType.MESH
LANES = 128


def dot(a, b, precision=None):
    return jnp.dot(a, b, preferred_element_type=F32, precision=precision)


def dot_nt(a, b, precision=None):
    return lax.dot_general(
        a, b, (((1,), (1,)), ((), ())), preferred_element_type=F32, precision=precision
    )


def dot_tn(a, b, precision=None):
    return lax.dot_general(
        a, b, (((0,), (0,)), ((), ())), preferred_element_type=F32, precision=precision
    )


def wide(cell, lanes):
    return jnp.concatenate([cell] * (lanes // LANES), axis=1)


def fold(cells):
    rows, lanes = cells.shape
    return jnp.sum(cells.reshape(rows // 8, 8, lanes), axis=0)


def fold_images(cells, images):
    rows, lanes = cells.shape
    return jnp.sum(cells.reshape(rows // images, images, lanes), axis=0)


def total_row(cells):
    return jnp.sum(cells, axis=0, keepdims=True)


def put(ref, row, vector):
    for j in range(vector.shape[1] // LANES):
        ref[row + j : row + j + 1, :] = vector[:, j * LANES : (j + 1) * LANES]


def get(cells, row, lanes):
    return jnp.concatenate(
        [cells[row + j : row + j + 1, :] for j in range(lanes // LANES)], axis=1
    )


def moments(sums, squares, total):
    mean = sums / total
    spread = squares / total - mean * mean
    return mean, lax.rsqrt(spread + EPS)


def gate(half):
    bend = jnp.tanh(half)
    rise = 1.0 + bend
    value = half * rise
    return value, 0.5 * (rise + value * (1.0 - bend))


def split_bf16(cells):
    high = cells.astype(BF16)
    return high, (cells - high.astype(F32)).astype(BF16)


def thirds(cells):
    high = cells.astype(BF16)
    rest = cells - high.astype(F32)
    middle = rest.astype(BF16)
    return jnp.concatenate([high, middle, (rest - middle.astype(F32)).astype(BF16)], axis=0)


def add_thirds(cells):
    rows = cells.shape[0] // 3
    return cells[0:rows] + cells[rows : 2 * rows] + cells[2 * rows :]


class Dims:
    def __init__(self, n_img, n_ha, inputs, w_group, w_squeeze):
        self.n_img, self.n_ha = n_img, n_ha
        self.nb, self.nh, self.nw, self.cin = inputs
        self.radix, _, _, self.gin, self.width = w_group
        self.mid = self.radix * self.gin
        self.wide = self.radix * self.width
        self.inter = w_squeeze[1]
        self.line = self.nw * self.nb
        self.rows = self.nh * self.line
        self.padded = (self.nw + 2) * self.nb
        self.split = 5
        self.half = (self.cin // 2, 5 * self.gin, self.cin // 2, 4 * self.gin, self.width, self.cin // 2)
        self.sets = 5
        self.inside = n_img == 8 and n_ha == 4
        self.sums = dict(cnt=4, s1=4, s2=8, act=4, v0=8, s3=16, b3=16, b2=8, misc=8, b1=4)
        self.paired = ("s3",)
        self.narrow = ("b3",)
        self.shared = dict(b1="s1", b2="s2")


def block_kernel(
    d,
    x_hbm, ct_hbm, mask_in, count_in, w1_hbm, g1, c1, w2_hbm, g2, c2, wsq, gs, cs, wex, bex, w3_hbm, g3, c3,
    dn_hbm, ost, xv, wg0, wg1, wg2, wg3, wg4, small,
    w1, w2, w3, mb, live, ctv, y1, a1p, y2, act2, slope2, mixed, dm, acc_c, acc_g, w3p, w2x, w2l, w2r,
    mix_t, rows16, att, q2, q4, vecs, vecs2, pools, v0, cols,
    parts, rcs, rxys, rzs, mids, vres, sums, ga_src, ga_buf, pf_src, pf_buf, fc_src, fc_buf,
    sem_w, sem_x, sem_ct, sem_dn, sem_back, ssa, rsa, ssi, rsi, ssh, rsh, ssw, rsw,
):
    n_img, n_ha = d.n_img, d.n_ha
    nb, nh, nw = d.nb, d.nh, d.nw
    cin, mid, wd, wide2, line, rows = d.cin, d.mid, d.width, d.wide, d.line, d.rows
    gin, padded = d.gin, d.padded
    dyp = ctv
    ress = (wg0, wg1, wg2, wg3, wg4)
    half = cin // 2
    i = lax.axis_index("img")
    h = lax.axis_index("ha")

    def ha_peer(k):
        return (i, lax.rem(h + k, n_ha))

    def img_peer(k):
        return (lax.rem(i + k, n_img), h)

    z_of, x_of, y_of, core = i // 2, lax.rem(i, 2), h // 2, lax.rem(h, 2)
    spot = x_of * 2 + y_of

    def core_peer():
        return (i, y_of * 2 + (1 - core))

    def plane_peer(k):
        other = lax.rem(spot + k, 4)
        return (z_of * 2 + other // 2, lax.rem(other, 2) * 2 + core)

    def z_peer(k):
        return (lax.rem(z_of + k, 4) * 2 + x_of, h)

    def any_peer(k):
        return (lax.rem(i + k // 4, 8), lax.rem(h + k % 4, 4))

    def chip_peer(k):
        return (lax.rem(i + k // 2, 8), lax.rem(y_of + k % 2, 2) * 2 + core)

    def remote(src, dst, send, recv, peer):
        return pltpu.make_async_remote_copy(
            src_ref=src, dst_ref=dst, send_sem=send, recv_sem=recv, device_id=peer, device_id_type=MESH
        )

    def line_rows(t):
        return pl.ds(pl.multiple_of(t * line, line), line)

    def block_rows(t, u, step):
        return pl.ds(pl.multiple_of(t * line + u * step, nb), step)

    def x_copy(t):
        return pltpu.make_async_copy(x_hbm.at[line_rows(t)], xv.at[line_rows(t)], sem_x.at[t])

    def half_rows(t, c):
        return pl.ds(pl.multiple_of(c * rows + t * line, nb), line)

    def ct_copy(t, c):
        return pltpu.make_async_copy(
            ct_hbm.at[line_rows(t), pl.ds(c * half, half)], ctv.at[half_rows(t, c)], sem_ct.at[c, t]
        )

    def start_inputs(t, carry):
        x_copy(t).start()
        return carry

    loads = [
        pltpu.make_async_copy(src, dst, sem_w.at[j])
        for j, (src, dst) in enumerate(((w1_hbm, w1), (w2_hbm, w2), (w3_hbm, w3)))
    ]
    loads[0].start()
    lax.fori_loop(0, nh, start_inputs, 0)
    loads[1].start()
    loads[2].start()

    barrier = pltpu.get_barrier_semaphore()
    if d.inside:
        peers = [any_peer(k) for k in range(1, 32)]
    else:
        peers = [ha_peer(k) for k in range(1, n_ha)] + [img_peer(k) for k in range(1, n_img)]
    for peer in peers:
        pl.semaphore_signal(barrier, inc=1, device_id=peer, device_id_type=MESH)

    slots = lax.broadcasted_iota(jnp.int32, (nb, LANES), 0)
    live[...] = (slots < count_in[0]).astype(F32)

    def spread(t, carry):
        cells = mask_in[t].astype(F32)
        alive = live[...]
        for w in range(nw):
            cell = jnp.broadcast_to(cells[:, w : w + 1], (nb, LANES)) * alive
            mb[block_rows(t, w, nb), :] = cell.astype(BF16)
            carry = carry + cell
        return carry

    pixels = lax.fori_loop(0, nh, spread, jnp.zeros((nb, LANES), F32))

    def mask_of(at, lanes):
        return wide(mb[at, :].astype(F32), lanes)

    def inner_rows(t, at=nb, count=line):
        return pl.ds(pl.multiple_of(t * padded + at, nb), count)

    def clear(ref):
        zero = jnp.zeros((nb, ref.shape[1]), BF16)

        def body(t, carry):
            ref[inner_rows(t, 0, nb), :] = zero
            ref[inner_rows(t, nb + line, nb), :] = zero
            return carry

        lax.fori_loop(0, nh + 2, body, 0)

        def edge(t, carry):
            ref[inner_rows(0, t * nb, nb), :] = zero
            ref[inner_rows(nh + 1, t * nb, nb), :] = zero
            return carry

        lax.fori_loop(0, nw + 2, edge, 0)

    clear(a1p)

    def swap(src, buf, send, recv, peer, n):
        def copy(k):
            return remote(src, buf.at[k], send.at[k], recv.at[k], peer(k))

        def each(act, carry):
            if n > 32:
                return lax.fori_loop(1, n, act, carry)
            for k in range(1, n):
                carry = act(k, carry)
            return carry

        def begin(k, carry):
            copy(k).start()
            return carry

        def sent(k, carry):
            copy(k).wait_send()
            return carry

        def take(k, carry):
            copy(k).wait_recv()
            return carry + buf[k].astype(F32)

        def finish():
            total = each(take, src[...].astype(F32))
            each(sent, 0)
            return total

        return (lambda: each(begin, 0)), finish

    class Everywhere:
        def __init__(self, name):
            refs = sums[d.shared.get(name, name)]
            self.at = refs["src"]
            self.refs = refs
            if not d.inside:
                return
            send, recv = refs["send"], refs["recv"]
            if name in d.paired:
                self.pair = remote(self.at, refs["other"], send.at[0], recv.at[0], core_peer())
                self.start_far, self.finish_far = swap(refs["mid"], refs["buf"], send, recv, chip_peer, 16)
            else:
                self.pair = None
                self.start_far, self.finish_far = swap(self.at, refs["buf"], send, recv, any_peer, 32)

        def start(self):
            if d.inside:
                if self.pair is not None:
                    self.pair.start()
                    self.pair.wait_recv()
                    self.refs["mid"][...] = self.at[...] + self.refs["other"][...]
                self.start_far()

        def finish(self):
            if d.inside:
                total = self.finish_far()
                if self.pair is not None:
                    self.pair.wait_send()
                return total
            refs = self.refs
            start, finish = swap(self.at, refs["buf_ha"], refs["send_ha"], refs["recv_ha"], ha_peer, n_ha)
            start()
            refs["mid"][...] = finish()
            start, finish = swap(refs["mid"], refs["buf_img"], refs["send"], refs["recv"], img_peer, n_img)
            start()
            return finish()

    def halo(ref, at):
        def down():
            return remote(
                ref.at[inner_rows(nh)], ref.at[inner_rows(0)], ssh.at[at, 0], rsh.at[at, 0],
                (i, jnp.minimum(h + 1, n_ha - 1)),
            )

        def up():
            return remote(
                ref.at[inner_rows(1)], ref.at[inner_rows(nh + 1)], ssh.at[at, 1], rsh.at[at, 1],
                (i, jnp.maximum(h - 1, 0)),
            )

        def start():
            @pl.when(h < n_ha - 1)
            def _():
                down().start()

            @pl.when(h > 0)
            def _():
                up().start()

        def wait_recv():
            @pl.when(h > 0)
            def _():
                down().wait_recv()

            @pl.when(h < n_ha - 1)
            def _():
                up().wait_recv()

        def wait_send():
            @pl.when(h < n_ha - 1)
            def _():
                down().wait_send()

            @pl.when(h > 0)
            def _():
                up().wait_send()

        return start, wait_recv, wait_send

    plane_rows, z_rows = wd // 4, wd // 16

    def plane_at(other):
        return pl.ds(pl.multiple_of(other * plane_rows, plane_rows), plane_rows)

    def z_at(other, base=0):
        return pl.ds(pl.multiple_of(base + other * z_rows, z_rows), z_rows)

    def w_copy(s, stage, k):
        sem = (s, stage * 4 + k)
        if stage == 0:
            src, dst, peer = parts[s].at[1 - core], rcs[s], core_peer()
        elif stage == 1:
            src = parts[s].at[core, plane_at(lax.rem(spot + k, 4))]
            dst, peer = rxys[s].at[k - 1], plane_peer(k)
        elif stage == 2:
            src = mids[s].at[z_at(lax.rem(z_of + k, 4))]
            dst, peer = rzs[s].at[k - 1], z_peer(k)
        elif stage == 3:
            src = dst = ress[s].at[core, z_at(z_of, spot * plane_rows)]
            peer = z_peer(k)
        elif stage == 4:
            src = dst = ress[s].at[core, plane_at(spot)]
            peer = plane_peer(k)
        else:
            src = dst = ress[s].at[core]
            peer = core_peer()
        return remote(src, dst, ssw.at[sem], rsw.at[sem], peer)

    def w_ks(stage):
        return (1,) if stage in (0, 5) else (1, 2, 3)

    def w_arrival(s, stage, k):
        sem = (s, stage * 4 + k)
        if stage == 3:
            dst = ress[s].at[core, z_at(lax.rem(z_of - k + 4, 4), spot * plane_rows)]
        elif stage == 4:
            dst = ress[s].at[core, plane_at(lax.rem(spot - k + 4, 4))]
        else:
            dst = ress[s].at[1 - core]
        return remote(dst, dst, ssw.at[sem], rsw.at[sem], core_peer())

    def w_start(s, stage):
        if d.inside:
            for k in w_ks(stage):
                w_copy(s, stage, k).start()

    def w_finish(s, stage, fix=None):
        if not d.inside:
            return
        for k in w_ks(stage):
            if stage <= 2:
                w_copy(s, stage, k).wait_recv()
            else:
                w_arrival(s, stage, k).wait_recv()
        part, inner = parts[s], mids[s]
        if stage == 0:
            rc = rcs[s]

            def add(t, carry):
                at = pl.ds(pl.multiple_of(t * 16, 16), 16)
                part[core, at, :] = (part[core, at, :].astype(F32) + rc[at, :].astype(F32)).astype(BF16)
                return carry

            lax.fori_loop(0, wd // 16, add, 0)
        elif stage == 1:
            buf = rxys[s]

            def add(t, carry):
                at = pl.ds(pl.multiple_of(t * 16, 16), 16)
                own = pl.ds(pl.multiple_of(spot * plane_rows + t * 16, 16), 16)
                total = part[core, own, :].astype(F32)
                for k in range(3):
                    total = total + buf[k, at, :].astype(F32)
                inner[at, :] = total.astype(BF16)
                return carry

            lax.fori_loop(0, plane_rows // 16, add, 0)
        elif stage == 2:
            buf = rzs[s]
            total = inner[z_at(z_of), :].astype(F32)
            for k in range(3):
                total = total + buf[k].astype(F32)
            if s >= d.sets:
                vres[...] = total
                return
            if fix is not None:
                total = fix(total)
            ress[s][core, z_at(z_of, spot * plane_rows), :] = total.astype(BF16)

    def w_step(s, stage, fix=None):
        w_finish(s, stage, fix)
        if stage < 5:
            w_start(s, stage + 1)

    def w_sent(s):
        if d.inside:
            for stage in range(6 if s < d.sets else 3):
                for k in w_ks(stage):
                    w_copy(s, stage, k).wait_send()

    def first(t, carry):
        sums, squares = carry
        x_copy(t).wait()
        ct_copy(t, 0).start()
        ct_copy(t, 1).start()
        at = line_rows(t)
        y = dot(xv[at, :], w1[...])
        y1[at, :] = y
        masked = y * mask_of(at, mid)
        return sums + fold(masked), squares + fold(masked * y)

    loads[0].wait()
    zeros = jnp.zeros((8, mid), F32)
    sums0 = lax.fori_loop(0, nh // 2, first, (zeros, zeros))
    pl.semaphore_wait(barrier, len(peers))
    count = Everywhere("cnt")
    count.at[...] = jnp.zeros((4, LANES), F32)
    count.at[0:1, :] = total_row(pixels)
    count.at[1:2, :] = total_row(live[...]) * (1.0 / n_ha)
    count.start()
    totals, squares = lax.fori_loop(nh // 2, nh, first, sums0)
    norm1 = Everywhere("s1")
    put(norm1.at, 0, total_row(totals))
    put(norm1.at, 2, total_row(squares))
    norm1.start()
    loads[1].wait()
    loads[2].wait()
    for r in range(d.radix):
        for ky in range(3):
            for e in range(4):
                if e <= 2:
                    left = w2[r, (ky * 3 + 2 - e) * gin : (ky * 3 + 3 - e) * gin, :]
                if e >= 1:
                    right = w2[r, (ky * 3 + 3 - e) * gin : (ky * 3 + 4 - e) * gin, :]
                if e == 0:
                    w2l[r, :, ky * wd : (ky + 1) * wd] = left
                elif e == 3:
                    w2r[r, :, ky * wd : (ky + 1) * wd] = right
                else:
                    lanes = slice((ky * 2 + e - 1) * wd, (ky * 2 + e) * wd)
                    w2x[r, 0:gin, lanes] = left
                    w2x[r, gin:, lanes] = right
    got = count.finish()
    total, images = got[0:1, :], got[1:2, :]
    got = norm1.finish()
    mean1, scale1 = moments(get(got, 0, mid), get(got, 2, mid), wide(total, mid))
    half_a1 = 0.5 * g1[...] * scale1
    half_b1 = 0.5 * c1[...] - half_a1 * mean1

    step1 = 4 * nb

    def act_first(t, carry):
        def cells(u, carry):
            at = block_rows(t, u, step1)
            value, _ = gate(y1[at, :] * half_a1 + half_b1)
            value = value * mask_of(at, mid)
            a1p[inner_rows(t + 1, nb + u * step1, step1), :] = value.astype(BF16)
            return carry + fold(value)

        return lax.fori_loop(0, line // step1, cells, carry, unroll=True)

    def edges(body, carry):
        return lax.fori_loop(0, 2, lambda t, c: body(t * (nh - 1), c), carry)

    totals = edges(act_first, jnp.zeros((8, mid), F32))
    halo1_start, halo1_recv, halo1_sent = halo(a1p, 0)
    halo1_start()
    totals = lax.fori_loop(1, nh - 1, act_first, totals)
    act_sum = Everywhere("act")
    act_sum.at[...] = jnp.zeros((4, LANES), F32)
    put(act_sum.at, 0, total_row(totals))
    act_sum.start()

    def taps(t, r, first=0, last=9):
        return jnp.concatenate(
            [
                a1p[inner_rows(t + tap // 3, (tap % 3) * nb), r * gin : (r + 1) * gin]
                for tap in range(first, last)
            ],
            axis=1,
        )

    def group(t, carry):
        at = line_rows(t)
        mask = mask_of(at, wd)
        done = []
        for r in range(d.radix):
            sums, squares = carry[r]
            y = dot(taps(t, r), w2[r])
            y2[at, r * wd : (r + 1) * wd] = y.astype(BF16)
            masked = y * mask
            done.append((sums + fold(masked), squares + fold(masked * y)))
        return tuple(done)

    zeros = jnp.zeros((8, wd), F32)
    sums2 = lax.fori_loop(1, nh - 1, group, ((zeros, zeros),) * d.radix)
    halo1_recv()
    sums2 = edges(group, sums2)
    norm2 = Everywhere("s2")
    put(norm2.at, 0, jnp.concatenate([total_row(s) for s, _ in sums2], axis=1))
    put(norm2.at, 4, jnp.concatenate([total_row(q) for _, q in sums2], axis=1))
    norm2.start()

    acc_c[...] = jnp.zeros((wd, cin), F32)
    vecs[...] = jnp.zeros((8, cin), F32)

    def norm_products(t, carry):
        at = line_rows(t)
        mask = mask_of(at, mid)
        hat = ((y1[at, :] - mean1) * scale1 * mask).astype(BF16)
        x = xv[at, :]
        acc_c[...] += dot_tn(hat, x)
        vecs[...] += dot_tn(mb[at, :], x)[0:8, :]
        return carry

    lax.fori_loop(0, nh, norm_products, 0)
    norm2_done = norm2.finish()
    for c in range(2):
        parts[5][c] = acc_c[:, c * half : (c + 1) * half].astype(BF16)
    w_start(5, 0)
    v0_sum = Everywhere("v0")
    put(v0_sum.at, 0, vecs[0:1, :])
    v0_sum.start()
    mean2, scale2 = moments(get(norm2_done, 0, wide2), get(norm2_done, 4, wide2), wide(total, wide2))
    half_a2 = 0.5 * g2[...] * scale2
    half_b2 = 0.5 * c2[...] - half_a2 * mean2

    lane_blocks = wd // LANES
    step2 = (nw // 2) * nb
    zero = jnp.zeros((nb, LANES), F32)
    for j in range(lane_blocks):
        own = slice(j * LANES, (j + 1) * LANES)

        def act_group(t, pool):
            at = pl.ds(pl.multiple_of(t * step2, step2), step2)
            mask = mb[at, :]
            full = mask.astype(F32)
            for r in range(d.radix):
                lanes = slice(r * wd + j * LANES, r * wd + (j + 1) * LANES)
                value, _ = gate(y2[at, lanes].astype(F32) * half_a2[:, lanes] + half_b2[:, lanes])
                value = value * full
                act2[at, lanes] = value.astype(BF16)
                pool = pool + fold_images(value, nb)
            return pool

        pools[:, own] = lax.fori_loop(0, rows // step2, act_group, zero)

    pool = pools[...]
    pf_src[:, 0 : d.inter] = add_thirds(dot(thirds(pool), wsq[...]))
    pf_src[:, d.inter :] = pixels
    pf_start, pf_finish = swap(pf_src, pf_buf, ssa.at[0], rsa.at[0], ha_peer, n_ha)
    pf_start()

    def slopes(block):
        lanes = slice(block * LANES, (block + 1) * LANES)
        ha2, hb2 = half_a2[:, lanes], half_b2[:, lanes]

        def body(t, carry):
            slopes, bends = carry
            at = pl.ds(pl.multiple_of(t * step2, step2), step2)
            y = y2[at, lanes].astype(F32)
            _, slope = gate(y * ha2 + hb2)
            slope = slope * mb[at, :].astype(F32)
            slope2[at, lanes] = slope.astype(BF16)
            return slopes + fold_images(slope, nb), bends + fold_images(slope * y, nb)

        q2[:, lanes], q4[:, lanes] = lax.fori_loop(0, rows // step2, body, (zero, zero))

    total_blocks = d.radix * lane_blocks
    for block in range(total_blocks // 4):
        slopes(block)
    w_step(5, 0)
    both = pf_finish()
    floor = jnp.maximum(both[:, d.inter :], 1.0)
    squeezed = both[:, 0 : d.inter] / floor
    live_now = live[...]
    fc_src[...] = jnp.zeros(fc_src.shape, F32)
    put(fc_src.at[0], 0, total_row(squeezed * live_now))
    put(fc_src.at[0], 1, total_row(squeezed * squeezed * live_now))
    fc_start, fc_finish = swap(fc_src.at[0], fc_buf.at[0], ssi.at[0], rsi.at[0], img_peer, n_img)
    fc_start()
    for block in range(total_blocks // 4, total_blocks):
        slopes(block)
    got = fc_finish()
    mean_s, scale_s = moments(got[0:1, :], got[1:2, :], images)
    centered = (squeezed - mean_s) * scale_s
    hidden, hidden_slope = gate(0.5 * (centered * gs[...] + cs[...]))
    logits = add_thirds(dot(thirds(hidden), wex[...])) + bex[...]
    gap = logits[:, 0:wd] - logits[:, wd:]
    att[:, 0:wd] = jax.nn.sigmoid(gap)
    att[:, wd:] = jax.nn.sigmoid(-gap)

    step3 = 2 * nb

    def mix(t, carry):
        def cells(u, carry):
            at = block_rows(t, u, step3)
            weight = jnp.concatenate([att[...]] * (step3 // nb), axis=0)
            both = act2[at, :].astype(F32) * weight
            mixed[at, :] = (both[:, 0:wd] + both[:, wd:]).astype(BF16)
            return carry

        lax.fori_loop(0, line // step3, cells, 0, unroll=7)
        at = line_rows(t)
        for c in range(2):
            lanes = slice(c * half, (c + 1) * half)
            y = dot(mixed[at, :], w3[:, lanes])
            ost[at, lanes] = y.astype(BF16)
            vecs[:, lanes] += fold(y)
            vecs2[:, lanes] += fold(y * y)
        return carry

    vecs[...] = jnp.zeros((8, cin), F32)
    vecs2[...] = jnp.zeros((8, cin), F32)
    lax.fori_loop(0, nh, mix, 0)
    norm3 = Everywhere("s3")
    put(norm3.at, 0, total_row(vecs[...]))
    put(norm3.at, 8, total_row(vecs2[...]))
    norm3.start()

    def mix_products(t, carry):
        gram, sums = carry
        cells = mixed[line_rows(t), :]
        mix_t[t] = jnp.transpose(cells)
        ct_copy(t, 0).wait()
        ct_copy(t, 1).wait()
        return gram + dot(mix_t[t], cells), sums + fold(cells.astype(F32))

    gram, totals = lax.fori_loop(0, nh, mix_products, (jnp.zeros((wd, wd), F32), jnp.zeros((8, wd), F32)))
    mix_sum = total_row(totals)
    gram_high, gram_low = split_bf16(gram)
    acc_g[0, :, 0:cin] = dot(gram_high, w3[...]) + dot(gram_low, w3[...])
    w_step(5, 1)
    got = norm3.finish()
    mean3, scale3 = moments(get(got, 0, cin), get(got, 8, cin), wide(total, cin))
    grow3 = g3[...] * scale3
    half_a3 = 0.5 * grow3
    half_b3 = 0.5 * c3[...] - half_a3 * mean3

    step4 = (nw // 4) * nb
    blocks4 = 2 * LANES

    def dn_copy(t, c):
        return pltpu.make_async_copy(
            ctv.at[half_rows(t, c)], dn_hbm.at[line_rows(t), pl.ds(c * half, half)], sem_dn.at[c, t]
        )

    def dn_back(t, c):
        return pltpu.make_async_copy(
            dn_hbm.at[line_rows(t), pl.ds(c * half, half)], ctv.at[half_rows(t, c)], sem_back.at[c, t]
        )

    def grad_of(t):
        return jnp.concatenate([ctv[half_rows(t, 0), :], ctv[half_rows(t, 1), :]], axis=1)

    vecs[...] = jnp.zeros((8, cin), F32)
    vecs2[...] = jnp.zeros((8, cin), F32)

    def last(t, carry):
        for j in range(cin // blocks4):
            lanes = slice(j * blocks4, (j + 1) * blocks4)
            a3, b3 = half_a3[:, lanes], half_b3[:, lanes]

            def cells(u, carry):
                at = block_rows(t, u, step4)
                mask = wide(mb[at, :], blocks4)
                x = xv[at, lanes] * jnp.asarray(0.5, BF16)
                y = ost[at, lanes].astype(F32)
                arg = y * a3 + (b3 + x.astype(F32))
                bend = jnp.tanh(arg)
                rise = 1.0 + bend
                value = arg * rise
                ost[at, lanes] = value.astype(BF16) * mask
                side = j * blocks4 // half
                there = pl.ds(pl.multiple_of(side * rows + t * line + u * step4, nb), step4)
                inner = slice(j * blocks4 - side * half, (j + 1) * blocks4 - side * half)
                push = ctv[there, inner] * (mask * jnp.asarray(0.5, BF16))
                grad = push.astype(F32) * (rise + value * (1.0 - bend))
                ctv[there, inner] = grad.astype(BF16)
                sums, bends = carry
                return sums + fold(grad), bends + fold(grad * y)

            vecs[:, lanes], vecs2[:, lanes] = lax.fori_loop(
                0, line // step4, cells, (vecs[:, lanes], vecs2[:, lanes])
            )
        dn_copy(t, 0).start()
        dn_copy(t, 1).start()
        return carry

    lax.fori_loop(0, nh, last, 0)
    sum_grad = total_row(vecs[...])
    back3 = Everywhere("b3")
    put(rows16, 0, sum_grad)
    put(rows16, 8, scale3 * (total_row(vecs2[...]) - mean3 * sum_grad))
    back3.at[...] = rows16[...].astype(BF16)
    back3.start()

    w3p[...] = (w3[...].astype(F32) * grow3).astype(BF16)

    acc_c[...] = jnp.zeros((wd, cin), F32)

    def plain_back(t, carry):
        grad = grad_of(t)
        dm[line_rows(t), :] = dot_nt(grad, w3p[...])
        acc_c[...] += dot(mix_t[t], grad)
        return carry

    lax.fori_loop(0, nh, plain_back, 0)
    w_finish(5, 2)
    got = back3.finish()
    bias3, gain3 = get(got, 0, cin), get(got, 8, cin)
    put(small.at[0], 0, bias3)
    put(small.at[0], 8, gain3)
    all_wide = wide(total, cin)
    slant3 = scale3 * gain3 / all_wide
    level3 = bias3 / all_wide - mean3 * slant3
    fix = (w3[...].astype(F32) * slant3).astype(BF16)
    level_high, level_low = split_bf16(level3)
    levels = [jnp.broadcast_to(part, (16, cin)) for part in (level_high, level_low)]
    stack = dot_nt(jnp.concatenate([fix, *levels], axis=0), w3p[...])
    fix = stack[0:wd, :].astype(BF16)
    shift = stack[wd : wd + 1, :] + stack[wd + 16 : wd + 17, :]

    def back_mix(t, carry):
        at = line_rows(t)
        dm[at, :] = dm[at, :] - dot(mixed[at, :], fix) - mask_of(at, wd) * shift
        return carry

    lax.fori_loop(0, nh, back_mix, 0)

    step5 = 4 * nb
    sums5 = []
    for j in range(lane_blocks):
        lanes = slice(j * LANES, (j + 1) * LANES)

        def image_sums(t, carry):
            at = pl.ds(pl.multiple_of(t * step5, step5), step5)
            grad = dm[at, lanes]
            done = []
            for r in range(d.radix):
                own = slice(r * wd + j * LANES, r * wd + (j + 1) * LANES)
                a, b, c = carry[r]
                a = a + fold_images(grad * act2[at, own].astype(F32), nb)
                part = grad * slope2[at, own].astype(F32)
                b = b + fold_images(part, nb)
                c = c + fold_images(part * y2[at, own].astype(F32), nb)
                done.append((a, b, c))
            return tuple(done)

        sums5.append(lax.fori_loop(0, rows // step5, image_sums, ((zero, zero, zero),) * d.radix, unroll=7))
    pick = lambda which: jnp.concatenate(
        [sums5[j][r][which] for r in range(d.radix) for j in range(lane_blocks)], axis=1
    )
    q1, q3 = pick(1), pick(2)

    def dn_out(t, carry):
        dn_copy(t, 0).wait()
        dn_copy(t, 1).wait()
        return carry

    lax.fori_loop(0, nh, dn_out, 0)
    clear(dyp)
    ga_src[...] = pick(0).astype(BF16)
    ga_start, ga_finish = swap(ga_src, ga_buf, ssa.at[1], rsa.at[1], ha_peer, n_ha)
    ga_start()

    mix_column = jnp.transpose(jnp.broadcast_to(mix_sum, (LANES, wd)))
    for j in range(cin // LANES):
        lanes = slice(j * LANES, (j + 1) * LANES)
        c = 0 if j * LANES < half else 1
        grad = grow3[:, lanes] * (
            acc_c[:, lanes] - mix_column * level3[:, lanes] - acc_g[0, :, lanes] * slant3[:, lanes]
        )
        parts[2][c, :, j * LANES - c * half : (j + 1) * LANES - c * half] = grad.astype(BF16)
    w_start(2, 0)

    grad_att = ga_finish()
    weight = att[...]
    weighed = weight * grad_att
    both = weighed[:, 0:wd] + weighed[:, wd:]
    grad_logits = weight * (grad_att - jnp.concatenate([both, both], axis=1))
    grad_fc = add_thirds(dot_nt(thirds(grad_logits), wex[...])) * hidden_slope
    put(fc_src.at[1], 0, total_row(grad_fc))
    put(fc_src.at[1], 1, total_row(grad_fc * centered))
    pooled = pool / wide(floor, wd)
    put(fc_src.at[1], 2, total_row(pooled))
    fc_start, fc_finish = swap(fc_src.at[1], fc_buf.at[1], ssi.at[1], rsi.at[1], img_peer, n_img)
    fc_start()
    w_step(2, 0)
    grad_excite = dot_tn(hidden, grad_logits, HIGH)
    grad_bex = total_row(grad_logits) * (1.0 / n_ha)
    got = fc_finish()
    bias_s, gain_s = got[0:1, :], got[1:2, :]
    put(small.at[0], 16, bias_s)
    put(small.at[0], 17, gain_s)
    grad_squeezed = (gs[...] * scale_s) * (
        grad_fc - live_now * (bias_s + centered * gain_s) / images
    )
    grad_pool = add_thirds(dot_nt(thirds(grad_squeezed), wsq[...])) / wide(floor, wd)
    pool2 = jnp.concatenate([grad_pool] * d.radix, axis=1)
    sum_grad = total_row(weight * q1 + pool2 * q2[...])
    sum_bend = total_row(weight * q3 + pool2 * q4[...])
    back2 = Everywhere("b2")
    put(back2.at, 0, sum_grad)
    put(back2.at, 4, scale2 * (sum_bend - mean2 * sum_grad))
    back2.start()
    level = get(got, 2, wd) / wide(images, wd)
    grad_squeeze = dot_tn(pooled - level, grad_squeezed, HIGH)
    grow2 = g2[...] * scale2
    att[...] = weight * grow2
    q2[...] = pool2 * grow2
    def first_slopes(t, carry):
        at = pl.ds(pl.multiple_of(t * step1, step1), step1)
        _, slope = gate(y1[at, :] * half_a1 + half_b1)
        mixed[at, :] = (slope * mask_of(at, mid)).astype(BF16)
        return carry

    lax.fori_loop(0, rows // step1, first_slopes, 0)

    parts[4][0] = jnp.concatenate([grad_excite[:, 0:wd], grad_excite[:, wd:]], axis=0).astype(
        BF16
    ) * jnp.asarray(1.0 / n_ha, BF16)
    parts[4][1, :, 0 : d.inter] = grad_squeeze.astype(BF16)
    parts[4][1, :, d.inter :] = jnp.zeros((wd, wd - d.inter), BF16)
    w_start(4, 0)
    w_step(2, 1)
    acc_g[...] = jnp.zeros((d.radix, wd, 9 * gin), F32)
    mean_act1 = get(act_sum.finish(), 0, mid) / (wide(images, mid) * float(nh * n_ha * nw))
    w_step(4, 0)
    got = back2.finish()
    bias2, gain2 = get(got, 0, wide2), get(got, 4, wide2)
    put(small.at[0], 20, bias2)
    put(small.at[0], 24, gain2)
    slant2 = grow2 * scale2 * gain2 / wide(total, wide2)
    level2 = grow2 * bias2 / wide(total, wide2) - mean2 * slant2

    step6 = 2 * nb

    def back_group(t, carry):
        def cells(u, carry):
            at = block_rows(t, u, step6)
            to = inner_rows(t + 1, nb + u * step6, step6)
            again = step6 // nb
            grad = dm[at, :]
            mask = mask_of(at, wd)
            sums = []
            for r in range(d.radix):
                own = slice(r * wd, (r + 1) * wd)
                grow = jnp.concatenate([att[:, own]] * again, axis=0)
                lift = jnp.concatenate([q2[:, own]] * again, axis=0)
                push = (grow * grad + lift) * slope2[at, own].astype(F32)
                pull = mask * (level2[:, own] + slant2[:, own] * y2[at, own].astype(F32))
                dyp[to, own] = (push - pull).astype(BF16)
                sums.append(carry[r] + fold(push - pull))
            return tuple(sums)

        return lax.fori_loop(0, line // step6, cells, carry, unroll=7)

    zeros = jnp.zeros((8, wd), F32)
    sums2 = edges(back_group, (zeros,) * d.radix)
    halo2_start, halo2_recv, halo2_sent = halo(dyp, 1)
    halo2_start()
    sums2 = lax.fori_loop(1, nh - 1, back_group, sums2)
    sum_dy2 = [total_row(s) for s in sums2]
    misc = Everywhere("misc")
    put(misc.at, 0, jnp.concatenate(sum_dy2, axis=1))
    put(misc.at, 4, grad_bex)
    misc.start()
    w_step(2, 2)
    w_step(4, 1)

    def weights_group(t, carry):
        for r in range(d.radix):
            grad = jnp.transpose(dyp[inner_rows(t + 1), r * wd : (r + 1) * wd])
            acc_g[r] += dot(grad, taps(t, r))
        return carry

    lax.fori_loop(0, nh, weights_group, 0)

    def send_group(s, first, last):
        lanes = (last - first) * gin
        for r in range(d.radix):
            base = wide(mean_act1[:, r * gin : (r + 1) * gin], lanes)
            column = jnp.transpose(jnp.broadcast_to(sum_dy2[r], (LANES, wd)))
            grad = acc_g[r, :, first * gin : last * gin] - wide(column, lanes) * base
            parts[s][r, :, 0:lanes] = grad.astype(BF16)
        w_start(s, 0)

    send_group(1, 0, d.split)
    send_group(3, d.split, 9)
    w_step(2, 3)
    w_step(4, 2)

    pairs = nw // 2

    def back_taps(t, r, which):
        cells = []
        for ky in range(3):
            for e in which:
                block = dyp[inner_rows(t + 2 - ky, e * nb), r * wd : (r + 1) * wd]
                block = block.reshape(pairs, 2 * nb, wd)[:, 0:nb, :].reshape(pairs * nb, wd)
                cells.append(block)
        return jnp.concatenate(cells, axis=1)

    def transposed(t, carry):
        sums, bends = carry
        at = line_rows(t)
        done = []
        for r in range(d.radix):
            both = dot_nt(back_taps(t, r, (1, 2)), w2x[r])
            left = both[:, 0:gin] + dot_nt(back_taps(t, r, (0,)), w2l[r])
            right = both[:, gin:] + dot_nt(back_taps(t, r, (3,)), w2r[r])
            both = jnp.concatenate(
                [left.reshape(pairs, nb, gin), right.reshape(pairs, nb, gin)], axis=1
            )
            done.append(both.reshape(line, gin))
        dm[at, :] = jnp.concatenate(done, axis=1)

        def cells(u, carry):
            sums, bends = carry
            at = block_rows(t, u, step1)
            grad = dm[at, :] * mixed[at, :].astype(F32)
            dm[at, :] = grad
            mixed[at, :] = grad.astype(BF16)
            return sums + fold(grad), bends + fold(grad * y1[at, :])

        return lax.fori_loop(0, line // step1, cells, (sums, bends))

    zeros = jnp.zeros((8, mid), F32)
    middle = 1 + (nh - 2) // 3
    sums1 = lax.fori_loop(1, middle, transposed, (zeros, zeros))
    w_step(1, 0)
    w_step(3, 0)
    sums1 = lax.fori_loop(middle, nh - 1, transposed, sums1)
    w_step(4, 3)
    halo2_recv()
    sums1 = edges(transposed, sums1)
    sum_grad = total_row(sums1[0])
    back1 = Everywhere("b1")
    put(back1.at, 0, sum_grad)
    put(back1.at, 2, scale1 * (total_row(sums1[1]) - mean1 * sum_grad))
    back1.start()
    halo2_sent()

    def fetch_back(t, carry):
        dn_back(t, 0).start()
        dn_back(t, 1).start()
        return carry

    lax.fori_loop(0, nh, fetch_back, 0)

    acc_c[...] = jnp.zeros((wd, cin), F32)

    def first_weights(t, carry):
        at = line_rows(t)
        acc_c[...] += dot_tn(mixed[at, :], xv[at, :])
        return carry

    lax.fori_loop(0, nh, first_weights, 0)
    if d.inside:
        for c in range(2):
            parts[0][c] = acc_c[:, c * half : (c + 1) * half].astype(BF16)
    w_start(0, 0)
    w_step(1, 1)
    w_step(0, 0)
    w_step(3, 1)
    got = back1.finish()
    bias1, gain1 = get(got, 0, mid), get(got, 2, mid)
    grow1 = g1[...] * scale1
    bias_all, gain_all = bias1 / wide(total, mid), gain1 / wide(total, mid)
    slant1 = grow1 * scale1 * gain_all
    level1 = grow1 * bias_all - mean1 * slant1
    w_step(2, 4)
    w_step(4, 4)

    def back_first(t, carry):
        def cells(u, carry):
            at = block_rows(t, u, step1)
            pull = mask_of(at, mid) * (level1 + slant1 * y1[at, :])
            mixed[at, :] = (grow1 * dm[at, :] - pull).astype(BF16)
            return carry

        lax.fori_loop(0, line // step1, cells, 0)
        return carry

    lax.fori_loop(0, nh, back_first, 0)
    put(small.at[0], 32, bias1)
    put(small.at[0], 34, gain1)
    put(small.at[0], 36, mean_act1)
    small[0, 18:20, :] = jnp.zeros((2, LANES), F32)
    small[0, 38:40, :] = jnp.zeros((2, LANES), F32)
    small[0, 44:48, :] = jnp.zeros((4, LANES), F32)
    got = misc.finish()
    put(small.at[0], 28, get(got, 4, wide2))
    put(small.at[0], 40, get(got, 0, wide2))
    got = v0_sum.finish()
    for c in range(2):
        v0[c] = jnp.broadcast_to(get(got, 0, cin)[:, c * half : (c + 1) * half], (8, half))
    for j, vector in enumerate((grow1, bias_all, gain_all)):
        cols[j] = jnp.transpose(jnp.broadcast_to(vector, (LANES, mid)))

    def norm_terms(total, at, taken, flat):
        lanes = total.shape[1]
        grow, level, slant = (wide(cols[j, at, :], lanes) for j in range(3))
        return grow * (total - level * flat - slant * taken)

    def fix_first(total):
        return norm_terms(total, z_at(z_of, spot * plane_rows), vres[...], v0[core, 0:1, :])

    def grad_inputs(t, carry):
        at = line_rows(t)
        for c in range(2):
            lanes = slice(c * half, (c + 1) * half)
            dn_back(t, c).wait()
            grad = ctv[half_rows(t, c), :].astype(F32) + dot_nt(mixed[at, :], w1[lanes, :])
            xv[at, lanes] = grad.astype(BF16)
        return carry

    w_step(1, 2)
    lax.fori_loop(0, nh // 2, grad_inputs, 0)
    w_step(3, 2)
    w_step(0, 1)
    w_step(1, 3)
    w_step(3, 3)
    w_step(0, 2, fix_first)
    lax.fori_loop(nh // 2, nh, grad_inputs, 0)
    w_step(1, 4)
    w_step(0, 3)
    w_step(3, 4)
    w_step(0, 4)
    for s in (2, 4, 1, 3, 0):
        w_step(s, 5)
    if not d.inside:
        whole = slice(0, wd)
        for c in range(2):
            lanes = slice(c * half, (c + 1) * half)
            local = wide(cols[0, whole, :], half) * (
                acc_c[:, lanes]
                - wide(cols[1, whole, :], half) * get(v0_sum.at[...], 0, cin)[:, lanes]
                - wide(cols[2, whole, :], half) * parts[5][c].astype(F32)
            )
            parts[0][c] = local.astype(BF16)

    for s in range(d.sets + 1):
        w_sent(s)
    halo1_sent()
    if not d.inside:
        for s in range(d.sets):
            ress[s][...] = parts[s][...]


def call_block(d, args):
    f32, bf16 = F32, BF16
    cin, wd, mid, rows, nb, nh = d.cin, d.width, d.mid, d.rows, d.nb, d.nh
    vmem, dma = pltpu.VMEM, pltpu.SemaphoreType.DMA
    halves = [(2, wd, lanes) for lanes in d.half]
    shape = jax.ShapeDtypeStruct
    outs = [
        shape((rows, cin), bf16),
        vmem((rows, cin), bf16),
        vmem((rows, cin), bf16),
        *[vmem(s, bf16) for s in halves[: d.sets]],
        vmem((1, 48, LANES), f32),
    ]
    anywhere = pl.BlockSpec(memory_space=pl.ANY)
    inside = pl.BlockSpec(memory_space=pltpu.VMEM)
    plane, zed = wd // 4, wd // 16

    def sums_of(name, count):
        kind = bf16 if name in d.narrow else f32
        if not d.inside:
            return dict(
                src=vmem((count, LANES), kind),
                mid=vmem((count, LANES), f32),
                buf_ha=vmem((d.n_ha, count, LANES), kind),
                buf_img=vmem((d.n_img, count, LANES), f32),
                send_ha=dma((d.n_ha,)), recv_ha=dma((d.n_ha,)),
                send=dma((d.n_img,)), recv=dma((d.n_img,)),
            )
        if name in d.paired:
            return dict(
                src=vmem((count, LANES), kind),
                mid=vmem((count, LANES), f32),
                other=vmem((count, LANES), f32),
                buf=vmem((16, count, LANES), f32),
                send=dma((16,)), recv=dma((16,)),
            )
        return dict(
            src=vmem((count, LANES), kind),
            buf=vmem((32, count, LANES), kind),
            send=dma((32,)), recv=dma((32,)),
        )

    scratch = [
        vmem((cin, mid), bf16),
        vmem((d.radix, 9 * d.gin, wd), bf16),
        vmem((wd, cin), bf16),
        vmem((rows, LANES), bf16),
        vmem((nb, LANES), f32),
        vmem((max(2 * rows, (nh + 2) * d.padded), cin // 2), bf16),
        vmem((rows, mid), f32),
        vmem(((nh + 2) * d.padded, mid), bf16),
        vmem((rows, d.wide), bf16),
        vmem((rows, d.wide), bf16),
        vmem((rows, d.wide), bf16),
        vmem((rows, wd), bf16),
        vmem((rows, wd), f32),
        vmem((wd, cin), f32),
        vmem((d.radix, wd, 9 * d.gin), f32),
        vmem((wd, cin), bf16),
        vmem((d.radix, 2 * d.gin, 6 * wd), bf16),
        vmem((d.radix, d.gin, 3 * wd), bf16),
        vmem((d.radix, d.gin, 3 * wd), bf16),
        vmem((nh, wd, d.line), bf16),
        vmem((16, LANES), f32),
        vmem((nb, d.wide), f32),
        vmem((nb, d.wide), f32),
        vmem((nb, d.wide), f32),
        vmem((8, cin), f32),
        vmem((8, cin), f32),
        vmem((nb, wd), f32),
        vmem((2, 8, cin // 2), f32),
        vmem((3, mid, LANES), f32),
        [vmem(s, bf16) for s in halves],
        [vmem((wd, lanes), bf16) for lanes in d.half],
        [vmem((3, plane, lanes), bf16) for lanes in d.half],
        [vmem((3, zed, lanes), bf16) for lanes in d.half],
        [vmem((plane, lanes), bf16) for lanes in d.half],
        vmem((zed, d.half[0]), f32),
        {name: sums_of(name, count) for name, count in d.sums.items() if name not in d.shared},
        vmem((nb, d.wide), bf16),
        vmem((d.n_ha, nb, d.wide), bf16),
        vmem((nb, 2 * LANES), f32),
        vmem((d.n_ha, nb, 2 * LANES), f32),
        vmem((2, 4, LANES), f32),
        vmem((2, d.n_img, 4, LANES), f32),
        dma((3,)),
        dma((nh,)),
        dma((2, nh)),
        dma((2, nh)),
        dma((2, nh)),
        dma((2, d.n_ha)),
        dma((2, d.n_ha)),
        dma((2, d.n_img)),
        dma((2, d.n_img)),
        dma((2, 2)),
        dma((2, 2)),
        dma((6, 24)),
        dma((6, 24)),
    ]
    return pl.pallas_call(
        functools.partial(block_kernel, d),
        out_shape=outs,
        in_specs=[anywhere, anywhere, inside, pl.BlockSpec(memory_space=pltpu.SMEM)]
        + [anywhere, inside, inside, anywhere] + [inside] * 7 + [anywhere, inside, inside],
        out_specs=[anywhere] + [inside] * 8,
        scratch_shapes=scratch,
        name="block",
        compiler_params=pltpu.CompilerParams(
            collective_id=0, has_side_effects=True, vmem_limit_bytes=47 << 20
        ),
    )(*args)


def finish_kernel(
    d, out_in, gin_in, wg0, wg1, wg2, wg3, wg4, small,
    out, gin_hbm, gw1_hbm, gg1, gb1, gw2_hbm, gg2, gb2, gwsq, ggs, gbs, gwex, gbex, gw3_hbm, gg3, gb3,
    gw1, gw2, gw3, sem_out, sem_gw,
):
    wd = d.width
    parts = 4
    copies = [
        pltpu.make_async_copy(src.at[at], dst.at[at], sem_out.at[which, t])
        for which, (src, dst) in enumerate(((out_in, out), (gin_in, gin_hbm)))
        for t in range(parts)
        for at in (pl.ds(t * (d.rows // parts), d.rows // parts),)
    ]
    for copy in copies:
        copy.start()
    stores = [
        pltpu.make_async_copy(src, dst, sem_gw.at[j])
        for j, (src, dst) in enumerate(((gw1, gw1_hbm), (gw3, gw3_hbm), (gw2, gw2_hbm)))
    ]

    def weights(step):
        half = d.cin // 2
        if step < 2:
            gw1[step * half : (step + 1) * half, :] = jnp.transpose(wg0[step]).astype(F32)
            gw3[:, step * half : (step + 1) * half] = wg2[step].astype(F32)
        elif step < 4:
            r = step - 2
            rows = small[0]
            mean = get(rows, 36, d.mid)[:, r * d.gin : (r + 1) * d.gin]
            taken = get(rows, 40, d.wide)[:, r * wd : (r + 1) * wd]
            mean = jnp.transpose(jnp.broadcast_to(mean, (LANES, d.gin)))
            back = wide(mean, wd) * taken
            for tap in range(9):
                held, first = (wg1, 0) if tap < d.split else (wg3, d.split)
                cells = held[r, :, (tap - first) * d.gin : (tap - first + 1) * d.gin]
                gw2[r, tap] = jnp.transpose(cells).astype(F32) + back
        elif step == 4:
            cells = wg4[0].astype(F32)
            gwex[:, 0:wd] = cells[0 : d.inter, :]
            gwex[:, wd:] = cells[d.inter :, :]
            gwsq[...] = wg4[1, :, 0 : d.inter].astype(F32)
            rows = small[0]
            gb3[...] = get(rows, 0, d.cin)
            gg3[...] = get(rows, 8, d.cin)
            gbs[...] = rows[16:17, :]
            ggs[...] = rows[17:18, :]
            gb2[...] = get(rows, 20, d.wide)
            gg2[...] = get(rows, 24, d.wide)
            gbex[...] = get(rows, 28, d.wide)
            gb1[...] = get(rows, 32, d.mid)
            gg1[...] = get(rows, 34, d.mid)

    for t in range(5):
        weights(t)
        if t == 1:
            stores[0].start()
            stores[1].start()
        elif t == 3:
            stores[2].start()
    for copy in stores + copies:
        copy.wait()


def call_finish(d, *args):
    shape = jax.ShapeDtypeStruct
    cin, wd, mid = d.cin, d.width, d.mid
    vmem, dma = pltpu.VMEM, pltpu.SemaphoreType.DMA
    small_dims = [
        (cin, mid), (1, mid), (1, mid), (d.radix, 9, d.gin, wd), (1, d.wide), (1, d.wide), (wd, d.inter),
        (1, d.inter), (1, d.inter), (d.inter, d.wide), (1, d.wide), (wd, cin), (1, cin), (1, cin),
    ]
    anywhere = pl.BlockSpec(memory_space=pl.ANY)
    inside = pl.BlockSpec(memory_space=pltpu.VMEM)
    return pl.pallas_call(
        functools.partial(finish_kernel, d),
        out_shape=[shape((d.rows, cin), BF16), shape((d.rows, cin), BF16)]
        + [shape(s, F32) for s in small_dims],
        in_specs=[inside] * 8,
        out_specs=[anywhere] * 3 + [inside] * 2 + [anywhere] + [inside] * 7 + [anywhere] + [inside] * 2,
        scratch_shapes=[
            vmem((cin, mid), F32), vmem((d.radix, 9, d.gin, wd), F32), vmem((wd, cin), F32),
            dma((2, 4)), dma((3,)),
        ],
        name="finish",
        compiler_params=pltpu.CompilerParams(vmem_limit_bytes=16 << 20),
    )(*[pltpu.with_memory_space_constraint(arg, pltpu.VMEM) for arg in args])


def on_device(
    inputs, image_count, pixel_mask, w_first, gain_first, bias_first, w_group, gain_group, bias_group,
    w_squeeze, gain_squeeze, bias_squeeze, w_excite, bias_excite, w_last, gain_last, bias_last, cotangent,
):
    n_img, n_ha = lax.axis_size("img"), lax.axis_size("ha")
    d = Dims(n_img, n_ha, inputs.shape, w_group.shape, w_squeeze.shape)
    nb, nh, nw, cin = inputs.shape

    def by_rows(cells):
        return jnp.transpose(cells, (1, 2, 0, 3)).reshape(d.rows, cin)

    def by_image(cells):
        return jnp.transpose(cells.reshape(nh, nw, nb, cin), (2, 0, 1, 3))

    row = lambda v: v.reshape(1, -1)
    args = (
        by_rows(inputs), by_rows(cotangent), jnp.transpose(pixel_mask, (1, 0, 2)), image_count,
        w_first, row(gain_first), row(bias_first),
        w_group.reshape(d.radix, 9 * d.gin, d.width), row(gain_group), row(bias_group),
        w_squeeze, row(gain_squeeze), row(bias_squeeze), w_excite, row(bias_excite),
        w_last, row(gain_last), row(bias_last),
    )
    _, out, gin, *sets, small = call_block(d, args)
    if not d.inside:
        sets = lax.psum(sets, ("img", "ha"))
    done = call_finish(d, out, gin, *sets, small)
    (out, gin, gw1, gg1, gb1, gw2, gg2, gb2, gwsq, ggs, gbs, gwex, gbex, gw3, gg3, gb3) = done
    flat = lambda v: v.reshape(-1)
    return (
        by_image(out), by_image(gin), gw1, flat(gg1), flat(gb1), gw2.reshape(w_group.shape), flat(gg2), flat(gb2),
        gwsq, flat(ggs), flat(gbs), gwex, flat(gbex), gw3, flat(gg3), flat(gb3),
    )


def solution(mesh):
    cells = P("img", "ha", None, None)
    placed = (cells, P("img"), P("img", "ha", None)) + (P(),) * 14 + (cells,)
    return jax.shard_map(
        on_device,
        mesh=mesh,
        in_specs=placed,
        out_specs=(cells, cells) + (P(),) * 14,
        check_vma=False,
    )
```

```python
import functools

import jax
import jax.numpy as jnp
from jax import lax
from jax.experimental import pallas as pl
from jax.experimental.pallas import tpu as pltpu
from jax.sharding import PartitionSpec as P

EPS = 1e-05
F32 = jnp.float32
BF16 = jnp.bfloat16
HIGH = lax.Precision.HIGHEST
MESH = pl.DeviceIdType.MESH
LANES = 128


def dot(a, b, precision=None):
    return jnp.dot(a, b, preferred_element_type=F32, precision=precision)


def dot_nt(a, b, precision=None):
    return lax.dot_general(
        a, b, (((1,), (1,)), ((), ())), preferred_element_type=F32, precision=precision
    )


def dot_tn(a, b, precision=None):
    return lax.dot_general(
        a, b, (((0,), (0,)), ((), ())), preferred_element_type=F32, precision=precision
    )


def wide(cell, lanes):
    return jnp.concatenate([cell] * (lanes // LANES), axis=1)


def fold(cells):
    rows, lanes = cells.shape
    return jnp.sum(cells.reshape(rows // 8, 8, lanes), axis=0)


def fold_images(cells, images):
    rows, lanes = cells.shape
    return jnp.sum(cells.reshape(rows // images, images, lanes), axis=0)


def total_row(cells):
    return jnp.sum(cells, axis=0, keepdims=True)


def put(ref, row, vector):
    for j in range(vector.shape[1] // LANES):
        ref[row + j : row + j + 1, :] = vector[:, j * LANES : (j + 1) * LANES]


def get(cells, row, lanes):
    return jnp.concatenate(
        [cells[row + j : row + j + 1, :] for j in range(lanes // LANES)], axis=1
    )


def moments(sums, squares, total):
    mean = sums / total
    spread = squares / total - mean * mean
    return mean, lax.rsqrt(spread + EPS)


def gate(half):
    bend = jnp.tanh(half)
    rise = 1.0 + bend
    value = half * rise
    return value, 0.5 * (rise + value * (1.0 - bend))


def split_bf16(cells):
    high = cells.astype(BF16)
    return high, (cells - high.astype(F32)).astype(BF16)


def thirds(cells):
    high = cells.astype(BF16)
    rest = cells - high.astype(F32)
    middle = rest.astype(BF16)
    return jnp.concatenate([high, middle, (rest - middle.astype(F32)).astype(BF16)], axis=0)


def add_thirds(cells):
    rows = cells.shape[0] // 3
    return cells[0:rows] + cells[rows : 2 * rows] + cells[2 * rows :]


class Dims:
    def __init__(self, n_img, n_ha, inputs, w_group, w_squeeze):
        self.n_img, self.n_ha = n_img, n_ha
        self.nb, self.nh, self.nw, self.cin = inputs
        self.radix, _, _, self.gin, self.width = w_group
        self.mid = self.radix * self.gin
        self.wide = self.radix * self.width
        self.inter = w_squeeze[1]
        self.line = self.nw * self.nb
        self.rows = self.nh * self.line
        self.padded = (self.nw + 2) * self.nb
        self.split = 5
        self.half = (self.cin // 2, 5 * self.gin, self.cin // 2, 4 * self.gin, self.width, self.cin // 2)
        self.sets = 5
        self.inside = n_img == 8 and n_ha == 4
        self.sums = dict(cnt=4, s1=4, s2=8, act=4, v0=8, s3=16, b3=16, b2=8, misc=8, b1=4)
        self.paired = ("s3",)
        self.narrow = ("b3",)
        self.shared = dict(b1="s1", b2="s2")


def block_kernel(
    d,
    x_hbm, ct_hbm, mask_in, count_in, w1_hbm, g1, c1, w2_hbm, g2, c2, wsq, gs, cs, wex, bex, w3_hbm, g3, c3,
    dn_hbm, ost, xv, wg0, wg1, wg2, wg3, wg4, small,
    w1, w2, w3, mb, live, ctv, y1, a1p, y2, act2, slope2, mixed, dm, acc_c, acc_g, w3p, w2x, w2l, w2r,
    mix_t, rows16, att, q2, q4, vecs, vecs2, pools, v0, cols,
    parts, rcs, rxys, rzs, mids, vres, sums, ga_src, ga_buf, pf_src, pf_buf, fc_src, fc_buf,
    sem_w, sem_x, sem_ct, sem_dn, sem_back, ssa, rsa, ssi, rsi, ssh, rsh, ssw, rsw,
):
    n_img, n_ha = d.n_img, d.n_ha
    nb, nh, nw = d.nb, d.nh, d.nw
    cin, mid, wd, wide2, line, rows = d.cin, d.mid, d.width, d.wide, d.line, d.rows
    gin, padded = d.gin, d.padded
    dyp = ctv
    ress = (wg0, wg1, wg2, wg3, wg4)
    half = cin // 2
    i = lax.axis_index("img")
    h = lax.axis_index("ha")

    def ha_peer(k):
        return (i, lax.rem(h + k, n_ha))

    def img_peer(k):
        return (lax.rem(i + k, n_img), h)

    z_of, x_of, y_of, core = i // 2, lax.rem(i, 2), h // 2, lax.rem(h, 2)
    spot = x_of * 2 + y_of

    def core_peer():
        return (i, y_of * 2 + (1 - core))

    def plane_peer(k):
        other = lax.rem(spot + k, 4)
        return (z_of * 2 + other // 2, lax.rem(other, 2) * 2 + core)

    def z_peer(k):
        return (lax.rem(z_of + k, 4) * 2 + x_of, h)

    def any_peer(k):
        return (lax.rem(i + k // 4, 8), lax.rem(h + k % 4, 4))

    def chip_peer(k):
        return (lax.rem(i + k // 2, 8), lax.rem(y_of + k % 2, 2) * 2 + core)

    def remote(src, dst, send, recv, peer):
        return pltpu.make_async_remote_copy(
            src_ref=src, dst_ref=dst, send_sem=send, recv_sem=recv, device_id=peer, device_id_type=MESH
        )

    def line_rows(t):
        return pl.ds(pl.multiple_of(t * line, line), line)

    def block_rows(t, u, step):
        return pl.ds(pl.multiple_of(t * line + u * step, nb), step)

    def x_copy(t):
        return pltpu.make_async_copy(x_hbm.at[line_rows(t)], xv.at[line_rows(t)], sem_x.at[t])

    def half_rows(t, c):
        return pl.ds(pl.multiple_of(c * rows + t * line, nb), line)

    def ct_copy(t, c):
        return pltpu.make_async_copy(
            ct_hbm.at[line_rows(t), pl.ds(c * half, half)], ctv.at[half_rows(t, c)], sem_ct.at[c, t]
        )

    def start_inputs(t, carry):
        x_copy(t).start()
        return carry

    loads = [
        pltpu.make_async_copy(src, dst, sem_w.at[j])
        for j, (src, dst) in enumerate(((w1_hbm, w1), (w2_hbm, w2), (w3_hbm, w3)))
    ]
    loads[0].start()
    lax.fori_loop(0, nh, start_inputs, 0)
    loads[1].start()
    loads[2].start()

    barrier = pltpu.get_barrier_semaphore()
    if d.inside:
        peers = [any_peer(k) for k in range(1, 32)]
    else:
        peers = [ha_peer(k) for k in range(1, n_ha)] + [img_peer(k) for k in range(1, n_img)]
    for peer in peers:
        pl.semaphore_signal(barrier, inc=1, device_id=peer, device_id_type=MESH)

    slots = lax.broadcasted_iota(jnp.int32, (nb, LANES), 0)
    live[...] = (slots < count_in[0]).astype(F32)

    def spread(t, carry):
        cells = mask_in[t].astype(F32)
        alive = live[...]
        for w in range(nw):
            cell = jnp.broadcast_to(cells[:, w : w + 1], (nb, LANES)) * alive
            mb[block_rows(t, w, nb), :] = cell.astype(BF16)
            carry = carry + cell
        return carry

    pixels = lax.fori_loop(0, nh, spread, jnp.zeros((nb, LANES), F32))

    def mask_of(at, lanes):
        return wide(mb[at, :].astype(F32), lanes)

    def inner_rows(t, at=nb, count=line):
        return pl.ds(pl.multiple_of(t * padded + at, nb), count)

    def clear(ref):
        zero = jnp.zeros((nb, ref.shape[1]), BF16)

        def body(t, carry):
            ref[inner_rows(t, 0, nb), :] = zero
            ref[inner_rows(t, nb + line, nb), :] = zero
            return carry

        lax.fori_loop(0, nh + 2, body, 0)

        def edge(t, carry):
            ref[inner_rows(0, t * nb, nb), :] = zero
            ref[inner_rows(nh + 1, t * nb, nb), :] = zero
            return carry

        lax.fori_loop(0, nw + 2, edge, 0)

    clear(a1p)

    def swap(src, buf, send, recv, peer, n):
        def copy(k):
            return remote(src, buf.at[k], send.at[k], recv.at[k], peer(k))

        def each(act, carry):
            if n > 32:
                return lax.fori_loop(1, n, act, carry)
            for k in range(1, n):
                carry = act(k, carry)
            return carry

        def begin(k, carry):
            copy(k).start()
            return carry

        def sent(k, carry):
            copy(k).wait_send()
            return carry

        def take(k, carry):
            copy(k).wait_recv()
            return carry + buf[k].astype(F32)

        def finish():
            total = each(take, src[...].astype(F32))
            each(sent, 0)
            return total

        return (lambda: each(begin, 0)), finish

    class Everywhere:
        def __init__(self, name):
            refs = sums[d.shared.get(name, name)]
            self.at = refs["src"]
            self.refs = refs
            if not d.inside:
                return
            send, recv = refs["send"], refs["recv"]
            if name in d.paired:
                self.pair = remote(self.at, refs["other"], send.at[0], recv.at[0], core_peer())
                self.start_far, self.finish_far = swap(refs["mid"], refs["buf"], send, recv, chip_peer, 16)
            else:
                self.pair = None
                self.start_far, self.finish_far = swap(self.at, refs["buf"], send, recv, any_peer, 32)

        def start(self):
            if d.inside:
                if self.pair is not None:
                    self.pair.start()
                    self.pair.wait_recv()
                    self.refs["mid"][...] = self.at[...] + self.refs["other"][...]
                self.start_far()

        def finish(self):
            if d.inside:
                total = self.finish_far()
                if self.pair is not None:
                    self.pair.wait_send()
                return total
            refs = self.refs
            start, finish = swap(self.at, refs["buf_ha"], refs["send_ha"], refs["recv_ha"], ha_peer, n_ha)
            start()
            refs["mid"][...] = finish()
            start, finish = swap(refs["mid"], refs["buf_img"], refs["send"], refs["recv"], img_peer, n_img)
            start()
            return finish()

    def halo(ref, at):
        def down():
            return remote(
                ref.at[inner_rows(nh)], ref.at[inner_rows(0)], ssh.at[at, 0], rsh.at[at, 0],
                (i, jnp.minimum(h + 1, n_ha - 1)),
            )

        def up():
            return remote(
                ref.at[inner_rows(1)], ref.at[inner_rows(nh + 1)], ssh.at[at, 1], rsh.at[at, 1],
                (i, jnp.maximum(h - 1, 0)),
            )

        def start():
            @pl.when(h < n_ha - 1)
            def _():
                down().start()

            @pl.when(h > 0)
            def _():
                up().start()

        def wait_recv():
            @pl.when(h > 0)
            def _():
                down().wait_recv()

            @pl.when(h < n_ha - 1)
            def _():
                up().wait_recv()

        def wait_send():
            @pl.when(h < n_ha - 1)
            def _():
                down().wait_send()

            @pl.when(h > 0)
            def _():
                up().wait_send()

        return start, wait_recv, wait_send

    plane_rows, z_rows = wd // 4, wd // 16

    def plane_at(other):
        return pl.ds(pl.multiple_of(other * plane_rows, plane_rows), plane_rows)

    def z_at(other, base=0):
        return pl.ds(pl.multiple_of(base + other * z_rows, z_rows), z_rows)

    def w_copy(s, stage, k):
        sem = (s, stage * 4 + k)
        if stage == 0:
            src, dst, peer = parts[s].at[1 - core], rcs[s], core_peer()
        elif stage == 1:
            src = parts[s].at[core, plane_at(lax.rem(spot + k, 4))]
            dst, peer = rxys[s].at[k - 1], plane_peer(k)
        elif stage == 2:
            src = mids[s].at[z_at(lax.rem(z_of + k, 4))]
            dst, peer = rzs[s].at[k - 1], z_peer(k)
        elif stage == 3:
            src = dst = ress[s].at[core, z_at(z_of, spot * plane_rows)]
            peer = z_peer(k)
        elif stage == 4:
            src = dst = ress[s].at[core, plane_at(spot)]
            peer = plane_peer(k)
        else:
            src = dst = ress[s].at[core]
            peer = core_peer()
        return remote(src, dst, ssw.at[sem], rsw.at[sem], peer)

    def w_ks(stage):
        return (1,) if stage in (0, 5) else (1, 2, 3)

    def w_arrival(s, stage, k):
        sem = (s, stage * 4 + k)
        if stage == 3:
            dst = ress[s].at[core, z_at(lax.rem(z_of - k + 4, 4), spot * plane_rows)]
        elif stage == 4:
            dst = ress[s].at[core, plane_at(lax.rem(spot - k + 4, 4))]
        else:
            dst = ress[s].at[1 - core]
        return remote(dst, dst, ssw.at[sem], rsw.at[sem], core_peer())

    def w_start(s, stage):
        if d.inside:
            for k in w_ks(stage):
                w_copy(s, stage, k).start()

    def w_finish(s, stage, fix=None):
        if not d.inside:
            return
        for k in w_ks(stage):
            if stage <= 2:
                w_copy(s, stage, k).wait_recv()
            else:
                w_arrival(s, stage, k).wait_recv()
        part, inner = parts[s], mids[s]
        if stage == 0:
            rc = rcs[s]

            def add(t, carry):
                at = pl.ds(pl.multiple_of(t * 16, 16), 16)
                part[core, at, :] = (part[core, at, :].astype(F32) + rc[at, :].astype(F32)).astype(BF16)
                return carry

            lax.fori_loop(0, wd // 16, add, 0)
        elif stage == 1:
            buf = rxys[s]

            def add(t, carry):
                at = pl.ds(pl.multiple_of(t * 16, 16), 16)
                own = pl.ds(pl.multiple_of(spot * plane_rows + t * 16, 16), 16)
                total = part[core, own, :].astype(F32)
                for k in range(3):
                    total = total + buf[k, at, :].astype(F32)
                inner[at, :] = total.astype(BF16)
                return carry

            lax.fori_loop(0, plane_rows // 16, add, 0)
        elif stage == 2:
            buf = rzs[s]
            total = inner[z_at(z_of), :].astype(F32)
            for k in range(3):
                total = total + buf[k].astype(F32)
            if s >= d.sets:
                vres[...] = total
                return
            if fix is not None:
                total = fix(total)
            ress[s][core, z_at(z_of, spot * plane_rows), :] = total.astype(BF16)

    def w_step(s, stage, fix=None):
        w_finish(s, stage, fix)
        if stage < 5:
            w_start(s, stage + 1)

    def w_sent(s):
        if d.inside:
            for stage in range(6 if s < d.sets else 3):
                for k in w_ks(stage):
                    w_copy(s, stage, k).wait_send()

    def first(t, carry):
        sums, squares = carry
        x_copy(t).wait()
        ct_copy(t, 0).start()
        ct_copy(t, 1).start()
        at = line_rows(t)
        y = dot(xv[at, :], w1[...])
        y1[at, :] = y
        masked = y * mask_of(at, mid)
        return sums + fold(masked), squares + fold(masked * y)

    loads[0].wait()
    zeros = jnp.zeros((8, mid), F32)
    sums0 = lax.fori_loop(0, nh // 2, first, (zeros, zeros))
    pl.semaphore_wait(barrier, len(peers))
    count = Everywhere("cnt")
    count.at[...] = jnp.zeros((4, LANES), F32)
    count.at[0:1, :] = total_row(pixels)
    count.at[1:2, :] = total_row(live[...]) * (1.0 / n_ha)
    count.start()
    totals, squares = lax.fori_loop(nh // 2, nh, first, sums0)
    norm1 = Everywhere("s1")
    put(norm1.at, 0, total_row(totals))
    put(norm1.at, 2, total_row(squares))
    norm1.start()
    loads[1].wait()
    loads[2].wait()
    for r in range(d.radix):
        for ky in range(3):
            for e in range(4):
                if e <= 2:
                    left = w2[r, (ky * 3 + 2 - e) * gin : (ky * 3 + 3 - e) * gin, :]
                if e >= 1:
                    right = w2[r, (ky * 3 + 3 - e) * gin : (ky * 3 + 4 - e) * gin, :]
                if e == 0:
                    w2l[r, :, ky * wd : (ky + 1) * wd] = left
                elif e == 3:
                    w2r[r, :, ky * wd : (ky + 1) * wd] = right
                else:
                    lanes = slice((ky * 2 + e - 1) * wd, (ky * 2 + e) * wd)
                    w2x[r, 0:gin, lanes] = left
                    w2x[r, gin:, lanes] = right
    got = count.finish()
    total, images = got[0:1, :], got[1:2, :]
    got = norm1.finish()
    mean1, scale1 = moments(get(got, 0, mid), get(got, 2, mid), wide(total, mid))
    half_a1 = 0.5 * g1[...] * scale1
    half_b1 = 0.5 * c1[...] - half_a1 * mean1

    step1 = 4 * nb

    def act_first(t, carry):
        def cells(u, carry):
            at = block_rows(t, u, step1)
            value, _ = gate(y1[at, :] * half_a1 + half_b1)
            value = value * mask_of(at, mid)
            a1p[inner_rows(t + 1, nb + u * step1, step1), :] = value.astype(BF16)
            return carry + fold(value)

        return lax.fori_loop(0, line // step1, cells, carry, unroll=True)

    def edges(body, carry):
        return lax.fori_loop(0, 2, lambda t, c: body(t * (nh - 1), c), carry)

    totals = edges(act_first, jnp.zeros((8, mid), F32))
    halo1_start, halo1_recv, halo1_sent = halo(a1p, 0)
    halo1_start()
    totals = lax.fori_loop(1, nh - 1, act_first, totals)
    act_sum = Everywhere("act")
    act_sum.at[...] = jnp.zeros((4, LANES), F32)
    put(act_sum.at, 0, total_row(totals))
    act_sum.start()

    def taps(t, r, first=0, last=9):
        return jnp.concatenate(
            [
                a1p[inner_rows(t + tap // 3, (tap % 3) * nb), r * gin : (r + 1) * gin]
                for tap in range(first, last)
            ],
            axis=1,
        )

    def group(t, carry):
        at = line_rows(t)
        mask = mask_of(at, wd)
        done = []
        for r in range(d.radix):
            sums, squares = carry[r]
            y = dot(taps(t, r), w2[r])
            y2[at, r * wd : (r + 1) * wd] = y.astype(BF16)
            masked = y * mask
            done.append((sums + fold(masked), squares + fold(masked * y)))
        return tuple(done)

    zeros = jnp.zeros((8, wd), F32)
    sums2 = lax.fori_loop(1, nh - 1, group, ((zeros, zeros),) * d.radix)
    halo1_recv()
    sums2 = edges(group, sums2)
    norm2 = Everywhere("s2")
    put(norm2.at, 0, jnp.concatenate([total_row(s) for s, _ in sums2], axis=1))
    put(norm2.at, 4, jnp.concatenate([total_row(q) for _, q in sums2], axis=1))
    norm2.start()

    acc_c[...] = jnp.zeros((wd, cin), F32)
    vecs[...] = jnp.zeros((8, cin), F32)

    def norm_products(t, carry):
        at = line_rows(t)
        mask = mask_of(at, mid)
        hat = ((y1[at, :] - mean1) * scale1 * mask).astype(BF16)
        x = xv[at, :]
        acc_c[...] += dot_tn(hat, x)
        vecs[...] += dot_tn(mb[at, :], x)[0:8, :]
        return carry

    lax.fori_loop(0, nh, norm_products, 0)
    norm2_done = norm2.finish()
    for c in range(2):
        parts[5][c] = acc_c[:, c * half : (c + 1) * half].astype(BF16)
    w_start(5, 0)
    v0_sum = Everywhere("v0")
    put(v0_sum.at, 0, vecs[0:1, :])
    v0_sum.start()
    mean2, scale2 = moments(get(norm2_done, 0, wide2), get(norm2_done, 4, wide2), wide(total, wide2))
    half_a2 = 0.5 * g2[...] * scale2
    half_b2 = 0.5 * c2[...] - half_a2 * mean2

    lane_blocks = wd // LANES
    step2 = (nw // 2) * nb
    zero = jnp.zeros((nb, LANES), F32)
    for j in range(lane_blocks):
        own = slice(j * LANES, (j + 1) * LANES)

        def act_group(t, pool):
            at = pl.ds(pl.multiple_of(t * step2, step2), step2)
            mask = mb[at, :]
            full = mask.astype(F32)
            for r in range(d.radix):
                lanes = slice(r * wd + j * LANES, r * wd + (j + 1) * LANES)
                value, _ = gate(y2[at, lanes].astype(F32) * half_a2[:, lanes] + half_b2[:, lanes])
                value = value * full
                act2[at, lanes] = value.astype(BF16)
                pool = pool + fold_images(value, nb)
            return pool

        pools[:, own] = lax.fori_loop(0, rows // step2, act_group, zero)

    pool = pools[...]
    pf_src[:, 0 : d.inter] = add_thirds(dot(thirds(pool), wsq[...]))
    pf_src[:, d.inter :] = pixels
    pf_start, pf_finish = swap(pf_src, pf_buf, ssa.at[0], rsa.at[0], ha_peer, n_ha)
    pf_start()

    def slopes(block):
        lanes = slice(block * LANES, (block + 1) * LANES)
        ha2, hb2 = half_a2[:, lanes], half_b2[:, lanes]

        def body(t, carry):
            slopes, bends = carry
            at = pl.ds(pl.multiple_of(t * step2, step2), step2)
            y = y2[at, lanes].astype(F32)
            _, slope = gate(y * ha2 + hb2)
            slope = slope * mb[at, :].astype(F32)
            slope2[at, lanes] = slope.astype(BF16)
            return slopes + fold_images(slope, nb), bends + fold_images(slope * y, nb)

        q2[:, lanes], q4[:, lanes] = lax.fori_loop(0, rows // step2, body, (zero, zero))

    total_blocks = d.radix * lane_blocks
    for block in range(total_blocks // 4):
        slopes(block)
    w_step(5, 0)
    both = pf_finish()
    floor = jnp.maximum(both[:, d.inter :], 1.0)
    squeezed = both[:, 0 : d.inter] / floor
    live_now = live[...]
    fc_src[...] = jnp.zeros(fc_src.shape, F32)
    put(fc_src.at[0], 0, total_row(squeezed * live_now))
    put(fc_src.at[0], 1, total_row(squeezed * squeezed * live_now))
    fc_start, fc_finish = swap(fc_src.at[0], fc_buf.at[0], ssi.at[0], rsi.at[0], img_peer, n_img)
    fc_start()
    for block in range(total_blocks // 4, total_blocks):
        slopes(block)
    got = fc_finish()
    mean_s, scale_s = moments(got[0:1, :], got[1:2, :], images)
    centered = (squeezed - mean_s) * scale_s
    hidden, hidden_slope = gate(0.5 * (centered * gs[...] + cs[...]))
    logits = add_thirds(dot(thirds(hidden), wex[...])) + bex[...]
    gap = logits[:, 0:wd] - logits[:, wd:]
    att[:, 0:wd] = jax.nn.sigmoid(gap)
    att[:, wd:] = jax.nn.sigmoid(-gap)

    step3 = 2 * nb

    def mix(t, carry):
        def cells(u, carry):
            at = block_rows(t, u, step3)
            weight = jnp.concatenate([att[...]] * (step3 // nb), axis=0)
            both = act2[at, :].astype(F32) * weight
            mixed[at, :] = (both[:, 0:wd] + both[:, wd:]).astype(BF16)
            return carry

        lax.fori_loop(0, line // step3, cells, 0, unroll=7)
        at = line_rows(t)
        for c in range(2):
            lanes = slice(c * half, (c + 1) * half)
            y = dot(mixed[at, :], w3[:, lanes])
            ost[at, lanes] = y.astype(BF16)
            vecs[:, lanes] += fold(y)
            vecs2[:, lanes] += fold(y * y)
        return carry

    vecs[...] = jnp.zeros((8, cin), F32)
    vecs2[...] = jnp.zeros((8, cin), F32)
    lax.fori_loop(0, nh, mix, 0, unroll=True)
    norm3 = Everywhere("s3")
    put(norm3.at, 0, total_row(vecs[...]))
    put(norm3.at, 8, total_row(vecs2[...]))
    norm3.start()

    def mix_products(t, carry):
        gram, sums = carry
        cells = mixed[line_rows(t), :]
        mix_t[t] = jnp.transpose(cells)
        ct_copy(t, 0).wait()
        ct_copy(t, 1).wait()
        return gram + dot(mix_t[t], cells), sums + fold(cells.astype(F32))

    gram, totals = lax.fori_loop(0, nh, mix_products, (jnp.zeros((wd, wd), F32), jnp.zeros((8, wd), F32)))
    mix_sum = total_row(totals)
    gram_high, gram_low = split_bf16(gram)
    acc_g[0, :, 0:cin] = dot(gram_high, w3[...]) + dot(gram_low, w3[...])
    w_step(5, 1)
    got = norm3.finish()
    mean3, scale3 = moments(get(got, 0, cin), get(got, 8, cin), wide(total, cin))
    grow3 = g3[...] * scale3
    half_a3 = 0.5 * grow3
    half_b3 = 0.5 * c3[...] - half_a3 * mean3

    step4 = (nw // 4) * nb
    blocks4 = 2 * LANES

    def dn_copy(t, c):
        return pltpu.make_async_copy(
            ctv.at[half_rows(t, c)], dn_hbm.at[line_rows(t), pl.ds(c * half, half)], sem_dn.at[c, t]
        )

    def dn_back(t, c):
        return pltpu.make_async_copy(
            dn_hbm.at[line_rows(t), pl.ds(c * half, half)], ctv.at[half_rows(t, c)], sem_back.at[c, t]
        )

    def grad_of(t):
        return jnp.concatenate([ctv[half_rows(t, 0), :], ctv[half_rows(t, 1), :]], axis=1)

    vecs[...] = jnp.zeros((8, cin), F32)
    vecs2[...] = jnp.zeros((8, cin), F32)

    def last(t, carry):
        for j in range(cin // blocks4):
            lanes = slice(j * blocks4, (j + 1) * blocks4)
            a3, b3 = half_a3[:, lanes], half_b3[:, lanes]

            def cells(u, carry):
                at = block_rows(t, u, step4)
                mask = wide(mb[at, :], blocks4)
                x = xv[at, lanes] * jnp.asarray(0.5, BF16)
                y = ost[at, lanes].astype(F32)
                arg = y * a3 + (b3 + x.astype(F32))
                bend = jnp.tanh(arg)
                rise = 1.0 + bend
                value = arg * rise
                ost[at, lanes] = value.astype(BF16) * mask
                side = j * blocks4 // half
                there = pl.ds(pl.multiple_of(side * rows + t * line + u * step4, nb), step4)
                inner = slice(j * blocks4 - side * half, (j + 1) * blocks4 - side * half)
                push = ctv[there, inner] * (mask * jnp.asarray(0.5, BF16))
                grad = push.astype(F32) * (rise + value * (1.0 - bend))
                ctv[there, inner] = grad.astype(BF16)
                sums, bends = carry
                return sums + fold(grad), bends + fold(grad * y)

            vecs[:, lanes], vecs2[:, lanes] = lax.fori_loop(
                0, line // step4, cells, (vecs[:, lanes], vecs2[:, lanes])
            )
        dn_copy(t, 0).start()
        dn_copy(t, 1).start()
        return carry

    lax.fori_loop(0, nh, last, 0)
    sum_grad = total_row(vecs[...])
    back3 = Everywhere("b3")
    put(rows16, 0, sum_grad)
    put(rows16, 8, scale3 * (total_row(vecs2[...]) - mean3 * sum_grad))
    back3.at[...] = rows16[...].astype(BF16)
    back3.start()

    w3p[...] = (w3[...].astype(F32) * grow3).astype(BF16)

    acc_c[...] = jnp.zeros((wd, cin), F32)

    def plain_back(t, carry):
        grad = grad_of(t)
        dm[line_rows(t), :] = dot_nt(grad, w3p[...])
        acc_c[...] += dot(mix_t[t], grad)
        return carry

    lax.fori_loop(0, nh, plain_back, 0)
    w_finish(5, 2)
    got = back3.finish()
    bias3, gain3 = get(got, 0, cin), get(got, 8, cin)
    put(small.at[0], 0, bias3)
    put(small.at[0], 8, gain3)
    all_wide = wide(total, cin)
    slant3 = scale3 * gain3 / all_wide
    level3 = bias3 / all_wide - mean3 * slant3
    fix = (w3[...].astype(F32) * slant3).astype(BF16)
    level_high, level_low = split_bf16(level3)
    levels = [jnp.broadcast_to(part, (16, cin)) for part in (level_high, level_low)]
    stack = dot_nt(jnp.concatenate([fix, *levels], axis=0), w3p[...])
    fix = stack[0:wd, :].astype(BF16)
    shift = stack[wd : wd + 1, :] + stack[wd + 16 : wd + 17, :]

    def back_mix(t, carry):
        at = line_rows(t)
        dm[at, :] = dm[at, :] - dot(mixed[at, :], fix) - mask_of(at, wd) * shift
        return carry

    lax.fori_loop(0, nh, back_mix, 0, unroll=True)

    step5 = 4 * nb
    sums5 = []
    for j in range(lane_blocks):
        lanes = slice(j * LANES, (j + 1) * LANES)

        def image_sums(t, carry):
            at = pl.ds(pl.multiple_of(t * step5, step5), step5)
            grad = dm[at, lanes]
            done = []
            for r in range(d.radix):
                own = slice(r * wd + j * LANES, r * wd + (j + 1) * LANES)
                a, b, c = carry[r]
                a = a + fold_images(grad * act2[at, own].astype(F32), nb)
                part = grad * slope2[at, own].astype(F32)
                b = b + fold_images(part, nb)
                c = c + fold_images(part * y2[at, own].astype(F32), nb)
                done.append((a, b, c))
            return tuple(done)

        sums5.append(lax.fori_loop(0, rows // step5, image_sums, ((zero, zero, zero),) * d.radix, unroll=7))
    pick = lambda which: jnp.concatenate(
        [sums5[j][r][which] for r in range(d.radix) for j in range(lane_blocks)], axis=1
    )
    q1, q3 = pick(1), pick(2)

    def dn_out(t, carry):
        dn_copy(t, 0).wait()
        dn_copy(t, 1).wait()
        return carry

    lax.fori_loop(0, nh, dn_out, 0)
    clear(dyp)
    ga_src[...] = pick(0).astype(BF16)
    ga_start, ga_finish = swap(ga_src, ga_buf, ssa.at[1], rsa.at[1], ha_peer, n_ha)
    ga_start()

    mix_column = jnp.transpose(jnp.broadcast_to(mix_sum, (LANES, wd)))
    for j in range(cin // LANES):
        lanes = slice(j * LANES, (j + 1) * LANES)
        c = 0 if j * LANES < half else 1
        grad = grow3[:, lanes] * (
            acc_c[:, lanes] - mix_column * level3[:, lanes] - acc_g[0, :, lanes] * slant3[:, lanes]
        )
        parts[2][c, :, j * LANES - c * half : (j + 1) * LANES - c * half] = grad.astype(BF16)
    w_start(2, 0)

    grad_att = ga_finish()
    weight = att[...]
    weighed = weight * grad_att
    both = weighed[:, 0:wd] + weighed[:, wd:]
    grad_logits = weight * (grad_att - jnp.concatenate([both, both], axis=1))
    grad_fc = add_thirds(dot_nt(thirds(grad_logits), wex[...])) * hidden_slope
    put(fc_src.at[1], 0, total_row(grad_fc))
    put(fc_src.at[1], 1, total_row(grad_fc * centered))
    pooled = pool / wide(floor, wd)
    put(fc_src.at[1], 2, total_row(pooled))
    fc_start, fc_finish = swap(fc_src.at[1], fc_buf.at[1], ssi.at[1], rsi.at[1], img_peer, n_img)
    fc_start()
    w_step(2, 0)
    grad_excite = dot_tn(hidden, grad_logits, HIGH)
    grad_bex = total_row(grad_logits) * (1.0 / n_ha)
    got = fc_finish()
    bias_s, gain_s = got[0:1, :], got[1:2, :]
    put(small.at[0], 16, bias_s)
    put(small.at[0], 17, gain_s)
    grad_squeezed = (gs[...] * scale_s) * (
        grad_fc - live_now * (bias_s + centered * gain_s) / images
    )
    grad_pool = add_thirds(dot_nt(thirds(grad_squeezed), wsq[...])) / wide(floor, wd)
    pool2 = jnp.concatenate([grad_pool] * d.radix, axis=1)
    sum_grad = total_row(weight * q1 + pool2 * q2[...])
    sum_bend = total_row(weight * q3 + pool2 * q4[...])
    back2 = Everywhere("b2")
    put(back2.at, 0, sum_grad)
    put(back2.at, 4, scale2 * (sum_bend - mean2 * sum_grad))
    back2.start()
    level = get(got, 2, wd) / wide(images, wd)
    grad_squeeze = dot_tn(pooled - level, grad_squeezed, HIGH)
    grow2 = g2[...] * scale2
    att[...] = weight * grow2
    q2[...] = pool2 * grow2
    def first_slopes(t, carry):
        at = pl.ds(pl.multiple_of(t * step1, step1), step1)
        _, slope = gate(y1[at, :] * half_a1 + half_b1)
        mixed[at, :] = (slope * mask_of(at, mid)).astype(BF16)
        return carry

    lax.fori_loop(0, rows // step1, first_slopes, 0)

    parts[4][0] = jnp.concatenate([grad_excite[:, 0:wd], grad_excite[:, wd:]], axis=0).astype(
        BF16
    ) * jnp.asarray(1.0 / n_ha, BF16)
    parts[4][1, :, 0 : d.inter] = grad_squeeze.astype(BF16)
    parts[4][1, :, d.inter :] = jnp.zeros((wd, wd - d.inter), BF16)
    w_start(4, 0)
    w_step(2, 1)
    acc_g[...] = jnp.zeros((d.radix, wd, 9 * gin), F32)
    mean_act1 = get(act_sum.finish(), 0, mid) / (wide(images, mid) * float(nh * n_ha * nw))
    w_step(4, 0)
    got = back2.finish()
    bias2, gain2 = get(got, 0, wide2), get(got, 4, wide2)
    put(small.at[0], 20, bias2)
    put(small.at[0], 24, gain2)
    slant2 = grow2 * scale2 * gain2 / wide(total, wide2)
    level2 = grow2 * bias2 / wide(total, wide2) - mean2 * slant2

    step6 = 2 * nb

    def back_group(t, carry):
        def cells(u, carry):
            at = block_rows(t, u, step6)
            to = inner_rows(t + 1, nb + u * step6, step6)
            again = step6 // nb
            grad = dm[at, :]
            mask = mask_of(at, wd)
            sums = []
            for r in range(d.radix):
                own = slice(r * wd, (r + 1) * wd)
                grow = jnp.concatenate([att[:, own]] * again, axis=0)
                lift = jnp.concatenate([q2[:, own]] * again, axis=0)
                push = (grow * grad + lift) * slope2[at, own].astype(F32)
                pull = mask * (level2[:, own] + slant2[:, own] * y2[at, own].astype(F32))
                dyp[to, own] = (push - pull).astype(BF16)
                sums.append(carry[r] + fold(push - pull))
            return tuple(sums)

        return lax.fori_loop(0, line // step6, cells, carry, unroll=7)

    zeros = jnp.zeros((8, wd), F32)
    sums2 = edges(back_group, (zeros,) * d.radix)
    halo2_start, halo2_recv, halo2_sent = halo(dyp, 1)
    halo2_start()
    sums2 = lax.fori_loop(1, nh - 1, back_group, sums2)
    sum_dy2 = [total_row(s) for s in sums2]
    misc = Everywhere("misc")
    put(misc.at, 0, jnp.concatenate(sum_dy2, axis=1))
    put(misc.at, 4, grad_bex)
    misc.start()
    w_step(2, 2)
    w_step(4, 1)

    def weights_group(t, carry):
        for r in range(d.radix):
            grad = jnp.transpose(dyp[inner_rows(t + 1), r * wd : (r + 1) * wd])
            acc_g[r] += dot(grad, taps(t, r))
        return carry

    lax.fori_loop(0, nh, weights_group, 0, unroll=True)

    def send_group(s, first, last):
        lanes = (last - first) * gin
        for r in range(d.radix):
            base = wide(mean_act1[:, r * gin : (r + 1) * gin], lanes)
            column = jnp.transpose(jnp.broadcast_to(sum_dy2[r], (LANES, wd)))
            grad = acc_g[r, :, first * gin : last * gin] - wide(column, lanes) * base
            parts[s][r, :, 0:lanes] = grad.astype(BF16)
        w_start(s, 0)

    send_group(1, 0, d.split)
    send_group(3, d.split, 9)
    w_step(2, 3)
    w_step(4, 2)

    pairs = nw // 2

    def back_taps(t, r, which):
        cells = []
        for ky in range(3):
            for e in which:
                block = dyp[inner_rows(t + 2 - ky, e * nb), r * wd : (r + 1) * wd]
                block = block.reshape(pairs, 2 * nb, wd)[:, 0:nb, :].reshape(pairs * nb, wd)
                cells.append(block)
        return jnp.concatenate(cells, axis=1)

    def transposed(t, carry):
        sums, bends = carry
        at = line_rows(t)
        done = []
        for r in range(d.radix):
            both = dot_nt(back_taps(t, r, (1, 2)), w2x[r])
            left = both[:, 0:gin] + dot_nt(back_taps(t, r, (0,)), w2l[r])
            right = both[:, gin:] + dot_nt(back_taps(t, r, (3,)), w2r[r])
            both = jnp.concatenate(
                [left.reshape(pairs, nb, gin), right.reshape(pairs, nb, gin)], axis=1
            )
            done.append(both.reshape(line, gin))
        dm[at, :] = jnp.concatenate(done, axis=1)

        def cells(u, carry):
            sums, bends = carry
            at = block_rows(t, u, step1)
            grad = dm[at, :] * mixed[at, :].astype(F32)
            dm[at, :] = grad
            mixed[at, :] = grad.astype(BF16)
            return sums + fold(grad), bends + fold(grad * y1[at, :])

        return lax.fori_loop(0, line // step1, cells, (sums, bends))

    zeros = jnp.zeros((8, mid), F32)
    middle = 1 + (nh - 2) // 3
    sums1 = lax.fori_loop(1, middle, transposed, (zeros, zeros))
    w_step(1, 0)
    w_step(3, 0)
    sums1 = lax.fori_loop(middle, nh - 1, transposed, sums1)
    w_step(4, 3)
    halo2_recv()
    sums1 = edges(transposed, sums1)
    sum_grad = total_row(sums1[0])
    back1 = Everywhere("b1")
    put(back1.at, 0, sum_grad)
    put(back1.at, 2, scale1 * (total_row(sums1[1]) - mean1 * sum_grad))
    back1.start()
    halo2_sent()

    def fetch_back(t, carry):
        dn_back(t, 0).start()
        dn_back(t, 1).start()
        return carry

    lax.fori_loop(0, nh, fetch_back, 0)

    acc_c[...] = jnp.zeros((wd, cin), F32)

    def first_weights(t, carry):
        at = line_rows(t)
        acc_c[...] += dot_tn(mixed[at, :], xv[at, :])
        return carry

    lax.fori_loop(0, nh, first_weights, 0, unroll=True)
    if d.inside:
        for c in range(2):
            parts[0][c] = acc_c[:, c * half : (c + 1) * half].astype(BF16)
    w_start(0, 0)
    w_step(1, 1)
    w_step(0, 0)
    w_step(3, 1)
    got = back1.finish()
    bias1, gain1 = get(got, 0, mid), get(got, 2, mid)
    grow1 = g1[...] * scale1
    bias_all, gain_all = bias1 / wide(total, mid), gain1 / wide(total, mid)
    slant1 = grow1 * scale1 * gain_all
    level1 = grow1 * bias_all - mean1 * slant1
    w_step(2, 4)
    w_step(4, 4)

    def back_first(t, carry):
        def cells(u, carry):
            at = block_rows(t, u, step1)
            pull = mask_of(at, mid) * (level1 + slant1 * y1[at, :])
            mixed[at, :] = (grow1 * dm[at, :] - pull).astype(BF16)
            return carry

        lax.fori_loop(0, line // step1, cells, 0)
        return carry

    lax.fori_loop(0, nh, back_first, 0)
    put(small.at[0], 32, bias1)
    put(small.at[0], 34, gain1)
    put(small.at[0], 36, mean_act1)
    small[0, 18:20, :] = jnp.zeros((2, LANES), F32)
    small[0, 38:40, :] = jnp.zeros((2, LANES), F32)
    small[0, 44:48, :] = jnp.zeros((4, LANES), F32)
    got = misc.finish()
    put(small.at[0], 28, get(got, 4, wide2))
    put(small.at[0], 40, get(got, 0, wide2))
    got = v0_sum.finish()
    for c in range(2):
        v0[c] = jnp.broadcast_to(get(got, 0, cin)[:, c * half : (c + 1) * half], (8, half))
    for j, vector in enumerate((grow1, bias_all, gain_all)):
        cols[j] = jnp.transpose(jnp.broadcast_to(vector, (LANES, mid)))

    def norm_terms(total, at, taken, flat):
        lanes = total.shape[1]
        grow, level, slant = (wide(cols[j, at, :], lanes) for j in range(3))
        return grow * (total - level * flat - slant * taken)

    def fix_first(total):
        return norm_terms(total, z_at(z_of, spot * plane_rows), vres[...], v0[core, 0:1, :])

    def grad_inputs(t, carry):
        at = line_rows(t)
        for c in range(2):
            lanes = slice(c * half, (c + 1) * half)
            dn_back(t, c).wait()
            grad = ctv[half_rows(t, c), :].astype(F32) + dot_nt(mixed[at, :], w1[lanes, :])
            xv[at, lanes] = grad.astype(BF16)
        return carry

    w_step(1, 2)
    lax.fori_loop(0, nh // 2, grad_inputs, 0)
    w_step(3, 2)
    w_step(0, 1)
    w_step(1, 3)
    w_step(3, 3)
    w_step(0, 2, fix_first)
    lax.fori_loop(nh // 2, nh, grad_inputs, 0)
    w_step(1, 4)
    w_step(0, 3)
    w_step(3, 4)
    w_step(0, 4)
    for s in (2, 4, 1, 3, 0):
        w_step(s, 5)
    if not d.inside:
        whole = slice(0, wd)
        for c in range(2):
            lanes = slice(c * half, (c + 1) * half)
            local = wide(cols[0, whole, :], half) * (
                acc_c[:, lanes]
                - wide(cols[1, whole, :], half) * get(v0_sum.at[...], 0, cin)[:, lanes]
                - wide(cols[2, whole, :], half) * parts[5][c].astype(F32)
            )
            parts[0][c] = local.astype(BF16)

    for s in range(d.sets + 1):
        w_sent(s)
    halo1_sent()
    if not d.inside:
        for s in range(d.sets):
            ress[s][...] = parts[s][...]


def call_block(d, args):
    f32, bf16 = F32, BF16
    cin, wd, mid, rows, nb, nh = d.cin, d.width, d.mid, d.rows, d.nb, d.nh
    vmem, dma = pltpu.VMEM, pltpu.SemaphoreType.DMA
    halves = [(2, wd, lanes) for lanes in d.half]
    shape = jax.ShapeDtypeStruct
    outs = [
        shape((rows, cin), bf16),
        vmem((rows, cin), bf16),
        vmem((rows, cin), bf16),
        *[vmem(s, bf16) for s in halves[: d.sets]],
        vmem((1, 48, LANES), f32),
    ]
    anywhere = pl.BlockSpec(memory_space=pl.ANY)
    inside = pl.BlockSpec(memory_space=pltpu.VMEM)
    plane, zed = wd // 4, wd // 16

    def sums_of(name, count):
        kind = bf16 if name in d.narrow else f32
        if not d.inside:
            return dict(
                src=vmem((count, LANES), kind),
                mid=vmem((count, LANES), f32),
                buf_ha=vmem((d.n_ha, count, LANES), kind),
                buf_img=vmem((d.n_img, count, LANES), f32),
                send_ha=dma((d.n_ha,)), recv_ha=dma((d.n_ha,)),
                send=dma((d.n_img,)), recv=dma((d.n_img,)),
            )
        if name in d.paired:
            return dict(
                src=vmem((count, LANES), kind),
                mid=vmem((count, LANES), f32),
                other=vmem((count, LANES), f32),
                buf=vmem((16, count, LANES), f32),
                send=dma((16,)), recv=dma((16,)),
            )
        return dict(
            src=vmem((count, LANES), kind),
            buf=vmem((32, count, LANES), kind),
            send=dma((32,)), recv=dma((32,)),
        )

    scratch = [
        vmem((cin, mid), bf16),
        vmem((d.radix, 9 * d.gin, wd), bf16),
        vmem((wd, cin), bf16),
        vmem((rows, LANES), bf16),
        vmem((nb, LANES), f32),
        vmem((max(2 * rows, (nh + 2) * d.padded), cin // 2), bf16),
        vmem((rows, mid), f32),
        vmem(((nh + 2) * d.padded, mid), bf16),
        vmem((rows, d.wide), bf16),
        vmem((rows, d.wide), bf16),
        vmem((rows, d.wide), bf16),
        vmem((rows, wd), bf16),
        vmem((rows, wd), f32),
        vmem((wd, cin), f32),
        vmem((d.radix, wd, 9 * d.gin), f32),
        vmem((wd, cin), bf16),
        vmem((d.radix, 2 * d.gin, 6 * wd), bf16),
        vmem((d.radix, d.gin, 3 * wd), bf16),
        vmem((d.radix, d.gin, 3 * wd), bf16),
        vmem((nh, wd, d.line), bf16),
        vmem((16, LANES), f32),
        vmem((nb, d.wide), f32),
        vmem((nb, d.wide), f32),
        vmem((nb, d.wide), f32),
        vmem((8, cin), f32),
        vmem((8, cin), f32),
        vmem((nb, wd), f32),
        vmem((2, 8, cin // 2), f32),
        vmem((3, mid, LANES), f32),
        [vmem(s, bf16) for s in halves],
        [vmem((wd, lanes), bf16) for lanes in d.half],
        [vmem((3, plane, lanes), bf16) for lanes in d.half],
        [vmem((3, zed, lanes), bf16) for lanes in d.half],
        [vmem((plane, lanes), bf16) for lanes in d.half],
        vmem((zed, d.half[0]), f32),
        {name: sums_of(name, count) for name, count in d.sums.items() if name not in d.shared},
        vmem((nb, d.wide), bf16),
        vmem((d.n_ha, nb, d.wide), bf16),
        vmem((nb, 2 * LANES), f32),
        vmem((d.n_ha, nb, 2 * LANES), f32),
        vmem((2, 4, LANES), f32),
        vmem((2, d.n_img, 4, LANES), f32),
        dma((3,)),
        dma((nh,)),
        dma((2, nh)),
        dma((2, nh)),
        dma((2, nh)),
        dma((2, d.n_ha)),
        dma((2, d.n_ha)),
        dma((2, d.n_img)),
        dma((2, d.n_img)),
        dma((2, 2)),
        dma((2, 2)),
        dma((6, 24)),
        dma((6, 24)),
    ]
    return pl.pallas_call(
        functools.partial(block_kernel, d),
        out_shape=outs,
        in_specs=[anywhere, anywhere, inside, pl.BlockSpec(memory_space=pltpu.SMEM)]
        + [anywhere, inside, inside, anywhere] + [inside] * 7 + [anywhere, inside, inside],
        out_specs=[anywhere] + [inside] * 8,
        scratch_shapes=scratch,
        name="block",
        compiler_params=pltpu.CompilerParams(
            collective_id=0, has_side_effects=True, vmem_limit_bytes=47 << 20
        ),
    )(*args)


def finish_kernel(
    d, out_in, gin_in, wg0, wg1, wg2, wg3, wg4, small,
    out, gin_hbm, gw1_hbm, gg1, gb1, gw2_hbm, gg2, gb2, gwsq, ggs, gbs, gwex, gbex, gw3_hbm, gg3, gb3,
    gw1, gw2, gw3, sem_out, sem_gw,
):
    wd = d.width
    parts = 4
    copies = [
        pltpu.make_async_copy(src.at[at], dst.at[at], sem_out.at[which, t])
        for which, (src, dst) in enumerate(((out_in, out), (gin_in, gin_hbm)))
        for t in range(parts)
        for at in (pl.ds(t * (d.rows // parts), d.rows // parts),)
    ]
    for copy in copies:
        copy.start()
    stores = [
        pltpu.make_async_copy(src, dst, sem_gw.at[j])
        for j, (src, dst) in enumerate(((gw1, gw1_hbm), (gw3, gw3_hbm), (gw2, gw2_hbm)))
    ]

    def weights(step):
        half = d.cin // 2
        if step < 2:
            gw1[step * half : (step + 1) * half, :] = jnp.transpose(wg0[step]).astype(F32)
            gw3[:, step * half : (step + 1) * half] = wg2[step].astype(F32)
        elif step < 4:
            r = step - 2
            rows = small[0]
            mean = get(rows, 36, d.mid)[:, r * d.gin : (r + 1) * d.gin]
            taken = get(rows, 40, d.wide)[:, r * wd : (r + 1) * wd]
            mean = jnp.transpose(jnp.broadcast_to(mean, (LANES, d.gin)))
            back = wide(mean, wd) * taken
            for tap in range(9):
                held, first = (wg1, 0) if tap < d.split else (wg3, d.split)
                cells = held[r, :, (tap - first) * d.gin : (tap - first + 1) * d.gin]
                gw2[r, tap] = jnp.transpose(cells).astype(F32) + back
        elif step == 4:
            cells = wg4[0].astype(F32)
            gwex[:, 0:wd] = cells[0 : d.inter, :]
            gwex[:, wd:] = cells[d.inter :, :]
            gwsq[...] = wg4[1, :, 0 : d.inter].astype(F32)
            rows = small[0]
            gb3[...] = get(rows, 0, d.cin)
            gg3[...] = get(rows, 8, d.cin)
            gbs[...] = rows[16:17, :]
            ggs[...] = rows[17:18, :]
            gb2[...] = get(rows, 20, d.wide)
            gg2[...] = get(rows, 24, d.wide)
            gbex[...] = get(rows, 28, d.wide)
            gb1[...] = get(rows, 32, d.mid)
            gg1[...] = get(rows, 34, d.mid)

    for t in range(5):
        weights(t)
        if t == 1:
            stores[0].start()
            stores[1].start()
        elif t == 3:
            stores[2].start()
    for copy in stores + copies:
        copy.wait()


def call_finish(d, *args):
    shape = jax.ShapeDtypeStruct
    cin, wd, mid = d.cin, d.width, d.mid
    vmem, dma = pltpu.VMEM, pltpu.SemaphoreType.DMA
    small_dims = [
        (cin, mid), (1, mid), (1, mid), (d.radix, 9, d.gin, wd), (1, d.wide), (1, d.wide), (wd, d.inter),
        (1, d.inter), (1, d.inter), (d.inter, d.wide), (1, d.wide), (wd, cin), (1, cin), (1, cin),
    ]
    anywhere = pl.BlockSpec(memory_space=pl.ANY)
    inside = pl.BlockSpec(memory_space=pltpu.VMEM)
    return pl.pallas_call(
        functools.partial(finish_kernel, d),
        out_shape=[shape((d.rows, cin), BF16), shape((d.rows, cin), BF16)]
        + [shape(s, F32) for s in small_dims],
        in_specs=[inside] * 8,
        out_specs=[anywhere] * 3 + [inside] * 2 + [anywhere] + [inside] * 7 + [anywhere] + [inside] * 2,
        scratch_shapes=[
            vmem((cin, mid), F32), vmem((d.radix, 9, d.gin, wd), F32), vmem((wd, cin), F32),
            dma((2, 4)), dma((3,)),
        ],
        name="finish",
        compiler_params=pltpu.CompilerParams(vmem_limit_bytes=16 << 20),
    )(*[pltpu.with_memory_space_constraint(arg, pltpu.VMEM) for arg in args])


def on_device(
    inputs, image_count, pixel_mask, w_first, gain_first, bias_first, w_group, gain_group, bias_group,
    w_squeeze, gain_squeeze, bias_squeeze, w_excite, bias_excite, w_last, gain_last, bias_last, cotangent,
):
    n_img, n_ha = lax.axis_size("img"), lax.axis_size("ha")
    d = Dims(n_img, n_ha, inputs.shape, w_group.shape, w_squeeze.shape)
    nb, nh, nw, cin = inputs.shape

    def by_rows(cells):
        return jnp.transpose(cells, (1, 2, 0, 3)).reshape(d.rows, cin)

    def by_image(cells):
        return jnp.transpose(cells.reshape(nh, nw, nb, cin), (2, 0, 1, 3))

    row = lambda v: v.reshape(1, -1)
    args = (
        by_rows(inputs), by_rows(cotangent), jnp.transpose(pixel_mask, (1, 0, 2)), image_count,
        w_first, row(gain_first), row(bias_first),
        w_group.reshape(d.radix, 9 * d.gin, d.width), row(gain_group), row(bias_group),
        w_squeeze, row(gain_squeeze), row(bias_squeeze), w_excite, row(bias_excite),
        w_last, row(gain_last), row(bias_last),
    )
    _, out, gin, *sets, small = call_block(d, args)
    if not d.inside:
        sets = lax.psum(sets, ("img", "ha"))
    done = call_finish(d, out, gin, *sets, small)
    (out, gin, gw1, gg1, gb1, gw2, gg2, gb2, gwsq, ggs, gbs, gwex, gbex, gw3, gg3, gb3) = done
    flat = lambda v: v.reshape(-1)
    return (
        by_image(out), by_image(gin), gw1, flat(gg1), flat(gb1), gw2.reshape(w_group.shape), flat(gg2), flat(gb2),
        gwsq, flat(ggs), flat(gbs), gwex, flat(gbex), gw3, flat(gg3), flat(gb3),
    )


def solution(mesh):
    cells = P("img", "ha", None, None)
    placed = (cells, P("img"), P("img", "ha", None)) + (P(),) * 14 + (cells,)
    return jax.shard_map(
        on_device,
        mesh=mesh,
        in_specs=placed,
        out_specs=(cells, cells) + (P(),) * 14,
        check_vma=False,
    )
```

```python
import functools

import jax
import jax.numpy as jnp
from jax import lax
from jax.experimental import pallas as pl
from jax.experimental.pallas import tpu as pltpu
from jax.sharding import PartitionSpec as P

EPS = 1e-05
F32 = jnp.float32
BF16 = jnp.bfloat16
HIGH = lax.Precision.HIGHEST
MESH = pl.DeviceIdType.MESH
LANES = 128


def dot(a, b, precision=None):
    return jnp.dot(a, b, preferred_element_type=F32, precision=precision)


def dot_nt(a, b, precision=None):
    return lax.dot_general(
        a, b, (((1,), (1,)), ((), ())), preferred_element_type=F32, precision=precision
    )


def dot_tn(a, b, precision=None):
    return lax.dot_general(
        a, b, (((0,), (0,)), ((), ())), preferred_element_type=F32, precision=precision
    )


def wide(cell, lanes):
    return jnp.concatenate([cell] * (lanes // LANES), axis=1)


def fold(cells):
    rows, lanes = cells.shape
    return jnp.sum(cells.reshape(rows // 8, 8, lanes), axis=0)


def fold_images(cells, images):
    rows, lanes = cells.shape
    return jnp.sum(cells.reshape(rows // images, images, lanes), axis=0)


def total_row(cells):
    return jnp.sum(cells, axis=0, keepdims=True)


def put(ref, row, vector):
    for j in range(vector.shape[1] // LANES):
        ref[row + j : row + j + 1, :] = vector[:, j * LANES : (j + 1) * LANES]


def get(cells, row, lanes):
    return jnp.concatenate(
        [cells[row + j : row + j + 1, :] for j in range(lanes // LANES)], axis=1
    )


def moments(sums, squares, total):
    mean = sums / total
    spread = squares / total - mean * mean
    return mean, lax.rsqrt(spread + EPS)


def gate(half):
    bend = jnp.tanh(half)
    rise = 1.0 + bend
    value = half * rise
    return value, 0.5 * (rise + value * (1.0 - bend))


def split_bf16(cells):
    high = cells.astype(BF16)
    return high, (cells - high.astype(F32)).astype(BF16)


def thirds(cells):
    high = cells.astype(BF16)
    rest = cells - high.astype(F32)
    middle = rest.astype(BF16)
    return jnp.concatenate([high, middle, (rest - middle.astype(F32)).astype(BF16)], axis=0)


def add_thirds(cells):
    rows = cells.shape[0] // 3
    return cells[0:rows] + cells[rows : 2 * rows] + cells[2 * rows :]


class Dims:
    def __init__(self, n_img, n_ha, inputs, w_group, w_squeeze):
        self.n_img, self.n_ha = n_img, n_ha
        self.nb, self.nh, self.nw, self.cin = inputs
        self.radix, _, _, self.gin, self.width = w_group
        self.mid = self.radix * self.gin
        self.wide = self.radix * self.width
        self.inter = w_squeeze[1]
        self.line = self.nw * self.nb
        self.rows = self.nh * self.line
        self.padded = (self.nw + 2) * self.nb
        self.split = 5
        self.half = (self.cin // 2, 5 * self.gin, self.cin // 2, 4 * self.gin, self.width, self.cin // 2)
        self.sets = 5
        self.inside = n_img == 8 and n_ha == 4
        self.sums = dict(cnt=4, s1=4, s2=8, act=4, v0=8, s3=16, b3=16, b2=8, misc=8, b1=4)
        self.paired = ("s3",)
        self.narrow = ("b3",)
        self.shared = dict(b1="s1", b2="s2")


def block_kernel(
    d,
    x_hbm, ct_hbm, mask_in, count_in, w1_hbm, g1, c1, w2_hbm, g2, c2, wsq, gs, cs, wex, bex, w3_hbm, g3, c3,
    dn_hbm, ost, xv, wg0, wg1, wg2, wg3, wg4, small,
    w1, w2, w3, mb, live, ctv, y1, a1p, y2, act2, slope2, mixed, dm, acc_c, acc_g, w3p, w2x, w2l, w2r,
    mix_t, rows16, att, q2, q4, vecs, vecs2, pools, v0, cols,
    parts, rcs, rxys, rzs, mids, vres, sums, ga_src, ga_buf, pf_src, pf_buf, fc_src, fc_buf,
    sem_w, sem_x, sem_ct, sem_dn, sem_back, ssa, rsa, ssi, rsi, ssh, rsh, ssw, rsw,
):
    n_img, n_ha = d.n_img, d.n_ha
    nb, nh, nw = d.nb, d.nh, d.nw
    cin, mid, wd, wide2, line, rows = d.cin, d.mid, d.width, d.wide, d.line, d.rows
    gin, padded = d.gin, d.padded
    dyp = ctv
    ress = (wg0, wg1, wg2, wg3, wg4)
    half = cin // 2
    i = lax.axis_index("img")
    h = lax.axis_index("ha")

    def ha_peer(k):
        return (i, lax.rem(h + k, n_ha))

    def img_peer(k):
        return (lax.rem(i + k, n_img), h)

    z_of, x_of, y_of, core = i // 2, lax.rem(i, 2), h // 2, lax.rem(h, 2)
    spot = x_of * 2 + y_of

    def core_peer():
        return (i, y_of * 2 + (1 - core))

    def plane_peer(k):
        other = lax.rem(spot + k, 4)
        return (z_of * 2 + other // 2, lax.rem(other, 2) * 2 + core)

    def z_peer(k):
        return (lax.rem(z_of + k, 4) * 2 + x_of, h)

    def any_peer(k):
        return (lax.rem(i + k // 4, 8), lax.rem(h + k % 4, 4))

    def chip_peer(k):
        return (lax.rem(i + k // 2, 8), lax.rem(y_of + k % 2, 2) * 2 + core)

    def remote(src, dst, send, recv, peer):
        return pltpu.make_async_remote_copy(
            src_ref=src, dst_ref=dst, send_sem=send, recv_sem=recv, device_id=peer, device_id_type=MESH
        )

    def line_rows(t):
        return pl.ds(pl.multiple_of(t * line, line), line)

    def block_rows(t, u, step):
        return pl.ds(pl.multiple_of(t * line + u * step, nb), step)

    def x_copy(t):
        return pltpu.make_async_copy(x_hbm.at[line_rows(t)], xv.at[line_rows(t)], sem_x.at[t])

    def half_rows(t, c):
        return pl.ds(pl.multiple_of(c * rows + t * line, nb), line)

    def ct_copy(t, c):
        return pltpu.make_async_copy(
            ct_hbm.at[line_rows(t), pl.ds(c * half, half)], ctv.at[half_rows(t, c)], sem_ct.at[c, t]
        )

    def start_inputs(t, carry):
        x_copy(t).start()
        return carry

    loads = [
        pltpu.make_async_copy(src, dst, sem_w.at[j])
        for j, (src, dst) in enumerate(((w1_hbm, w1), (w2_hbm, w2), (w3_hbm, w3)))
    ]
    loads[0].start()
    lax.fori_loop(0, nh, start_inputs, 0)
    loads[1].start()
    loads[2].start()

    barrier = pltpu.get_barrier_semaphore()
    if d.inside:
        peers = [any_peer(k) for k in range(1, 32)]
    else:
        peers = [ha_peer(k) for k in range(1, n_ha)] + [img_peer(k) for k in range(1, n_img)]
    for peer in peers:
        pl.semaphore_signal(barrier, inc=1, device_id=peer, device_id_type=MESH)

    slots = lax.broadcasted_iota(jnp.int32, (nb, LANES), 0)
    live[...] = (slots < count_in[0]).astype(F32)

    def spread(t, carry):
        cells = mask_in[t].astype(F32)
        alive = live[...]
        for w in range(nw):
            cell = jnp.broadcast_to(cells[:, w : w + 1], (nb, LANES)) * alive
            mb[block_rows(t, w, nb), :] = cell.astype(BF16)
            carry = carry + cell
        return carry

    pixels = lax.fori_loop(0, nh, spread, jnp.zeros((nb, LANES), F32))

    def mask_of(at, lanes):
        return wide(mb[at, :].astype(F32), lanes)

    def inner_rows(t, at=nb, count=line):
        return pl.ds(pl.multiple_of(t * padded + at, nb), count)

    def clear(ref):
        zero = jnp.zeros((nb, ref.shape[1]), BF16)

        def body(t, carry):
            ref[inner_rows(t, 0, nb), :] = zero
            ref[inner_rows(t, nb + line, nb), :] = zero
            return carry

        lax.fori_loop(0, nh + 2, body, 0)

        def edge(t, carry):
            ref[inner_rows(0, t * nb, nb), :] = zero
            ref[inner_rows(nh + 1, t * nb, nb), :] = zero
            return carry

        lax.fori_loop(0, nw + 2, edge, 0)

    clear(a1p)

    def swap(src, buf, send, recv, peer, n):
        def copy(k):
            return remote(src, buf.at[k], send.at[k], recv.at[k], peer(k))

        def each(act, carry):
            if n > 32:
                return lax.fori_loop(1, n, act, carry)
            for k in range(1, n):
                carry = act(k, carry)
            return carry

        def begin(k, carry):
            copy(k).start()
            return carry

        def sent(k, carry):
            copy(k).wait_send()
            return carry

        def take(k, carry):
            copy(k).wait_recv()
            return carry + buf[k].astype(F32)

        def finish():
            total = each(take, src[...].astype(F32))
            each(sent, 0)
            return total

        return (lambda: each(begin, 0)), finish

    class Everywhere:
        def __init__(self, name):
            refs = sums[d.shared.get(name, name)]
            self.at = refs["src"]
            self.refs = refs
            if not d.inside:
                return
            send, recv = refs["send"], refs["recv"]
            if name in d.paired:
                self.pair = remote(self.at, refs["other"], send.at[0], recv.at[0], core_peer())
                self.start_far, self.finish_far = swap(refs["mid"], refs["buf"], send, recv, chip_peer, 16)
            else:
                self.pair = None
                self.start_far, self.finish_far = swap(self.at, refs["buf"], send, recv, any_peer, 32)

        def start(self):
            if d.inside:
                if self.pair is not None:
                    self.pair.start()
                    self.pair.wait_recv()
                    self.refs["mid"][...] = self.at[...] + self.refs["other"][...]
                self.start_far()

        def finish(self):
            if d.inside:
                total = self.finish_far()
                if self.pair is not None:
                    self.pair.wait_send()
                return total
            refs = self.refs
            start, finish = swap(self.at, refs["buf_ha"], refs["send_ha"], refs["recv_ha"], ha_peer, n_ha)
            start()
            refs["mid"][...] = finish()
            start, finish = swap(refs["mid"], refs["buf_img"], refs["send"], refs["recv"], img_peer, n_img)
            start()
            return finish()

    def halo(ref, at):
        def down():
            return remote(
                ref.at[inner_rows(nh)], ref.at[inner_rows(0)], ssh.at[at, 0], rsh.at[at, 0],
                (i, jnp.minimum(h + 1, n_ha - 1)),
            )

        def up():
            return remote(
                ref.at[inner_rows(1)], ref.at[inner_rows(nh + 1)], ssh.at[at, 1], rsh.at[at, 1],
                (i, jnp.maximum(h - 1, 0)),
            )

        def start():
            @pl.when(h < n_ha - 1)
            def _():
                down().start()

            @pl.when(h > 0)
            def _():
                up().start()

        def wait_recv():
            @pl.when(h > 0)
            def _():
                down().wait_recv()

            @pl.when(h < n_ha - 1)
            def _():
                up().wait_recv()

        def wait_send():
            @pl.when(h < n_ha - 1)
            def _():
                down().wait_send()

            @pl.when(h > 0)
            def _():
                up().wait_send()

        return start, wait_recv, wait_send

    plane_rows, z_rows = wd // 4, wd // 16

    def plane_at(other):
        return pl.ds(pl.multiple_of(other * plane_rows, plane_rows), plane_rows)

    def z_at(other, base=0):
        return pl.ds(pl.multiple_of(base + other * z_rows, z_rows), z_rows)

    def w_copy(s, stage, k):
        sem = (s, stage * 4 + k)
        if stage == 0:
            src, dst, peer = parts[s].at[1 - core], rcs[s], core_peer()
        elif stage == 1:
            src = parts[s].at[core, plane_at(lax.rem(spot + k, 4))]
            dst, peer = rxys[s].at[k - 1], plane_peer(k)
        elif stage == 2:
            src = mids[s].at[z_at(lax.rem(z_of + k, 4))]
            dst, peer = rzs[s].at[k - 1], z_peer(k)
        elif stage == 3:
            src = dst = ress[s].at[core, z_at(z_of, spot * plane_rows)]
            peer = z_peer(k)
        elif stage == 4:
            src = dst = ress[s].at[core, plane_at(spot)]
            peer = plane_peer(k)
        else:
            src = dst = ress[s].at[core]
            peer = core_peer()
        return remote(src, dst, ssw.at[sem], rsw.at[sem], peer)

    def w_ks(stage):
        return (1,) if stage in (0, 5) else (1, 2, 3)

    def w_arrival(s, stage, k):
        sem = (s, stage * 4 + k)
        if stage == 3:
            dst = ress[s].at[core, z_at(lax.rem(z_of - k + 4, 4), spot * plane_rows)]
        elif stage == 4:
            dst = ress[s].at[core, plane_at(lax.rem(spot - k + 4, 4))]
        else:
            dst = ress[s].at[1 - core]
        return remote(dst, dst, ssw.at[sem], rsw.at[sem], core_peer())

    def w_start(s, stage):
        if d.inside:
            for k in w_ks(stage):
                w_copy(s, stage, k).start()

    def w_finish(s, stage, fix=None):
        if not d.inside:
            return
        for k in w_ks(stage):
            if stage <= 2:
                w_copy(s, stage, k).wait_recv()
            else:
                w_arrival(s, stage, k).wait_recv()
        part, inner = parts[s], mids[s]
        if stage == 0:
            rc = rcs[s]

            def add(t, carry):
                at = pl.ds(pl.multiple_of(t * 16, 16), 16)
                part[core, at, :] = (part[core, at, :].astype(F32) + rc[at, :].astype(F32)).astype(BF16)
                return carry

            lax.fori_loop(0, wd // 16, add, 0)
        elif stage == 1:
            buf = rxys[s]

            def add(t, carry):
                at = pl.ds(pl.multiple_of(t * 16, 16), 16)
                own = pl.ds(pl.multiple_of(spot * plane_rows + t * 16, 16), 16)
                total = part[core, own, :].astype(F32)
                for k in range(3):
                    total = total + buf[k, at, :].astype(F32)
                inner[at, :] = total.astype(BF16)
                return carry

            lax.fori_loop(0, plane_rows // 16, add, 0)
        elif stage == 2:
            buf = rzs[s]
            total = inner[z_at(z_of), :].astype(F32)
            for k in range(3):
                total = total + buf[k].astype(F32)
            if s >= d.sets:
                vres[...] = total
                return
            if fix is not None:
                total = fix(total)
            ress[s][core, z_at(z_of, spot * plane_rows), :] = total.astype(BF16)

    def w_step(s, stage, fix=None):
        w_finish(s, stage, fix)
        if stage < 5:
            w_start(s, stage + 1)

    def w_sent(s):
        if d.inside:
            for stage in range(6 if s < d.sets else 3):
                for k in w_ks(stage):
                    w_copy(s, stage, k).wait_send()

    def first(t, carry):
        sums, squares = carry
        x_copy(t).wait()
        ct_copy(t, 0).start()
        ct_copy(t, 1).start()
        at = line_rows(t)
        y = dot(xv[at, :], w1[...])
        y1[at, :] = y
        masked = y * mask_of(at, mid)
        return sums + fold(masked), squares + fold(masked * y)

    loads[0].wait()
    zeros = jnp.zeros((8, mid), F32)
    sums0 = lax.fori_loop(0, nh // 2, first, (zeros, zeros))
    pl.semaphore_wait(barrier, len(peers))
    count = Everywhere("cnt")
    count.at[...] = jnp.zeros((4, LANES), F32)
    count.at[0:1, :] = total_row(pixels)
    count.at[1:2, :] = total_row(live[...]) * (1.0 / n_ha)
    count.start()
    totals, squares = lax.fori_loop(nh // 2, nh, first, sums0)
    norm1 = Everywhere("s1")
    put(norm1.at, 0, total_row(totals))
    put(norm1.at, 2, total_row(squares))
    norm1.start()
    loads[1].wait()
    loads[2].wait()
    for r in range(d.radix):
        for ky in range(3):
            for e in range(4):
                if e <= 2:
                    left = w2[r, (ky * 3 + 2 - e) * gin : (ky * 3 + 3 - e) * gin, :]
                if e >= 1:
                    right = w2[r, (ky * 3 + 3 - e) * gin : (ky * 3 + 4 - e) * gin, :]
                if e == 0:
                    w2l[r, :, ky * wd : (ky + 1) * wd] = left
                elif e == 3:
                    w2r[r, :, ky * wd : (ky + 1) * wd] = right
                else:
                    lanes = slice((ky * 2 + e - 1) * wd, (ky * 2 + e) * wd)
                    w2x[r, 0:gin, lanes] = left
                    w2x[r, gin:, lanes] = right
    got = count.finish()
    total, images = got[0:1, :], got[1:2, :]
    got = norm1.finish()
    mean1, scale1 = moments(get(got, 0, mid), get(got, 2, mid), wide(total, mid))
    half_a1 = 0.5 * g1[...] * scale1
    half_b1 = 0.5 * c1[...] - half_a1 * mean1

    step1 = 4 * nb

    def act_first(t, carry):
        def cells(u, carry):
            at = block_rows(t, u, step1)
            value, _ = gate(y1[at, :] * half_a1 + half_b1)
            value = value * mask_of(at, mid)
            a1p[inner_rows(t + 1, nb + u * step1, step1), :] = value.astype(BF16)
            return carry + fold(value)

        return lax.fori_loop(0, line // step1, cells, carry, unroll=True)

    def edges(body, carry):
        return lax.fori_loop(0, 2, lambda t, c: body(t * (nh - 1), c), carry)

    totals = edges(act_first, jnp.zeros((8, mid), F32))
    halo1_start, halo1_recv, halo1_sent = halo(a1p, 0)
    halo1_start()
    totals = lax.fori_loop(1, nh - 1, act_first, totals)
    act_sum = Everywhere("act")
    act_sum.at[...] = jnp.zeros((4, LANES), F32)
    put(act_sum.at, 0, total_row(totals))
    act_sum.start()

    def taps(t, r, first=0, last=9):
        return jnp.concatenate(
            [
                a1p[inner_rows(t + tap // 3, (tap % 3) * nb), r * gin : (r + 1) * gin]
                for tap in range(first, last)
            ],
            axis=1,
        )

    def group(t, carry):
        at = line_rows(t)
        mask = mask_of(at, wd)
        done = []
        for r in range(d.radix):
            sums, squares = carry[r]
            y = dot(taps(t, r), w2[r])
            y2[at, r * wd : (r + 1) * wd] = y.astype(BF16)
            masked = y * mask
            done.append((sums + fold(masked), squares + fold(masked * y)))
        return tuple(done)

    zeros = jnp.zeros((8, wd), F32)
    sums2 = lax.fori_loop(1, nh - 1, group, ((zeros, zeros),) * d.radix, unroll=True)
    halo1_recv()
    sums2 = edges(group, sums2)
    norm2 = Everywhere("s2")
    put(norm2.at, 0, jnp.concatenate([total_row(s) for s, _ in sums2], axis=1))
    put(norm2.at, 4, jnp.concatenate([total_row(q) for _, q in sums2], axis=1))
    norm2.start()

    acc_c[...] = jnp.zeros((wd, cin), F32)
    vecs[...] = jnp.zeros((8, cin), F32)

    def norm_products(t, carry):
        at = line_rows(t)
        mask = mask_of(at, mid)
        hat = ((y1[at, :] - mean1) * scale1 * mask).astype(BF16)
        x = xv[at, :]
        acc_c[...] += dot_tn(hat, x)
        vecs[...] += dot_tn(mb[at, :], x)[0:8, :]
        return carry

    lax.fori_loop(0, nh, norm_products, 0)
    norm2_done = norm2.finish()
    for c in range(2):
        parts[5][c] = acc_c[:, c * half : (c + 1) * half].astype(BF16)
    w_start(5, 0)
    v0_sum = Everywhere("v0")
    put(v0_sum.at, 0, vecs[0:1, :])
    v0_sum.start()
    mean2, scale2 = moments(get(norm2_done, 0, wide2), get(norm2_done, 4, wide2), wide(total, wide2))
    half_a2 = 0.5 * g2[...] * scale2
    half_b2 = 0.5 * c2[...] - half_a2 * mean2

    lane_blocks = wd // LANES
    step2 = (nw // 2) * nb
    zero = jnp.zeros((nb, LANES), F32)
    for j in range(lane_blocks):
        own = slice(j * LANES, (j + 1) * LANES)

        def act_group(t, pool):
            at = pl.ds(pl.multiple_of(t * step2, step2), step2)
            mask = mb[at, :]
            full = mask.astype(F32)
            for r in range(d.radix):
                lanes = slice(r * wd + j * LANES, r * wd + (j + 1) * LANES)
                value, _ = gate(y2[at, lanes].astype(F32) * half_a2[:, lanes] + half_b2[:, lanes])
                value = value * full
                act2[at, lanes] = value.astype(BF16)
                pool = pool + fold_images(value, nb)
            return pool

        pools[:, own] = lax.fori_loop(0, rows // step2, act_group, zero)

    pool = pools[...]
    pf_src[:, 0 : d.inter] = add_thirds(dot(thirds(pool), wsq[...]))
    pf_src[:, d.inter :] = pixels
    pf_start, pf_finish = swap(pf_src, pf_buf, ssa.at[0], rsa.at[0], ha_peer, n_ha)
    pf_start()

    def slopes(block):
        lanes = slice(block * LANES, (block + 1) * LANES)
        ha2, hb2 = half_a2[:, lanes], half_b2[:, lanes]

        def body(t, carry):
            slopes, bends = carry
            at = pl.ds(pl.multiple_of(t * step2, step2), step2)
            y = y2[at, lanes].astype(F32)
            _, slope = gate(y * ha2 + hb2)
            slope = slope * mb[at, :].astype(F32)
            slope2[at, lanes] = slope.astype(BF16)
            return slopes + fold_images(slope, nb), bends + fold_images(slope * y, nb)

        q2[:, lanes], q4[:, lanes] = lax.fori_loop(0, rows // step2, body, (zero, zero))

    total_blocks = d.radix * lane_blocks
    for block in range(total_blocks // 4):
        slopes(block)
    w_step(5, 0)
    both = pf_finish()
    floor = jnp.maximum(both[:, d.inter :], 1.0)
    squeezed = both[:, 0 : d.inter] / floor
    live_now = live[...]
    fc_src[...] = jnp.zeros(fc_src.shape, F32)
    put(fc_src.at[0], 0, total_row(squeezed * live_now))
    put(fc_src.at[0], 1, total_row(squeezed * squeezed * live_now))
    fc_start, fc_finish = swap(fc_src.at[0], fc_buf.at[0], ssi.at[0], rsi.at[0], img_peer, n_img)
    fc_start()
    for block in range(total_blocks // 4, total_blocks):
        slopes(block)
    got = fc_finish()
    mean_s, scale_s = moments(got[0:1, :], got[1:2, :], images)
    centered = (squeezed - mean_s) * scale_s
    hidden, hidden_slope = gate(0.5 * (centered * gs[...] + cs[...]))
    logits = add_thirds(dot(thirds(hidden), wex[...])) + bex[...]
    gap = logits[:, 0:wd] - logits[:, wd:]
    att[:, 0:wd] = jax.nn.sigmoid(gap)
    att[:, wd:] = jax.nn.sigmoid(-gap)

    step3 = 2 * nb

    def mix(t, carry):
        def cells(u, carry):
            at = block_rows(t, u, step3)
            weight = jnp.concatenate([att[...]] * (step3 // nb), axis=0)
            both = act2[at, :].astype(F32) * weight
            mixed[at, :] = (both[:, 0:wd] + both[:, wd:]).astype(BF16)
            return carry

        lax.fori_loop(0, line // step3, cells, 0, unroll=7)
        at = line_rows(t)
        for c in range(2):
            lanes = slice(c * half, (c + 1) * half)
            y = dot(mixed[at, :], w3[:, lanes])
            ost[at, lanes] = y.astype(BF16)
            vecs[:, lanes] += fold(y)
            vecs2[:, lanes] += fold(y * y)
        return carry

    vecs[...] = jnp.zeros((8, cin), F32)
    vecs2[...] = jnp.zeros((8, cin), F32)
    lax.fori_loop(0, nh, mix, 0, unroll=True)
    norm3 = Everywhere("s3")
    put(norm3.at, 0, total_row(vecs[...]))
    put(norm3.at, 8, total_row(vecs2[...]))
    norm3.start()

    def mix_products(t, carry):
        gram, sums = carry
        cells = mixed[line_rows(t), :]
        mix_t[t] = jnp.transpose(cells)
        ct_copy(t, 0).wait()
        ct_copy(t, 1).wait()
        return gram + dot(mix_t[t], cells), sums + fold(cells.astype(F32))

    gram, totals = lax.fori_loop(0, nh, mix_products, (jnp.zeros((wd, wd), F32), jnp.zeros((8, wd), F32)))
    mix_sum = total_row(totals)
    gram_high, gram_low = split_bf16(gram)
    acc_g[0, :, 0:cin] = dot(gram_high, w3[...]) + dot(gram_low, w3[...])
    w_step(5, 1)
    got = norm3.finish()
    mean3, scale3 = moments(get(got, 0, cin), get(got, 8, cin), wide(total, cin))
    grow3 = g3[...] * scale3
    half_a3 = 0.5 * grow3
    half_b3 = 0.5 * c3[...] - half_a3 * mean3

    step4 = (nw // 4) * nb
    blocks4 = 2 * LANES

    def dn_copy(t, c):
        return pltpu.make_async_copy(
            ctv.at[half_rows(t, c)], dn_hbm.at[line_rows(t), pl.ds(c * half, half)], sem_dn.at[c, t]
        )

    def dn_back(t, c):
        return pltpu.make_async_copy(
            dn_hbm.at[line_rows(t), pl.ds(c * half, half)], ctv.at[half_rows(t, c)], sem_back.at[c, t]
        )

    def grad_of(t):
        return jnp.concatenate([ctv[half_rows(t, 0), :], ctv[half_rows(t, 1), :]], axis=1)

    vecs[...] = jnp.zeros((8, cin), F32)
    vecs2[...] = jnp.zeros((8, cin), F32)

    def last(t, carry):
        for j in range(cin // blocks4):
            lanes = slice(j * blocks4, (j + 1) * blocks4)
            a3, b3 = half_a3[:, lanes], half_b3[:, lanes]

            def cells(u, carry):
                at = block_rows(t, u, step4)
                mask = wide(mb[at, :], blocks4)
                x = xv[at, lanes] * jnp.asarray(0.5, BF16)
                y = ost[at, lanes].astype(F32)
                arg = y * a3 + (b3 + x.astype(F32))
                bend = jnp.tanh(arg)
                rise = 1.0 + bend
                value = arg * rise
                ost[at, lanes] = value.astype(BF16) * mask
                side = j * blocks4 // half
                there = pl.ds(pl.multiple_of(side * rows + t * line + u * step4, nb), step4)
                inner = slice(j * blocks4 - side * half, (j + 1) * blocks4 - side * half)
                push = ctv[there, inner] * (mask * jnp.asarray(0.5, BF16))
                grad = push.astype(F32) * (rise + value * (1.0 - bend))
                ctv[there, inner] = grad.astype(BF16)
                sums, bends = carry
                return sums + fold(grad), bends + fold(grad * y)

            vecs[:, lanes], vecs2[:, lanes] = lax.fori_loop(
                0, line // step4, cells, (vecs[:, lanes], vecs2[:, lanes])
            )
        dn_copy(t, 0).start()
        dn_copy(t, 1).start()
        return carry

    lax.fori_loop(0, nh, last, 0)
    sum_grad = total_row(vecs[...])
    back3 = Everywhere("b3")
    put(rows16, 0, sum_grad)
    put(rows16, 8, scale3 * (total_row(vecs2[...]) - mean3 * sum_grad))
    back3.at[...] = rows16[...].astype(BF16)
    back3.start()

    w3p[...] = (w3[...].astype(F32) * grow3).astype(BF16)

    acc_c[...] = jnp.zeros((wd, cin), F32)

    def plain_back(t, carry):
        grad = grad_of(t)
        dm[line_rows(t), :] = dot_nt(grad, w3p[...])
        acc_c[...] += dot(mix_t[t], grad)
        return carry

    lax.fori_loop(0, nh, plain_back, 0)
    w_finish(5, 2)
    got = back3.finish()
    bias3, gain3 = get(got, 0, cin), get(got, 8, cin)
    put(small.at[0], 0, bias3)
    put(small.at[0], 8, gain3)
    all_wide = wide(total, cin)
    slant3 = scale3 * gain3 / all_wide
    level3 = bias3 / all_wide - mean3 * slant3
    fix = (w3[...].astype(F32) * slant3).astype(BF16)
    level_high, level_low = split_bf16(level3)
    levels = [jnp.broadcast_to(part, (16, cin)) for part in (level_high, level_low)]
    stack = dot_nt(jnp.concatenate([fix, *levels], axis=0), w3p[...])
    fix = stack[0:wd, :].astype(BF16)
    shift = stack[wd : wd + 1, :] + stack[wd + 16 : wd + 17, :]

    def back_mix(t, carry):
        at = line_rows(t)
        dm[at, :] = dm[at, :] - dot(mixed[at, :], fix) - mask_of(at, wd) * shift
        return carry

    lax.fori_loop(0, nh, back_mix, 0, unroll=True)

    step5 = 4 * nb
    sums5 = []
    for j in range(lane_blocks):
        lanes = slice(j * LANES, (j + 1) * LANES)

        def image_sums(t, carry):
            at = pl.ds(pl.multiple_of(t * step5, step5), step5)
            grad = dm[at, lanes]
            done = []
            for r in range(d.radix):
                own = slice(r * wd + j * LANES, r * wd + (j + 1) * LANES)
                a, b, c = carry[r]
                a = a + fold_images(grad * act2[at, own].astype(F32), nb)
                part = grad * slope2[at, own].astype(F32)
                b = b + fold_images(part, nb)
                c = c + fold_images(part * y2[at, own].astype(F32), nb)
                done.append((a, b, c))
            return tuple(done)

        sums5.append(lax.fori_loop(0, rows // step5, image_sums, ((zero, zero, zero),) * d.radix, unroll=7))
    pick = lambda which: jnp.concatenate(
        [sums5[j][r][which] for r in range(d.radix) for j in range(lane_blocks)], axis=1
    )
    q1, q3 = pick(1), pick(2)

    def dn_out(t, carry):
        dn_copy(t, 0).wait()
        dn_copy(t, 1).wait()
        return carry

    lax.fori_loop(0, nh, dn_out, 0)
    clear(dyp)
    ga_src[...] = pick(0).astype(BF16)
    ga_start, ga_finish = swap(ga_src, ga_buf, ssa.at[1], rsa.at[1], ha_peer, n_ha)
    ga_start()

    mix_column = jnp.transpose(jnp.broadcast_to(mix_sum, (LANES, wd)))
    for j in range(cin // LANES):
        lanes = slice(j * LANES, (j + 1) * LANES)
        c = 0 if j * LANES < half else 1
        grad = grow3[:, lanes] * (
            acc_c[:, lanes] - mix_column * level3[:, lanes] - acc_g[0, :, lanes] * slant3[:, lanes]
        )
        parts[2][c, :, j * LANES - c * half : (j + 1) * LANES - c * half] = grad.astype(BF16)
    w_start(2, 0)

    grad_att = ga_finish()
    weight = att[...]
    weighed = weight * grad_att
    both = weighed[:, 0:wd] + weighed[:, wd:]
    grad_logits = weight * (grad_att - jnp.concatenate([both, both], axis=1))
    grad_fc = add_thirds(dot_nt(thirds(grad_logits), wex[...])) * hidden_slope
    put(fc_src.at[1], 0, total_row(grad_fc))
    put(fc_src.at[1], 1, total_row(grad_fc * centered))
    pooled = pool / wide(floor, wd)
    put(fc_src.at[1], 2, total_row(pooled))
    fc_start, fc_finish = swap(fc_src.at[1], fc_buf.at[1], ssi.at[1], rsi.at[1], img_peer, n_img)
    fc_start()
    w_step(2, 0)
    grad_excite = dot_tn(hidden, grad_logits, HIGH)
    grad_bex = total_row(grad_logits) * (1.0 / n_ha)
    got = fc_finish()
    bias_s, gain_s = got[0:1, :], got[1:2, :]
    put(small.at[0], 16, bias_s)
    put(small.at[0], 17, gain_s)
    grad_squeezed = (gs[...] * scale_s) * (
        grad_fc - live_now * (bias_s + centered * gain_s) / images
    )
    grad_pool = add_thirds(dot_nt(thirds(grad_squeezed), wsq[...])) / wide(floor, wd)
    pool2 = jnp.concatenate([grad_pool] * d.radix, axis=1)
    sum_grad = total_row(weight * q1 + pool2 * q2[...])
    sum_bend = total_row(weight * q3 + pool2 * q4[...])
    back2 = Everywhere("b2")
    put(back2.at, 0, sum_grad)
    put(back2.at, 4, scale2 * (sum_bend - mean2 * sum_grad))
    back2.start()
    level = get(got, 2, wd) / wide(images, wd)
    grad_squeeze = dot_tn(pooled - level, grad_squeezed, HIGH)
    grow2 = g2[...] * scale2
    att[...] = weight * grow2
    q2[...] = pool2 * grow2
    def first_slopes(t, carry):
        at = pl.ds(pl.multiple_of(t * step1, step1), step1)
        _, slope = gate(y1[at, :] * half_a1 + half_b1)
        mixed[at, :] = (slope * mask_of(at, mid)).astype(BF16)
        return carry

    lax.fori_loop(0, rows // step1, first_slopes, 0)

    parts[4][0] = jnp.concatenate([grad_excite[:, 0:wd], grad_excite[:, wd:]], axis=0).astype(
        BF16
    ) * jnp.asarray(1.0 / n_ha, BF16)
    parts[4][1, :, 0 : d.inter] = grad_squeeze.astype(BF16)
    parts[4][1, :, d.inter :] = jnp.zeros((wd, wd - d.inter), BF16)
    w_start(4, 0)
    w_step(2, 1)
    acc_g[...] = jnp.zeros((d.radix, wd, 9 * gin), F32)
    mean_act1 = get(act_sum.finish(), 0, mid) / (wide(images, mid) * float(nh * n_ha * nw))
    w_step(4, 0)
    got = back2.finish()
    bias2, gain2 = get(got, 0, wide2), get(got, 4, wide2)
    put(small.at[0], 20, bias2)
    put(small.at[0], 24, gain2)
    slant2 = grow2 * scale2 * gain2 / wide(total, wide2)
    lift2 = grow2 * bias2 / wide(total, wide2)
    level2 = lift2 - mean2 * slant2
    own_pixels = wide(total_row(pixels), wide2)
    own_sum = jnp.concatenate([total_row(s) for s, _ in sums2], axis=1)
    sum_dy2 = grow2 * sum_grad - lift2 * own_pixels - slant2 * (own_sum - mean2 * own_pixels)
    misc = Everywhere("misc")
    put(misc.at, 0, sum_dy2)
    put(misc.at, 4, grad_bex)
    misc.start()
    sum_dy2 = [sum_dy2[:, r * wd : (r + 1) * wd] for r in range(d.radix)]

    step6 = 2 * nb

    def back_group(t, carry):
        def cells(u, carry):
            at = block_rows(t, u, step6)
            to = inner_rows(t + 1, nb + u * step6, step6)
            again = step6 // nb
            grad = dm[at, :]
            mask = mask_of(at, wd)
            for r in range(d.radix):
                own = slice(r * wd, (r + 1) * wd)
                grow = jnp.concatenate([att[:, own]] * again, axis=0)
                lift = jnp.concatenate([q2[:, own]] * again, axis=0)
                push = (grow * grad + lift) * slope2[at, own].astype(F32)
                pull = mask * (level2[:, own] + slant2[:, own] * y2[at, own].astype(F32))
                dyp[to, own] = (push - pull).astype(BF16)
            return carry

        return lax.fori_loop(0, line // step6, cells, carry, unroll=7)

    edges(back_group, 0)
    halo2_start, halo2_recv, halo2_sent = halo(dyp, 1)
    halo2_start()
    lax.fori_loop(1, nh - 1, back_group, 0)
    w_step(2, 2)
    w_step(4, 1)

    def weights_group(t, carry):
        for r in range(d.radix):
            grad = jnp.transpose(dyp[inner_rows(t + 1), r * wd : (r + 1) * wd])
            acc_g[r] += dot(grad, taps(t, r))
        return carry

    lax.fori_loop(0, nh, weights_group, 0, unroll=True)

    def send_group(s, first, last):
        lanes = (last - first) * gin
        for r in range(d.radix):
            base = wide(mean_act1[:, r * gin : (r + 1) * gin], lanes)
            column = jnp.transpose(jnp.broadcast_to(sum_dy2[r], (LANES, wd)))
            grad = acc_g[r, :, first * gin : last * gin] - wide(column, lanes) * base
            parts[s][r, :, 0:lanes] = grad.astype(BF16)
        w_start(s, 0)

    send_group(1, 0, d.split)
    send_group(3, d.split, 9)
    w_step(2, 3)
    w_step(4, 2)

    pairs = nw // 2

    def back_taps(t, r, which):
        cells = []
        for ky in range(3):
            for e in which:
                block = dyp[inner_rows(t + 2 - ky, e * nb), r * wd : (r + 1) * wd]
                block = block.reshape(pairs, 2 * nb, wd)[:, 0:nb, :].reshape(pairs * nb, wd)
                cells.append(block)
        return jnp.concatenate(cells, axis=1)

    def transposed(t, carry):
        sums, bends = carry
        at = line_rows(t)
        done = []
        for r in range(d.radix):
            both = dot_nt(back_taps(t, r, (1, 2)), w2x[r])
            left = both[:, 0:gin] + dot_nt(back_taps(t, r, (0,)), w2l[r])
            right = both[:, gin:] + dot_nt(back_taps(t, r, (3,)), w2r[r])
            both = jnp.concatenate(
                [left.reshape(pairs, nb, gin), right.reshape(pairs, nb, gin)], axis=1
            )
            done.append(both.reshape(line, gin))
        dm[at, :] = jnp.concatenate(done, axis=1)

        def cells(u, carry):
            sums, bends = carry
            at = block_rows(t, u, step1)
            grad = dm[at, :] * mixed[at, :].astype(F32)
            dm[at, :] = grad
            mixed[at, :] = grad.astype(BF16)
            return sums + fold(grad), bends + fold(grad * y1[at, :])

        return lax.fori_loop(0, line // step1, cells, (sums, bends))

    zeros = jnp.zeros((8, mid), F32)
    middle = 1 + (nh - 2) // 3
    sums1 = lax.fori_loop(1, middle, transposed, (zeros, zeros))
    w_step(1, 0)
    w_step(3, 0)
    sums1 = lax.fori_loop(middle, nh - 1, transposed, sums1)
    w_step(4, 3)
    halo2_recv()
    sums1 = edges(transposed, sums1)
    sum_grad = total_row(sums1[0])
    back1 = Everywhere("b1")
    put(back1.at, 0, sum_grad)
    put(back1.at, 2, scale1 * (total_row(sums1[1]) - mean1 * sum_grad))
    back1.start()
    halo2_sent()

    def fetch_back(t, carry):
        dn_back(t, 0).start()
        dn_back(t, 1).start()
        return carry

    lax.fori_loop(0, nh, fetch_back, 0)

    acc_c[...] = jnp.zeros((wd, cin), F32)

    def first_weights(t, carry):
        at = line_rows(t)
        acc_c[...] += dot_tn(mixed[at, :], xv[at, :])
        return carry

    lax.fori_loop(0, nh, first_weights, 0, unroll=True)
    if d.inside:
        for c in range(2):
            parts[0][c] = acc_c[:, c * half : (c + 1) * half].astype(BF16)
    w_start(0, 0)
    w_step(1, 1)
    w_step(0, 0)
    w_step(3, 1)
    got = back1.finish()
    bias1, gain1 = get(got, 0, mid), get(got, 2, mid)
    grow1 = g1[...] * scale1
    bias_all, gain_all = bias1 / wide(total, mid), gain1 / wide(total, mid)
    slant1 = grow1 * scale1 * gain_all
    level1 = grow1 * bias_all - mean1 * slant1
    w_step(2, 4)
    w_step(4, 4)

    def back_first(t, carry):
        def cells(u, carry):
            at = block_rows(t, u, step1)
            pull = mask_of(at, mid) * (level1 + slant1 * y1[at, :])
            mixed[at, :] = (grow1 * dm[at, :] - pull).astype(BF16)
            return carry

        lax.fori_loop(0, line // step1, cells, 0)
        return carry

    lax.fori_loop(0, nh, back_first, 0)
    put(small.at[0], 32, bias1)
    put(small.at[0], 34, gain1)
    put(small.at[0], 36, mean_act1)
    small[0, 18:20, :] = jnp.zeros((2, LANES), F32)
    small[0, 38:40, :] = jnp.zeros((2, LANES), F32)
    small[0, 44:48, :] = jnp.zeros((4, LANES), F32)
    got = misc.finish()
    put(small.at[0], 28, get(got, 4, wide2))
    put(small.at[0], 40, get(got, 0, wide2))
    got = v0_sum.finish()
    for c in range(2):
        v0[c] = jnp.broadcast_to(get(got, 0, cin)[:, c * half : (c + 1) * half], (8, half))
    for j, vector in enumerate((grow1, bias_all, gain_all)):
        cols[j] = jnp.transpose(jnp.broadcast_to(vector, (LANES, mid)))

    def norm_terms(total, at, taken, flat):
        lanes = total.shape[1]
        grow, level, slant = (wide(cols[j, at, :], lanes) for j in range(3))
        return grow * (total - level * flat - slant * taken)

    def fix_first(total):
        return norm_terms(total, z_at(z_of, spot * plane_rows), vres[...], v0[core, 0:1, :])

    def grad_inputs(t, carry):
        at = line_rows(t)
        for c in range(2):
            lanes = slice(c * half, (c + 1) * half)
            dn_back(t, c).wait()
            grad = ctv[half_rows(t, c), :].astype(F32) + dot_nt(mixed[at, :], w1[lanes, :])
            xv[at, lanes] = grad.astype(BF16)
        return carry

    w_step(1, 2)
    lax.fori_loop(0, nh // 2, grad_inputs, 0)
    w_step(3, 2)
    w_step(0, 1)
    w_step(1, 3)
    w_step(3, 3)
    w_step(0, 2, fix_first)
    lax.fori_loop(nh // 2, nh, grad_inputs, 0)
    w_step(1, 4)
    w_step(0, 3)
    w_step(3, 4)
    w_step(0, 4)
    for s in (2, 4, 1, 3, 0):
        w_step(s, 5)
    if not d.inside:
        whole = slice(0, wd)
        for c in range(2):
            lanes = slice(c * half, (c + 1) * half)
            local = wide(cols[0, whole, :], half) * (
                acc_c[:, lanes]
                - wide(cols[1, whole, :], half) * get(v0_sum.at[...], 0, cin)[:, lanes]
                - wide(cols[2, whole, :], half) * parts[5][c].astype(F32)
            )
            parts[0][c] = local.astype(BF16)

    for s in range(d.sets + 1):
        w_sent(s)
    halo1_sent()
    if not d.inside:
        for s in range(d.sets):
            ress[s][...] = parts[s][...]


def call_block(d, args):
    f32, bf16 = F32, BF16
    cin, wd, mid, rows, nb, nh = d.cin, d.width, d.mid, d.rows, d.nb, d.nh
    vmem, dma = pltpu.VMEM, pltpu.SemaphoreType.DMA
    halves = [(2, wd, lanes) for lanes in d.half]
    shape = jax.ShapeDtypeStruct
    outs = [
        shape((rows, cin), bf16),
        vmem((rows, cin), bf16),
        vmem((rows, cin), bf16),
        *[vmem(s, bf16) for s in halves[: d.sets]],
        vmem((1, 48, LANES), f32),
    ]
    anywhere = pl.BlockSpec(memory_space=pl.ANY)
    inside = pl.BlockSpec(memory_space=pltpu.VMEM)
    plane, zed = wd // 4, wd // 16

    def sums_of(name, count):
        kind = bf16 if name in d.narrow else f32
        if not d.inside:
            return dict(
                src=vmem((count, LANES), kind),
                mid=vmem((count, LANES), f32),
                buf_ha=vmem((d.n_ha, count, LANES), kind),
                buf_img=vmem((d.n_img, count, LANES), f32),
                send_ha=dma((d.n_ha,)), recv_ha=dma((d.n_ha,)),
                send=dma((d.n_img,)), recv=dma((d.n_img,)),
            )
        if name in d.paired:
            return dict(
                src=vmem((count, LANES), kind),
                mid=vmem((count, LANES), f32),
                other=vmem((count, LANES), f32),
                buf=vmem((16, count, LANES), f32),
                send=dma((16,)), recv=dma((16,)),
            )
        return dict(
            src=vmem((count, LANES), kind),
            buf=vmem((32, count, LANES), kind),
            send=dma((32,)), recv=dma((32,)),
        )

    scratch = [
        vmem((cin, mid), bf16),
        vmem((d.radix, 9 * d.gin, wd), bf16),
        vmem((wd, cin), bf16),
        vmem((rows, LANES), bf16),
        vmem((nb, LANES), f32),
        vmem((max(2 * rows, (nh + 2) * d.padded), cin // 2), bf16),
        vmem((rows, mid), f32),
        vmem(((nh + 2) * d.padded, mid), bf16),
        vmem((rows, d.wide), bf16),
        vmem((rows, d.wide), bf16),
        vmem((rows, d.wide), bf16),
        vmem((rows, wd), bf16),
        vmem((rows, wd), f32),
        vmem((wd, cin), f32),
        vmem((d.radix, wd, 9 * d.gin), f32),
        vmem((wd, cin), bf16),
        vmem((d.radix, 2 * d.gin, 6 * wd), bf16),
        vmem((d.radix, d.gin, 3 * wd), bf16),
        vmem((d.radix, d.gin, 3 * wd), bf16),
        vmem((nh, wd, d.line), bf16),
        vmem((16, LANES), f32),
        vmem((nb, d.wide), f32),
        vmem((nb, d.wide), f32),
        vmem((nb, d.wide), f32),
        vmem((8, cin), f32),
        vmem((8, cin), f32),
        vmem((nb, wd), f32),
        vmem((2, 8, cin // 2), f32),
        vmem((3, mid, LANES), f32),
        [vmem(s, bf16) for s in halves],
        [vmem((wd, lanes), bf16) for lanes in d.half],
        [vmem((3, plane, lanes), bf16) for lanes in d.half],
        [vmem((3, zed, lanes), bf16) for lanes in d.half],
        [vmem((plane, lanes), bf16) for lanes in d.half],
        vmem((zed, d.half[0]), f32),
        {name: sums_of(name, count) for name, count in d.sums.items() if name not in d.shared},
        vmem((nb, d.wide), bf16),
        vmem((d.n_ha, nb, d.wide), bf16),
        vmem((nb, 2 * LANES), f32),
        vmem((d.n_ha, nb, 2 * LANES), f32),
        vmem((2, 4, LANES), f32),
        vmem((2, d.n_img, 4, LANES), f32),
        dma((3,)),
        dma((nh,)),
        dma((2, nh)),
        dma((2, nh)),
        dma((2, nh)),
        dma((2, d.n_ha)),
        dma((2, d.n_ha)),
        dma((2, d.n_img)),
        dma((2, d.n_img)),
        dma((2, 2)),
        dma((2, 2)),
        dma((6, 24)),
        dma((6, 24)),
    ]
    return pl.pallas_call(
        functools.partial(block_kernel, d),
        out_shape=outs,
        in_specs=[anywhere, anywhere, inside, pl.BlockSpec(memory_space=pltpu.SMEM)]
        + [anywhere, inside, inside, anywhere] + [inside] * 7 + [anywhere, inside, inside],
        out_specs=[anywhere] + [inside] * 8,
        scratch_shapes=scratch,
        name="block",
        compiler_params=pltpu.CompilerParams(
            collective_id=0, has_side_effects=True, vmem_limit_bytes=47 << 20
        ),
    )(*args)


def finish_kernel(
    d, out_in, gin_in, wg0, wg1, wg2, wg3, wg4, small,
    out, gin_hbm, gw1_hbm, gg1, gb1, gw2_hbm, gg2, gb2, gwsq, ggs, gbs, gwex, gbex, gw3_hbm, gg3, gb3,
    gw1, gw2, gw3, sem_out, sem_gw,
):
    wd = d.width
    parts = 4
    copies = [
        pltpu.make_async_copy(src.at[at], dst.at[at], sem_out.at[which, t])
        for which, (src, dst) in enumerate(((out_in, out), (gin_in, gin_hbm)))
        for t in range(parts)
        for at in (pl.ds(t * (d.rows // parts), d.rows // parts),)
    ]
    for copy in copies:
        copy.start()
    stores = [
        pltpu.make_async_copy(src, dst, sem_gw.at[j])
        for j, (src, dst) in enumerate(((gw1, gw1_hbm), (gw3, gw3_hbm), (gw2, gw2_hbm)))
    ]

    def weights(step):
        half = d.cin // 2
        if step < 2:
            gw1[step * half : (step + 1) * half, :] = jnp.transpose(wg0[step]).astype(F32)
            gw3[:, step * half : (step + 1) * half] = wg2[step].astype(F32)
        elif step < 4:
            r = step - 2
            rows = small[0]
            mean = get(rows, 36, d.mid)[:, r * d.gin : (r + 1) * d.gin]
            taken = get(rows, 40, d.wide)[:, r * wd : (r + 1) * wd]
            mean = jnp.transpose(jnp.broadcast_to(mean, (LANES, d.gin)))
            back = wide(mean, wd) * taken
            for tap in range(9):
                held, first = (wg1, 0) if tap < d.split else (wg3, d.split)
                cells = held[r, :, (tap - first) * d.gin : (tap - first + 1) * d.gin]
                gw2[r, tap] = jnp.transpose(cells).astype(F32) + back
        elif step == 4:
            cells = wg4[0].astype(F32)
            gwex[:, 0:wd] = cells[0 : d.inter, :]
            gwex[:, wd:] = cells[d.inter :, :]
            gwsq[...] = wg4[1, :, 0 : d.inter].astype(F32)
            rows = small[0]
            gb3[...] = get(rows, 0, d.cin)
            gg3[...] = get(rows, 8, d.cin)
            gbs[...] = rows[16:17, :]
            ggs[...] = rows[17:18, :]
            gb2[...] = get(rows, 20, d.wide)
            gg2[...] = get(rows, 24, d.wide)
            gbex[...] = get(rows, 28, d.wide)
            gb1[...] = get(rows, 32, d.mid)
            gg1[...] = get(rows, 34, d.mid)

    for t in range(5):
        weights(t)
        if t == 1:
            stores[0].start()
            stores[1].start()
        elif t == 3:
            stores[2].start()
    for copy in stores + copies:
        copy.wait()


def call_finish(d, *args):
    shape = jax.ShapeDtypeStruct
    cin, wd, mid = d.cin, d.width, d.mid
    vmem, dma = pltpu.VMEM, pltpu.SemaphoreType.DMA
    small_dims = [
        (cin, mid), (1, mid), (1, mid), (d.radix, 9, d.gin, wd), (1, d.wide), (1, d.wide), (wd, d.inter),
        (1, d.inter), (1, d.inter), (d.inter, d.wide), (1, d.wide), (wd, cin), (1, cin), (1, cin),
    ]
    anywhere = pl.BlockSpec(memory_space=pl.ANY)
    inside = pl.BlockSpec(memory_space=pltpu.VMEM)
    return pl.pallas_call(
        functools.partial(finish_kernel, d),
        out_shape=[shape((d.rows, cin), BF16), shape((d.rows, cin), BF16)]
        + [shape(s, F32) for s in small_dims],
        in_specs=[inside] * 8,
        out_specs=[anywhere] * 3 + [inside] * 2 + [anywhere] + [inside] * 7 + [anywhere] + [inside] * 2,
        scratch_shapes=[
            vmem((cin, mid), F32), vmem((d.radix, 9, d.gin, wd), F32), vmem((wd, cin), F32),
            dma((2, 4)), dma((3,)),
        ],
        name="finish",
        compiler_params=pltpu.CompilerParams(vmem_limit_bytes=16 << 20),
    )(*[pltpu.with_memory_space_constraint(arg, pltpu.VMEM) for arg in args])


def on_device(
    inputs, image_count, pixel_mask, w_first, gain_first, bias_first, w_group, gain_group, bias_group,
    w_squeeze, gain_squeeze, bias_squeeze, w_excite, bias_excite, w_last, gain_last, bias_last, cotangent,
):
    n_img, n_ha = lax.axis_size("img"), lax.axis_size("ha")
    d = Dims(n_img, n_ha, inputs.shape, w_group.shape, w_squeeze.shape)
    nb, nh, nw, cin = inputs.shape

    def by_rows(cells):
        return jnp.transpose(cells, (1, 2, 0, 3)).reshape(d.rows, cin)

    def by_image(cells):
        return jnp.transpose(cells.reshape(nh, nw, nb, cin), (2, 0, 1, 3))

    row = lambda v: v.reshape(1, -1)
    args = (
        by_rows(inputs), by_rows(cotangent), jnp.transpose(pixel_mask, (1, 0, 2)), image_count,
        w_first, row(gain_first), row(bias_first),
        w_group.reshape(d.radix, 9 * d.gin, d.width), row(gain_group), row(bias_group),
        w_squeeze, row(gain_squeeze), row(bias_squeeze), w_excite, row(bias_excite),
        w_last, row(gain_last), row(bias_last),
    )
    _, out, gin, *sets, small = call_block(d, args)
    if not d.inside:
        sets = lax.psum(sets, ("img", "ha"))
    done = call_finish(d, out, gin, *sets, small)
    (out, gin, gw1, gg1, gb1, gw2, gg2, gb2, gwsq, ggs, gbs, gwex, gbex, gw3, gg3, gb3) = done
    flat = lambda v: v.reshape(-1)
    return (
        by_image(out), by_image(gin), gw1, flat(gg1), flat(gb1), gw2.reshape(w_group.shape), flat(gg2), flat(gb2),
        gwsq, flat(ggs), flat(gbs), gwex, flat(gbex), gw3, flat(gg3), flat(gb3),
    )


def solution(mesh):
    cells = P("img", "ha", None, None)
    placed = (cells, P("img"), P("img", "ha", None)) + (P(),) * 14 + (cells,)
    return jax.shard_map(
        on_device,
        mesh=mesh,
        in_specs=placed,
        out_specs=(cells, cells) + (P(),) * 14,
        check_vma=False,
    )
```
